32 devices in a mesh: head: 4 (over y, x), seq: 8 (over z, core).
Axes of the slice: x: 2, y: 2, z: 4, core: 2. Of those that a mesh axis runs over, the one named last changes fastest.
Arguments:
- tokens: bfloat16 [4, 1024, 1024], P('head', 'seq'), may hold values from -6 to 6
- w_query: bfloat16 [1024, 1024], P(('head', 'seq')), may hold values from -0.1875 to 0.1875
- w_key: bfloat16 [1024, 1024], P(('head', 'seq')), may hold values from -0.1875 to 0.1875
- w_value: bfloat16 [1024, 1024], P(('head', 'seq')), may hold values from -0.1875 to 0.1875
- w_out: bfloat16 [1024, 1024], P(('head', 'seq')), may hold values from -0.75 to 0.75
- w_gate: bfloat16 [1024, 1024], P(('head', 'seq')), may hold values from -0.1875 to 0.1875
- persist_keys: bfloat16 [16, 1024], P(None, ('head', 'seq')), may hold values from -5 to 5
- persist_values: bfloat16 [16, 1024], P(None, ('head', 'seq')), may hold values from -5 to 5
- norm_gain: bfloat16 [1024], P(('head', 'seq')), may hold values from 0.5 to 1.5
- ff_gate: bfloat16 [1024, 2816], P(('head', 'seq')), may hold values from -0.1875 to 0.1875
- ff_up: bfloat16 [1024, 2816], P(('head', 'seq')), may hold values from -0.1875 to 0.1875
- ff_down: bfloat16 [2816, 1024], P(('head', 'seq')), may hold values from -0.109375 to 0.109375
- retention: float32 [4, 1024, 8], P(None, 'seq', 'head'), may hold values from 0.4 to 1
- doc_starts: int32 [4, 6], replicated, may hold values from 0 to 1024, as said below
- valid: int32 [4, 1024], P('head', 'seq'), may hold values from 0 to 1
- teacher: bfloat16 [4, 1024, 1024], P('head', 'seq'), may hold values from -4 to 4
Outputs:
- output: bfloat16 [4, 1024, 1024], P('head', 'seq')
- loss: float32 [], replicated
- grad_tokens: float32 [4, 1024, 1024], P('head', 'seq')
- grad_w_query: float32 [1024, 1024], P(('head', 'seq'))
- grad_w_key: float32 [1024, 1024], P(('head', 'seq'))
- grad_w_value: float32 [1024, 1024], P(('head', 'seq'))
- grad_w_out: float32 [1024, 1024], P(('head', 'seq'))
- grad_w_gate: float32 [1024, 1024], P(('head', 'seq'))
- grad_persist_keys: float32 [16, 1024], P(None, ('head', 'seq'))
- grad_persist_values: float32 [16, 1024], P(None, ('head', 'seq'))
- grad_norm_gain: float32 [1024], P(('head', 'seq'))
- grad_ff_gate: float32 [1024, 2816], P(('head', 'seq'))
- grad_ff_up: float32 [1024, 2816], P(('head', 'seq'))
- grad_ff_down: float32 [2816, 1024], P(('head', 'seq'))
The draws below stay inside these ranges and needn't reach their ends.
Inputs may be any that keep to these rules, and one draw needn't show every extreme that they name: `doc_starts`: per sequence the starts of its documents in increasing order, beginning with 0; unused entries equal 1024. Every document except a sequence's last has 200 to max(512, 200) positions; one sequence is a single document.
All inputs are finite; a program needn't handle non-finite values.
Results may differ from the reference program's by a relative error of at most 0.018.
Values may be sent and summed in bfloat16 or wider, within the bound.
A program may use at most 256 MiB of HBM per device.

```python
import math
import jax
import jax.numpy as jnp
from jax import lax

HEAD_COUNT = 8
HD = 128
FF = 2816
P_SIZE = 16
BLK = 128
DOC_MIN = 200
D = 1024
SEQUENCE_TOTAL = 4
SEQUENCE_LENGTH = 1024
NDOC = 6


def draw_retention(key, part):
    key = jax.random.fold_in(key, 11)
    key_entries = jax.random.split(key, 7)
    share = 0.5
    slow = jax.random.uniform(key_entries[0], (SEQUENCE_TOTAL, 1, HEAD_COUNT)) < share
    tau = jnp.exp(jax.random.uniform(key_entries[1], (SEQUENCE_TOTAL, 1, HEAD_COUNT), minval=math.log(20.0), maxval=math.log(50.0)))
    slow_rate = 0.2 * jax.random.uniform(key_entries[2], (SEQUENCE_TOTAL, 1, HEAD_COUNT), minval=0.5, maxval=1.0) / SEQUENCE_LENGTH
    decay_speed = jnp.where(slow, slow_rate, 1.0 / tau)
    blocks = SEQUENCE_LENGTH // BLK
    block_decay_factor = jnp.exp(jax.random.uniform(key_entries[3], (SEQUENCE_TOTAL, blocks, 1, HEAD_COUNT), minval=math.log(0.6), maxval=math.log(1.6)))
    block_decay_factor = jnp.broadcast_to(block_decay_factor, (SEQUENCE_TOTAL, blocks, BLK, HEAD_COUNT)).reshape(SEQUENCE_TOTAL, SEQUENCE_LENGTH, HEAD_COUNT)
    token_decay_factor = jnp.exp(jax.random.uniform(key_entries[4], (SEQUENCE_TOTAL, SEQUENCE_LENGTH, HEAD_COUNT), minval=math.log(0.7), maxval=math.log(1.4)))
    impulse_position = jax.random.randint(key_entries[5], (SEQUENCE_TOTAL, 3, HEAD_COUNT), 0, SEQUENCE_LENGTH)
    impulse_hit = jnp.any(jnp.arange(SEQUENCE_LENGTH)[None, :, None, None] == impulse_position[:, None, :, :], axis=2)
    impulse_amount = jnp.log(jax.random.uniform(key_entries[6], (SEQUENCE_TOTAL, SEQUENCE_LENGTH, HEAD_COUNT), minval=0.5, maxval=0.8))
    log_retention = -decay_speed * block_decay_factor * token_decay_factor + jnp.where(impulse_hit, impulse_amount, 0.0)
    return jnp.exp(log_retention).astype(jnp.float32)


def draw_doc_starts(key, part):
    key = jax.random.fold_in(key, 12)
    key_entries = jax.random.split(key, 2)
    longest = max(SEQUENCE_LENGTH // 2, DOC_MIN)
    spans = jax.random.randint(key_entries[0], (SEQUENCE_TOTAL, NDOC), DOC_MIN, longest + 1)
    ends = jnp.cumsum(spans, axis=1)
    starts = jnp.concatenate([jnp.zeros((SEQUENCE_TOTAL, 1), jnp.int32), ends[:, :-1].astype(jnp.int32)], axis=1)
    starts = jnp.minimum(starts, SEQUENCE_LENGTH)
    whole = jax.random.randint(key_entries[1], (), 0, SEQUENCE_TOTAL)
    single_row = jnp.arange(SEQUENCE_TOTAL)[:, None] == whole
    later_col = jnp.arange(NDOC)[None, :] > 0
    starts = jnp.where(single_row & later_col, SEQUENCE_LENGTH, starts)
    return starts.astype(jnp.int32)


def draw_valid(key, part):
    key = jax.random.fold_in(key, 13)
    positions = jnp.arange(SEQUENCE_LENGTH, dtype=jnp.int32)[None, :]
    level = 300 + 600 * positions // SEQUENCE_LENGTH
    rolled = jax.random.randint(key, (SEQUENCE_TOTAL, SEQUENCE_LENGTH), 0, 1000)
    return (rolled < level).astype(jnp.int32)


def draw_teacher(key, part):
    key = jax.random.fold_in(key, 14)
    values = jnp.clip(jax.random.normal(key, (SEQUENCE_TOTAL, SEQUENCE_LENGTH, D)), -4.0, 4.0)
    return values.astype(jnp.float32).astype(jnp.bfloat16)


def with_spikes(drawn, own_key, source, target, blocks, factor):
    def block_of(axis_at):
        return (jnp.arange(drawn.shape[axis_at]) // (drawn.shape[axis_at] // blocks)).reshape((-1,) + (1,) * (drawn.ndim - 1 - axis_at))

    one_side = jax.random.permutation(own_key, blocks)[block_of(target)]
    second = (block_of(target) + blocks // 2) % blocks
    return jnp.where((block_of(source) == one_side) | (block_of(source) == second), factor * drawn, drawn)


def block_scale(stream_key, extent, cuts, least, high):
    gain, own = 1.0, jax.random.fold_in(stream_key, 6)
    for dim, shards_of in cuts:
        heights = jnp.exp(jax.random.uniform(jax.random.fold_in(own, dim), (shards_of,), jnp.float32, least / len(cuts), high / len(cuts)))
        gain = gain * jnp.repeat(heights, extent[dim] // shards_of).reshape([-1 if axis == dim else 1 for axis in range(len(extent))])
    return gain


def scatter_about(own_key, extent, scale, bound, cuts=(), kind=jnp.bfloat16):
    values = scale * jax.random.normal(own_key, extent, jnp.float32)
    if cuts:
        values = values * block_scale(own_key, extent, cuts, -0.22, 0.18)
    return jnp.clip(values, -bound, bound).astype(kind)


def bell_draw_with(key, shape, scale, reach, cuts, heavy, kind=jnp.bfloat16):
    values = scale * jax.random.normal(key, shape, jnp.float32)
    if cuts:
        values = values * block_scale(key, shape, cuts, -0.22, 0.18)
    return jnp.clip(with_spikes(values, jax.random.fold_in(key, 3), *heavy), -reach, reach).astype(kind)


def setup_inputs(seed: int = 0) -> dict:
    streams_of = jax.random.split(jax.random.key(seed), 17)
    tokens = bell_draw_with(streams_of[0], (SEQUENCE_TOTAL, SEQUENCE_LENGTH, D), 1.0, 6.0, ((0, 4), (1, 8)), (1, 2, 8, 2.0))
    w_query = scatter_about(streams_of[1], (D, D), D ** -0.5, 0.1875, ((0, 32),))
    w_key = scatter_about(streams_of[2], (D, D), D ** -0.5, 0.1875, ((0, 32),))
    w_value = scatter_about(streams_of[3], (D, D), D ** -0.5, 0.1875, ((0, 32),))
    w_out = scatter_about(streams_of[4], (D, D), (D // 16) ** -0.5, 0.75, ((0, 32),))
    w_gate = scatter_about(streams_of[5], (D, D), D ** -0.5, 0.1875, ((0, 32),))
    persist_keys = scatter_about(streams_of[6], (P_SIZE, D), 1.0, 5.0, ((1, 32),))
    persist_values = scatter_about(streams_of[7], (P_SIZE, D), 1.0, 5.0, ((1, 32),))
    norm_gain = jnp.clip(1.0 + 0.1 * jax.random.normal(streams_of[8], (D,), jnp.float32), 0.5, 1.5).astype(jnp.bfloat16)
    ff_gate = scatter_about(streams_of[9], (D, FF), D ** -0.5, 0.1875, ((0, 32),))
    ff_up = scatter_about(streams_of[10], (D, FF), D ** -0.5, 0.1875, ((0, 32),))
    ff_down = scatter_about(streams_of[11], (FF, D), FF ** -0.5, 0.109375, ((0, 32),))
    retention = draw_retention(jax.random.fold_in(streams_of[16], 71), 0)
    doc_starts = draw_doc_starts(jax.random.fold_in(streams_of[16], 71), 0)
    valid = draw_valid(jax.random.fold_in(streams_of[16], 71), 0)
    teacher = draw_teacher(jax.random.fold_in(streams_of[16], 71), 0)
    return {"tokens": tokens, "w_query": w_query, "w_key": w_key, "w_value": w_value, "w_out": w_out, "w_gate": w_gate, "persist_keys": persist_keys, "persist_values": persist_values, "norm_gain": norm_gain, "ff_gate": ff_gate, "ff_up": ff_up, "ff_down": ff_down, "retention": retention, "doc_starts": doc_starts, "valid": valid, "teacher": teacher}


HIGHEST = lax.Precision.HIGHEST
MASKED = -1e+30
EPSILON = 1e-06

@jax.custom_vjp
def low(v):
    return lax.optimization_barrier(v.astype(jnp.bfloat16)).astype(jnp.float32)

@jax.custom_vjp
def low_back(v):
    return v

def low_keep(v):
    return (low(v), None)

def low_pass(kept, grad):
    return (grad,)

def back_keep(v):
    return (v, None)

def back_low(kept, grad):
    return (low(grad),)
low.defvjp(low_keep, low_pass)
low_back.defvjp(back_keep, back_low)

def matmul_high(left, right):
    return jnp.dot(left, right, precision=HIGHEST, preferred_element_type=jnp.float32)

def doc_index(starts, positions):
    return lax.optimization_barrier(jnp.sum((starts[:, None, :] <= positions[None, :, None]).astype(jnp.int32), axis=-1)) - 1

def doc_begin(starts, positions):
    return jnp.any(starts[:, None, :] == positions[None, :, None], axis=-1)

def attend_sequence(queries, key_entries, values, segment, fixed_keys, fixed_values):
    positions = jnp.arange(SEQUENCE_LENGTH, dtype=jnp.int32)
    scale = HD ** (-0.5)

    def one_block(block_args):
        block_queries, block_pos, block_seg = block_args
        scores = low_back(jnp.einsum('qhd,khd->hqk', block_queries, key_entries, precision=HIGHEST) * scale)
        fixed_scores = low_back(jnp.einsum('qhd,phd->hqp', block_queries, fixed_keys, precision=HIGHEST) * scale)
        allowed = (positions[None, :] <= block_pos[:, None]) & (segment[None, :] == block_seg[:, None])
        scores = jnp.where(allowed[None], scores, MASKED)
        joined = jnp.concatenate([fixed_scores, scores], axis=-1)
        shifted = jnp.exp(joined - lax.optimization_barrier(jnp.max(joined, axis=-1, keepdims=True)))
        probs = low(shifted / lax.optimization_barrier(jnp.sum(shifted, axis=-1, keepdims=True)))
        persistent_part = jnp.einsum('hqp,phd->qhd', probs[..., :P_SIZE], fixed_values, precision=HIGHEST)
        return persistent_part + jnp.einsum('hqk,khd->qhd', probs[..., P_SIZE:], values, precision=HIGHEST)
    blocks = SEQUENCE_LENGTH // BLK
    result = lax.map(jax.checkpoint(one_block), (queries.reshape(blocks, BLK, HEAD_COUNT, HD), positions.reshape(blocks, BLK), segment.reshape(blocks, BLK)))
    return result.reshape(SEQUENCE_LENGTH, HEAD_COUNT, HD)

def remember_sequence(queries, key_entries, values, log_retention, segment, begin):
    mem_scale = 0.125 / HD
    index = jnp.arange(BLK)

    def one_block(state, block_args):
        block_q, block_k, block_v, block_keep, block_seg, block_begin = block_args
        running = jnp.cumsum(block_keep, axis=0)
        spread = running[:, None, :] - running[None, :, :]
        linked = (index[None, :] <= index[:, None]) & (block_seg[None, :] == block_seg[:, None])
        decay = jnp.where(linked[:, :, None], jnp.exp(jnp.minimum(spread, 0.0)), 0.0)
        intersection = low_back(jnp.einsum('thd,shd->hts', block_q, block_k, precision=HIGHEST))
        mixing = low(mem_scale * intersection * jnp.transpose(decay, (2, 0, 1)))
        inner = jnp.einsum('hts,shd->thd', mixing, block_v, precision=HIGHEST)
        carried = jnp.where((block_seg == block_seg[0]) & jnp.logical_not(block_begin[0]), 1.0, 0.0)
        factor = jnp.exp(running) * carried[:, None]
        outer = mem_scale * factor[:, :, None] * jnp.einsum('thd,hde->the', block_q, state, precision=HIGHEST)
        tail = jnp.where((block_seg == block_seg[-1])[:, None], jnp.exp(running[-1][None, :] - running), 0.0)
        new_state = factor[-1][:, None, None] * state + jnp.einsum('shd,she->hde', block_k * tail[:, :, None], block_v, precision=HIGHEST)
        return (new_state, inner + outer)
    blocks = SEQUENCE_LENGTH // BLK
    start_state = jnp.zeros((HEAD_COUNT, HD, HD), jnp.float32)
    pieces = (queries.reshape(blocks, BLK, HEAD_COUNT, HD), key_entries.reshape(blocks, BLK, HEAD_COUNT, HD), values.reshape(blocks, BLK, HEAD_COUNT, HD), log_retention.reshape(blocks, BLK, HEAD_COUNT), segment.reshape(blocks, BLK), begin.reshape(blocks, BLK))
    final_state, result = lax.scan(jax.checkpoint(one_block), start_state, pieces)
    return result.reshape(SEQUENCE_LENGTH, HEAD_COUNT, HD)

def forward(tokens_f, query_weight, key_weight, value_weight, out_weight, gate_weight, fixed_key_all, fixed_value_all, gain_weight, ffn_gate, ffn_up, ffn_down, segment, begin, log_retention):
    token_rows = tokens_f.reshape(SEQUENCE_TOTAL * SEQUENCE_LENGTH, D)

    def project_heads(weight):
        return low(low_back(matmul_high(token_rows, weight))).reshape(SEQUENCE_TOTAL, SEQUENCE_LENGTH, HEAD_COUNT, HD)
    queries = project_heads(query_weight)
    keys_all = project_heads(key_weight)
    values_all = project_heads(value_weight)
    gate_pre = low_back(matmul_high(token_rows, gate_weight))
    fixed_keys = fixed_key_all.reshape(P_SIZE, HEAD_COUNT, HD)
    fixed_values = fixed_value_all.reshape(P_SIZE, HEAD_COUNT, HD)

    def one_sequence(seq_args):
        seq_q, seq_k, seq_v, seq_seg, seq_begin, seq_keep = seq_args
        attention_part = attend_sequence(seq_q, seq_k, seq_v, seq_seg, fixed_keys, fixed_values)
        return attention_part + remember_sequence(seq_q, seq_k, seq_v, seq_keep, seq_seg, seq_begin)
    mixed = lax.map(one_sequence, (queries, keys_all, values_all, segment, begin, log_retention))
    joined = low(low_back(mixed)).reshape(SEQUENCE_TOTAL * SEQUENCE_LENGTH, D)
    branch = low_back(matmul_high(joined, out_weight))
    hidden = token_rows + jax.nn.sigmoid(gate_pre) * branch
    normed = hidden * lax.rsqrt(lax.optimization_barrier(jnp.mean(hidden * hidden, axis=-1, keepdims=True)) + EPSILON)
    scaled = low(normed * gain_weight)
    gate_act = low_back(matmul_high(scaled, ffn_gate))
    up_act = low_back(matmul_high(scaled, ffn_up))
    inner = low(jax.nn.silu(gate_act) * up_act)
    final = hidden + low_back(matmul_high(inner, ffn_down))
    return final.reshape(SEQUENCE_TOTAL, SEQUENCE_LENGTH, D)

def reference(tokens, w_query, w_key, w_value, w_out, w_gate, persist_keys, persist_values, norm_gain, ff_gate, ff_up, ff_down, retention, doc_starts, valid, teacher):
    positions = jnp.arange(SEQUENCE_LENGTH, dtype=jnp.int32)
    segment = doc_index(doc_starts, positions)
    begin = doc_begin(doc_starts, positions)
    log_retention = jnp.log(retention)
    primals = tuple((array.astype(jnp.float32) for array in (tokens, w_query, w_key, w_value, w_out, w_gate, persist_keys, persist_values, norm_gain, ff_gate, ff_up, ff_down)))

    def apply(*weights):
        return forward(*weights, segment, begin, log_retention)
    result, pullback = jax.vjp(apply, *primals)
    valid_f = valid.astype(jnp.float32)
    count_valid = jnp.sum(valid_f)
    error = result - teacher.astype(jnp.float32)
    loss = jnp.sum(valid_f[..., None] * error * error) / (2.0 * D * count_valid)
    cotangent = valid_f[..., None] * error * (SEQUENCE_TOTAL * SEQUENCE_LENGTH / count_valid)
    grads = pullback(cotangent)
    return (result.astype(jnp.bfloat16), loss, grads[0], grads[1], grads[2], grads[3], grads[4], grads[5], grads[6], grads[7], grads[8], grads[9], grads[10], grads[11])
```

```python
import functools
import types

import jax
import jax.numpy as jnp
from jax import lax
from jax.experimental import pallas as pl
from jax.experimental.pallas import tpu as pltpu
from jax.sharding import PartitionSpec as P

HEAD_COUNT = 8
HD = 128
P_SIZE = 16


HIGHEST = lax.Precision.HIGHEST
MASKED = -1e30
EPSILON = 1e-06
F32 = jnp.float32
BF16 = jnp.bfloat16
MESH_IDS = pl.DeviceIdType.MESH


def nn(left, right):
    return lax.dot_general(left, right, (((1,), (0,)), ((), ())), preferred_element_type=F32)


def nt(left, right):
    return lax.dot_general(left, right, (((1,), (1,)), ((), ())), preferred_element_type=F32)


def tn(left, right):
    return lax.dot_general(left, right, (((0,), (0,)), ((), ())), preferred_element_type=F32)


def tn_exact(left, right):
    return lax.dot_general(
        left, right, (((0,), (0,)), ((), ())), precision=HIGHEST, preferred_element_type=F32
    )


def nt_exact(left, right):
    return lax.dot_general(
        left, right, (((1,), (1,)), ((), ())), precision=HIGHEST, preferred_element_type=F32
    )


def nn_exact(left, right):
    return lax.dot_general(
        left, right, (((1,), (0,)), ((), ())), precision=HIGHEST, preferred_element_type=F32
    )


def block_rows(index, size):
    return pl.ds(pl.multiple_of(index * size, size), size)


def each(first, last, body):
    def step(index, carry):
        body(index)
        return carry

    lax.fori_loop(first, last, step, 0)


SEQ_FLAGS = dict(
    w1=8, t2=8, p2=8, x=8, wo=8, fgu=8, fd=8, gp=8, mx=8, dm=8, dg=8, rgu=8, rgd=8, rgo=8, gt=8,
    gwa=8, fin2=8,
)
XY_FLAGS = dict(t1=4, p1=4, w2=4, fx=4, wox=4, sc=4, y=4, df=4, ds=4, gwo=4, gw=4, gfx=4, fin1=4)
FLAGS = SEQ_FLAGS | XY_FLAGS


def scratch_table(width, tokens, hidden, hidden_pad, length):
    seqs, blocks, block = 4, 8, 128
    table = dict(
        x_all=((length, width), BF16),
        wcs=((blocks, 32, 512), BF16),
        wqk=((width, 512), BF16),
        t1=((4, 8, 128), F32),
        p1=((4, 32, 128), BF16),
        t2s=((16, 128), F32),
        t2=((8, 16, 128), F32),
        p2=((8, 32, 128), BF16),
        fs=((4, 2, 32, hidden_pad), BF16),
        fgu=((2, 4, 256, hidden_pad), BF16),
        fdp=((8, 96, width), BF16),
        ffd=((hidden_pad, width), BF16),
        wo_all=((width, width), BF16),
        q=((length, HD), BF16),
        k=((length, HD), BF16),
        v=((length, HD), BF16),
        gps=((length, HD), BF16),
        fkv=((32, HD), BF16),
        gain=((1, width), F32),
        rrow=((1, length), F32),
        rcol=((block, 8), F32),
        probs=((length, length), BF16),
        decay=((length, length), BF16),
        both=((length, length), BF16),
        fprobs=((length, P_SIZE), BF16),
        mxs=((length, HD), BF16),
        mx=((block, width), BF16),
        gp=((block, width), BF16),
        hid=((block, width), F32),
        br=((block, width), F32),
        inv=((block, 128), F32),
        own=((block, width), F32),
        dout=((block, width), F32),
        sc=((4 * block, width), BF16),
        gact=((4 * block, hidden_pad), F32),
        uact=((4 * block, hidden_pad), F32),
        inner=((4 * block, hidden_pad), BF16),
        ysend=((4, block, width), BF16),
        yrecv=((4, block, width), BF16),
        df=((4 * block, width), BF16),
        dga=((4 * block, hidden_pad), BF16),
        dua=((4 * block, hidden_pad), BF16),
        dbr=((block, width), BF16),
        dgt=((block, width), BF16),
        dms=((block, width), BF16),
        dm=((length, HD), BF16),
        dq=((length, 512), BF16),
        ggain=((1, width), F32),
        gus=((4, 2, 2, 4, 32, hidden_pad), BF16),
        gur=((4, 2, 4, 32, hidden_pad), BF16),
        guz=((4, 2, 4, 32, hidden_pad), BF16),
        gux=((4, 2, 32, hidden_pad), BF16),
        guxr=((4, 2, 32, hidden_pad), BF16),
        gds=((4, 2, 96, width), BF16),
        gdr=((4, 96, width), BF16),
        gdz=((4, 96, width), BF16),
        gwos=((4, 256, width), BF16),
        gwor=((4, 256, width), BF16),
        gos=((4, 2, 32, width), BF16),
        gor=((4, 32, width), BF16),
        goz=((4, 32, width), BF16),
        gws=((4, 256, 512), BF16),
        gwr=((4, 256, 512), BF16),
        gas=((8, 32, 512), BF16),
        gar=((8, 32, 512), BF16),
        gts=((4, 2, block, width), BF16),
        gtr=((4, block, width), BF16),
        pgrad=((32, HD), F32),
        fin0=((48, 128), F32),
        fin1=((4, 48, 128), F32),
        fin2s=((48, 128), F32),
        fin2=((8, 48, 128), F32),
    )
    return table


def block_kernel(names, width, hidden, ndoc, *refs):
    (
        tok, wq, wk, wv, wo, wg, fgi, fui, fdi, tea, tile, pin, vcol, docs,
        out_o, gtok_o, gq_o, gk_o, gv_o, gwo_o, gwg_o, fin_o, pers_o, fg_o, fu_o, fd_o,
    ) = refs[:26]
    m = types.SimpleNamespace(**dict(zip(names, refs[26 : 26 + len(names)])))
    sems = refs[26 + len(names) :]
    s = types.SimpleNamespace(**dict(zip(FLAGS, zip(sems[0::2], sems[1::2]))))
    pad = m.ffd.shape[0]
    length = m.x_all.shape[0]
    scale = HD ** (-0.5)
    mem_scale = 0.125 / HD

    a = lax.axis_index("head")
    b = lax.axis_index("seq")
    z = lax.div(b, 2)
    c = lax.rem(b, 2)
    sib = 2 * z + 1 - c

    def copy(src, dst, ssem, rsem, device):
        return pltpu.make_async_remote_copy(
            src_ref=src, dst_ref=dst, send_sem=ssem, recv_sem=rsem,
            device_id=device, device_id_type=MESH_IDS,
        )

    def seq_peers(body):
        each(1, 8, lambda step: body(lax.rem(b + step, 8)))

    def xy_peers(body):
        each(1, 4, lambda step: body(lax.rem(a + step, 4)))

    def z_peers(body):
        each(1, 4, lambda step: body(lax.rem(z + step, 4)))

    def seq_copy(pair, src, dst, peer, slot=None):
        slot = peer if slot is None else slot
        return copy(src, dst, pair[0].at[peer], pair[1].at[slot], (a, peer))

    def seq_start(pair, src, dst, peer):
        seq_copy(pair, src, dst, peer, b).start()

    def seq_wait(pair, dst, peer):
        seq_copy(pair, dst, dst, peer).wait_recv()

    def xy_copy(pair, src, dst, peer, slot=None):
        slot = peer if slot is None else slot
        return copy(src, dst, pair[0].at[peer], pair[1].at[slot], (peer, b))

    def xy_start(pair, src, dst, peer):
        xy_copy(pair, src, dst, peer, a).start()

    def xy_wait(pair, dst, peer):
        xy_copy(pair, dst, dst, peer).wait_recv()

    finals = []

    def seq_drain(pair, view):
        finals.append(lambda: seq_peers(lambda p: seq_copy(pair, view, view, p).wait_send()))

    def xy_drain(pair, view):
        finals.append(lambda: xy_peers(lambda p: xy_copy(pair, view, view, p).wait_send()))

    def line_copy(pair, src, dst, zt):
        return copy(src, dst, pair[0].at[zt], pair[1].at[z], (a, 2 * zt + c))

    def pass_copy(pair, src, dst, zs):
        return copy(src, dst, pair[0].at[4 + zs], pair[1].at[4 + zs], (a, sib))

    def gather_start(pair, src, view):
        z_peers(lambda zt: line_copy(pair, src, view(b), zt).start())
        pass_copy(pair, src, view(b), z).start()
        finals.append(lambda: z_peers(lambda zt: line_copy(pair, src, src, zt).wait_send()))
        finals.append(lambda: each(0, 4, lambda zs: pass_copy(pair, src, src, zs).wait_send()))

    def gather_line(pair, view, zs):
        block = view(2 * zs + c)
        copy(block, block, pair[0].at[zs], pair[1].at[zs], (a, 2 * zs + c)).wait_recv()
        pass_copy(pair, block, block, zs).start()

    def gather_pass(pair, view, zs):
        block = view(2 * zs + 1 - c)
        pass_copy(pair, block, block, zs).wait_recv()

    barrier = pltpu.get_barrier_semaphore()
    seq_peers(lambda p: pl.semaphore_signal(barrier, 1, device_id=(a, p), device_id_type=MESH_IDS))
    xy_peers(lambda p: pl.semaphore_signal(barrier, 1, device_id=(p, b), device_id_type=MESH_IDS))

    for head in range(8):
        for place, weight in enumerate((wq, wk, wv, wg)):
            m.wcs[head, :, place * 128 : place * 128 + 128] = weight[
                :, head * 128 : head * 128 + 128
            ]
    for part in range(4):
        for place, weight in enumerate((fgi, fui)):
            m.fs[part, place, :, 0:hidden] = weight[:, part * hidden : (part + 1) * hidden]
            m.fs[part, place, :, hidden:pad] = jnp.zeros((32, pad - hidden), BF16)
    own_rows = block_rows(b, 128)
    piece = pl.ds(pl.multiple_of(a * 256 + b * 32, 32), 32)
    m.x_all[own_rows, :] = tok[...]
    m.wqk[piece, :] = m.wcs[b]
    m.wo_all[piece, :] = wo[...]
    m.fdp[b] = fdi[...]
    slot32 = block_rows(b, 32)
    m.fgu[:, a, slot32, :] = m.fs[a]
    m.t1[a] = tile[a]
    m.p1[a] = pin[...]
    pl.semaphore_wait(barrier, 10)

    xy_peers(lambda p: xy_start(s.t1, tile.at[p], m.t1.at[a], p))
    xy_peers(lambda p: xy_start(s.p1, pin, m.p1.at[a], p))
    seq_peers(lambda p: seq_start(s.w1, m.wcs.at[p], m.wqk.at[piece, :], p))
    x_view = lambda i: m.x_all.at[block_rows(i, 128), :]
    gather_start(s.x, tok, x_view)
    xy_peers(lambda p: xy_start(s.fx, m.fs.at[p], m.fgu.at[:, a, slot32, :], p))
    xy_drain(s.t1, tile.at[0])
    xy_drain(s.p1, pin)
    seq_drain(s.w1, m.wcs.at[0])
    xy_drain(s.fx, m.fs.at[0])

    xy_peers(lambda p: xy_wait(s.t1, m.t1.at[p], p))
    xy_peers(lambda p: xy_wait(s.p1, m.p1.at[p], p))
    for group in range(4):
        m.t2s[2 * group : 2 * group + 2, :] = m.t1[group, 0:2, :]
        m.t2s[8 + group : 9 + group, :] = m.t1[group, 3:4, :]
    m.t2s[12:13, :] = (m.t1[0, 2:3, :] + m.t1[1, 2:3, :]) + (m.t1[2, 2:3, :] + m.t1[3, 2:3, :])
    m.t2s[13:16, :] = jnp.zeros((3, 128), F32)
    m.t2[b] = m.t2s[...]
    m.p2[b] = m.p1[lax.div(b, 2)]
    seq_peers(lambda p: seq_start(s.t2, m.t2s, m.t2.at[b], p))
    seq_peers(lambda p: seq_start(s.p2, m.p1.at[lax.div(p, 2)], m.p2.at[b], p))
    seq_drain(s.t2, m.t2s)
    seq_drain(s.p2, m.p1.at[0])

    seq_peers(lambda p: seq_wait(s.w1, m.wqk.at[pl.ds(pl.multiple_of(a * 256 + p * 32, 32), 32), :], p))
    quarter = lambda i: m.wqk.at[block_rows(i, 256), :]
    xy_peers(lambda p: xy_start(s.w2, quarter(a), quarter(a), p))
    xy_drain(s.w2, quarter(a))

    def project(i):
        rows = block_rows(i, 128)
        wide = nn(m.x_all[rows, :], m.wqk[...])
        m.q[rows, :] = wide[:, 0:128].astype(BF16)
        m.k[rows, :] = wide[:, 128:256].astype(BF16)
        m.v[rows, :] = wide[:, 256:384].astype(BF16)
        m.gps[rows, :] = wide[:, 384:512].astype(BF16)

    head_cols = pl.ds(pl.multiple_of(b * 128, 128), 128)

    def send_gate(i):
        seq_start(s.gp, m.gps.at[block_rows(i, 128), :], m.gp.at[:, head_cols], i)

    xy_peers(lambda p: xy_wait(s.w2, quarter(p), p))
    project(b)
    m.gp[:, head_cols] = m.gps[own_rows, :]
    gather_pass(s.x, x_view, z)
    project(sib)
    send_gate(sib)

    def arrived_line(step):
        zs = lax.rem(z + step, 4)
        gather_line(s.x, x_view, zs)
        project(2 * zs + c)
        send_gate(2 * zs + c)

    each(1, 4, arrived_line)

    def arrived_pass(step):
        zs = lax.rem(z + step, 4)
        gather_pass(s.x, x_view, zs)
        project(2 * zs + 1 - c)
        send_gate(2 * zs + 1 - c)

    wo_view = lambda i: m.wo_all.at[pl.ds(pl.multiple_of(a * 256 + i * 32, 32), 32), :]
    gather_start(s.wo, wo, wo_view)
    xy_peers(lambda p: xy_wait(s.fx, m.fgu.at[:, p, slot32, :], p))
    fgu_view = lambda i: m.fgu.at[:, :, block_rows(i, 32), :]
    fd_view = lambda i: m.fdp.at[i]
    gather_start(s.fgu, fgu_view(b), fgu_view)
    gather_start(s.fd, fdi, fd_view)
    each(1, 4, arrived_pass)
    seq_drain(s.gp, m.gps.at[own_rows, :])

    seq_peers(lambda p: seq_wait(s.t2, m.t2.at[p], p))
    seq_peers(lambda p: seq_wait(s.p2, m.p2.at[p], p))
    small = m.t2[...]
    place16 = lax.broadcasted_iota(jnp.int32, (8, 16, 128), 1)
    rates = jnp.sum(jnp.where(place16 == b, small, 0.0), axis=1)
    valid_total = jnp.sum(jnp.where(place16 == 12, small, 0.0))
    for group in range(8):
        line = 8 + group // 2
        first = 4 * (group % 2)
        m.gain[:, group * 128 : group * 128 + 128] = (
            m.t2[first, line : line + 1, :] + m.t2[first + 1, line : line + 1, :]
        ) + (m.t2[first + 2, line : line + 1, :] + m.t2[first + 3, line : line + 1, :])
    half = 4 * lax.rem(b, 2)
    m.fkv[...] = (
        (m.p2[half].astype(F32) + m.p2[half + 1].astype(F32))
        + (m.p2[half + 2].astype(F32) + m.p2[half + 3].astype(F32))
    ).astype(BF16)
    row_id = lax.broadcasted_iota(jnp.int32, (128, 128), 0)
    col_id = lax.broadcasted_iota(jnp.int32, (128, 128), 1)
    lower = (col_id <= row_id).astype(F32)
    within = nt_exact(rates, lower)
    earlier = (
        lax.broadcasted_iota(jnp.int32, (8, 8), 1) < lax.broadcasted_iota(jnp.int32, (8, 8), 0)
    ).astype(F32)
    base = nn_exact(earlier, jnp.broadcast_to(jnp.sum(rates, axis=1, keepdims=True), (8, 128)))
    running = within + base
    for i in range(8):
        m.rrow[:, i * 128 : i * 128 + 128] = running[i : i + 1, :]
    eye = (col_id == row_id).astype(F32)
    m.rcol[...] = nt_exact(eye, running)

    key_pos = lax.broadcasted_iota(jnp.int32, (128, length), 1)
    local_pos = lax.broadcasted_iota(jnp.int32, (128, 1), 0)
    lane8 = lax.broadcasted_iota(jnp.int32, (128, 8), 1)

    def attend(i):
        rows = block_rows(i, 128)
        query = m.q[rows, :]
        raw = nt(query, m.k[...])
        pos = i * 128 + local_pos
        begin = jnp.zeros_like(pos)
        for j in range(ndoc):
            start = docs[a, j]
            begin = jnp.where(start <= pos, jnp.maximum(begin, start), begin)
        allowed = (key_pos <= pos) & (key_pos >= begin)
        scores = jnp.where(allowed, raw * scale, MASKED)
        fixed = nt(query, m.fkv[0:16, :]) * scale
        top = jnp.maximum(
            jnp.max(scores, axis=1, keepdims=True), jnp.max(fixed, axis=1, keepdims=True)
        )
        weight = jnp.exp(scores - top)
        fixed_weight = jnp.exp(fixed - top)
        share = 1.0 / (
            jnp.sum(weight, axis=1, keepdims=True) + jnp.sum(fixed_weight, axis=1, keepdims=True)
        )
        prob = weight * share
        fixed_prob = (fixed_weight * share).astype(BF16)
        reach = jnp.sum(jnp.where(lane8 == i, m.rcol[...], 0.0), axis=1, keepdims=True)
        kept = jnp.where(
            allowed, jnp.exp(jnp.minimum(reach - m.rrow[...], 0.0)) * mem_scale, 0.0
        )
        joint = (prob + kept * raw).astype(BF16)
        m.probs[rows, :] = prob.astype(BF16)
        m.decay[rows, :] = kept.astype(BF16)
        m.both[rows, :] = joint
        m.fprobs[rows, :] = fixed_prob
        mixed = nn(joint, m.v[...]) + nn(fixed_prob, m.fkv[16:32, :])
        m.mxs[rows, :] = mixed.astype(BF16)

    def attend_send(step):
        i = lax.rem(b + step, 8)
        attend(i)
        seq_start(s.mx, m.mxs.at[block_rows(i, 128), :], m.mx.at[:, head_cols], i)

    each(1, 4, attend_send)
    z_peers(lambda zs: gather_line(s.wo, wo_view, zs))
    each(4, 6, attend_send)
    each(0, 4, lambda zs: gather_pass(s.wo, wo_view, zs))
    wo_quarter = lambda i: m.wo_all.at[block_rows(i, 256), :]
    xy_peers(lambda p: xy_start(s.wox, wo_quarter(a), wo_quarter(a), p))
    xy_drain(s.wox, wo_quarter(a))
    each(6, 8, attend_send)
    seq_drain(s.mx, m.mxs.at[own_rows, :])
    attend(b)
    m.mx[:, head_cols] = m.mxs[own_rows, :]

    seq_peers(lambda p: seq_wait(s.gp, m.gp.at[:, pl.ds(pl.multiple_of(p * 128, 128), 128)], p))
    xy_peers(lambda p: xy_wait(s.wox, wo_quarter(p), p))
    seq_peers(lambda p: seq_wait(s.mx, m.mx.at[:, pl.ds(pl.multiple_of(p * 128, 128), 128)], p))

    m.br[...] = nn(m.mx[...], m.wo_all[...])

    def normalise(i):
        rows = block_rows(i, 32)
        opened = jax.nn.sigmoid(m.gp[rows, :].astype(F32))
        hidden_rows = tok[rows, :].astype(F32) + opened * m.br[rows, :]
        inv = lax.rsqrt(jnp.mean(hidden_rows * hidden_rows, axis=1, keepdims=True) + EPSILON)
        m.hid[rows, :] = hidden_rows
        m.inv[rows, :] = jnp.broadcast_to(inv, (32, 128))
        m.sc[pl.ds(pl.multiple_of(a * 128 + i * 32, 32), 32), :] = (
            hidden_rows * inv * m.gain[...]
        ).astype(BF16)

    each(0, 4, normalise)
    quad = lambda ref, i: ref.at[block_rows(i, 128), :]
    xy_peers(lambda p: xy_start(s.sc, quad(m.sc, a), quad(m.sc, a), p))
    xy_drain(s.sc, quad(m.sc, a))

    z_peers(lambda zs: gather_line(s.fgu, fgu_view, zs))
    z_peers(lambda zs: gather_line(s.fd, fd_view, zs))
    each(0, 4, lambda zs: gather_pass(s.fgu, fgu_view, zs))
    xy_peers(lambda p: xy_wait(s.sc, quad(m.sc, p), p))

    gate_w = lambda: m.fgu[0].reshape(width, pad)
    up_w = lambda: m.fgu[1].reshape(width, pad)

    def feed(i):
        rows = block_rows(i, 256)
        scaled = m.sc[rows, :]
        gate_act = nn(scaled, gate_w())
        up_act = nn(scaled, up_w())
        m.gact[rows, :] = gate_act
        m.uact[rows, :] = up_act
        m.inner[rows, :] = (gate_act * jax.nn.sigmoid(gate_act) * up_act).astype(BF16)

    each(0, 2, feed)
    each(0, 4, lambda zs: gather_pass(s.fd, fd_view, zs))
    share_rows = m.fdp.shape[1] - 8
    for i in range(4):
        m.ffd[2 * i * share_rows : 2 * (i + 1) * share_rows, :] = jnp.concatenate(
            [m.fdp[2 * i + j, 0:share_rows, :].astype(F32) for j in range(2)], axis=0
        ).astype(BF16)
    m.ffd[hidden:pad, :] = jnp.zeros((pad - hidden, width), BF16)

    def feed_out(step):
        i = lax.rem(a + step, 4)
        m.ysend[i] = nn(m.inner[block_rows(i, 128), :], m.ffd[...]).astype(BF16)
        xy_start(s.y, m.ysend.at[i], m.yrecv.at[a], i)

    each(1, 4, feed_out)
    m.own[...] = nn(m.inner[block_rows(a, 128), :], m.ffd[...])
    xy_peers(lambda p: xy_wait(s.y, m.yrecv.at[p], p))

    token_total = float(4 * length)
    m.fin0[...] = jnp.zeros_like(m.fin0)

    def finish(i):
        rows = block_rows(i, 32)
        final = m.hid[rows, :] + m.own[rows, :]
        a1, a2, a3 = lax.rem(a + 1, 4), lax.rem(a + 2, 4), lax.rem(a + 3, 4)
        final = final + m.yrecv[a1, rows, :].astype(F32)
        final = final + m.yrecv[a2, rows, :].astype(F32)
        final = final + m.yrecv[a3, rows, :].astype(F32)
        out_o[rows, :] = final.astype(BF16)
        error = final - tea[rows, :].astype(F32)
        counted = vcol[rows, :] * error
        grad = counted * (token_total / valid_total)
        m.dout[rows, :] = grad
        m.df[pl.ds(pl.multiple_of(a * 128 + i * 32, 32), 32), :] = grad.astype(BF16)
        squares = jnp.sum(counted * error, axis=0, keepdims=True)
        lanes = squares[:, 0:128]
        for j in range(1, width // 128):
            lanes = lanes + squares[:, j * 128 : j * 128 + 128]
        m.fin0[40:41, :] += lanes

    each(0, 4, finish)
    xy_peers(lambda p: xy_start(s.df, quad(m.df, a), quad(m.df, a), p))
    xy_drain(s.df, quad(m.df, a))
    xy_peers(lambda p: xy_wait(s.df, quad(m.df, p), p))

    def feed_back(i):
        rows = block_rows(i, 256)
        d_inner = nt(m.df[rows, :], m.ffd[...])
        gate_act = m.gact[rows, :]
        opened = jax.nn.sigmoid(gate_act)
        m.dga[rows, :] = (
            d_inner * m.uact[rows, :] * opened * (1.0 + gate_act * (1.0 - opened))
        ).astype(BF16)
        m.dua[rows, :] = (d_inner * gate_act * opened).astype(BF16)

    each(0, 2, feed_back)

    def scaled_grad(i):
        rows = block_rows(i, 128)
        return nt(m.dga[rows, :], gate_w()) + nt(m.dua[rows, :], up_w())

    def feed_in(step):
        i = lax.rem(a + step, 4)
        m.ysend[i] = scaled_grad(i).astype(BF16)
        xy_start(s.ds, m.ysend.at[i], m.yrecv.at[a], i)

    xy_peers(lambda p: xy_copy(s.y, m.ysend.at[0], m.ysend.at[0], p).wait_send())
    each(1, 4, feed_in)
    xy_drain(s.ds, m.ysend.at[0])
    m.own[...] = scaled_grad(a)

    def down_grad(i):
        cols = pl.ds(pl.multiple_of(i * 256, 256), 256)
        m.ffd[block_rows(i, 256), :] = tn(m.inner[:, cols], m.df[...]).astype(BF16)

    each(0, pad // 256, down_grad)
    for i in range(4):
        pair = m.ffd[2 * i * share_rows : 2 * (i + 1) * share_rows, :].astype(F32)
        for j in range(2):
            m.gds[i, j] = jnp.concatenate(
                [pair[j * share_rows : (j + 1) * share_rows, :], jnp.zeros((8, width), F32)], axis=0
            ).astype(BF16)
    rgd_copy = copy(m.gds.at[:, 1 - c], m.gdr, s.rgd[0].at[4], s.rgd[1].at[4], (a, sib))
    rgd_copy.start()

    xy_peers(lambda p: xy_wait(s.ds, m.yrecv.at[p], p))
    m.ggain[...] = jnp.zeros_like(m.ggain)

    def norm_back(i):
        rows = block_rows(i, 32)
        a1, a2, a3 = lax.rem(a + 1, 4), lax.rem(a + 2, 4), lax.rem(a + 3, 4)
        d_scaled = m.own[rows, :] + m.yrecv[a1, rows, :].astype(F32)
        d_scaled = d_scaled + m.yrecv[a2, rows, :].astype(F32)
        d_scaled = d_scaled + m.yrecv[a3, rows, :].astype(F32)
        inv = m.inv[rows, 0:1]
        normed = m.hid[rows, :] * inv
        m.ggain[...] += jnp.sum(d_scaled * normed, axis=0, keepdims=True)
        d_normed = d_scaled * m.gain[...]
        lean = jnp.mean(d_normed * normed, axis=1, keepdims=True)
        d_hidden = m.dout[rows, :] + inv * (d_normed - normed * lean)
        m.dout[rows, :] = d_hidden
        opened = jax.nn.sigmoid(m.gp[rows, :].astype(F32))
        m.dbr[rows, :] = (d_hidden * opened).astype(BF16)
        m.dgt[rows, :] = (d_hidden * m.br[rows, :] * opened * (1.0 - opened)).astype(BF16)

    each(0, 4, norm_back)
    gate_cols = pl.ds(384, 128)
    cols_of = lambda i: pl.ds(pl.multiple_of(i * 128, 128), 128)
    m.dms[...] = nt(m.dbr[...], m.wo_all[...]).astype(BF16)
    seq_peers(lambda p: seq_start(s.dm, m.dms.at[:, cols_of(p)], m.dm.at[own_rows, :], p))
    seq_peers(
        lambda p: seq_start(s.dg, m.dgt.at[:, cols_of(p)], m.dq.at[own_rows, gate_cols], p)
    )
    seq_drain(s.dm, m.dms.at[:, 0:128])
    seq_drain(s.dg, m.dgt.at[:, 0:128])
    m.dm[own_rows, :] = m.dms[:, head_cols]
    m.dq[own_rows, gate_cols] = m.dgt[:, head_cols]

    def out_grad(i):
        cols = pl.ds(pl.multiple_of(i * 256, 256), 256)
        m.gwos[i] = tn(m.mx[:, cols], m.dbr[...]).astype(BF16)

    def out_grad_send(step):
        i = lax.rem(a + step, 4)
        out_grad(i)
        xy_start(s.gwo, m.gwos.at[i], m.gwor.at[a], i)

    each(1, 4, out_grad_send)
    xy_drain(s.gwo, m.gwos.at[0])
    out_grad(a)

    def up_gate_grad(i):
        cols = pl.ds(pl.multiple_of(i * 256, 256), 256)
        scaled = m.sc[:, cols]
        m.gus[:, :, 0, i] = tn(scaled, m.dga[...]).astype(BF16).reshape(4, 2, 32, pad)
        m.gus[:, :, 1, i] = tn(scaled, m.dua[...]).astype(BF16).reshape(4, 2, 32, pad)

    each(0, 4, up_gate_grad)
    rgu_copy = copy(m.gus.at[:, 1 - c], m.gur, s.rgu[0].at[4], s.rgu[1].at[4], (a, sib))
    rgu_copy.start()

    def sum_line_start(pair, combined, landing, zt):
        copy(
            combined.at[zt, c], landing.at[z], pair[0].at[zt], pair[1].at[z], (a, 2 * zt + c)
        ).start()

    def sum_line_wait(pair, landing, zs):
        copy(
            landing.at[zs], landing.at[zs], pair[0].at[zs], pair[1].at[zs], (a, 2 * zs + c)
        ).wait_recv()

    def sum_line_drain(pair, combined):
        finals.append(
            lambda: z_peers(
                lambda zt: copy(
                    combined.at[zt, c], combined.at[zt, c], pair[0].at[zt], pair[1].at[zt],
                    (a, 2 * zt + c),
                ).wait_send()
            )
        )

    rgd_copy.wait_recv()

    def add_down(zt):
        m.gds[zt, c] = (m.gds[zt, c].astype(F32) + m.gdr[zt].astype(F32)).astype(BF16)

    z_peers(lambda zt: (add_down(zt), sum_line_start(s.rgd, m.gds, m.gdz, zt))[0])
    sum_line_drain(s.rgd, m.gds)
    rgu_copy.wait_recv()

    def add_up_gate(zt):
        def one(i):
            j = lax.div(i, 4)
            g = lax.rem(i, 4)
            m.gus[zt, c, j, g] = (
                m.gus[zt, c, j, g].astype(F32) + m.gur[zt, j, g].astype(F32)
            ).astype(BF16)

        each(0, 8, one)

    z_peers(lambda zt: (add_up_gate(zt), sum_line_start(s.rgu, m.gus, m.guz, zt))[0])
    sum_line_drain(s.rgu, m.gus)

    m.pgrad[...] = jnp.zeros_like(m.pgrad)

    def attend_back(i):
        rows = block_rows(i, 128)
        d_mixed = m.dm[rows, :]
        d_joint = nt(d_mixed, m.v[...])
        prob = m.probs[rows, :].astype(F32)
        turned = prob * d_joint
        fixed_prob = m.fprobs[rows, :]
        fixed_full = fixed_prob.astype(F32)
        fixed_turned = fixed_full * nt(d_mixed, m.fkv[16:32, :])
        delta = jnp.sum(turned, axis=1, keepdims=True) + jnp.sum(
            fixed_turned, axis=1, keepdims=True
        )
        d_raw = (
            scale * (turned - prob * delta) + m.decay[rows, :].astype(F32) * d_joint
        ).astype(BF16)
        m.probs[rows, :] = d_raw
        d_fixed = (fixed_turned - fixed_full * delta).astype(BF16)
        m.dq[rows, 0:128] = (
            nn(d_raw, m.k[...]) + scale * nn(d_fixed, m.fkv[0:16, :])
        ).astype(BF16)
        m.pgrad[0:16, :] += scale * tn(d_fixed, m.q[rows, :])
        m.pgrad[16:32, :] += tn(fixed_prob, d_mixed)

    attend_back(b)

    def attend_back_next(step):
        i = lax.rem(b + step, 8)
        seq_wait(s.dm, m.dm.at[block_rows(i, 128), :], i)
        seq_wait(s.dg, m.dq.at[block_rows(i, 128), gate_cols], i)
        attend_back(i)

    each(1, 8, attend_back_next)

    m.fin0[0:32, :] = m.pgrad[...]
    for j in range(8):
        m.fin0[32 + j : 33 + j, :] = m.ggain[:, j * 128 : j * 128 + 128]
    m.fin1[a] = m.fin0[...]
    xy_peers(lambda p: xy_start(s.fin1, m.fin0, m.fin1.at[a], p))
    xy_drain(s.fin1, m.fin0)

    query_turned = jnp.transpose(m.q[...].astype(F32)).astype(BF16)
    mixed_turned = jnp.transpose(m.dm[...].astype(F32)).astype(BF16)

    def key_value_grad(i):
        cols = cols_of(i)
        rows = block_rows(i, 128)
        m.dq[rows, 128:256] = jnp.transpose(nn(query_turned, m.probs[:, cols])).astype(BF16)
        m.dq[rows, 256:384] = jnp.transpose(nn(mixed_turned, m.both[:, cols])).astype(BF16)

    each(0, 8, key_value_grad)

    def head_weight_grad(i):
        cols = pl.ds(pl.multiple_of(i * 256, 256), 256)
        m.gws[i] = tn(m.x_all[:, cols], m.dq[...]).astype(BF16)

    def head_weight_send(step):
        i = lax.rem(a + step, 4)
        head_weight_grad(i)
        xy_start(s.gw, m.gws.at[i], m.gwr.at[a], i)

    each(1, 4, head_weight_send)
    xy_drain(s.gw, m.gws.at[0])
    head_weight_grad(a)

    def token_grad(i):
        return nt(m.dq[block_rows(i, 128), :], m.wqk[...])

    def token_sib(step):
        zt = lax.rem(z + step, 4)
        m.gts[zt, 1 - c] = token_grad(2 * zt + 1 - c).astype(BF16)
        copy(
            m.gts.at[zt, 1 - c], m.gtr.at[zt], s.gt[0].at[4 + zt], s.gt[1].at[4 + zt],
            (a, sib),
        ).start()

    each(1, 5, token_sib)

    def token_line(step):
        zt = lax.rem(z + step, 4)
        mine = token_grad(2 * zt + c)
        copy(
            m.gtr.at[zt], m.gtr.at[zt], s.gt[0].at[4 + zt], s.gt[1].at[4 + zt], (a, sib)
        ).wait_recv()
        m.gts[zt, c] = (mine + m.gtr[zt].astype(F32)).astype(BF16)
        copy(
            m.gts.at[zt, c], m.yrecv.at[z], s.gt[0].at[zt], s.gt[1].at[z], (a, 2 * zt + c)
        ).start()

    each(1, 4, token_line)
    m.own[...] = token_grad(b)
    finals.append(
        lambda: each(
            0, 4,
            lambda zt: copy(
                m.gtr.at[zt], m.gtr.at[zt], s.gt[0].at[4 + zt], s.gt[1].at[4 + zt], (a, sib)
            ).wait_send(),
        )
    )
    finals.append(
        lambda: z_peers(
            lambda zt: copy(
                m.yrecv.at[zt], m.yrecv.at[zt], s.gt[0].at[zt], s.gt[1].at[zt], (a, 2 * zt + c)
            ).wait_send()
        )
    )

    xy_peers(lambda p: xy_wait(s.fin1, m.fin1.at[p], p))
    m.fin2s[...] = (m.fin1[0] + m.fin1[1]) + (m.fin1[2] + m.fin1[3])
    m.fin2[b] = m.fin2s[...]
    seq_peers(lambda p: seq_start(s.fin2, m.fin2s, m.fin2.at[b], p))
    seq_drain(s.fin2, m.fin2s)

    xy_peers(lambda p: xy_wait(s.gw, m.gwr.at[p], p))
    a1, a2, a3 = lax.rem(a + 1, 4), lax.rem(a + 2, 4), lax.rem(a + 3, 4)

    def head_sum(p):
        rows = block_rows(p, 32)
        total = m.gws[a, rows, :].astype(F32) + m.gwr[a1, rows, :].astype(F32)
        total = total + m.gwr[a2, rows, :].astype(F32)
        total = total + m.gwr[a3, rows, :].astype(F32)
        m.gas[p] = total.astype(BF16)

    def head_sum_send(p):
        head_sum(p)
        seq_start(s.gwa, m.gas.at[p], m.gar.at[b], p)

    seq_peers(head_sum_send)
    seq_drain(s.gwa, m.gas.at[0])
    head_sum(b)
    m.gar[b] = m.gas[b]

    xy_peers(lambda p: xy_wait(s.gwo, m.gwor.at[p], p))

    def out_sum(i):
        rows = block_rows(i, 32)
        total = m.gwos[a, rows, :].astype(F32) + m.gwor[a1, rows, :].astype(F32)
        total = total + m.gwor[a2, rows, :].astype(F32)
        total = total + m.gwor[a3, rows, :].astype(F32)
        m.gos[lax.div(i, 2), lax.rem(i, 2)] = total.astype(BF16)

    each(0, 8, out_sum)
    rgo_copy = copy(m.gos.at[:, 1 - c], m.gor, s.rgo[0].at[4], s.rgo[1].at[4], (a, sib))
    rgo_copy.start()

    z1, z2, z3 = lax.rem(z + 1, 4), lax.rem(z + 2, 4), lax.rem(z + 3, 4)
    z_peers(lambda zs: sum_line_wait(s.rgu, m.guz, zs))

    def up_gate_sum(i):
        j = lax.div(i, 4)
        g = lax.rem(i, 4)
        total = m.gus[z, c, j, g].astype(F32) + m.gur[z, j, g].astype(F32)
        total = total + m.guz[z1, j, g].astype(F32)
        total = total + m.guz[z2, j, g].astype(F32)
        total = total + m.guz[z3, j, g].astype(F32)
        m.gux[g, j] = total.astype(BF16)

    each(0, 8, up_gate_sum)
    xy_peers(lambda p: xy_start(s.gfx, m.gux.at[p], m.guxr.at[a], p))
    xy_drain(s.gfx, m.gux.at[0])
    m.guxr[a] = m.gux[a]

    rgo_copy.wait_recv()

    def add_out(zt):
        m.gos[zt, c] = (m.gos[zt, c].astype(F32) + m.gor[zt].astype(F32)).astype(BF16)

    z_peers(lambda zt: (add_out(zt), sum_line_start(s.rgo, m.gos, m.goz, zt))[0])
    sum_line_drain(s.rgo, m.gos)

    z_peers(lambda zs: sum_line_wait(s.rgd, m.gdz, zs))
    fd_o[...] = (
        (m.gds[z, c, 0:share_rows, :].astype(F32) + m.gdr[z, 0:share_rows, :].astype(F32))
        + (m.gdz[z1, 0:share_rows, :].astype(F32) + m.gdz[z2, 0:share_rows, :].astype(F32))
    ) + m.gdz[z3, 0:share_rows, :].astype(F32)

    z_peers(
        lambda zs: copy(
            m.yrecv.at[zs], m.yrecv.at[zs], s.gt[0].at[zs], s.gt[1].at[zs], (a, 2 * zs + c)
        ).wait_recv()
    )
    copy(
        m.gtr.at[z], m.gtr.at[z], s.gt[0].at[4 + z], s.gt[1].at[4 + z], (a, sib)
    ).wait_recv()

    def token_sum(i):
        rows = block_rows(i, 32)
        total = m.dout[rows, :] + m.own[rows, :]
        total = total + m.gtr[z, rows, :].astype(F32)
        total = total + m.yrecv[z1, rows, :].astype(F32)
        total = total + m.yrecv[z2, rows, :].astype(F32)
        gtok_o[rows, :] = total + m.yrecv[z3, rows, :].astype(F32)

    each(0, 4, token_sum)

    seq_peers(lambda p: seq_wait(s.gwa, m.gar.at[p], p))
    for head in range(8):
        cols = slice(head * 128, head * 128 + 128)
        gq_o[:, cols] = m.gar[head, :, 0:128].astype(F32)
        gk_o[:, cols] = m.gar[head, :, 128:256].astype(F32)
        gv_o[:, cols] = m.gar[head, :, 256:384].astype(F32)
        gwg_o[:, cols] = m.gar[head, :, 384:512].astype(F32)

    xy_peers(lambda p: xy_wait(s.gfx, m.guxr.at[p], p))
    for part in range(4):
        fg_o[:, part * hidden : (part + 1) * hidden] = m.guxr[part, 0, :, 0:hidden].astype(F32)
        fu_o[:, part * hidden : (part + 1) * hidden] = m.guxr[part, 1, :, 0:hidden].astype(F32)

    z_peers(lambda zs: sum_line_wait(s.rgo, m.goz, zs))
    gwo_o[...] = (
        (m.gos[z, c].astype(F32) + m.gor[z].astype(F32))
        + (m.goz[z1].astype(F32) + m.goz[z2].astype(F32))
    ) + m.goz[z3].astype(F32)

    seq_peers(lambda p: seq_wait(s.fin2, m.fin2.at[p], p))
    everything = jnp.sum(m.fin2[:, 32:48, :], axis=0)
    fin_o[0:8, :] = everything[0:8, :]
    loss = jnp.sum(everything[8:9, :]) / (2.0 * width * valid_total)
    fin_o[8:16, :] = jnp.full((8, 128), loss, F32)
    pers_o[...] = m.fin2[2 * a + lax.div(b, 4), 0:32, :]

    rgd_copy.wait_send()
    rgu_copy.wait_send()
    rgo_copy.wait_send()
    for last in finals:
        last()


def local_block(
    tokens, w_query, w_key, w_value, w_out, w_gate, persist_keys, persist_values, norm_gain,
    ff_gate, ff_up, ff_down, retention, doc_starts, valid, teacher,
):
    _, block, width = tokens.shape
    length = block * lax.axis_size("seq")
    hidden = ff_gate.shape[1] // 4
    pad = -(-hidden // 256) * 256
    share = ff_down.shape[0]
    a = lax.axis_index("head")
    b = lax.axis_index("seq")
    place = a * 8 + b
    lanes = (jnp.arange(128) // 32) == lax.rem(b, 4)
    spread = lambda v: jnp.where(lanes, jnp.tile(v, (1, 4)), jnp.zeros((), v.dtype))
    rates = jnp.transpose(jnp.log(retention), (0, 2, 1))
    line = lambda v: jnp.broadcast_to(v[None], (4, 1, 128))
    tile = jnp.concatenate(
        [
            rates,
            line(valid.astype(F32)),
            line(spread(norm_gain.astype(F32)[None])),
            jnp.zeros((4, 4, 128), F32),
        ],
        axis=1,
    )
    persist = spread(jnp.concatenate([persist_keys, persist_values], axis=0))
    table = scratch_table(width, block, hidden, pad, length)
    names = tuple(table)
    vmem = pl.BlockSpec(memory_space=pltpu.VMEM)
    shape = jax.ShapeDtypeStruct
    outs = (
        shape((block, width), BF16),
        shape((block, width), F32),
        shape((32, width), F32),
        shape((32, width), F32),
        shape((32, width), F32),
        shape((32, width), F32),
        shape((32, width), F32),
        shape((16, 128), F32),
        shape((32, 128), F32),
        shape((32, 4 * hidden), F32),
        shape((32, 4 * hidden), F32),
        shape((share, width), F32),
    )
    scratch = [pltpu.VMEM(*table[name]) for name in names]
    for count in FLAGS.values():
        scratch += [pltpu.SemaphoreType.DMA((count,))] * 2
    result = pl.pallas_call(
        functools.partial(block_kernel, names, width, hidden, doc_starts.shape[1]),
        out_shape=outs,
        in_specs=[vmem] * 13 + [pl.BlockSpec(memory_space=pltpu.SMEM)],
        out_specs=[vmem] * len(outs),
        scratch_shapes=scratch,
        compiler_params=pltpu.CompilerParams(
            collective_id=0, has_side_effects=True, vmem_limit_bytes=VMEM_LIMIT
        ),
        name="block",
    )(
        tokens[0], w_query, w_key, w_value, w_out, w_gate, ff_gate, ff_up,
        jnp.pad(ff_down, ((0, 96 - share), (0, 0))), teacher[0], tile, persist,
        valid.astype(F32).reshape(block, 1), doc_starts,
    )
    (out, gtok, gq, gk, gv, gwo, gwg, fin, pers, fg, fu, fd) = result
    own = lax.dynamic_slice_in_dim(pers, lax.rem(b, 4) * 32, 32, 1)
    gain = lax.dynamic_slice_in_dim(fin[0:8].reshape(width), place * 32, 32, 0)
    return (
        out[None], fin[8, 0], gtok[None], gq, gk, gv, gwo, gwg, own[:P_SIZE], own[P_SIZE:],
        gain, fg, fu, fd,
    )


VMEM_LIMIT = 62 << 20


def entering(value, axis, join, neutral, backward):
    count = lax.axis_size(axis)
    place = lax.axis_index(axis)
    ahead = count - 1 - place if backward else place
    gathered = jax.tree.map(
        lambda a, kind: lax.all_gather(a.astype(kind), axis), value, (jnp.bfloat16, jnp.bfloat16)
    )
    state = jax.tree.map(lambda a, e: jnp.zeros_like(a) + jnp.asarray(e, a.dtype), value, neutral)

    def one(hop, state):
        source = count - 1 - hop if backward else hop
        return join(
            state,
            jax.tree.map(
                lambda a, own: lax.dynamic_index_in_dim(a, source, 0, False).astype(own.dtype),
                gathered,
                value,
            ),
        )

    return lax.fori_loop(0, ahead, one, state)


def passed_along(value, axis, by):
    peers = lax.axis_size(axis)
    pairs = [(i, i + by) for i in range(peers) if 0 <= i + by < peers]
    return lax.ppermute(value, axis, pairs)


def from_behind(block, axis, distance):
    devices = range(lax.axis_size(axis))
    route = [((i - distance) % len(devices), i) for i in devices]
    return lax.ppermute(block, axis, route)


def product(left, right):
    return jnp.dot(left, right, preferred_element_type=jnp.float32)


def rows_outer(left, right):
    return jnp.einsum("nd,ne->de", left, right, preferred_element_type=jnp.float32)


def back_product(grad, weight):
    return jnp.einsum("ne,de->nd", grad, weight, preferred_element_type=jnp.float32)


def doc_index(starts, positions):
    return jnp.sum((starts[:, None, :] <= positions[None, :, None]).astype(jnp.int32), axis=-1) - 1


def doc_begin(starts, positions):
    return jnp.any(starts[:, None, :] == positions[None, :, None], axis=-1)


def chain_forward(earlier, later):
    return (earlier[0] * later[0], later[0][..., None, None] * earlier[1] + later[1])


def chain_backward(earlier, later):
    return (earlier[0] * later[0], later[1] + later[0][..., None, None] * earlier[1])


def masked_scores(query_rows, key_rows, query_pos, key_pos, query_seg, key_seg, scale):
    raw = (
        jnp.einsum("sqhd,skhd->sqhk", query_rows, key_rows, preferred_element_type=jnp.float32)
        * scale
    )
    allowed = (key_pos[None, None, :] <= query_pos[None, :, None]) & (
        key_seg[:, None, :] == query_seg[:, :, None]
    )
    return jnp.where(allowed[:, :, None, :], raw, MASKED)


def softmax_grads(
    query_rows,
    key_rows,
    value_rows,
    dout_rows,
    query_pos,
    key_pos,
    query_seg,
    key_seg,
    query_lse,
    query_delta,
    scale,
):
    scores = masked_scores(query_rows, key_rows, query_pos, key_pos, query_seg, key_seg, scale)
    probs = jnp.exp(scores - query_lse[..., None])
    prob_grad = jnp.einsum(
        "sqhd,skhd->sqhk", dout_rows, value_rows, preferred_element_type=jnp.float32
    )
    score_grad = (probs * (prob_grad - query_delta[..., None])).astype(jnp.bfloat16)
    return (probs.astype(jnp.bfloat16), score_grad)


def local(
    tokens,
    w_query,
    w_key,
    w_value,
    w_out,
    w_gate,
    persist_keys,
    persist_values,
    norm_gain,
    ff_gate,
    ff_up,
    ff_down,
    retention,
    doc_starts,
    valid,
    teacher,
):
    gathered = (
        lax.all_gather(w_query, ("head", "seq"), axis=0, tiled=True),
        lax.all_gather(w_key, ("head", "seq"), axis=0, tiled=True),
        lax.all_gather(w_value, ("head", "seq"), axis=0, tiled=True),
        lax.all_gather(w_out, ("head", "seq"), axis=0, tiled=True),
        lax.all_gather(w_gate, ("head", "seq"), axis=0, tiled=True),
        lax.all_gather(jnp.transpose(persist_keys), ("head", "seq"), axis=0, tiled=True),
        lax.all_gather(jnp.transpose(persist_values), ("head", "seq"), axis=0, tiled=True),
        lax.all_gather(norm_gain, ("head", "seq"), axis=0, tiled=True),
        lax.all_gather(ff_gate, ("head", "seq"), axis=0, tiled=True),
        lax.all_gather(ff_up, ("head", "seq"), axis=0, tiled=True),
        lax.all_gather(ff_down, ("head", "seq"), axis=0, tiled=True),
    )
    (
        query_weight,
        key_weight,
        value_weight,
        out_weight,
        gate_weight,
        fixed_key_cols,
        fixed_value_cols,
        gain_weight,
        ffn_gate,
        ffn_up,
        ffn_down,
    ) = gathered
    fixed_key_all = jnp.transpose(fixed_key_cols)
    fixed_value_all = jnp.transpose(fixed_value_cols)
    local_seqs, block, width = tokens.shape
    groups = lax.axis_size("head")
    heads = HEAD_COUNT // groups
    head_place = lax.axis_index("head")
    seq_place = lax.axis_index("seq")
    seq_count = lax.axis_size("seq")
    all_seqs = local_seqs * groups
    length = block * seq_count
    token_count = local_seqs * block
    scale = HD ** (-0.5)
    mem_scale = 0.125 / HD
    token_rows = tokens.reshape(token_count, width)
    query_tok = (
        product(token_rows, query_weight)
        .astype(jnp.bfloat16)
        .reshape(local_seqs, block, HEAD_COUNT, HD)
    )
    key_tok = (
        product(token_rows, key_weight)
        .astype(jnp.bfloat16)
        .reshape(local_seqs, block, HEAD_COUNT, HD)
    )
    value_tok = (
        product(token_rows, value_weight)
        .astype(jnp.bfloat16)
        .reshape(local_seqs, block, HEAD_COUNT, HD)
    )
    gate_pre = product(token_rows, gate_weight)
    query_heads, key_heads, value_heads = (
        lax.all_to_all(query_tok, "head", split_axis=2, concat_axis=0, tiled=True),
        lax.all_to_all(key_tok, "head", split_axis=2, concat_axis=0, tiled=True),
        lax.all_to_all(value_tok, "head", split_axis=2, concat_axis=0, tiled=True),
    )
    fixed_keys = lax.dynamic_slice_in_dim(
        fixed_key_all.reshape(P_SIZE, HEAD_COUNT, HD), head_place * heads, heads, 1
    )
    fixed_values = lax.dynamic_slice_in_dim(
        fixed_value_all.reshape(P_SIZE, HEAD_COUNT, HD), head_place * heads, heads, 1
    )
    own_start = seq_place * block
    own_pos = own_start + jnp.arange(block, dtype=jnp.int32)
    own_seg = doc_index(doc_starts, own_pos)
    own_begin = doc_begin(doc_starts, own_pos)
    last_row = own_start + block - 1
    fixed_scores = (
        jnp.einsum("sqhd,phd->sqhp", query_heads, fixed_keys, preferred_element_type=jnp.float32)
        * scale
    )
    top_start = jnp.max(fixed_scores, axis=-1)
    fixed_exp = jnp.exp(fixed_scores - top_start[..., None])
    acc_start = jnp.einsum(
        "sqhp,phd->sqhd",
        fixed_exp.astype(jnp.bfloat16),
        fixed_values,
        preferred_element_type=jnp.float32,
    )
    key_rows = lax.all_gather(key_heads, "seq", axis=1, tiled=True)
    value_rows = lax.all_gather(value_heads, "seq", axis=1, tiled=True)
    piece_keys = key_rows.shape[1]

    def attend_compute(state):
        running_top, running_total, running_acc = state
        key_pos = jnp.arange(piece_keys, dtype=jnp.int32)
        scores = masked_scores(
            query_heads, key_rows, own_pos, key_pos, own_seg, doc_index(doc_starts, key_pos), scale
        )
        new_top = jnp.maximum(running_top, jnp.max(scores, axis=-1))
        shrink = jnp.exp(running_top - new_top)
        weights_exp = jnp.exp(scores - new_top[..., None])
        new_total = running_total * shrink + jnp.sum(weights_exp, axis=-1)
        new_acc = running_acc * shrink[..., None] + jnp.einsum(
            "sqhk,skhd->sqhd",
            weights_exp.astype(jnp.bfloat16),
            value_rows,
            preferred_element_type=jnp.float32,
        )
        return (new_top, new_total, new_acc)

    final_top, final_total, final_acc = lax.cond(
        jnp.int32(0) <= last_row,
        attend_compute,
        lambda state: state,
        (top_start, jnp.sum(fixed_exp, axis=-1), acc_start),
    )
    attn_rows = final_acc / final_total[..., None]
    lse = final_top + jnp.log(final_total)
    log_retention = jnp.log(retention)
    running = jnp.cumsum(log_retention, axis=1)
    lane = jnp.transpose(running, (0, 2, 1))
    index = jnp.arange(block)
    linked = (index[None, :] <= index[:, None])[None] & (own_seg[:, None, :] == own_seg[:, :, None])
    decay = jnp.where(
        linked[:, None], jnp.exp(jnp.minimum(lane[:, :, :, None] - lane[:, :, None, :], 0.0)), 0.0
    )
    intersection = jnp.einsum(
        "sthd,suhd->shtu", query_heads, key_heads, preferred_element_type=jnp.float32
    )
    mixing = (mem_scale * intersection * decay).astype(jnp.bfloat16)
    inner_mem = jnp.einsum(
        "shtu,suhd->sthd", mixing, value_heads, preferred_element_type=jnp.float32
    )
    carried = ((own_seg == own_seg[:, :1]) & jnp.logical_not(own_begin[:, :1])).astype(jnp.float32)
    lead = jnp.exp(running) * carried[..., None]
    trail = jnp.where(
        (own_seg == own_seg[:, -1:])[..., None], jnp.exp(running[:, -1:, :] - running), 0.0
    )
    query_full = query_heads.astype(jnp.float32)
    key_full = key_heads.astype(jnp.float32)
    value_full = value_heads.astype(jnp.float32)
    block_state = jnp.einsum(
        "suhd,suhe->shde", key_full * trail[..., None], value_full, precision=HIGHEST
    )
    block_keep = lead[:, -1, :]
    identity = (jnp.ones_like(block_keep), jnp.zeros_like(block_state))
    chained = entering((block_keep, block_state), "seq", chain_forward, identity, False)
    state_in = chained[1]
    outer_mem = (
        mem_scale
        * lead[..., None]
        * jnp.einsum("sthd,shde->sthe", query_full, state_in, precision=HIGHEST)
    )
    mixed_heads = (attn_rows + inner_mem + outer_mem).astype(jnp.bfloat16)
    mixed_rows = lax.all_to_all(
        mixed_heads, "head", split_axis=0, concat_axis=2, tiled=True
    ).reshape(token_count, width)
    branch = product(mixed_rows, out_weight)
    gate_sigmoid = jax.nn.sigmoid(gate_pre)
    hidden = token_rows.astype(jnp.float32) + gate_sigmoid * branch
    inv_rms = lax.rsqrt(jnp.mean(hidden * hidden, axis=-1, keepdims=True) + EPSILON)
    normed = hidden * inv_rms
    gain_full = gain_weight.astype(jnp.float32)
    scaled = (normed * gain_full).astype(jnp.bfloat16)
    gate_act = product(scaled, ffn_gate)
    up_act = product(scaled, ffn_up)
    act_sigmoid = jax.nn.sigmoid(gate_act)
    silu_act = gate_act * act_sigmoid
    inner = (silu_act * up_act).astype(jnp.bfloat16)
    final = hidden + product(inner, ffn_down)
    output = final.astype(jnp.bfloat16).reshape(local_seqs, block, width)
    valid_rows = valid.reshape(token_count).astype(jnp.float32)
    error = final - teacher.reshape(token_count, width).astype(jnp.float32)
    sums = lax.psum(
        (jnp.sum(valid_rows * jnp.sum(error * error, axis=-1)), jnp.sum(valid_rows)),
        ("head", "seq"),
    )
    loss = sums[0] / (2.0 * width * sums[1])
    total_tokens = all_seqs * length
    d_out = valid_rows[:, None] * error * (total_tokens / sums[1])
    d_ffn = d_out.astype(jnp.bfloat16)
    grad_down = rows_outer(inner, d_ffn)
    d_inner = back_product(d_ffn, ffn_down)
    d_gate_act = (d_inner * up_act * act_sigmoid * (1.0 + gate_act * (1.0 - act_sigmoid))).astype(
        jnp.bfloat16
    )
    d_up_act = (d_inner * silu_act).astype(jnp.bfloat16)
    grad_ffn_gate = rows_outer(scaled, d_gate_act)
    grad_ffn_up = rows_outer(scaled, d_up_act)
    d_scaled = back_product(d_gate_act, ffn_gate) + back_product(d_up_act, ffn_up)
    grad_gain = jnp.sum(d_scaled * normed, axis=0)
    d_normed = d_scaled * gain_full
    d_hidden = d_out + inv_rms * (
        d_normed - normed * jnp.mean(d_normed * normed, axis=-1, keepdims=True)
    )
    d_branch = (d_hidden * gate_sigmoid).astype(jnp.bfloat16)
    d_gate = (d_hidden * branch * gate_sigmoid * (1.0 - gate_sigmoid)).astype(jnp.bfloat16)
    grad_out_weight = rows_outer(mixed_rows, d_branch)
    grad_gate_weight = rows_outer(token_rows, d_gate)
    d_mixed = (
        back_product(d_branch, out_weight)
        .astype(jnp.bfloat16)
        .reshape(local_seqs, block, HEAD_COUNT, HD)
    )
    dout_heads = lax.all_to_all(d_mixed, "head", split_axis=2, concat_axis=0, tiled=True)
    dout_full = dout_heads.astype(jnp.float32)
    delta = jnp.sum(dout_full * attn_rows, axis=-1)
    fixed_probs = jnp.exp(fixed_scores - lse[..., None])
    fixed_prob_grad = jnp.einsum(
        "sqhd,phd->sqhp", dout_heads, fixed_values, preferred_element_type=jnp.float32
    )
    fixed_score_grad = (fixed_probs * (fixed_prob_grad - delta[..., None])).astype(jnp.bfloat16)
    fixed_key_grad = (
        jnp.einsum(
            "sqhp,sqhd->phd", fixed_score_grad, query_heads, preferred_element_type=jnp.float32
        )
        * scale
    )
    fixed_value_grad = jnp.einsum(
        "sqhp,sqhd->phd",
        fixed_probs.astype(jnp.bfloat16),
        dout_heads,
        preferred_element_type=jnp.float32,
    )
    query_grad_start = (
        jnp.einsum(
            "sqhp,phd->sqhd", fixed_score_grad, fixed_keys, preferred_element_type=jnp.float32
        )
        * scale
    )
    fold_start = (query_grad_start,)
    back_key_rows = lax.all_gather(key_heads, "seq", axis=1, tiled=True)
    back_value_rows = lax.all_gather(value_heads, "seq", axis=1, tiled=True)
    back_piece_keys = back_key_rows.shape[1]

    def back_compute(state):
        key_pos = jnp.arange(back_piece_keys, dtype=jnp.int32)
        probs_low, score_grad = softmax_grads(
            query_heads,
            back_key_rows,
            back_value_rows,
            dout_heads,
            own_pos,
            key_pos,
            own_seg,
            doc_index(doc_starts, key_pos),
            lse,
            delta,
            scale,
        )
        query_grad = (
            state[0]
            + jnp.einsum(
                "sqhk,skhd->sqhd", score_grad, back_key_rows, preferred_element_type=jnp.float32
            )
            * scale
        )
        return (query_grad,)

    folded = lax.cond(jnp.int32(0) <= last_row, back_compute, lambda state: state, fold_start)
    query_att = folded[0]
    empty_local = jnp.zeros((all_seqs, block, heads, HD), jnp.float32)

    def visit(turn, state):
        key_rows, value_rows, key_acc, value_acc = state
        owner = (seq_place - turn) % seq_count
        start = owner * block

        def visit_compute(accs):
            key_pos = start + jnp.arange(block, dtype=jnp.int32)
            probs_low, score_grad = softmax_grads(
                query_heads,
                key_rows,
                value_rows,
                dout_heads,
                own_pos,
                key_pos,
                own_seg,
                doc_index(doc_starts, key_pos),
                lse,
                delta,
                scale,
            )
            key_next = (
                accs[0]
                + jnp.einsum(
                    "sqhk,sqhd->skhd", score_grad, query_heads, preferred_element_type=jnp.float32
                )
                * scale
            )
            value_next = accs[1] + jnp.einsum(
                "sqhk,sqhd->skhd", probs_low, dout_heads, preferred_element_type=jnp.float32
            )
            return (key_next, value_next)

        key_acc, value_acc = lax.cond(
            start <= last_row, visit_compute, lambda accs: accs, (key_acc, value_acc)
        )
        key_rows, value_rows = passed_along((key_rows, value_rows), "seq", 1)
        key_acc, value_acc = (
            from_behind(key_acc.astype(jnp.bfloat16), "seq", 1).astype(key_acc.dtype),
            from_behind(value_acc.astype(jnp.bfloat16), "seq", 1).astype(value_acc.dtype),
        )
        return (key_rows, value_rows, key_acc, value_acc)

    travelled = lax.fori_loop(
        0, seq_count, visit, (key_heads, value_heads, empty_local, empty_local)
    )
    key_att = travelled[2]
    value_att = travelled[3]
    mix_grad_raw = jnp.einsum(
        "sthe,suhe->shtu", dout_heads, value_heads, preferred_element_type=jnp.float32
    )
    intersection_grad = (mem_scale * mix_grad_raw * decay).astype(jnp.bfloat16)
    local_grad = mem_scale * jnp.einsum(
        "sthd,sthe->shde", query_full * lead[..., None], dout_full, precision=HIGHEST
    )
    state_grads = entering((block_keep, local_grad), "seq", chain_backward, identity, True)
    carry_grad = state_grads[1]
    query_mem = jnp.einsum(
        "shtu,suhd->sthd", intersection_grad, key_heads, preferred_element_type=jnp.float32
    )
    query_mem = query_mem + mem_scale * lead[..., None] * jnp.einsum(
        "sthe,shde->sthd", dout_full, state_in, precision=HIGHEST
    )
    key_mem = jnp.einsum(
        "shtu,sthd->suhd", intersection_grad, query_heads, preferred_element_type=jnp.float32
    )
    key_mem = key_mem + trail[..., None] * jnp.einsum(
        "suhe,shde->suhd", value_full, carry_grad, precision=HIGHEST
    )
    value_mem = jnp.einsum(
        "shtu,sthe->suhe", mixing, dout_heads, preferred_element_type=jnp.float32
    )
    value_mem = value_mem + jnp.einsum(
        "suhd,shde->suhe", key_full * trail[..., None], carry_grad, precision=HIGHEST
    )
    query_grad_heads = (query_att + query_mem).astype(jnp.bfloat16)
    key_grad_heads = (key_att + key_mem).astype(jnp.bfloat16)
    value_grad_heads = (value_att + value_mem).astype(jnp.bfloat16)
    query_back, key_back, value_back = (
        lax.all_to_all(query_grad_heads, "head", split_axis=0, concat_axis=2, tiled=True),
        lax.all_to_all(key_grad_heads, "head", split_axis=0, concat_axis=2, tiled=True),
        lax.all_to_all(value_grad_heads, "head", split_axis=0, concat_axis=2, tiled=True),
    )
    query_back = query_back.reshape(token_count, width)
    key_back = key_back.reshape(token_count, width)
    value_back = value_back.reshape(token_count, width)
    grad_query_weight = rows_outer(token_rows, query_back)
    grad_key_weight = rows_outer(token_rows, key_back)
    grad_value_weight = rows_outer(token_rows, value_back)
    token_grad = (
        d_hidden + back_product(d_gate, gate_weight) + back_product(query_back, query_weight)
    )
    token_grad = (
        token_grad + back_product(key_back, key_weight) + back_product(value_back, value_weight)
    )
    fixed_key_full = lax.dynamic_update_slice_in_dim(
        jnp.zeros((P_SIZE, HEAD_COUNT, HD), jnp.float32), fixed_key_grad, head_place * heads, 1
    ).reshape(P_SIZE, width)
    fixed_value_full = lax.dynamic_update_slice_in_dim(
        jnp.zeros((P_SIZE, HEAD_COUNT, HD), jnp.float32), fixed_value_grad, head_place * heads, 1
    ).reshape(P_SIZE, width)
    shards = (
        lax.psum_scatter(grad_query_weight, ("head", "seq"), scatter_dimension=0, tiled=True),
        lax.psum_scatter(grad_key_weight, ("head", "seq"), scatter_dimension=0, tiled=True),
        lax.psum_scatter(grad_value_weight, ("head", "seq"), scatter_dimension=0, tiled=True),
        lax.psum_scatter(grad_out_weight, ("head", "seq"), scatter_dimension=0, tiled=True),
        lax.psum_scatter(grad_gate_weight, ("head", "seq"), scatter_dimension=0, tiled=True),
        lax.psum_scatter(
            jnp.transpose(fixed_key_full), ("head", "seq"), scatter_dimension=0, tiled=True
        ),
        lax.psum_scatter(
            jnp.transpose(fixed_value_full), ("head", "seq"), scatter_dimension=0, tiled=True
        ),
        lax.psum_scatter(grad_gain, ("head", "seq"), scatter_dimension=0, tiled=True),
        lax.psum_scatter(grad_ffn_gate, ("head", "seq"), scatter_dimension=0, tiled=True),
        lax.psum_scatter(grad_ffn_up, ("head", "seq"), scatter_dimension=0, tiled=True),
        lax.psum_scatter(grad_down, ("head", "seq"), scatter_dimension=0, tiled=True),
    )
    return (
        output,
        loss,
        token_grad.reshape(local_seqs, block, width),
        shards[0],
        shards[1],
        shards[2],
        shards[3],
        shards[4],
        jnp.transpose(shards[5]),
        jnp.transpose(shards[6]),
        shards[7],
        shards[8],
        shards[9],
        shards[10],
    )


def solution(mesh):
    in_specs = (
        P("head", "seq", None),
        P(("head", "seq"), None),
        P(("head", "seq"), None),
        P(("head", "seq"), None),
        P(("head", "seq"), None),
        P(("head", "seq"), None),
        P(None, ("head", "seq")),
        P(None, ("head", "seq")),
        P(("head", "seq")),
        P(("head", "seq"), None),
        P(("head", "seq"), None),
        P(("head", "seq"), None),
        P(None, "seq", "head"),
        P(),
        P("head", "seq"),
        P("head", "seq", None),
    )
    out_specs = (
        P("head", "seq", None),
        P(),
        P("head", "seq", None),
        P(("head", "seq"), None),
        P(("head", "seq"), None),
        P(("head", "seq"), None),
        P(("head", "seq"), None),
        P(("head", "seq"), None),
        P(None, ("head", "seq")),
        P(None, ("head", "seq")),
        P(("head", "seq")),
        P(("head", "seq"), None),
        P(("head", "seq"), None),
        P(("head", "seq"), None),
    )
    fits = mesh.shape["head"] == 4 and mesh.shape["seq"] == HEAD_COUNT
    body = local_block if fits else local
    return jax.shard_map(body, mesh=mesh, in_specs=in_specs, out_specs=out_specs, check_vma=False)
```

```python
import functools
import types

import jax
import jax.numpy as jnp
from jax import lax
from jax.experimental import pallas as pl
from jax.experimental.pallas import tpu as pltpu
from jax.sharding import PartitionSpec as P

HEAD_COUNT = 8
HD = 128
P_SIZE = 16


HIGHEST = lax.Precision.HIGHEST
MASKED = -1e30
EPSILON = 1e-06
F32 = jnp.float32
BF16 = jnp.bfloat16
MESH_IDS = pl.DeviceIdType.MESH


def nn(left, right):
    return lax.dot_general(left, right, (((1,), (0,)), ((), ())), preferred_element_type=F32)


def nt(left, right):
    return lax.dot_general(left, right, (((1,), (1,)), ((), ())), preferred_element_type=F32)


def tn(left, right):
    return lax.dot_general(left, right, (((0,), (0,)), ((), ())), preferred_element_type=F32)


def tn_exact(left, right):
    return lax.dot_general(
        left, right, (((0,), (0,)), ((), ())), precision=HIGHEST, preferred_element_type=F32
    )


def nt_exact(left, right):
    return lax.dot_general(
        left, right, (((1,), (1,)), ((), ())), precision=HIGHEST, preferred_element_type=F32
    )


def nn_exact(left, right):
    return lax.dot_general(
        left, right, (((1,), (0,)), ((), ())), precision=HIGHEST, preferred_element_type=F32
    )


def block_rows(index, size):
    return pl.ds(pl.multiple_of(index * size, size), size)


def each(first, last, body):
    def step(index, carry):
        body(index)
        return carry

    lax.fori_loop(first, last, step, 0)


SEQ_FLAGS = dict(
    w1=8, t2=8, p2=8, x=8, wo=8, fg=8, fd=8, fu=8, gp=8, mx=8, dm=8, dg=8, rgu=8, rgd=8, rgo=8,
    gt=8, gwa=8, fin2=8, pers=8,
)
XY_FLAGS = dict(t1=4, p1=4, w2=4, fx=4, wox=4, sc=4, y=4, df=4, ds=4, gwo=4, gw=4, gfx=4, fin1=4)
FLAGS = SEQ_FLAGS | XY_FLAGS


def scratch_table(width, tokens, hidden, hidden_pad, length):
    seqs, blocks, block = 4, 8, 128
    table = dict(
        x_all=((length, width), BF16),
        wcs=((blocks, 32, 512), BF16),
        wqk=((width, 512), BF16),
        tile=((4, 8, 128), F32),
        pin=((32, 128), BF16),
        vcol=((block, 1), F32),
        t1=((4, 8, 128), F32),
        p1=((4, 32, 128), BF16),
        t2s=((16, 128), F32),
        t2=((8, 16, 128), F32),
        p2=((8, 32, 128), BF16),
        fs=((4, 2, 32, hidden_pad), BF16),
        fgu=((2, 4, 256, hidden_pad), BF16),
        fdp=((8, 96, width), BF16),
        ffd=((hidden_pad, width), BF16),
        wo_all=((width, width), BF16),
        q=((length, HD), BF16),
        k=((length, HD), BF16),
        v=((length, HD), BF16),
        gps=((length, HD), BF16),
        fkv=((32, HD), BF16),
        gain=((1, width), F32),
        rrow=((1, length), F32),
        rcol=((block, 8), F32),
        probs=((length, length), BF16),
        decay=((length, length), BF16),
        both=((length, length), BF16),
        fprobs=((length, P_SIZE), BF16),
        mxs=((length, HD), BF16),
        mx=((block, width), BF16),
        gp=((block, width), BF16),
        hid=((block, width), F32),
        br=((block, width), F32),
        inv=((block, 128), F32),
        own=((block, width), F32),
        dout=((block, width), F32),
        sc=((4 * block, width), BF16),
        gact=((4 * block, hidden_pad), F32),
        uact=((4 * block, hidden_pad), F32),
        inner=((4 * block, hidden_pad), BF16),
        ysend=((4, block, width), BF16),
        yrecv=((4, block, width), BF16),
        df=((4 * block, width), BF16),
        dga=((4 * block, hidden_pad), BF16),
        dua=((4 * block, hidden_pad), BF16),
        dbr=((block, width), BF16),
        dgt=((block, width), BF16),
        dms=((block, width), BF16),
        dm=((length, HD), BF16),
        dq=((length, 512), BF16),
        ggain=((1, width), F32),
        gus=((4, 2, 2, 4, 32, hidden_pad), BF16),
        gur=((4, 2, 4, 32, hidden_pad), BF16),
        guz=((4, 2, 4, 32, hidden_pad), BF16),
        gux=((4, 2, 32, hidden_pad), BF16),
        guxr=((4, 2, 32, hidden_pad), BF16),
        gds=((4, 2, 96, width), BF16),
        gdr=((4, 96, width), BF16),
        gdz=((4, 96, width), BF16),
        gwos=((4, 256, width), BF16),
        gwor=((4, 256, width), BF16),
        gos=((4, 2, 32, width), BF16),
        gor=((4, 32, width), BF16),
        goz=((4, 32, width), BF16),
        gws=((4, 256, 512), BF16),
        gwr=((4, 256, 512), BF16),
        gas=((8, 32, 512), BF16),
        gar=((8, 32, 512), BF16),
        gts=((4, 2, block, width), BF16),
        gtr=((4, block, width), BF16),
        pgrad=((32, HD), F32),
        fin0=((48, 128), F32),
        fin1=((4, 48, 128), F32),
        fin2s=((48, 128), F32),
        fin2=((8, 16, 128), F32),
        pers=((32, 128), F32),
    )
    return table


def block_kernel(names, width, hidden, ndoc, *refs):
    (
        tok, wq, wk, wv, wo, wg, fgi, fui, fdi, tea, ret, pk, pv, gin, val, docs,
        out_o, gtok_o, gar_o, gwo_o, fin_o, pers_o, gux_o, fd_o,
    ) = refs[:24]
    m = types.SimpleNamespace(**dict(zip(names, refs[24 : 24 + len(names)])))
    sems = refs[24 + len(names) :]
    s = types.SimpleNamespace(**dict(zip(FLAGS, zip(sems[0::2], sems[1::2]))))
    pad = m.ffd.shape[0]
    length = m.x_all.shape[0]
    scale = HD ** (-0.5)
    mem_scale = 0.125 / HD

    a = lax.axis_index("head")
    b = lax.axis_index("seq")
    z = lax.div(b, 2)
    c = lax.rem(b, 2)
    sib = 2 * z + 1 - c
    near = z + 1 - 2 * lax.rem(z, 2)
    mirror = 3 - z
    across = 3 - near
    inner_chip = (z == 1) | (z == 2)

    def copy(src, dst, ssem, rsem, device):
        return pltpu.make_async_remote_copy(
            src_ref=src, dst_ref=dst, send_sem=ssem, recv_sem=rsem,
            device_id=device, device_id_type=MESH_IDS,
        )

    def seq_peers(body):
        each(1, 8, lambda step: body(lax.rem(b + step, 8)))

    def xy_peers(body):
        each(1, 4, lambda step: body(lax.rem(a + step, 4)))

    def z_peers(body):
        each(1, 4, lambda step: body(lax.rem(z + step, 4)))

    def seq_copy(pair, src, dst, peer, slot=None):
        slot = peer if slot is None else slot
        return copy(src, dst, pair[0].at[peer], pair[1].at[slot], (a, peer))

    def seq_start(pair, src, dst, peer):
        seq_copy(pair, src, dst, peer, b).start()

    def seq_wait(pair, dst, peer):
        seq_copy(pair, dst, dst, peer).wait_recv()

    def xy_copy(pair, src, dst, peer, slot=None):
        slot = peer if slot is None else slot
        return copy(src, dst, pair[0].at[peer], pair[1].at[slot], (peer, b))

    def xy_start(pair, src, dst, peer):
        xy_copy(pair, src, dst, peer, a).start()

    def xy_wait(pair, dst, peer):
        xy_copy(pair, dst, dst, peer).wait_recv()

    finals = []

    def seq_drain(pair, view):
        finals.append(lambda: seq_peers(lambda p: seq_copy(pair, view, view, p).wait_send()))

    def xy_drain(pair, view):
        finals.append(lambda: xy_peers(lambda p: xy_copy(pair, view, view, p).wait_send()))

    def line_copy(pair, src, dst, zt):
        return copy(src, dst, pair[0].at[zt], pair[1].at[z], (a, 2 * zt + c))

    def pass_copy(pair, src, dst, zs):
        return copy(src, dst, pair[0].at[4 + zs], pair[1].at[4 + zs], (a, sib))

    def gather_start(pair, src, view):
        line_copy(pair, src, view(b), mirror).start()
        line_copy(pair, src, view(b), near).start()

        @pl.when(jnp.logical_not(inner_chip))
        def _():
            line_copy(pair, src, view(b), across).start()

        pass_copy(pair, src, view(b), z).start()
        finals.append(lambda: z_peers(lambda zt: line_copy(pair, src, src, zt).wait_send()))
        finals.append(lambda: each(0, 4, lambda zs: pass_copy(pair, src, src, zs).wait_send()))

    def gather_line(pair, view, zs):
        block = view(2 * zs + c)
        copy(block, block, pair[0].at[zs], pair[1].at[zs], (a, 2 * zs + c)).wait_recv()
        pass_copy(pair, block, block, zs).start()

    def gather_mirror(pair, view):
        gather_line(pair, view, mirror)
        block = view(2 * mirror + c)

        @pl.when(inner_chip)
        def _():
            copy(
                block, block, pair[0].at[across], pair[1].at[mirror], (a, 2 * near + c)
            ).start()

    def gather_pass(pair, view, zs):
        block = view(2 * zs + 1 - c)
        pass_copy(pair, block, block, zs).wait_recv()

    barrier = pltpu.get_barrier_semaphore()
    seq_peers(lambda p: pl.semaphore_signal(barrier, 1, device_id=(a, p), device_id_type=MESH_IDS))
    xy_peers(lambda p: pl.semaphore_signal(barrier, 1, device_id=(p, b), device_id_type=MESH_IDS))

    for head in range(8):
        for place, weight in enumerate((wq, wk, wv, wg)):
            m.wcs[head, :, place * 128 : place * 128 + 128] = weight[
                :, head * 128 : head * 128 + 128
            ]
    for part in range(4):
        for place, weight in enumerate((fgi, fui)):
            m.fs[part, place, :, 0:hidden] = weight[:, part * hidden : (part + 1) * hidden]
            m.fs[part, place, :, hidden:pad] = jnp.zeros((32, pad - hidden), BF16)
    own_rows = block_rows(b, 128)
    piece = pl.ds(pl.multiple_of(a * 256 + b * 32, 32), 32)
    m.x_all[own_rows, :] = tok[...]
    m.wqk[piece, :] = m.wcs[b]
    m.wo_all[piece, :] = wo[...]
    down = fdi[...].astype(F32)
    m.fdp[b] = jnp.concatenate(
        [down, jnp.zeros((96 - down.shape[0], width), F32)], axis=0
    ).astype(BF16)
    slot32 = block_rows(b, 32)
    m.fgu[:, a, slot32, :] = m.fs[a]
    row_id = lax.broadcasted_iota(jnp.int32, (128, 128), 0)
    col_id = lax.broadcasted_iota(jnp.int32, (128, 128), 1)
    place = (
        lax.broadcasted_iota(jnp.int32, (32, 128), 1)
        == lax.broadcasted_iota(jnp.int32, (32, 128), 0) + 32 * lax.rem(b, 4)
    ).astype(BF16)
    m.pin[0:16, :] = nn(pk[...], place).astype(BF16)
    m.pin[16:32, :] = nn(pv[...], place).astype(BF16)
    counted_row = val[...].astype(F32)
    m.vcol[...] = jnp.sum(jnp.where(row_id == col_id, counted_row, 0.0), axis=1, keepdims=True)
    gain_row = nn(gin[...], place)
    m.tile[...] = jnp.zeros_like(m.tile)
    for group in range(4):
        m.tile[group, 0:2, :] = jnp.log(ret[group])
        m.tile[group, 2:3, :] = counted_row
        m.tile[group, 3:4, :] = gain_row
    m.t1[a] = m.tile[a]
    m.p1[a] = m.pin[...]
    pl.semaphore_wait(barrier, 10)

    xy_peers(lambda p: xy_start(s.t1, m.tile.at[p], m.t1.at[a], p))
    xy_peers(lambda p: xy_start(s.p1, m.pin, m.p1.at[a], p))
    seq_peers(lambda p: seq_start(s.w1, m.wcs.at[p], m.wqk.at[piece, :], p))
    x_view = lambda i: m.x_all.at[block_rows(i, 128), :]
    gather_start(s.x, tok, x_view)
    xy_peers(lambda p: xy_start(s.fx, m.fs.at[p], m.fgu.at[:, a, slot32, :], p))
    xy_drain(s.t1, m.tile.at[0])
    xy_drain(s.p1, m.pin)
    seq_drain(s.w1, m.wcs.at[0])
    xy_drain(s.fx, m.fs.at[0])

    xy_peers(lambda p: xy_wait(s.t1, m.t1.at[p], p))
    xy_peers(lambda p: xy_wait(s.p1, m.p1.at[p], p))
    for group in range(4):
        m.t2s[2 * group : 2 * group + 2, :] = m.t1[group, 0:2, :]
        m.t2s[8 + group : 9 + group, :] = m.t1[group, 3:4, :]
    m.t2s[12:13, :] = (m.t1[0, 2:3, :] + m.t1[1, 2:3, :]) + (m.t1[2, 2:3, :] + m.t1[3, 2:3, :])
    m.t2s[13:16, :] = jnp.zeros((3, 128), F32)
    m.t2[b] = m.t2s[...]
    m.p2[b] = m.p1[lax.div(b, 2)]
    seq_peers(lambda p: seq_start(s.t2, m.t2s, m.t2.at[b], p))
    half = 4 * c

    def persist_send(p):
        @pl.when(lax.rem(p, 2) == lax.div(b, 4))
        def _():
            seq_start(s.p2, m.p1.at[lax.div(p, 2)], m.p2.at[b], p)

    def persist_drain(p):
        @pl.when(lax.rem(p, 2) == lax.div(b, 4))
        def _():
            seq_copy(s.p2, m.pin, m.pin, p).wait_send()

    def persist_wait(p):
        @pl.when(lax.div(p, 4) == c)
        def _():
            seq_wait(s.p2, m.p2.at[p], p)

    seq_peers(persist_send)
    finals.append(lambda: seq_peers(persist_drain))
    seq_drain(s.t2, m.t2s)

    seq_peers(lambda p: seq_wait(s.w1, m.wqk.at[pl.ds(pl.multiple_of(a * 256 + p * 32, 32), 32), :], p))
    quarter = lambda i: m.wqk.at[block_rows(i, 256), :]
    xy_peers(lambda p: xy_start(s.w2, quarter(a), quarter(a), p))
    xy_drain(s.w2, quarter(a))

    def project(i):
        rows = block_rows(i, 128)
        wide = nn(m.x_all[rows, :], m.wqk[...])
        m.q[rows, :] = wide[:, 0:128].astype(BF16)
        m.k[rows, :] = wide[:, 128:256].astype(BF16)
        m.v[rows, :] = wide[:, 256:384].astype(BF16)
        m.gps[rows, :] = wide[:, 384:512].astype(BF16)

    head_cols = pl.ds(pl.multiple_of(b * 128, 128), 128)

    def send_gate(i):
        seq_start(s.gp, m.gps.at[block_rows(i, 128), :], m.gp.at[:, head_cols], i)

    xy_peers(lambda p: xy_wait(s.w2, quarter(p), p))
    project(b)
    m.gp[:, head_cols] = m.gps[own_rows, :]
    gather_pass(s.x, x_view, z)
    project(sib)
    send_gate(sib)

    def arrived_line(step):
        zs = lax.rem(z + step, 4)
        gather_line(s.x, x_view, zs)
        project(2 * zs + c)
        send_gate(2 * zs + c)

    def arrived(i):
        project(i)
        send_gate(i)

    gather_mirror(s.x, x_view)
    arrived(2 * mirror + c)
    gather_line(s.x, x_view, near)
    arrived(2 * near + c)
    gather_line(s.x, x_view, across)

    def arrived_pass(step):
        zs = lax.rem(z + step, 4)
        gather_pass(s.x, x_view, zs)
        arrived(2 * zs + 1 - c)

    wo_view = lambda i: m.wo_all.at[pl.ds(pl.multiple_of(a * 256 + i * 32, 32), 32), :]
    gather_start(s.wo, wo, wo_view)
    xy_peers(lambda p: xy_wait(s.fx, m.fgu.at[:, p, slot32, :], p))
    fg_view = lambda i: m.fgu.at[0, :, block_rows(i, 32), :]
    fu_view = lambda i: m.fgu.at[1, :, block_rows(i, 32), :]
    fd_view = lambda i: m.fdp.at[i]
    gather_start(s.fg, fg_view(b), fg_view)
    arrived(2 * across + c)
    each(1, 4, arrived_pass)
    seq_drain(s.gp, m.gps.at[own_rows, :])

    seq_peers(lambda p: seq_wait(s.t2, m.t2.at[p], p))
    seq_peers(persist_wait)
    small = m.t2[...]
    place16 = lax.broadcasted_iota(jnp.int32, (8, 16, 128), 1)
    rates = jnp.sum(jnp.where(place16 == b, small, 0.0), axis=1)
    valid_total = jnp.sum(jnp.where(place16 == 12, small, 0.0))
    for group in range(8):
        line = 8 + group // 2
        first = 4 * (group % 2)
        m.gain[:, group * 128 : group * 128 + 128] = (
            m.t2[first, line : line + 1, :] + m.t2[first + 1, line : line + 1, :]
        ) + (m.t2[first + 2, line : line + 1, :] + m.t2[first + 3, line : line + 1, :])
    m.fkv[...] = (
        (m.p2[half].astype(F32) + m.p2[half + 1].astype(F32))
        + (m.p2[half + 2].astype(F32) + m.p2[half + 3].astype(F32))
    ).astype(BF16)
    lower = (col_id <= row_id).astype(F32)
    within = nt_exact(rates, lower)
    earlier = (
        lax.broadcasted_iota(jnp.int32, (8, 8), 1) < lax.broadcasted_iota(jnp.int32, (8, 8), 0)
    ).astype(F32)
    base = nn_exact(earlier, jnp.broadcast_to(jnp.sum(rates, axis=1, keepdims=True), (8, 128)))
    running = within + base
    for i in range(8):
        m.rrow[:, i * 128 : i * 128 + 128] = running[i : i + 1, :]
    eye = (col_id == row_id).astype(F32)
    m.rcol[...] = nt_exact(eye, running)

    key_pos = lax.broadcasted_iota(jnp.int32, (128, length), 1)
    local_pos = lax.broadcasted_iota(jnp.int32, (128, 1), 0)
    lane8 = lax.broadcasted_iota(jnp.int32, (128, 8), 1)

    def attend(i):
        rows = block_rows(i, 128)
        query = m.q[rows, :]
        raw = nt(query, m.k[...])
        pos = i * 128 + local_pos
        begin = jnp.zeros_like(pos)
        for j in range(ndoc):
            start = docs[a, j]
            begin = jnp.where(start <= pos, jnp.maximum(begin, start), begin)
        allowed = (key_pos <= pos) & (key_pos >= begin)
        scores = jnp.where(allowed, raw * scale, MASKED)
        fixed = nt(query, m.fkv[0:16, :]) * scale
        top = jnp.maximum(
            jnp.max(scores, axis=1, keepdims=True), jnp.max(fixed, axis=1, keepdims=True)
        )
        weight = jnp.exp(scores - top)
        fixed_weight = jnp.exp(fixed - top)
        share = 1.0 / (
            jnp.sum(weight, axis=1, keepdims=True) + jnp.sum(fixed_weight, axis=1, keepdims=True)
        )
        prob = weight * share
        fixed_prob = (fixed_weight * share).astype(BF16)
        reach = jnp.sum(jnp.where(lane8 == i, m.rcol[...], 0.0), axis=1, keepdims=True)
        kept = jnp.where(
            allowed, jnp.exp(jnp.minimum(reach - m.rrow[...], 0.0)) * mem_scale, 0.0
        )
        joint = (prob + kept * raw).astype(BF16)
        m.probs[rows, :] = prob.astype(BF16)
        m.decay[rows, :] = kept.astype(BF16)
        m.both[rows, :] = joint
        m.fprobs[rows, :] = fixed_prob
        mixed = nn(joint, m.v[...]) + nn(fixed_prob, m.fkv[16:32, :])
        m.mxs[rows, :] = mixed.astype(BF16)

    def attend_send(step):
        i = lax.rem(b + step, 8)
        attend(i)
        seq_start(s.mx, m.mxs.at[block_rows(i, 128), :], m.mx.at[:, head_cols], i)

    each(1, 4, attend_send)
    gather_mirror(s.wo, wo_view)
    gather_line(s.wo, wo_view, near)
    gather_line(s.wo, wo_view, across)
    each(4, 6, attend_send)
    each(0, 4, lambda zs: gather_pass(s.wo, wo_view, zs))
    wo_quarter = lambda i: m.wo_all.at[block_rows(i, 256), :]
    xy_peers(lambda p: xy_start(s.wox, wo_quarter(a), wo_quarter(a), p))
    xy_drain(s.wox, wo_quarter(a))
    each(6, 7, attend_send)
    gather_mirror(s.fg, fg_view)
    gather_start(s.fu, fu_view(b), fu_view)
    each(7, 8, attend_send)
    seq_drain(s.mx, m.mxs.at[own_rows, :])
    attend(b)
    m.mx[:, head_cols] = m.mxs[own_rows, :]

    seq_peers(lambda p: seq_wait(s.gp, m.gp.at[:, pl.ds(pl.multiple_of(p * 128, 128), 128)], p))
    xy_peers(lambda p: xy_wait(s.wox, wo_quarter(p), p))
    seq_peers(lambda p: seq_wait(s.mx, m.mx.at[:, pl.ds(pl.multiple_of(p * 128, 128), 128)], p))

    m.br[...] = nn(m.mx[...], m.wo_all[...])

    def normalise(i):
        rows = block_rows(i, 32)
        opened = jax.nn.sigmoid(m.gp[rows, :].astype(F32))
        hidden_rows = tok[rows, :].astype(F32) + opened * m.br[rows, :]
        inv = lax.rsqrt(jnp.mean(hidden_rows * hidden_rows, axis=1, keepdims=True) + EPSILON)
        m.hid[rows, :] = hidden_rows
        m.inv[rows, :] = jnp.broadcast_to(inv, (32, 128))
        m.sc[pl.ds(pl.multiple_of(a * 128 + i * 32, 32), 32), :] = (
            hidden_rows * inv * m.gain[...]
        ).astype(BF16)

    each(0, 4, normalise)
    quad = lambda ref, i: ref.at[block_rows(i, 128), :]
    xy_peers(lambda p: xy_start(s.sc, quad(m.sc, a), quad(m.sc, a), p))
    xy_drain(s.sc, quad(m.sc, a))

    gather_mirror(s.fu, fu_view)
    gather_start(s.fd, fd_view(b), fd_view)
    gather_line(s.fg, fg_view, near)
    gather_line(s.fg, fg_view, across)
    each(0, 4, lambda zs: gather_pass(s.fg, fg_view, zs))
    gather_mirror(s.fd, fd_view)
    gather_line(s.fu, fu_view, near)
    gather_line(s.fu, fu_view, across)
    each(0, 4, lambda zs: gather_pass(s.fu, fu_view, zs))
    xy_peers(lambda p: xy_wait(s.sc, quad(m.sc, p), p))

    gate_w = lambda: m.fgu[0].reshape(width, pad)
    up_w = lambda: m.fgu[1].reshape(width, pad)

    def feed(i):
        rows = block_rows(i, 256)
        scaled = m.sc[rows, :]
        gate_act = nn(scaled, gate_w())
        up_act = nn(scaled, up_w())
        m.gact[rows, :] = gate_act
        m.uact[rows, :] = up_act
        m.inner[rows, :] = (gate_act * jax.nn.sigmoid(gate_act) * up_act).astype(BF16)

    each(0, 2, feed)
    gather_line(s.fd, fd_view, near)
    gather_line(s.fd, fd_view, across)
    each(0, 4, lambda zs: gather_pass(s.fd, fd_view, zs))
    share_rows = m.fdp.shape[1] - 8
    for i in range(4):
        m.ffd[2 * i * share_rows : 2 * (i + 1) * share_rows, :] = jnp.concatenate(
            [m.fdp[2 * i + j, 0:share_rows, :].astype(F32) for j in range(2)], axis=0
        ).astype(BF16)
    m.ffd[hidden:pad, :] = jnp.zeros((pad - hidden, width), BF16)

    def feed_out(step):
        i = lax.rem(a + step, 4)
        m.ysend[i] = nn(m.inner[block_rows(i, 128), :], m.ffd[...]).astype(BF16)
        xy_start(s.y, m.ysend.at[i], m.yrecv.at[a], i)

    each(1, 4, feed_out)
    m.own[...] = nn(m.inner[block_rows(a, 128), :], m.ffd[...])
    xy_peers(lambda p: xy_wait(s.y, m.yrecv.at[p], p))

    token_total = float(4 * length)
    m.fin0[...] = jnp.zeros_like(m.fin0)

    def finish(i):
        rows = block_rows(i, 32)
        final = m.hid[rows, :] + m.own[rows, :]
        a1, a2, a3 = lax.rem(a + 1, 4), lax.rem(a + 2, 4), lax.rem(a + 3, 4)
        final = final + m.yrecv[a1, rows, :].astype(F32)
        final = final + m.yrecv[a2, rows, :].astype(F32)
        final = final + m.yrecv[a3, rows, :].astype(F32)
        out_o[rows, :] = final.astype(BF16)
        error = final - tea[rows, :].astype(F32)
        counted = m.vcol[rows, :] * error
        grad = counted * (token_total / valid_total)
        m.dout[rows, :] = grad
        m.df[pl.ds(pl.multiple_of(a * 128 + i * 32, 32), 32), :] = grad.astype(BF16)
        squares = jnp.sum(counted * error, axis=0, keepdims=True)
        lanes = squares[:, 0:128]
        for j in range(1, width // 128):
            lanes = lanes + squares[:, j * 128 : j * 128 + 128]
        m.fin0[40:41, :] += lanes

    each(0, 4, finish)
    xy_peers(lambda p: xy_start(s.df, quad(m.df, a), quad(m.df, a), p))
    xy_drain(s.df, quad(m.df, a))
    xy_peers(lambda p: xy_wait(s.df, quad(m.df, p), p))

    def feed_back(i):
        rows = block_rows(i, 256)
        d_inner = nt(m.df[rows, :], m.ffd[...])
        gate_act = m.gact[rows, :]
        opened = jax.nn.sigmoid(gate_act)
        m.dga[rows, :] = (
            d_inner * m.uact[rows, :] * opened * (1.0 + gate_act * (1.0 - opened))
        ).astype(BF16)
        m.dua[rows, :] = (d_inner * gate_act * opened).astype(BF16)

    each(0, 2, feed_back)

    def scaled_grad(i):
        rows = block_rows(i, 128)
        return nt(m.dga[rows, :], gate_w()) + nt(m.dua[rows, :], up_w())

    def feed_in(step):
        i = lax.rem(a + step, 4)
        m.ysend[i] = scaled_grad(i).astype(BF16)
        xy_start(s.ds, m.ysend.at[i], m.yrecv.at[a], i)

    xy_peers(lambda p: xy_copy(s.y, m.ysend.at[0], m.ysend.at[0], p).wait_send())
    each(1, 4, feed_in)
    xy_drain(s.ds, m.ysend.at[0])
    m.own[...] = scaled_grad(a)

    def share_copy(pair, share, landing, slot, zt):
        return copy(share, landing.at[slot], pair[0].at[zt], pair[1].at[slot], (a, 2 * zt + c))

    def sum_start(pair, share, landing):
        share_copy(pair, share(near), landing, z, near).start()

        @pl.when(inner_chip)
        def _():
            share_copy(pair, share(across), landing, z, across).start()

        @pl.when(jnp.logical_not(inner_chip))
        def _():
            share_copy(pair, share(mirror), landing, z, mirror).start()
            copy(
                share(across), landing.at[mirror], pair[0].at[across], pair[1].at[mirror],
                (a, 2 * near + c),
            ).start()

    def sum_wait(pair, landing, zs):
        copy(
            landing.at[zs], landing.at[zs], pair[0].at[zs], pair[1].at[zs], (a, 2 * zs + c)
        ).wait_recv()

    def sum_pass(pair, share, landing, add):
        @pl.when(inner_chip)
        def _():
            sum_wait(pair, landing, across)
            add(mirror, across)
            share_copy(pair, share(mirror), landing, z, mirror).start()

    def sum_finish(pair, share, landing):
        sum_wait(pair, landing, near)
        sum_wait(pair, landing, mirror)

        @pl.when(jnp.logical_not(inner_chip))
        def _():
            sum_wait(pair, landing, across)

        finals.append(
            lambda: z_peers(
                lambda zt: share_copy(pair, share(zt), landing, zt, zt).wait_send()
            )
        )

    def landed(landing, where):
        total = landing[(near,) + where].astype(F32) + landing[(mirror,) + where].astype(F32)
        last = landing[(across,) + where].astype(F32)
        return total + jnp.where(inner_chip, 0.0, last)

    def down_grad(i):
        cols = pl.ds(pl.multiple_of(i * 256, 256), 256)
        m.ffd[block_rows(i, 256), :] = tn(m.inner[:, cols], m.df[...]).astype(BF16)

    each(0, pad // 256, down_grad)
    for i in range(4):
        pair = m.ffd[2 * i * share_rows : 2 * (i + 1) * share_rows, :].astype(F32)
        for j in range(2):
            m.gds[i, j] = jnp.concatenate(
                [pair[j * share_rows : (j + 1) * share_rows, :], jnp.zeros((8, width), F32)], axis=0
            ).astype(BF16)
    rgd_copy = copy(m.gds.at[:, 1 - c], m.gdr, s.rgd[0].at[4], s.rgd[1].at[4], (a, sib))
    rgd_copy.start()

    def up_gate_grad(i):
        cols = pl.ds(pl.multiple_of(i * 256, 256), 256)
        scaled = m.sc[:, cols]
        m.gus[:, :, 0, i] = tn(scaled, m.dga[...]).astype(BF16).reshape(4, 2, 32, pad)
        m.gus[:, :, 1, i] = tn(scaled, m.dua[...]).astype(BF16).reshape(4, 2, 32, pad)

    each(0, 4, up_gate_grad)
    rgu_copy = copy(m.gus.at[:, 1 - c], m.gur, s.rgu[0].at[4], s.rgu[1].at[4], (a, sib))
    rgu_copy.start()

    down_share = lambda zt: m.gds.at[zt, c]

    def add_down(zt):
        m.gds[zt, c] = (m.gds[zt, c].astype(F32) + m.gdr[zt].astype(F32)).astype(BF16)

    def pass_down(zt, slot):
        m.gds[zt, c] = (m.gds[zt, c].astype(F32) + m.gdz[slot].astype(F32)).astype(BF16)

    rgd_copy.wait_recv()
    z_peers(add_down)
    sum_start(s.rgd, down_share, m.gdz)

    xy_peers(lambda p: xy_wait(s.ds, m.yrecv.at[p], p))
    m.ggain[...] = jnp.zeros_like(m.ggain)

    def norm_back(i):
        rows = block_rows(i, 32)
        a1, a2, a3 = lax.rem(a + 1, 4), lax.rem(a + 2, 4), lax.rem(a + 3, 4)
        d_scaled = m.own[rows, :] + m.yrecv[a1, rows, :].astype(F32)
        d_scaled = d_scaled + m.yrecv[a2, rows, :].astype(F32)
        d_scaled = d_scaled + m.yrecv[a3, rows, :].astype(F32)
        inv = m.inv[rows, 0:1]
        normed = m.hid[rows, :] * inv
        m.ggain[...] += jnp.sum(d_scaled * normed, axis=0, keepdims=True)
        d_normed = d_scaled * m.gain[...]
        lean = jnp.mean(d_normed * normed, axis=1, keepdims=True)
        d_hidden = m.dout[rows, :] + inv * (d_normed - normed * lean)
        m.dout[rows, :] = d_hidden
        opened = jax.nn.sigmoid(m.gp[rows, :].astype(F32))
        m.dbr[rows, :] = (d_hidden * opened).astype(BF16)
        m.dgt[rows, :] = (d_hidden * m.br[rows, :] * opened * (1.0 - opened)).astype(BF16)

    each(0, 4, norm_back)
    gate_cols = pl.ds(384, 128)
    cols_of = lambda i: pl.ds(pl.multiple_of(i * 128, 128), 128)
    m.dms[...] = nt(m.dbr[...], m.wo_all[...]).astype(BF16)
    seq_peers(lambda p: seq_start(s.dm, m.dms.at[:, cols_of(p)], m.dm.at[own_rows, :], p))
    seq_peers(
        lambda p: seq_start(s.dg, m.dgt.at[:, cols_of(p)], m.dq.at[own_rows, gate_cols], p)
    )
    seq_drain(s.dm, m.dms.at[:, 0:128])
    seq_drain(s.dg, m.dgt.at[:, 0:128])
    m.dm[own_rows, :] = m.dms[:, head_cols]
    m.dq[own_rows, gate_cols] = m.dgt[:, head_cols]

    def out_grad(i):
        cols = pl.ds(pl.multiple_of(i * 256, 256), 256)
        m.gwos[i] = tn(m.mx[:, cols], m.dbr[...]).astype(BF16)

    def out_grad_send(step):
        i = lax.rem(a + step, 4)
        out_grad(i)
        xy_start(s.gwo, m.gwos.at[i], m.gwor.at[a], i)

    each(1, 4, out_grad_send)
    xy_drain(s.gwo, m.gwos.at[0])
    out_grad(a)

    up_gate_share = lambda zt: m.gus.at[zt, c]

    def add_up_gate(zt):
        def one(i):
            j = lax.div(i, 4)
            g = lax.rem(i, 4)
            m.gus[zt, c, j, g] = (
                m.gus[zt, c, j, g].astype(F32) + m.gur[zt, j, g].astype(F32)
            ).astype(BF16)

        each(0, 8, one)

    def pass_up_gate(zt, slot):
        def one(i):
            j = lax.div(i, 4)
            g = lax.rem(i, 4)
            m.gus[zt, c, j, g] = (
                m.gus[zt, c, j, g].astype(F32) + m.guz[slot, j, g].astype(F32)
            ).astype(BF16)

        each(0, 8, one)

    rgu_copy.wait_recv()
    z_peers(add_up_gate)
    sum_start(s.rgu, up_gate_share, m.guz)
    m.pgrad[...] = jnp.zeros_like(m.pgrad)

    def attend_back(i):
        rows = block_rows(i, 128)
        d_mixed = m.dm[rows, :]
        d_joint = nt(d_mixed, m.v[...])
        prob = m.probs[rows, :].astype(F32)
        turned = prob * d_joint
        fixed_prob = m.fprobs[rows, :]
        fixed_full = fixed_prob.astype(F32)
        fixed_turned = fixed_full * nt(d_mixed, m.fkv[16:32, :])
        delta = jnp.sum(turned, axis=1, keepdims=True) + jnp.sum(
            fixed_turned, axis=1, keepdims=True
        )
        d_raw = (
            scale * (turned - prob * delta) + m.decay[rows, :].astype(F32) * d_joint
        ).astype(BF16)
        m.probs[rows, :] = d_raw
        d_fixed = (fixed_turned - fixed_full * delta).astype(BF16)
        m.dq[rows, 0:128] = (
            nn(d_raw, m.k[...]) + scale * nn(d_fixed, m.fkv[0:16, :])
        ).astype(BF16)
        m.pgrad[0:16, :] += scale * tn(d_fixed, m.q[rows, :])
        m.pgrad[16:32, :] += tn(fixed_prob, d_mixed)

    attend_back(b)

    def attend_back_next(step):
        i = lax.rem(b + step, 8)
        seq_wait(s.dm, m.dm.at[block_rows(i, 128), :], i)
        seq_wait(s.dg, m.dq.at[block_rows(i, 128), gate_cols], i)
        attend_back(i)

    each(1, 4, attend_back_next)
    sum_pass(s.rgd, down_share, m.gdz, pass_down)
    each(4, 8, attend_back_next)

    m.fin0[0:32, :] = m.pgrad[...]
    for j in range(8):
        m.fin0[32 + j : 33 + j, :] = m.ggain[:, j * 128 : j * 128 + 128]
    m.fin1[a] = m.fin0[...]
    xy_peers(lambda p: xy_start(s.fin1, m.fin0, m.fin1.at[a], p))
    xy_drain(s.fin1, m.fin0)

    query_turned = jnp.transpose(m.q[...].astype(F32)).astype(BF16)
    mixed_turned = jnp.transpose(m.dm[...].astype(F32)).astype(BF16)

    def key_value_grad(i):
        cols = cols_of(i)
        rows = block_rows(i, 128)
        m.dq[rows, 128:256] = jnp.transpose(nn(query_turned, m.probs[:, cols])).astype(BF16)
        m.dq[rows, 256:384] = jnp.transpose(nn(mixed_turned, m.both[:, cols])).astype(BF16)

    each(0, 8, key_value_grad)

    sum_pass(s.rgu, up_gate_share, m.guz, pass_up_gate)
    def head_weight_grad(i):
        cols = pl.ds(pl.multiple_of(i * 256, 256), 256)
        m.gws[i] = tn(m.x_all[:, cols], m.dq[...]).astype(BF16)

    def head_weight_send(step):
        i = lax.rem(a + step, 4)
        head_weight_grad(i)
        xy_start(s.gw, m.gws.at[i], m.gwr.at[a], i)

    each(1, 4, head_weight_send)
    xy_drain(s.gw, m.gws.at[0])
    head_weight_grad(a)

    def token_grad(i):
        return nt(m.dq[block_rows(i, 128), :], m.wqk[...])

    def token_sib(step):
        zt = lax.rem(z + step, 4)
        m.gts[zt, 1 - c] = token_grad(2 * zt + 1 - c).astype(BF16)
        copy(
            m.gts.at[zt, 1 - c], m.gtr.at[zt], s.gt[0].at[4 + zt], s.gt[1].at[4 + zt],
            (a, sib),
        ).start()

    each(1, 5, token_sib)

    token_share = lambda zt: m.gts.at[zt, c]

    def token_line(step):
        zt = lax.rem(z + step, 4)
        mine = token_grad(2 * zt + c)
        copy(
            m.gtr.at[zt], m.gtr.at[zt], s.gt[0].at[4 + zt], s.gt[1].at[4 + zt], (a, sib)
        ).wait_recv()
        m.gts[zt, c] = (mine + m.gtr[zt].astype(F32)).astype(BF16)

    def pass_token(zt, slot):
        m.gts[zt, c] = (m.gts[zt, c].astype(F32) + m.yrecv[slot].astype(F32)).astype(BF16)

    each(1, 4, token_line)
    sum_start(s.gt, token_share, m.yrecv)
    m.own[...] = token_grad(b)
    finals.append(
        lambda: each(
            0, 4,
            lambda zt: copy(
                m.gtr.at[zt], m.gtr.at[zt], s.gt[0].at[4 + zt], s.gt[1].at[4 + zt], (a, sib)
            ).wait_send(),
        )
    )

    xy_peers(lambda p: xy_wait(s.fin1, m.fin1.at[p], p))
    m.fin2s[...] = (m.fin1[0] + m.fin1[1]) + (m.fin1[2] + m.fin1[3])
    m.fin2[b] = m.fin2s[32:48, :]
    seq_peers(lambda p: seq_start(s.fin2, m.fin2s.at[pl.ds(32, 16), :], m.fin2.at[b], p))
    seq_drain(s.fin2, m.fin2.at[0])
    holder = 2 * a + lax.div(b, 4)
    keeps = lambda p: (lax.div(b, 2) == a) & (lax.div(p, 4) == c)

    def pers_send(p):
        @pl.when(keeps(p))
        def _():
            copy(
                m.fin2s.at[pl.ds(0, 32), :], m.pers, s.pers[0].at[p], s.pers[1].at[0], (a, p)
            ).start()

    def pers_drain(p):
        @pl.when(keeps(p))
        def _():
            copy(m.pers, m.pers, s.pers[0].at[p], s.pers[1].at[0], (a, p)).wait_send()

    seq_peers(pers_send)
    finals.append(lambda: seq_peers(pers_drain))

    @pl.when(holder == b)
    def _():
        m.pers[...] = m.fin2s[0:32, :]

    sum_pass(s.gt, token_share, m.yrecv, pass_token)
    xy_peers(lambda p: xy_wait(s.gw, m.gwr.at[p], p))
    a1, a2, a3 = lax.rem(a + 1, 4), lax.rem(a + 2, 4), lax.rem(a + 3, 4)

    def head_sum(p):
        rows = block_rows(p, 32)
        total = m.gws[a, rows, :].astype(F32) + m.gwr[a1, rows, :].astype(F32)
        total = total + m.gwr[a2, rows, :].astype(F32)
        total = total + m.gwr[a3, rows, :].astype(F32)
        m.gas[p] = total.astype(BF16)

    def head_sum_send(p):
        head_sum(p)
        seq_start(s.gwa, m.gas.at[p], m.gar.at[b], p)

    seq_peers(head_sum_send)
    seq_drain(s.gwa, m.gas.at[0])
    head_sum(b)
    m.gar[b] = m.gas[b]

    xy_peers(lambda p: xy_wait(s.gwo, m.gwor.at[p], p))

    def out_sum(i):
        rows = block_rows(i, 32)
        total = m.gwos[a, rows, :].astype(F32) + m.gwor[a1, rows, :].astype(F32)
        total = total + m.gwor[a2, rows, :].astype(F32)
        total = total + m.gwor[a3, rows, :].astype(F32)
        m.gos[lax.div(i, 2), lax.rem(i, 2)] = total.astype(BF16)

    each(0, 8, out_sum)
    rgo_copy = copy(m.gos.at[:, 1 - c], m.gor, s.rgo[0].at[4], s.rgo[1].at[4], (a, sib))
    rgo_copy.start()

    sum_finish(s.rgu, up_gate_share, m.guz)

    def up_gate_sum(i):
        j = lax.div(i, 4)
        g = lax.rem(i, 4)
        total = m.gus[z, c, j, g].astype(F32) + m.gur[z, j, g].astype(F32)
        total = total + landed(m.guz, (j, g))
        m.gux[g, j] = total.astype(BF16)

    each(0, 8, up_gate_sum)
    xy_peers(lambda p: xy_start(s.gfx, m.gux.at[p], m.guxr.at[a], p))
    xy_drain(s.gfx, m.gux.at[0])
    m.guxr[a] = m.gux[a]

    rgo_copy.wait_recv()
    out_share = lambda zt: m.gos.at[zt, c]

    def add_out(zt):
        m.gos[zt, c] = (m.gos[zt, c].astype(F32) + m.gor[zt].astype(F32)).astype(BF16)

    def pass_out(zt, slot):
        m.gos[zt, c] = (m.gos[zt, c].astype(F32) + m.goz[slot].astype(F32)).astype(BF16)

    z_peers(add_out)
    sum_start(s.rgo, out_share, m.goz)
    sum_finish(s.rgd, down_share, m.gdz)
    some = slice(0, share_rows)
    fd_o[...] = (
        m.gds[z, c, some, :].astype(F32) + m.gdr[z, some, :].astype(F32)
    ) + landed(m.gdz, (some, slice(None)))
    sum_pass(s.rgo, out_share, m.goz, pass_out)

    sum_finish(s.gt, token_share, m.yrecv)
    copy(
        m.gtr.at[z], m.gtr.at[z], s.gt[0].at[4 + z], s.gt[1].at[4 + z], (a, sib)
    ).wait_recv()

    def token_sum(i):
        rows = block_rows(i, 32)
        total = m.dout[rows, :] + m.own[rows, :]
        total = total + m.gtr[z, rows, :].astype(F32)
        gtok_o[rows, :] = total + landed(m.yrecv, (rows, slice(None)))

    each(0, 4, token_sum)

    seq_peers(lambda p: seq_wait(s.gwa, m.gar.at[p], p))
    gar_o[...] = m.gar[...]

    xy_peers(lambda p: xy_wait(s.gfx, m.guxr.at[p], p))
    gux_o[...] = m.guxr[...]

    sum_finish(s.rgo, out_share, m.goz)
    gwo_o[...] = (m.gos[z, c].astype(F32) + m.gor[z].astype(F32)) + landed(m.goz, ())

    seq_peers(lambda p: seq_wait(s.fin2, m.fin2.at[p], p))
    everything = jnp.sum(m.fin2[...], axis=0)
    fin_o[0:8, :] = everything[0:8, :]
    loss = jnp.sum(everything[8:9, :]) / (2.0 * width * valid_total)
    fin_o[8:16, :] = jnp.full((8, 128), loss, F32)

    @pl.when(holder != b)
    def _():
        copy(m.pers, m.pers, s.pers[0].at[0], s.pers[1].at[0], (a, holder)).wait_recv()

    pers_o[...] = m.pers[...]

    rgd_copy.wait_send()
    rgu_copy.wait_send()
    rgo_copy.wait_send()
    for last in finals:
        last()


def finish_kernel(
    width, hidden, out, gtok, gar, gwo, fin, pers, gux, fd,
    out_o, loss_o, gtok_o, gq_o, gk_o, gv_o, gwo_o, gwg_o, pk_o, pv_o, gain_o, fg_o, fu_o, fd_o,
):
    a = lax.axis_index("head")
    b = lax.axis_index("seq")
    quarter = lax.rem(b, 4)

    def lanes(value):
        picked = value[:, 0:32]
        for j in range(1, 4):
            picked = jnp.where(quarter == j, value[:, 32 * j : 32 * j + 32], picked)
        return picked

    out_o[...] = out[...]
    gtok_o[...] = gtok[...]
    gwo_o[...] = gwo[...]
    fd_o[...] = fd[...]
    loss_o[...] = fin[8:9, 0:1]
    pk_o[...] = lanes(pers[0:16, :])
    pv_o[...] = lanes(pers[16:32, :])
    gain_o[...] = lanes(fin[pl.ds(2 * a + lax.div(b, 4), 1), :])
    for head in range(8):
        cols = slice(head * 128, head * 128 + 128)
        gq_o[:, cols] = gar[head, :, 0:128].astype(F32)
        gk_o[:, cols] = gar[head, :, 128:256].astype(F32)
        gv_o[:, cols] = gar[head, :, 256:384].astype(F32)
        gwg_o[:, cols] = gar[head, :, 384:512].astype(F32)
    for part in range(4):
        fg_o[:, part * hidden : (part + 1) * hidden] = gux[part, 0, :, 0:hidden].astype(F32)
        fu_o[:, part * hidden : (part + 1) * hidden] = gux[part, 1, :, 0:hidden].astype(F32)


def local_block(
    tokens, w_query, w_key, w_value, w_out, w_gate, persist_keys, persist_values, norm_gain,
    ff_gate, ff_up, ff_down, retention, doc_starts, valid, teacher,
):
    _, block, width = tokens.shape
    length = block * lax.axis_size("seq")
    hidden = ff_gate.shape[1] // 4
    pad = -(-hidden // 256) * 256
    share = ff_down.shape[0]
    table = scratch_table(width, block, hidden, pad, length)
    names = tuple(table)
    vmem = pl.BlockSpec(memory_space=pltpu.VMEM)
    shape = jax.ShapeDtypeStruct
    outs = (
        shape((block, width), BF16),
        shape((block, width), F32),
        shape((8, 32, 512), BF16),
        shape((32, width), F32),
        shape((16, 128), F32),
        shape((32, 128), F32),
        shape((4, 2, 32, pad), BF16),
        shape((share, width), F32),
    )
    scratch = [pltpu.VMEM(*table[name]) for name in names]
    for count in FLAGS.values():
        scratch += [pltpu.SemaphoreType.DMA((count,))] * 2
    result = pl.pallas_call(
        functools.partial(block_kernel, names, width, hidden, doc_starts.shape[1]),
        out_shape=outs,
        in_specs=[vmem] * 15 + [pl.BlockSpec(memory_space=pltpu.SMEM)],
        out_specs=[vmem] * len(outs),
        scratch_shapes=scratch,
        compiler_params=pltpu.CompilerParams(
            collective_id=0, has_side_effects=True, vmem_limit_bytes=VMEM_LIMIT
        ),
        name="block",
    )(
        tokens[0], w_query, w_key, w_value, w_out, w_gate, ff_gate, ff_up, ff_down, teacher[0],
        jnp.transpose(retention, (0, 2, 1)), persist_keys, persist_values, norm_gain[None],
        valid, doc_starts,
    )
    square = shape((32, width), F32)
    wide = shape((32, 4 * hidden), F32)
    finals = (
        outs[0], shape((1, 1), F32), outs[1], square, square, square, square, square,
        shape((P_SIZE, 32), F32), shape((P_SIZE, 32), F32), shape((1, 32), F32), wide, wide,
        outs[7],
    )
    done = pl.pallas_call(
        functools.partial(finish_kernel, width, hidden),
        out_shape=finals,
        in_specs=[vmem] * len(outs),
        out_specs=[vmem] * len(finals),
        name="finish",
    )(*result)
    (out, loss, gtok, gq, gk, gv, gwo, gwg, gpk, gpv, gain, fg, fu, fd) = done
    return (
        out[None], loss[0, 0], gtok[None], gq, gk, gv, gwo, gwg, gpk, gpv, gain[0], fg, fu, fd,
    )


VMEM_LIMIT = 62 << 20


def entering(value, axis, join, neutral, backward):
    count = lax.axis_size(axis)
    place = lax.axis_index(axis)
    ahead = count - 1 - place if backward else place
    gathered = jax.tree.map(
        lambda a, kind: lax.all_gather(a.astype(kind), axis), value, (jnp.bfloat16, jnp.bfloat16)
    )
    state = jax.tree.map(lambda a, e: jnp.zeros_like(a) + jnp.asarray(e, a.dtype), value, neutral)

    def one(hop, state):
        source = count - 1 - hop if backward else hop
        return join(
            state,
            jax.tree.map(
                lambda a, own: lax.dynamic_index_in_dim(a, source, 0, False).astype(own.dtype),
                gathered,
                value,
            ),
        )

    return lax.fori_loop(0, ahead, one, state)


def passed_along(value, axis, by):
    peers = lax.axis_size(axis)
    pairs = [(i, i + by) for i in range(peers) if 0 <= i + by < peers]
    return lax.ppermute(value, axis, pairs)


def from_behind(block, axis, distance):
    devices = range(lax.axis_size(axis))
    route = [((i - distance) % len(devices), i) for i in devices]
    return lax.ppermute(block, axis, route)


def product(left, right):
    return jnp.dot(left, right, preferred_element_type=jnp.float32)


def rows_outer(left, right):
    return jnp.einsum("nd,ne->de", left, right, preferred_element_type=jnp.float32)


def back_product(grad, weight):
    return jnp.einsum("ne,de->nd", grad, weight, preferred_element_type=jnp.float32)


def doc_index(starts, positions):
    return jnp.sum((starts[:, None, :] <= positions[None, :, None]).astype(jnp.int32), axis=-1) - 1


def doc_begin(starts, positions):
    return jnp.any(starts[:, None, :] == positions[None, :, None], axis=-1)


def chain_forward(earlier, later):
    return (earlier[0] * later[0], later[0][..., None, None] * earlier[1] + later[1])


def chain_backward(earlier, later):
    return (earlier[0] * later[0], later[1] + later[0][..., None, None] * earlier[1])


def masked_scores(query_rows, key_rows, query_pos, key_pos, query_seg, key_seg, scale):
    raw = (
        jnp.einsum("sqhd,skhd->sqhk", query_rows, key_rows, preferred_element_type=jnp.float32)
        * scale
    )
    allowed = (key_pos[None, None, :] <= query_pos[None, :, None]) & (
        key_seg[:, None, :] == query_seg[:, :, None]
    )
    return jnp.where(allowed[:, :, None, :], raw, MASKED)


def softmax_grads(
    query_rows,
    key_rows,
    value_rows,
    dout_rows,
    query_pos,
    key_pos,
    query_seg,
    key_seg,
    query_lse,
    query_delta,
    scale,
):
    scores = masked_scores(query_rows, key_rows, query_pos, key_pos, query_seg, key_seg, scale)
    probs = jnp.exp(scores - query_lse[..., None])
    prob_grad = jnp.einsum(
        "sqhd,skhd->sqhk", dout_rows, value_rows, preferred_element_type=jnp.float32
    )
    score_grad = (probs * (prob_grad - query_delta[..., None])).astype(jnp.bfloat16)
    return (probs.astype(jnp.bfloat16), score_grad)


def local(
    tokens,
    w_query,
    w_key,
    w_value,
    w_out,
    w_gate,
    persist_keys,
    persist_values,
    norm_gain,
    ff_gate,
    ff_up,
    ff_down,
    retention,
    doc_starts,
    valid,
    teacher,
):
    gathered = (
        lax.all_gather(w_query, ("head", "seq"), axis=0, tiled=True),
        lax.all_gather(w_key, ("head", "seq"), axis=0, tiled=True),
        lax.all_gather(w_value, ("head", "seq"), axis=0, tiled=True),
        lax.all_gather(w_out, ("head", "seq"), axis=0, tiled=True),
        lax.all_gather(w_gate, ("head", "seq"), axis=0, tiled=True),
        lax.all_gather(jnp.transpose(persist_keys), ("head", "seq"), axis=0, tiled=True),
        lax.all_gather(jnp.transpose(persist_values), ("head", "seq"), axis=0, tiled=True),
        lax.all_gather(norm_gain, ("head", "seq"), axis=0, tiled=True),
        lax.all_gather(ff_gate, ("head", "seq"), axis=0, tiled=True),
        lax.all_gather(ff_up, ("head", "seq"), axis=0, tiled=True),
        lax.all_gather(ff_down, ("head", "seq"), axis=0, tiled=True),
    )
    (
        query_weight,
        key_weight,
        value_weight,
        out_weight,
        gate_weight,
        fixed_key_cols,
        fixed_value_cols,
        gain_weight,
        ffn_gate,
        ffn_up,
        ffn_down,
    ) = gathered
    fixed_key_all = jnp.transpose(fixed_key_cols)
    fixed_value_all = jnp.transpose(fixed_value_cols)
    local_seqs, block, width = tokens.shape
    groups = lax.axis_size("head")
    heads = HEAD_COUNT // groups
    head_place = lax.axis_index("head")
    seq_place = lax.axis_index("seq")
    seq_count = lax.axis_size("seq")
    all_seqs = local_seqs * groups
    length = block * seq_count
    token_count = local_seqs * block
    scale = HD ** (-0.5)
    mem_scale = 0.125 / HD
    token_rows = tokens.reshape(token_count, width)
    query_tok = (
        product(token_rows, query_weight)
        .astype(jnp.bfloat16)
        .reshape(local_seqs, block, HEAD_COUNT, HD)
    )
    key_tok = (
        product(token_rows, key_weight)
        .astype(jnp.bfloat16)
        .reshape(local_seqs, block, HEAD_COUNT, HD)
    )
    value_tok = (
        product(token_rows, value_weight)
        .astype(jnp.bfloat16)
        .reshape(local_seqs, block, HEAD_COUNT, HD)
    )
    gate_pre = product(token_rows, gate_weight)
    query_heads, key_heads, value_heads = (
        lax.all_to_all(query_tok, "head", split_axis=2, concat_axis=0, tiled=True),
        lax.all_to_all(key_tok, "head", split_axis=2, concat_axis=0, tiled=True),
        lax.all_to_all(value_tok, "head", split_axis=2, concat_axis=0, tiled=True),
    )
    fixed_keys = lax.dynamic_slice_in_dim(
        fixed_key_all.reshape(P_SIZE, HEAD_COUNT, HD), head_place * heads, heads, 1
    )
    fixed_values = lax.dynamic_slice_in_dim(
        fixed_value_all.reshape(P_SIZE, HEAD_COUNT, HD), head_place * heads, heads, 1
    )
    own_start = seq_place * block
    own_pos = own_start + jnp.arange(block, dtype=jnp.int32)
    own_seg = doc_index(doc_starts, own_pos)
    own_begin = doc_begin(doc_starts, own_pos)
    last_row = own_start + block - 1
    fixed_scores = (
        jnp.einsum("sqhd,phd->sqhp", query_heads, fixed_keys, preferred_element_type=jnp.float32)
        * scale
    )
    top_start = jnp.max(fixed_scores, axis=-1)
    fixed_exp = jnp.exp(fixed_scores - top_start[..., None])
    acc_start = jnp.einsum(
        "sqhp,phd->sqhd",
        fixed_exp.astype(jnp.bfloat16),
        fixed_values,
        preferred_element_type=jnp.float32,
    )
    key_rows = lax.all_gather(key_heads, "seq", axis=1, tiled=True)
    value_rows = lax.all_gather(value_heads, "seq", axis=1, tiled=True)
    piece_keys = key_rows.shape[1]

    def attend_compute(state):
        running_top, running_total, running_acc = state
        key_pos = jnp.arange(piece_keys, dtype=jnp.int32)
        scores = masked_scores(
            query_heads, key_rows, own_pos, key_pos, own_seg, doc_index(doc_starts, key_pos), scale
        )
        new_top = jnp.maximum(running_top, jnp.max(scores, axis=-1))
        shrink = jnp.exp(running_top - new_top)
        weights_exp = jnp.exp(scores - new_top[..., None])
        new_total = running_total * shrink + jnp.sum(weights_exp, axis=-1)
        new_acc = running_acc * shrink[..., None] + jnp.einsum(
            "sqhk,skhd->sqhd",
            weights_exp.astype(jnp.bfloat16),
            value_rows,
            preferred_element_type=jnp.float32,
        )
        return (new_top, new_total, new_acc)

    final_top, final_total, final_acc = lax.cond(
        jnp.int32(0) <= last_row,
        attend_compute,
        lambda state: state,
        (top_start, jnp.sum(fixed_exp, axis=-1), acc_start),
    )
    attn_rows = final_acc / final_total[..., None]
    lse = final_top + jnp.log(final_total)
    log_retention = jnp.log(retention)
    running = jnp.cumsum(log_retention, axis=1)
    lane = jnp.transpose(running, (0, 2, 1))
    index = jnp.arange(block)
    linked = (index[None, :] <= index[:, None])[None] & (own_seg[:, None, :] == own_seg[:, :, None])
    decay = jnp.where(
        linked[:, None], jnp.exp(jnp.minimum(lane[:, :, :, None] - lane[:, :, None, :], 0.0)), 0.0
    )
    intersection = jnp.einsum(
        "sthd,suhd->shtu", query_heads, key_heads, preferred_element_type=jnp.float32
    )
    mixing = (mem_scale * intersection * decay).astype(jnp.bfloat16)
    inner_mem = jnp.einsum(
        "shtu,suhd->sthd", mixing, value_heads, preferred_element_type=jnp.float32
    )
    carried = ((own_seg == own_seg[:, :1]) & jnp.logical_not(own_begin[:, :1])).astype(jnp.float32)
    lead = jnp.exp(running) * carried[..., None]
    trail = jnp.where(
        (own_seg == own_seg[:, -1:])[..., None], jnp.exp(running[:, -1:, :] - running), 0.0
    )
    query_full = query_heads.astype(jnp.float32)
    key_full = key_heads.astype(jnp.float32)
    value_full = value_heads.astype(jnp.float32)
    block_state = jnp.einsum(
        "suhd,suhe->shde", key_full * trail[..., None], value_full, precision=HIGHEST
    )
    block_keep = lead[:, -1, :]
    identity = (jnp.ones_like(block_keep), jnp.zeros_like(block_state))
    chained = entering((block_keep, block_state), "seq", chain_forward, identity, False)
    state_in = chained[1]
    outer_mem = (
        mem_scale
        * lead[..., None]
        * jnp.einsum("sthd,shde->sthe", query_full, state_in, precision=HIGHEST)
    )
    mixed_heads = (attn_rows + inner_mem + outer_mem).astype(jnp.bfloat16)
    mixed_rows = lax.all_to_all(
        mixed_heads, "head", split_axis=0, concat_axis=2, tiled=True
    ).reshape(token_count, width)
    branch = product(mixed_rows, out_weight)
    gate_sigmoid = jax.nn.sigmoid(gate_pre)
    hidden = token_rows.astype(jnp.float32) + gate_sigmoid * branch
    inv_rms = lax.rsqrt(jnp.mean(hidden * hidden, axis=-1, keepdims=True) + EPSILON)
    normed = hidden * inv_rms
    gain_full = gain_weight.astype(jnp.float32)
    scaled = (normed * gain_full).astype(jnp.bfloat16)
    gate_act = product(scaled, ffn_gate)
    up_act = product(scaled, ffn_up)
    act_sigmoid = jax.nn.sigmoid(gate_act)
    silu_act = gate_act * act_sigmoid
    inner = (silu_act * up_act).astype(jnp.bfloat16)
    final = hidden + product(inner, ffn_down)
    output = final.astype(jnp.bfloat16).reshape(local_seqs, block, width)
    valid_rows = valid.reshape(token_count).astype(jnp.float32)
    error = final - teacher.reshape(token_count, width).astype(jnp.float32)
    sums = lax.psum(
        (jnp.sum(valid_rows * jnp.sum(error * error, axis=-1)), jnp.sum(valid_rows)),
        ("head", "seq"),
    )
    loss = sums[0] / (2.0 * width * sums[1])
    total_tokens = all_seqs * length
    d_out = valid_rows[:, None] * error * (total_tokens / sums[1])
    d_ffn = d_out.astype(jnp.bfloat16)
    grad_down = rows_outer(inner, d_ffn)
    d_inner = back_product(d_ffn, ffn_down)
    d_gate_act = (d_inner * up_act * act_sigmoid * (1.0 + gate_act * (1.0 - act_sigmoid))).astype(
        jnp.bfloat16
    )
    d_up_act = (d_inner * silu_act).astype(jnp.bfloat16)
    grad_ffn_gate = rows_outer(scaled, d_gate_act)
    grad_ffn_up = rows_outer(scaled, d_up_act)
    d_scaled = back_product(d_gate_act, ffn_gate) + back_product(d_up_act, ffn_up)
    grad_gain = jnp.sum(d_scaled * normed, axis=0)
    d_normed = d_scaled * gain_full
    d_hidden = d_out + inv_rms * (
        d_normed - normed * jnp.mean(d_normed * normed, axis=-1, keepdims=True)
    )
    d_branch = (d_hidden * gate_sigmoid).astype(jnp.bfloat16)
    d_gate = (d_hidden * branch * gate_sigmoid * (1.0 - gate_sigmoid)).astype(jnp.bfloat16)
    grad_out_weight = rows_outer(mixed_rows, d_branch)
    grad_gate_weight = rows_outer(token_rows, d_gate)
    d_mixed = (
        back_product(d_branch, out_weight)
        .astype(jnp.bfloat16)
        .reshape(local_seqs, block, HEAD_COUNT, HD)
    )
    dout_heads = lax.all_to_all(d_mixed, "head", split_axis=2, concat_axis=0, tiled=True)
    dout_full = dout_heads.astype(jnp.float32)
    delta = jnp.sum(dout_full * attn_rows, axis=-1)
    fixed_probs = jnp.exp(fixed_scores - lse[..., None])
    fixed_prob_grad = jnp.einsum(
        "sqhd,phd->sqhp", dout_heads, fixed_values, preferred_element_type=jnp.float32
    )
    fixed_score_grad = (fixed_probs * (fixed_prob_grad - delta[..., None])).astype(jnp.bfloat16)
    fixed_key_grad = (
        jnp.einsum(
            "sqhp,sqhd->phd", fixed_score_grad, query_heads, preferred_element_type=jnp.float32
        )
        * scale
    )
    fixed_value_grad = jnp.einsum(
        "sqhp,sqhd->phd",
        fixed_probs.astype(jnp.bfloat16),
        dout_heads,
        preferred_element_type=jnp.float32,
    )
    query_grad_start = (
        jnp.einsum(
            "sqhp,phd->sqhd", fixed_score_grad, fixed_keys, preferred_element_type=jnp.float32
        )
        * scale
    )
    fold_start = (query_grad_start,)
    back_key_rows = lax.all_gather(key_heads, "seq", axis=1, tiled=True)
    back_value_rows = lax.all_gather(value_heads, "seq", axis=1, tiled=True)
    back_piece_keys = back_key_rows.shape[1]

    def back_compute(state):
        key_pos = jnp.arange(back_piece_keys, dtype=jnp.int32)
        probs_low, score_grad = softmax_grads(
            query_heads,
            back_key_rows,
            back_value_rows,
            dout_heads,
            own_pos,
            key_pos,
            own_seg,
            doc_index(doc_starts, key_pos),
            lse,
            delta,
            scale,
        )
        query_grad = (
            state[0]
            + jnp.einsum(
                "sqhk,skhd->sqhd", score_grad, back_key_rows, preferred_element_type=jnp.float32
            )
            * scale
        )
        return (query_grad,)

    folded = lax.cond(jnp.int32(0) <= last_row, back_compute, lambda state: state, fold_start)
    query_att = folded[0]
    empty_local = jnp.zeros((all_seqs, block, heads, HD), jnp.float32)

    def visit(turn, state):
        key_rows, value_rows, key_acc, value_acc = state
        owner = (seq_place - turn) % seq_count
        start = owner * block

        def visit_compute(accs):
            key_pos = start + jnp.arange(block, dtype=jnp.int32)
            probs_low, score_grad = softmax_grads(
                query_heads,
                key_rows,
                value_rows,
                dout_heads,
                own_pos,
                key_pos,
                own_seg,
                doc_index(doc_starts, key_pos),
                lse,
                delta,
                scale,
            )
            key_next = (
                accs[0]
                + jnp.einsum(
                    "sqhk,sqhd->skhd", score_grad, query_heads, preferred_element_type=jnp.float32
                )
                * scale
            )
            value_next = accs[1] + jnp.einsum(
                "sqhk,sqhd->skhd", probs_low, dout_heads, preferred_element_type=jnp.float32
            )
            return (key_next, value_next)

        key_acc, value_acc = lax.cond(
            start <= last_row, visit_compute, lambda accs: accs, (key_acc, value_acc)
        )
        key_rows, value_rows = passed_along((key_rows, value_rows), "seq", 1)
        key_acc, value_acc = (
            from_behind(key_acc.astype(jnp.bfloat16), "seq", 1).astype(key_acc.dtype),
            from_behind(value_acc.astype(jnp.bfloat16), "seq", 1).astype(value_acc.dtype),
        )
        return (key_rows, value_rows, key_acc, value_acc)

    travelled = lax.fori_loop(
        0, seq_count, visit, (key_heads, value_heads, empty_local, empty_local)
    )
    key_att = travelled[2]
    value_att = travelled[3]
    mix_grad_raw = jnp.einsum(
        "sthe,suhe->shtu", dout_heads, value_heads, preferred_element_type=jnp.float32
    )
    intersection_grad = (mem_scale * mix_grad_raw * decay).astype(jnp.bfloat16)
    local_grad = mem_scale * jnp.einsum(
        "sthd,sthe->shde", query_full * lead[..., None], dout_full, precision=HIGHEST
    )
    state_grads = entering((block_keep, local_grad), "seq", chain_backward, identity, True)
    carry_grad = state_grads[1]
    query_mem = jnp.einsum(
        "shtu,suhd->sthd", intersection_grad, key_heads, preferred_element_type=jnp.float32
    )
    query_mem = query_mem + mem_scale * lead[..., None] * jnp.einsum(
        "sthe,shde->sthd", dout_full, state_in, precision=HIGHEST
    )
    key_mem = jnp.einsum(
        "shtu,sthd->suhd", intersection_grad, query_heads, preferred_element_type=jnp.float32
    )
    key_mem = key_mem + trail[..., None] * jnp.einsum(
        "suhe,shde->suhd", value_full, carry_grad, precision=HIGHEST
    )
    value_mem = jnp.einsum(
        "shtu,sthe->suhe", mixing, dout_heads, preferred_element_type=jnp.float32
    )
    value_mem = value_mem + jnp.einsum(
        "suhd,shde->suhe", key_full * trail[..., None], carry_grad, precision=HIGHEST
    )
    query_grad_heads = (query_att + query_mem).astype(jnp.bfloat16)
    key_grad_heads = (key_att + key_mem).astype(jnp.bfloat16)
    value_grad_heads = (value_att + value_mem).astype(jnp.bfloat16)
    query_back, key_back, value_back = (
        lax.all_to_all(query_grad_heads, "head", split_axis=0, concat_axis=2, tiled=True),
        lax.all_to_all(key_grad_heads, "head", split_axis=0, concat_axis=2, tiled=True),
        lax.all_to_all(value_grad_heads, "head", split_axis=0, concat_axis=2, tiled=True),
    )
    query_back = query_back.reshape(token_count, width)
    key_back = key_back.reshape(token_count, width)
    value_back = value_back.reshape(token_count, width)
    grad_query_weight = rows_outer(token_rows, query_back)
    grad_key_weight = rows_outer(token_rows, key_back)
    grad_value_weight = rows_outer(token_rows, value_back)
    token_grad = (
        d_hidden + back_product(d_gate, gate_weight) + back_product(query_back, query_weight)
    )
    token_grad = (
        token_grad + back_product(key_back, key_weight) + back_product(value_back, value_weight)
    )
    fixed_key_full = lax.dynamic_update_slice_in_dim(
        jnp.zeros((P_SIZE, HEAD_COUNT, HD), jnp.float32), fixed_key_grad, head_place * heads, 1
    ).reshape(P_SIZE, width)
    fixed_value_full = lax.dynamic_update_slice_in_dim(
        jnp.zeros((P_SIZE, HEAD_COUNT, HD), jnp.float32), fixed_value_grad, head_place * heads, 1
    ).reshape(P_SIZE, width)
    shards = (
        lax.psum_scatter(grad_query_weight, ("head", "seq"), scatter_dimension=0, tiled=True),
        lax.psum_scatter(grad_key_weight, ("head", "seq"), scatter_dimension=0, tiled=True),
        lax.psum_scatter(grad_value_weight, ("head", "seq"), scatter_dimension=0, tiled=True),
        lax.psum_scatter(grad_out_weight, ("head", "seq"), scatter_dimension=0, tiled=True),
        lax.psum_scatter(grad_gate_weight, ("head", "seq"), scatter_dimension=0, tiled=True),
        lax.psum_scatter(
            jnp.transpose(fixed_key_full), ("head", "seq"), scatter_dimension=0, tiled=True
        ),
        lax.psum_scatter(
            jnp.transpose(fixed_value_full), ("head", "seq"), scatter_dimension=0, tiled=True
        ),
        lax.psum_scatter(grad_gain, ("head", "seq"), scatter_dimension=0, tiled=True),
        lax.psum_scatter(grad_ffn_gate, ("head", "seq"), scatter_dimension=0, tiled=True),
        lax.psum_scatter(grad_ffn_up, ("head", "seq"), scatter_dimension=0, tiled=True),
        lax.psum_scatter(grad_down, ("head", "seq"), scatter_dimension=0, tiled=True),
    )
    return (
        output,
        loss,
        token_grad.reshape(local_seqs, block, width),
        shards[0],
        shards[1],
        shards[2],
        shards[3],
        shards[4],
        jnp.transpose(shards[5]),
        jnp.transpose(shards[6]),
        shards[7],
        shards[8],
        shards[9],
        shards[10],
    )


def solution(mesh):
    in_specs = (
        P("head", "seq", None),
        P(("head", "seq"), None),
        P(("head", "seq"), None),
        P(("head", "seq"), None),
        P(("head", "seq"), None),
        P(("head", "seq"), None),
        P(None, ("head", "seq")),
        P(None, ("head", "seq")),
        P(("head", "seq")),
        P(("head", "seq"), None),
        P(("head", "seq"), None),
        P(("head", "seq"), None),
        P(None, "seq", "head"),
        P(),
        P("head", "seq"),
        P("head", "seq", None),
    )
    out_specs = (
        P("head", "seq", None),
        P(),
        P("head", "seq", None),
        P(("head", "seq"), None),
        P(("head", "seq"), None),
        P(("head", "seq"), None),
        P(("head", "seq"), None),
        P(("head", "seq"), None),
        P(None, ("head", "seq")),
        P(None, ("head", "seq")),
        P(("head", "seq")),
        P(("head", "seq"), None),
        P(("head", "seq"), None),
        P(("head", "seq"), None),
    )
    fits = mesh.shape["head"] == 4 and mesh.shape["seq"] == HEAD_COUNT
    body = local_block if fits else local
    return jax.shard_map(body, mesh=mesh, in_specs=in_specs, out_specs=out_specs, check_vma=False)
```

```python
import functools
import types

import jax
import jax.numpy as jnp
from jax import lax
from jax.experimental import pallas as pl
from jax.experimental.pallas import tpu as pltpu
from jax.sharding import PartitionSpec as P

HEAD_COUNT = 8
HD = 128
P_SIZE = 16


HIGHEST = lax.Precision.HIGHEST
MASKED = -1e30
EPSILON = 1e-06
F32 = jnp.float32
BF16 = jnp.bfloat16
MESH_IDS = pl.DeviceIdType.MESH


def nn(left, right):
    return lax.dot_general(left, right, (((1,), (0,)), ((), ())), preferred_element_type=F32)


def nt(left, right):
    return lax.dot_general(left, right, (((1,), (1,)), ((), ())), preferred_element_type=F32)


def tn(left, right):
    return lax.dot_general(left, right, (((0,), (0,)), ((), ())), preferred_element_type=F32)


def tn_exact(left, right):
    return lax.dot_general(
        left, right, (((0,), (0,)), ((), ())), precision=HIGHEST, preferred_element_type=F32
    )


def nt_exact(left, right):
    return lax.dot_general(
        left, right, (((1,), (1,)), ((), ())), precision=HIGHEST, preferred_element_type=F32
    )


def nn_exact(left, right):
    return lax.dot_general(
        left, right, (((1,), (0,)), ((), ())), precision=HIGHEST, preferred_element_type=F32
    )


def block_rows(index, size):
    return pl.ds(pl.multiple_of(index * size, size), size)


def each(first, last, body):
    def step(index, carry):
        body(index)
        return carry

    lax.fori_loop(first, last, step, 0)


SEQ_FLAGS = dict(
    w1=8, t2=8, p2=8, x=8, wo=8, fg=8, fd=8, fu=8, gp=8, mx=8, dm=8, dg=8, rgu=8, rgd=8, rgo=8,
    gt=8, gwa=8, fin2=8, pers=8,
)
XY_FLAGS = dict(t1=4, p1=4, w2=4, fx=4, wox=4, sc=8, y=8, df=8, ds=8, gwo=4, gw=4, gfx=4, fin1=4)
FLAGS = SEQ_FLAGS | XY_FLAGS


def scratch_table(width, tokens, hidden, hidden_pad, length):
    seqs, blocks, block = 4, 8, 128
    table = dict(
        x_all=((length, width), BF16),
        wcs=((blocks, 32, 512), BF16),
        wqk=((width, 512), BF16),
        tile=((4, 8, 128), F32),
        pin=((32, 128), BF16),
        vcol=((block, 1), F32),
        t1=((4, 8, 128), F32),
        p1=((4, 32, 128), BF16),
        t2s=((16, 128), F32),
        t2=((8, 16, 128), F32),
        p2=((8, 32, 128), BF16),
        fs=((4, 2, 32, hidden_pad), BF16),
        fgu=((2, 4, 256, hidden_pad), BF16),
        fdp=((8, 96, width), BF16),
        ffd=((hidden_pad, width), BF16),
        wo_all=((4, 4, 2, 32, width), BF16),
        q=((length, HD), BF16),
        k=((length, HD), BF16),
        v=((length, HD), BF16),
        gps=((length, HD), BF16),
        fkv=((32, HD), BF16),
        gain=((1, width), F32),
        rrow=((1, length), F32),
        rcol=((block, 8), F32),
        probs=((length, length), BF16),
        decay=((length, length), BF16),
        both=((length, length), BF16),
        fprobs=((length, P_SIZE), BF16),
        mxs=((length, HD), BF16),
        mx=((block, width), BF16),
        gp=((block, width), BF16),
        hid=((block, width), F32),
        br=((block, width), F32),
        inv=((block, 128), F32),
        own=((block, width), F32),
        dout=((block, width), F32),
        sc=((4 * block, width), BF16),
        gact=((4 * block, hidden_pad), F32),
        uact=((4 * block, hidden_pad), F32),
        inner=((4 * block, hidden_pad), BF16),
        ysend=((4, block, width), BF16),
        yrecv=((4, block, width), BF16),
        df=((4 * block, width), BF16),
        dga=((4 * block, hidden_pad), BF16),
        dua=((4 * block, hidden_pad), BF16),
        dbr=((block, width), BF16),
        dgt=((block, width), BF16),
        dms=((block, width), BF16),
        dm=((length, HD), BF16),
        dq=((length, 512), BF16),
        ggain=((1, width), F32),
        gus=((4, 2, 2, 4, 32, hidden_pad), BF16),
        gur=((4, 2, 4, 32, hidden_pad), BF16),
        guz=((4, 2, 4, 32, hidden_pad), BF16),
        gux=((4, 2, 32, hidden_pad), BF16),
        guxr=((4, 2, 32, hidden_pad), BF16),
        gds=((4, 2, 96, width), BF16),
        gdr=((4, 96, width), BF16),
        gdz=((4, 96, width), BF16),
        gwos=((4, 256, width), BF16),
        gwor=((4, 256, width), BF16),
        gos=((4, 2, 32, width), BF16),
        gor=((4, 32, width), BF16),
        goz=((4, 32, width), BF16),
        gws=((4, 256, 512), BF16),
        gwr=((4, 256, 512), BF16),
        gas=((8, 32, 512), BF16),
        gar=((8, 32, 512), BF16),
        gts=((4, 2, block, width), BF16),
        gtr=((4, block, width), BF16),
        pgrad=((32, HD), F32),
        fin0=((48, 128), F32),
        fin1=((4, 48, 128), F32),
        fin2s=((48, 128), F32),
        fin2=((8, 16, 128), F32),
        pers=((32, 128), F32),
    )
    return table


def block_kernel(names, width, hidden, ndoc, *refs):
    (
        tok, wq, wk, wv, wo, wg, fgi, fui, fdi, tea, ret, pk, pv, gin, val, docs,
        out_o, gtok_o, gar_o, gwo_o, fin_o, pers_o, gux_o, fd_o,
    ) = refs[:24]
    m = types.SimpleNamespace(**dict(zip(names, refs[24 : 24 + len(names)])))
    sems = refs[24 + len(names) :]
    s = types.SimpleNamespace(**dict(zip(FLAGS, zip(sems[0::2], sems[1::2]))))
    pad = m.ffd.shape[0]
    length = m.x_all.shape[0]
    scale = HD ** (-0.5)
    mem_scale = 0.125 / HD

    a = lax.axis_index("head")
    b = lax.axis_index("seq")
    z = lax.div(b, 2)
    c = lax.rem(b, 2)
    sib = 2 * z + 1 - c
    near = z + 1 - 2 * lax.rem(z, 2)
    mirror = 3 - z
    across = 3 - near
    inner_chip = (z == 1) | (z == 2)

    def copy(src, dst, ssem, rsem, device):
        return pltpu.make_async_remote_copy(
            src_ref=src, dst_ref=dst, send_sem=ssem, recv_sem=rsem,
            device_id=device, device_id_type=MESH_IDS,
        )

    def seq_peers(body):
        each(1, 8, lambda step: body(lax.rem(b + step, 8)))

    def xy_peers(body):
        each(1, 4, lambda step: body(lax.rem(a + step, 4)))

    def z_peers(body):
        each(1, 4, lambda step: body(lax.rem(z + step, 4)))

    def seq_copy(pair, src, dst, peer, slot=None):
        slot = peer if slot is None else slot
        return copy(src, dst, pair[0].at[peer], pair[1].at[slot], (a, peer))

    def seq_start(pair, src, dst, peer):
        seq_copy(pair, src, dst, peer, b).start()

    def seq_wait(pair, dst, peer):
        seq_copy(pair, dst, dst, peer).wait_recv()

    def xy_copy(pair, src, dst, peer, slot=None):
        slot = peer if slot is None else slot
        return copy(src, dst, pair[0].at[peer], pair[1].at[slot], (peer, b))

    def xy_start(pair, src, dst, peer):
        xy_copy(pair, src, dst, peer, a).start()

    def xy_wait(pair, dst, peer):
        xy_copy(pair, dst, dst, peer).wait_recv()

    finals = []

    def seq_drain(pair, view):
        finals.append(lambda: seq_peers(lambda p: seq_copy(pair, view, view, p).wait_send()))

    def xy_drain(pair, view):
        finals.append(lambda: xy_peers(lambda p: xy_copy(pair, view, view, p).wait_send()))

    def line_copy(pair, src, dst, zt):
        return copy(src, dst, pair[0].at[zt], pair[1].at[z], (a, 2 * zt + c))

    def pass_copy(pair, src, dst, zs):
        return copy(src, dst, pair[0].at[4 + zs], pair[1].at[4 + zs], (a, sib))

    def line_start(pair, src, place):
        line_copy(pair, src, place(z), mirror).start()
        line_copy(pair, src, place(z), near).start()

        @pl.when(jnp.logical_not(inner_chip))
        def _():
            line_copy(pair, src, place(z), across).start()

        finals.append(lambda: z_peers(lambda zt: line_copy(pair, src, src, zt).wait_send()))

    def line_wait(pair, place, zs):
        block = place(zs)
        copy(block, block, pair[0].at[zs], pair[1].at[zs], (a, 2 * zs + c)).wait_recv()

    def line_hand_on(pair, place):
        block = place(mirror)

        @pl.when(inner_chip)
        def _():
            copy(
                block, block, pair[0].at[across], pair[1].at[mirror], (a, 2 * near + c)
            ).start()

    def gather_start(pair, src, view):
        line_start(pair, src, lambda zs: view(2 * zs + c))
        pass_copy(pair, src, view(b), z).start()
        finals.append(lambda: each(0, 4, lambda zs: pass_copy(pair, src, src, zs).wait_send()))

    def gather_line(pair, view, zs):
        block = view(2 * zs + c)
        line_wait(pair, lambda _: block, zs)
        pass_copy(pair, block, block, zs).start()

    def gather_mirror(pair, view):
        gather_line(pair, view, mirror)
        line_hand_on(pair, lambda zs: view(2 * zs + c))

    def gather_pass(pair, view, zs):
        block = view(2 * zs + 1 - c)
        pass_copy(pair, block, block, zs).wait_recv()

    barrier = pltpu.get_barrier_semaphore()
    seq_peers(lambda p: pl.semaphore_signal(barrier, 1, device_id=(a, p), device_id_type=MESH_IDS))
    xy_peers(lambda p: pl.semaphore_signal(barrier, 1, device_id=(p, b), device_id_type=MESH_IDS))

    for head in range(8):
        for place, weight in enumerate((wq, wk, wv, wg)):
            m.wcs[head, :, place * 128 : place * 128 + 128] = weight[
                :, head * 128 : head * 128 + 128
            ]
    for part in range(4):
        for place, weight in enumerate((fgi, fui)):
            m.fs[part, place, :, 0:hidden] = weight[:, part * hidden : (part + 1) * hidden]
            m.fs[part, place, :, hidden:pad] = jnp.zeros((32, pad - hidden), BF16)
    own_rows = block_rows(b, 128)
    piece = pl.ds(pl.multiple_of(a * 256 + b * 32, 32), 32)
    m.x_all[own_rows, :] = tok[...]
    m.wqk[piece, :] = m.wcs[b]
    m.wo_all[a, z, c] = wo[...]
    down = fdi[...].astype(F32)
    m.fdp[b] = jnp.concatenate(
        [down, jnp.zeros((96 - down.shape[0], width), F32)], axis=0
    ).astype(BF16)
    slot32 = block_rows(b, 32)
    m.fgu[:, a, slot32, :] = m.fs[a]
    row_id = lax.broadcasted_iota(jnp.int32, (128, 128), 0)
    col_id = lax.broadcasted_iota(jnp.int32, (128, 128), 1)
    place = (
        lax.broadcasted_iota(jnp.int32, (32, 128), 1)
        == lax.broadcasted_iota(jnp.int32, (32, 128), 0) + 32 * lax.rem(b, 4)
    ).astype(BF16)
    m.pin[0:16, :] = nn(pk[...], place).astype(BF16)
    m.pin[16:32, :] = nn(pv[...], place).astype(BF16)
    counted_row = val[...].astype(F32)
    m.vcol[...] = jnp.sum(jnp.where(row_id == col_id, counted_row, 0.0), axis=1, keepdims=True)
    gain_row = nn(gin[...], place)
    m.tile[...] = jnp.zeros_like(m.tile)
    for group in range(4):
        m.tile[group, 0:2, :] = jnp.log(ret[group])
        m.tile[group, 2:3, :] = counted_row
        m.tile[group, 3:4, :] = gain_row
    m.t1[a] = m.tile[a]
    m.p1[a] = m.pin[...]
    pl.semaphore_wait(barrier, 10)

    xy_peers(lambda p: xy_start(s.t1, m.tile.at[p], m.t1.at[a], p))
    xy_peers(lambda p: xy_start(s.p1, m.pin, m.p1.at[a], p))
    seq_peers(lambda p: seq_start(s.w1, m.wcs.at[p], m.wqk.at[piece, :], p))
    x_view = lambda i: m.x_all.at[block_rows(i, 128), :]
    gather_start(s.x, tok, x_view)
    wo_place = lambda zs: m.wo_all.at[a, zs, c]
    line_start(s.wo, wo, wo_place)
    xy_peers(lambda p: xy_start(s.fx, m.fs.at[p], m.fgu.at[:, a, slot32, :], p))
    xy_drain(s.t1, m.tile.at[0])
    xy_drain(s.p1, m.pin)
    seq_drain(s.w1, m.wcs.at[0])
    xy_drain(s.fx, m.fs.at[0])

    xy_peers(lambda p: xy_wait(s.t1, m.t1.at[p], p))
    xy_peers(lambda p: xy_wait(s.p1, m.p1.at[p], p))
    for group in range(4):
        m.t2s[2 * group : 2 * group + 2, :] = m.t1[group, 0:2, :]
        m.t2s[8 + group : 9 + group, :] = m.t1[group, 3:4, :]
    m.t2s[12:13, :] = (m.t1[0, 2:3, :] + m.t1[1, 2:3, :]) + (m.t1[2, 2:3, :] + m.t1[3, 2:3, :])
    m.t2s[13:16, :] = jnp.zeros((3, 128), F32)
    m.t2[b] = m.t2s[...]
    m.p2[b] = m.p1[lax.div(b, 2)]
    seq_peers(lambda p: seq_start(s.t2, m.t2s, m.t2.at[b], p))
    half = 4 * c

    def persist_send(p):
        @pl.when(lax.rem(p, 2) == lax.div(b, 4))
        def _():
            seq_start(s.p2, m.p1.at[lax.div(p, 2)], m.p2.at[b], p)

    def persist_drain(p):
        @pl.when(lax.rem(p, 2) == lax.div(b, 4))
        def _():
            seq_copy(s.p2, m.pin, m.pin, p).wait_send()

    def persist_wait(p):
        @pl.when(lax.div(p, 4) == c)
        def _():
            seq_wait(s.p2, m.p2.at[p], p)

    seq_peers(persist_send)
    finals.append(lambda: seq_peers(persist_drain))
    seq_drain(s.t2, m.t2s)

    seq_peers(lambda p: seq_wait(s.w1, m.wqk.at[pl.ds(pl.multiple_of(a * 256 + p * 32, 32), 32), :], p))
    quarter = lambda i: m.wqk.at[block_rows(i, 256), :]
    xy_peers(lambda p: xy_start(s.w2, quarter(a), quarter(a), p))
    xy_drain(s.w2, quarter(a))

    def project(i):
        rows = block_rows(i, 128)
        wide = nn(m.x_all[rows, :], m.wqk[...])
        m.q[rows, :] = wide[:, 0:128].astype(BF16)
        m.k[rows, :] = wide[:, 128:256].astype(BF16)
        m.v[rows, :] = wide[:, 256:384].astype(BF16)
        m.gps[rows, :] = wide[:, 384:512].astype(BF16)

    head_cols = pl.ds(pl.multiple_of(b * 128, 128), 128)

    xy_peers(lambda p: xy_wait(s.w2, quarter(p), p))
    project(b)
    m.gp[:, head_cols] = m.gps[own_rows, :]
    gather_pass(s.x, x_view, z)
    project(sib)

    def arrived_line(step):
        zs = lax.rem(z + step, 4)
        gather_line(s.x, x_view, zs)
        project(2 * zs + c)
        send_gate(2 * zs + c)

    gather_mirror(s.x, x_view)
    project(2 * mirror + c)
    gather_line(s.x, x_view, near)
    project(2 * near + c)
    gather_line(s.x, x_view, across)

    def arrived_pass(step):
        zs = lax.rem(z + step, 4)
        gather_pass(s.x, x_view, zs)
        project(2 * zs + 1 - c)

    wo_half = lambda i: m.wo_all.at[i, :, c]
    line_wait(s.wo, wo_place, mirror)
    line_hand_on(s.wo, wo_place)
    line_wait(s.wo, wo_place, near)
    line_wait(s.wo, wo_place, across)
    xy_peers(lambda p: xy_start(s.wox, wo_half(a), wo_half(a), p))
    xy_drain(s.wox, wo_half(a))
    wo_pass = lambda i, block: copy(
        block, block, s.wo[0].at[4 + i], s.wo[1].at[4 + i], (a, sib)
    )
    wo_pass(a, wo_half(a)).start()
    finals.append(lambda: each(0, 4, lambda i: wo_pass(i, wo_half(i)).wait_send()))
    project(2 * across + c)
    each(1, 4, arrived_pass)
    seq_peers(
        lambda p: seq_start(s.gp, m.gps.at[block_rows(p, 128), :], m.gp.at[:, head_cols], p)
    )
    seq_drain(s.gp, m.gps.at[own_rows, :])
    xy_peers(lambda p: xy_wait(s.fx, m.fgu.at[:, p, slot32, :], p))
    fg_view = lambda i: m.fgu.at[0, :, block_rows(i, 32), :]
    fu_view = lambda i: m.fgu.at[1, :, block_rows(i, 32), :]
    fd_view = lambda i: m.fdp.at[i]
    gather_start(s.fg, fg_view(b), fg_view)

    seq_peers(lambda p: seq_wait(s.t2, m.t2.at[p], p))
    seq_peers(persist_wait)
    small = m.t2[...]
    place16 = lax.broadcasted_iota(jnp.int32, (8, 16, 128), 1)
    rates = jnp.sum(jnp.where(place16 == b, small, 0.0), axis=1)
    valid_total = jnp.sum(jnp.where(place16 == 12, small, 0.0))
    for group in range(8):
        line = 8 + group // 2
        first = 4 * (group % 2)
        m.gain[:, group * 128 : group * 128 + 128] = (
            m.t2[first, line : line + 1, :] + m.t2[first + 1, line : line + 1, :]
        ) + (m.t2[first + 2, line : line + 1, :] + m.t2[first + 3, line : line + 1, :])
    m.fkv[...] = (
        (m.p2[half].astype(F32) + m.p2[half + 1].astype(F32))
        + (m.p2[half + 2].astype(F32) + m.p2[half + 3].astype(F32))
    ).astype(BF16)
    lower = (col_id <= row_id).astype(F32)
    within = nt_exact(rates, lower)
    earlier = (
        lax.broadcasted_iota(jnp.int32, (8, 8), 1) < lax.broadcasted_iota(jnp.int32, (8, 8), 0)
    ).astype(F32)
    base = nn_exact(earlier, jnp.broadcast_to(jnp.sum(rates, axis=1, keepdims=True), (8, 128)))
    running = within + base
    for i in range(8):
        m.rrow[:, i * 128 : i * 128 + 128] = running[i : i + 1, :]
    eye = (col_id == row_id).astype(F32)
    m.rcol[...] = nt_exact(eye, running)

    local_pos = lax.broadcasted_iota(jnp.int32, (128, 1), 0)
    lane8 = lax.broadcasted_iota(jnp.int32, (128, 8), 1)

    m.probs[...] = jnp.zeros_like(m.probs)
    m.both[...] = jnp.zeros_like(m.both)

    def by_extent(i, body):
        for j in range(4):
            pl.when(lax.div(i, 2) == j)(lambda j=j: body(i, 256 * (j + 1)))

    def attend_keys(i, extent):
        rows = block_rows(i, 128)
        keys = slice(0, extent)
        query = m.q[rows, :]
        raw = nt(query, m.k[keys, :])
        pos = i * 128 + local_pos
        begin = jnp.zeros_like(pos)
        for j in range(ndoc):
            start = docs[a, j]
            begin = jnp.where(start <= pos, jnp.maximum(begin, start), begin)
        key_pos = lax.broadcasted_iota(jnp.int32, (128, extent), 1)
        allowed = (key_pos <= pos) & (key_pos >= begin)
        scores = jnp.where(allowed, raw * scale, MASKED)
        fixed = nt(query, m.fkv[0:16, :]) * scale
        top = jnp.maximum(
            jnp.max(scores, axis=1, keepdims=True), jnp.max(fixed, axis=1, keepdims=True)
        )
        weight = jnp.exp(scores - top)
        fixed_weight = jnp.exp(fixed - top)
        share = 1.0 / (
            jnp.sum(weight, axis=1, keepdims=True) + jnp.sum(fixed_weight, axis=1, keepdims=True)
        )
        prob = weight * share
        fixed_prob = (fixed_weight * share).astype(BF16)
        reach = jnp.sum(jnp.where(lane8 == i, m.rcol[...], 0.0), axis=1, keepdims=True)
        kept = jnp.where(
            allowed, jnp.exp(jnp.minimum(reach - m.rrow[:, keys], 0.0)) * mem_scale, 0.0
        )
        joint = (prob + kept * raw).astype(BF16)
        m.probs[rows, keys] = prob.astype(BF16)
        m.decay[rows, keys] = kept.astype(BF16)
        m.both[rows, keys] = joint
        m.fprobs[rows, :] = fixed_prob
        mixed = nn(joint, m.v[keys, :]) + nn(fixed_prob, m.fkv[16:32, :])
        m.mxs[rows, :] = mixed.astype(BF16)

    attend = lambda i: by_extent(i, attend_keys)

    def attend_send(step):
        i = lax.rem(b + step, 8)
        attend(i)
        seq_start(s.mx, m.mxs.at[block_rows(i, 128), :], m.mx.at[:, head_cols], i)

    each(1, 6, attend_send)
    each(6, 7, attend_send)
    gather_mirror(s.fg, fg_view)
    gather_start(s.fu, fu_view(b), fu_view)
    each(7, 8, attend_send)
    seq_drain(s.mx, m.mxs.at[own_rows, :])
    attend(b)
    m.mx[:, head_cols] = m.mxs[own_rows, :]

    seq_peers(lambda p: seq_wait(s.gp, m.gp.at[:, pl.ds(pl.multiple_of(p * 128, 128), 128)], p))
    def wo_arrived(p):
        xy_wait(s.wox, wo_half(p), p)
        wo_pass(p, wo_half(p)).start()

    xy_peers(wo_arrived)
    each(0, 4, lambda i: wo_pass(i, m.wo_all.at[i, :, 1 - c]).wait_recv())
    seq_peers(lambda p: seq_wait(s.mx, m.mx.at[:, pl.ds(pl.multiple_of(p * 128, 128), 128)], p))

    out_w = lambda: m.wo_all[...].reshape(width, width)
    m.br[...] = nn(m.mx[...], out_w())

    half_row = lambda i: pl.ds(
        pl.multiple_of((4 * lax.div(i, 2) + a) * 64 + lax.rem(i, 2) * 32, 32), 32
    )
    quad = lambda ref, h, i: ref.at[block_rows(4 * h + i, 64), :]

    def half_copy(pair, src, dst, h, peer, slot):
        return copy(src, dst, pair[0].at[4 * h + peer], pair[1].at[4 * h + slot], (peer, b))

    def half_gather(pair, ref, h):
        xy_peers(lambda p: half_copy(pair, quad(ref, h, a), quad(ref, h, a), h, p, a).start())
        finals.append(
            lambda: xy_peers(
                lambda p: half_copy(pair, quad(ref, h, a), quad(ref, h, a), h, p, p).wait_send()
            )
        )

    def half_wait(pair, ref, h):
        xy_peers(lambda p: half_copy(pair, quad(ref, h, p), quad(ref, h, p), h, p, p).wait_recv())

    def half_scatter(pair, value, h):
        for i in range(4):
            m.ysend[i, h * 64 : h * 64 + 64, :] = value[i * 64 : i * 64 + 64, :].astype(BF16)
        rows = pl.ds(h * 64, 64)
        xy_peers(
            lambda p: half_copy(
                pair, m.ysend.at[p, rows, :], m.yrecv.at[a, rows, :], h, p, a
            ).start()
        )

    def half_sent(pair, h):
        rows = pl.ds(h * 64, 64)
        block = lambda p: m.ysend.at[p, rows, :]
        xy_peers(lambda p: half_copy(pair, block(p), block(p), h, p, p).wait_send())

    def half_land(pair, h):
        rows = pl.ds(h * 64, 64)
        block = lambda p: m.yrecv.at[p, rows, :]
        xy_peers(lambda p: half_copy(pair, block(p), block(p), h, p, p).wait_recv())

    def normalise(i):
        rows = block_rows(i, 32)
        opened = jax.nn.sigmoid(m.gp[rows, :].astype(F32))
        hidden_rows = tok[rows, :].astype(F32) + opened * m.br[rows, :]
        inv = lax.rsqrt(jnp.mean(hidden_rows * hidden_rows, axis=1, keepdims=True) + EPSILON)
        m.hid[rows, :] = hidden_rows
        m.inv[rows, :] = jnp.broadcast_to(inv, (32, 128))
        m.sc[half_row(i), :] = (
            hidden_rows * inv * m.gain[...]
        ).astype(BF16)

    each(0, 2, normalise)
    half_gather(s.sc, m.sc, 0)
    each(2, 4, normalise)
    half_gather(s.sc, m.sc, 1)

    gather_mirror(s.fu, fu_view)
    gather_start(s.fd, fd_view(b), fd_view)
    gather_line(s.fg, fg_view, near)
    gather_line(s.fg, fg_view, across)
    each(0, 4, lambda zs: gather_pass(s.fg, fg_view, zs))
    gather_mirror(s.fd, fd_view)
    gather_line(s.fu, fu_view, near)
    gather_line(s.fu, fu_view, across)
    each(0, 4, lambda zs: gather_pass(s.fu, fu_view, zs))
    half_wait(s.sc, m.sc, 0)

    gate_w = lambda: m.fgu[0].reshape(width, pad)
    up_w = lambda: m.fgu[1].reshape(width, pad)

    def feed(i):
        rows = block_rows(i, 256)
        scaled = m.sc[rows, :]
        gate_act = nn(scaled, gate_w())
        up_act = nn(scaled, up_w())
        m.gact[rows, :] = gate_act
        m.uact[rows, :] = up_act
        m.inner[rows, :] = (gate_act * jax.nn.sigmoid(gate_act) * up_act).astype(BF16)

    feed(0)
    gather_line(s.fd, fd_view, near)
    gather_line(s.fd, fd_view, across)
    each(0, 4, lambda zs: gather_pass(s.fd, fd_view, zs))
    share_rows = m.fdp.shape[1] - 8
    for i in range(4):
        m.ffd[2 * i * share_rows : 2 * (i + 1) * share_rows, :] = jnp.concatenate(
            [m.fdp[2 * i + j, 0:share_rows, :].astype(F32) for j in range(2)], axis=0
        ).astype(BF16)
    m.ffd[hidden:pad, :] = jnp.zeros((pad - hidden, width), BF16)

    def feed_out(h):
        half_scatter(s.y, nn(m.inner[block_rows(h, 256), :], m.ffd[...]), h)
        m.own[block_rows(h, 64), :] = nn(m.inner[block_rows(4 * h + a, 64), :], m.ffd[...])

    feed_out(0)
    half_wait(s.sc, m.sc, 1)
    feed(1)
    feed_out(1)
    half_land(s.y, 0)

    token_total = float(4 * length)
    m.fin0[...] = jnp.zeros_like(m.fin0)

    def finish(i):
        rows = block_rows(i, 32)
        final = m.hid[rows, :] + m.own[rows, :]
        a1, a2, a3 = lax.rem(a + 1, 4), lax.rem(a + 2, 4), lax.rem(a + 3, 4)
        final = final + m.yrecv[a1, rows, :].astype(F32)
        final = final + m.yrecv[a2, rows, :].astype(F32)
        final = final + m.yrecv[a3, rows, :].astype(F32)
        out_o[rows, :] = final.astype(BF16)
        error = final - tea[rows, :].astype(F32)
        counted = m.vcol[rows, :] * error
        grad = counted * (token_total / valid_total)
        m.dout[rows, :] = grad
        m.df[half_row(i), :] = grad.astype(BF16)
        squares = jnp.sum(counted * error, axis=0, keepdims=True)
        lanes = squares[:, 0:128]
        for j in range(1, width // 128):
            lanes = lanes + squares[:, j * 128 : j * 128 + 128]
        m.fin0[40:41, :] += lanes

    each(0, 2, finish)
    half_gather(s.df, m.df, 0)
    half_land(s.y, 1)
    each(2, 4, finish)
    half_gather(s.df, m.df, 1)
    half_wait(s.df, m.df, 0)

    def feed_back(i):
        rows = block_rows(i, 256)
        d_inner = nt(m.df[rows, :], m.ffd[...])
        gate_act = m.gact[rows, :]
        opened = jax.nn.sigmoid(gate_act)
        m.dga[rows, :] = (
            d_inner * m.uact[rows, :] * opened * (1.0 + gate_act * (1.0 - opened))
        ).astype(BF16)
        m.dua[rows, :] = (d_inner * gate_act * opened).astype(BF16)

    feed_back(0)

    def feed_in(h):
        rows = block_rows(h, 256)
        half_sent(s.y, h)
        half_scatter(s.ds, nt(m.dga[rows, :], gate_w()) + nt(m.dua[rows, :], up_w()), h)
        rows = block_rows(4 * h + a, 64)
        m.own[block_rows(h, 64), :] = nt(m.dga[rows, :], gate_w()) + nt(m.dua[rows, :], up_w())

    feed_in(0)
    half_wait(s.df, m.df, 1)
    feed_back(1)
    feed_in(1)
    finals.append(lambda: (half_sent(s.ds, 0), half_sent(s.ds, 1)))

    def share_copy(pair, share, landing, slot, zt):
        return copy(share, landing.at[slot], pair[0].at[zt], pair[1].at[slot], (a, 2 * zt + c))

    def sum_start(pair, share, landing):
        share_copy(pair, share(near), landing, z, near).start()

        @pl.when(inner_chip)
        def _():
            share_copy(pair, share(across), landing, z, across).start()

        @pl.when(jnp.logical_not(inner_chip))
        def _():
            share_copy(pair, share(mirror), landing, z, mirror).start()
            copy(
                share(across), landing.at[mirror], pair[0].at[across], pair[1].at[mirror],
                (a, 2 * near + c),
            ).start()

    def sum_wait(pair, landing, zs):
        copy(
            landing.at[zs], landing.at[zs], pair[0].at[zs], pair[1].at[zs], (a, 2 * zs + c)
        ).wait_recv()

    def sum_pass(pair, share, landing, add):
        @pl.when(inner_chip)
        def _():
            sum_wait(pair, landing, across)
            add(mirror, across)
            share_copy(pair, share(mirror), landing, z, mirror).start()

    def sum_finish(pair, share, landing):
        sum_wait(pair, landing, near)
        sum_wait(pair, landing, mirror)

        @pl.when(jnp.logical_not(inner_chip))
        def _():
            sum_wait(pair, landing, across)

        finals.append(
            lambda: z_peers(
                lambda zt: share_copy(pair, share(zt), landing, zt, zt).wait_send()
            )
        )

    def landed(landing, where):
        total = landing[(near,) + where].astype(F32) + landing[(mirror,) + where].astype(F32)
        last = landing[(across,) + where].astype(F32)
        return total + jnp.where(inner_chip, 0.0, last)

    def down_grad(i):
        cols = pl.ds(pl.multiple_of(i * 256, 256), 256)
        m.ffd[block_rows(i, 256), :] = tn(m.inner[:, cols], m.df[...]).astype(BF16)

    each(0, pad // 256, down_grad)
    for i in range(4):
        pair = m.ffd[2 * i * share_rows : 2 * (i + 1) * share_rows, :].astype(F32)
        for j in range(2):
            m.gds[i, j] = jnp.concatenate(
                [pair[j * share_rows : (j + 1) * share_rows, :], jnp.zeros((8, width), F32)], axis=0
            ).astype(BF16)
    rgd_copy = copy(m.gds.at[:, 1 - c], m.gdr, s.rgd[0].at[4], s.rgd[1].at[4], (a, sib))
    rgd_copy.start()

    def up_gate_grad(i):
        cols = pl.ds(pl.multiple_of(i * 256, 256), 256)
        scaled = m.sc[:, cols]
        m.gus[:, :, 0, i] = tn(scaled, m.dga[...]).astype(BF16).reshape(4, 2, 32, pad)
        m.gus[:, :, 1, i] = tn(scaled, m.dua[...]).astype(BF16).reshape(4, 2, 32, pad)

    each(0, 4, up_gate_grad)
    rgu_copy = copy(m.gus.at[:, 1 - c], m.gur, s.rgu[0].at[4], s.rgu[1].at[4], (a, sib))
    rgu_copy.start()

    down_share = lambda zt: m.gds.at[zt, c]

    def add_down(zt):
        m.gds[zt, c] = (m.gds[zt, c].astype(F32) + m.gdr[zt].astype(F32)).astype(BF16)

    def pass_down(zt, slot):
        m.gds[zt, c] = (m.gds[zt, c].astype(F32) + m.gdz[slot].astype(F32)).astype(BF16)

    rgd_copy.wait_recv()
    z_peers(add_down)
    sum_start(s.rgd, down_share, m.gdz)

    half_land(s.ds, 0)
    m.ggain[...] = jnp.zeros_like(m.ggain)

    def norm_back(i):
        rows = block_rows(i, 32)
        a1, a2, a3 = lax.rem(a + 1, 4), lax.rem(a + 2, 4), lax.rem(a + 3, 4)
        d_scaled = m.own[rows, :] + m.yrecv[a1, rows, :].astype(F32)
        d_scaled = d_scaled + m.yrecv[a2, rows, :].astype(F32)
        d_scaled = d_scaled + m.yrecv[a3, rows, :].astype(F32)
        inv = m.inv[rows, 0:1]
        normed = m.hid[rows, :] * inv
        m.ggain[...] += jnp.sum(d_scaled * normed, axis=0, keepdims=True)
        d_normed = d_scaled * m.gain[...]
        lean = jnp.mean(d_normed * normed, axis=1, keepdims=True)
        d_hidden = m.dout[rows, :] + inv * (d_normed - normed * lean)
        m.dout[rows, :] = d_hidden
        opened = jax.nn.sigmoid(m.gp[rows, :].astype(F32))
        m.dbr[rows, :] = (d_hidden * opened).astype(BF16)
        m.dgt[rows, :] = (d_hidden * m.br[rows, :] * opened * (1.0 - opened)).astype(BF16)

    each(0, 2, norm_back)
    half_land(s.ds, 1)
    each(2, 4, norm_back)
    gate_cols = pl.ds(384, 128)
    cols_of = lambda i: pl.ds(pl.multiple_of(i * 128, 128), 128)
    m.dms[...] = nt(m.dbr[...], out_w()).astype(BF16)
    seq_peers(lambda p: seq_start(s.dm, m.dms.at[:, cols_of(p)], m.dm.at[own_rows, :], p))
    seq_peers(
        lambda p: seq_start(s.dg, m.dgt.at[:, cols_of(p)], m.dq.at[own_rows, gate_cols], p)
    )
    seq_drain(s.dm, m.dms.at[:, 0:128])
    seq_drain(s.dg, m.dgt.at[:, 0:128])
    m.dm[own_rows, :] = m.dms[:, head_cols]
    m.dq[own_rows, gate_cols] = m.dgt[:, head_cols]

    def out_grad(i):
        cols = pl.ds(pl.multiple_of(i * 256, 256), 256)
        m.gwos[i] = tn(m.mx[:, cols], m.dbr[...]).astype(BF16)

    def out_grad_send(step):
        i = lax.rem(a + step, 4)
        out_grad(i)
        xy_start(s.gwo, m.gwos.at[i], m.gwor.at[a], i)

    each(1, 4, out_grad_send)
    xy_drain(s.gwo, m.gwos.at[0])
    out_grad(a)

    up_gate_share = lambda zt: m.gus.at[zt, c]

    def add_up_gate(zt):
        def one(i):
            j = lax.div(i, 4)
            g = lax.rem(i, 4)
            m.gus[zt, c, j, g] = (
                m.gus[zt, c, j, g].astype(F32) + m.gur[zt, j, g].astype(F32)
            ).astype(BF16)

        each(0, 8, one)

    def pass_up_gate(zt, slot):
        def one(i):
            j = lax.div(i, 4)
            g = lax.rem(i, 4)
            m.gus[zt, c, j, g] = (
                m.gus[zt, c, j, g].astype(F32) + m.guz[slot, j, g].astype(F32)
            ).astype(BF16)

        each(0, 8, one)

    rgu_copy.wait_recv()
    z_peers(add_up_gate)
    sum_start(s.rgu, up_gate_share, m.guz)
    m.pgrad[...] = jnp.zeros_like(m.pgrad)

    def attend_back_keys(i, extent):
        rows = block_rows(i, 128)
        keys = slice(0, extent)
        d_mixed = m.dm[rows, :]
        d_joint = nt(d_mixed, m.v[keys, :])
        prob = m.probs[rows, keys].astype(F32)
        turned = prob * d_joint
        fixed_prob = m.fprobs[rows, :]
        fixed_full = fixed_prob.astype(F32)
        fixed_turned = fixed_full * nt(d_mixed, m.fkv[16:32, :])
        delta = jnp.sum(turned, axis=1, keepdims=True) + jnp.sum(
            fixed_turned, axis=1, keepdims=True
        )
        d_raw = (
            scale * (turned - prob * delta) + m.decay[rows, keys].astype(F32) * d_joint
        ).astype(BF16)
        m.probs[rows, keys] = d_raw
        d_fixed = (fixed_turned - fixed_full * delta).astype(BF16)
        m.dq[rows, 0:128] = (
            nn(d_raw, m.k[keys, :]) + scale * nn(d_fixed, m.fkv[0:16, :])
        ).astype(BF16)
        m.pgrad[0:16, :] += scale * tn(d_fixed, m.q[rows, :])
        m.pgrad[16:32, :] += tn(fixed_prob, d_mixed)

    attend_back = lambda i: by_extent(i, attend_back_keys)

    attend_back(b)

    def attend_back_next(step):
        i = lax.rem(b + step, 8)
        seq_wait(s.dm, m.dm.at[block_rows(i, 128), :], i)
        seq_wait(s.dg, m.dq.at[block_rows(i, 128), gate_cols], i)
        attend_back(i)

    each(1, 4, attend_back_next)
    sum_pass(s.rgd, down_share, m.gdz, pass_down)
    each(4, 8, attend_back_next)

    m.fin0[0:32, :] = m.pgrad[...]
    for j in range(8):
        m.fin0[32 + j : 33 + j, :] = m.ggain[:, j * 128 : j * 128 + 128]
    m.fin1[a] = m.fin0[...]
    xy_peers(lambda p: xy_start(s.fin1, m.fin0, m.fin1.at[a], p))
    xy_drain(s.fin1, m.fin0)

    query_turned = jnp.transpose(m.q[...].astype(F32)).astype(BF16)
    mixed_turned = jnp.transpose(m.dm[...].astype(F32)).astype(BF16)

    def key_value_grad(i):
        cols = cols_of(i)
        rows = block_rows(i, 128)
        m.dq[rows, 128:256] = jnp.transpose(nn(query_turned, m.probs[:, cols])).astype(BF16)
        m.dq[rows, 256:384] = jnp.transpose(nn(mixed_turned, m.both[:, cols])).astype(BF16)

    each(0, 8, key_value_grad)

    sum_pass(s.rgu, up_gate_share, m.guz, pass_up_gate)
    def head_weight_grad(i):
        cols = pl.ds(pl.multiple_of(i * 256, 256), 256)
        m.gws[i] = tn(m.x_all[:, cols], m.dq[...]).astype(BF16)

    def head_weight_send(step):
        i = lax.rem(a + step, 4)
        head_weight_grad(i)
        xy_start(s.gw, m.gws.at[i], m.gwr.at[a], i)

    each(1, 4, head_weight_send)
    xy_drain(s.gw, m.gws.at[0])
    head_weight_grad(a)

    def token_grad(i):
        return nt(m.dq[block_rows(i, 128), :], m.wqk[...])

    def token_sib(step):
        zt = lax.rem(z + step, 4)
        m.gts[zt, 1 - c] = token_grad(2 * zt + 1 - c).astype(BF16)
        copy(
            m.gts.at[zt, 1 - c], m.gtr.at[zt], s.gt[0].at[4 + zt], s.gt[1].at[4 + zt],
            (a, sib),
        ).start()

    each(1, 5, token_sib)

    token_share = lambda zt: m.gts.at[zt, c]

    def token_line(step):
        zt = lax.rem(z + step, 4)
        mine = token_grad(2 * zt + c)
        copy(
            m.gtr.at[zt], m.gtr.at[zt], s.gt[0].at[4 + zt], s.gt[1].at[4 + zt], (a, sib)
        ).wait_recv()
        m.gts[zt, c] = (mine + m.gtr[zt].astype(F32)).astype(BF16)

    def pass_token(zt, slot):
        m.gts[zt, c] = (m.gts[zt, c].astype(F32) + m.yrecv[slot].astype(F32)).astype(BF16)

    each(1, 4, token_line)
    sum_start(s.gt, token_share, m.yrecv)
    m.own[...] = token_grad(b)
    finals.append(
        lambda: each(
            0, 4,
            lambda zt: copy(
                m.gtr.at[zt], m.gtr.at[zt], s.gt[0].at[4 + zt], s.gt[1].at[4 + zt], (a, sib)
            ).wait_send(),
        )
    )

    xy_peers(lambda p: xy_wait(s.fin1, m.fin1.at[p], p))
    m.fin2s[...] = (m.fin1[0] + m.fin1[1]) + (m.fin1[2] + m.fin1[3])
    m.fin2[b] = m.fin2s[32:48, :]
    seq_peers(lambda p: seq_start(s.fin2, m.fin2s.at[pl.ds(32, 16), :], m.fin2.at[b], p))
    seq_drain(s.fin2, m.fin2.at[0])
    holder = 2 * a + lax.div(b, 4)
    keeps = lambda p: (lax.div(b, 2) == a) & (lax.div(p, 4) == c)

    def pers_send(p):
        @pl.when(keeps(p))
        def _():
            copy(
                m.fin2s.at[pl.ds(0, 32), :], m.pers, s.pers[0].at[p], s.pers[1].at[0], (a, p)
            ).start()

    def pers_drain(p):
        @pl.when(keeps(p))
        def _():
            copy(m.pers, m.pers, s.pers[0].at[p], s.pers[1].at[0], (a, p)).wait_send()

    seq_peers(pers_send)
    finals.append(lambda: seq_peers(pers_drain))

    @pl.when(holder == b)
    def _():
        m.pers[...] = m.fin2s[0:32, :]

    sum_pass(s.gt, token_share, m.yrecv, pass_token)
    xy_peers(lambda p: xy_wait(s.gw, m.gwr.at[p], p))
    a1, a2, a3 = lax.rem(a + 1, 4), lax.rem(a + 2, 4), lax.rem(a + 3, 4)

    def head_sum(p):
        rows = block_rows(p, 32)
        total = m.gws[a, rows, :].astype(F32) + m.gwr[a1, rows, :].astype(F32)
        total = total + m.gwr[a2, rows, :].astype(F32)
        total = total + m.gwr[a3, rows, :].astype(F32)
        m.gas[p] = total.astype(BF16)

    def head_sum_send(p):
        head_sum(p)
        seq_start(s.gwa, m.gas.at[p], m.gar.at[b], p)

    seq_peers(head_sum_send)
    seq_drain(s.gwa, m.gas.at[0])
    head_sum(b)
    m.gar[b] = m.gas[b]

    xy_peers(lambda p: xy_wait(s.gwo, m.gwor.at[p], p))

    def out_sum(i):
        rows = block_rows(i, 32)
        total = m.gwos[a, rows, :].astype(F32) + m.gwor[a1, rows, :].astype(F32)
        total = total + m.gwor[a2, rows, :].astype(F32)
        total = total + m.gwor[a3, rows, :].astype(F32)
        m.gos[lax.div(i, 2), lax.rem(i, 2)] = total.astype(BF16)

    each(0, 8, out_sum)
    rgo_copy = copy(m.gos.at[:, 1 - c], m.gor, s.rgo[0].at[4], s.rgo[1].at[4], (a, sib))
    rgo_copy.start()

    sum_finish(s.rgu, up_gate_share, m.guz)

    def up_gate_sum(i):
        j = lax.div(i, 4)
        g = lax.rem(i, 4)
        total = m.gus[z, c, j, g].astype(F32) + m.gur[z, j, g].astype(F32)
        total = total + landed(m.guz, (j, g))
        m.gux[g, j] = total.astype(BF16)

    each(0, 8, up_gate_sum)
    xy_peers(lambda p: xy_start(s.gfx, m.gux.at[p], m.guxr.at[a], p))
    xy_drain(s.gfx, m.gux.at[0])
    m.guxr[a] = m.gux[a]

    rgo_copy.wait_recv()
    out_share = lambda zt: m.gos.at[zt, c]

    def add_out(zt):
        m.gos[zt, c] = (m.gos[zt, c].astype(F32) + m.gor[zt].astype(F32)).astype(BF16)

    def pass_out(zt, slot):
        m.gos[zt, c] = (m.gos[zt, c].astype(F32) + m.goz[slot].astype(F32)).astype(BF16)

    z_peers(add_out)
    sum_start(s.rgo, out_share, m.goz)
    sum_finish(s.rgd, down_share, m.gdz)
    some = slice(0, share_rows)
    fd_o[...] = (
        m.gds[z, c, some, :].astype(F32) + m.gdr[z, some, :].astype(F32)
    ) + landed(m.gdz, (some, slice(None)))
    sum_pass(s.rgo, out_share, m.goz, pass_out)

    sum_finish(s.gt, token_share, m.yrecv)
    copy(
        m.gtr.at[z], m.gtr.at[z], s.gt[0].at[4 + z], s.gt[1].at[4 + z], (a, sib)
    ).wait_recv()

    def token_sum(i):
        rows = block_rows(i, 32)
        total = m.dout[rows, :] + m.own[rows, :]
        total = total + m.gtr[z, rows, :].astype(F32)
        gtok_o[rows, :] = total + landed(m.yrecv, (rows, slice(None)))

    each(0, 4, token_sum)

    seq_peers(lambda p: seq_wait(s.gwa, m.gar.at[p], p))
    gar_o[...] = m.gar[...]

    xy_peers(lambda p: xy_wait(s.gfx, m.guxr.at[p], p))
    gux_o[...] = m.guxr[...]

    sum_finish(s.rgo, out_share, m.goz)
    gwo_o[...] = (m.gos[z, c].astype(F32) + m.gor[z].astype(F32)) + landed(m.goz, ())

    seq_peers(lambda p: seq_wait(s.fin2, m.fin2.at[p], p))
    everything = jnp.sum(m.fin2[...], axis=0)
    fin_o[0:8, :] = everything[0:8, :]
    loss = jnp.sum(everything[8:9, :]) / (2.0 * width * valid_total)
    fin_o[8:16, :] = jnp.full((8, 128), loss, F32)

    @pl.when(holder != b)
    def _():
        copy(m.pers, m.pers, s.pers[0].at[0], s.pers[1].at[0], (a, holder)).wait_recv()

    pers_o[...] = m.pers[...]

    rgd_copy.wait_send()
    rgu_copy.wait_send()
    rgo_copy.wait_send()
    for last in finals:
        last()


def finish_kernel(
    width, hidden, out, gtok, gar, gwo, fin, pers, gux, fd,
    out_o, loss_o, gtok_o, gq_o, gk_o, gv_o, gwo_o, gwg_o, pk_o, pv_o, gain_o, fg_o, fu_o, fd_o,
):
    a = lax.axis_index("head")
    b = lax.axis_index("seq")
    quarter = lax.rem(b, 4)

    def lanes(value):
        picked = value[:, 0:32]
        for j in range(1, 4):
            picked = jnp.where(quarter == j, value[:, 32 * j : 32 * j + 32], picked)
        return picked

    out_o[...] = out[...]
    gtok_o[...] = gtok[...]
    gwo_o[...] = gwo[...]
    fd_o[...] = fd[...]
    loss_o[...] = fin[8:9, 0:1]
    pk_o[...] = lanes(pers[0:16, :])
    pv_o[...] = lanes(pers[16:32, :])
    gain_o[...] = lanes(fin[pl.ds(2 * a + lax.div(b, 4), 1), :])
    for head in range(8):
        cols = slice(head * 128, head * 128 + 128)
        gq_o[:, cols] = gar[head, :, 0:128].astype(F32)
        gk_o[:, cols] = gar[head, :, 128:256].astype(F32)
        gv_o[:, cols] = gar[head, :, 256:384].astype(F32)
        gwg_o[:, cols] = gar[head, :, 384:512].astype(F32)
    for part in range(4):
        fg_o[:, part * hidden : (part + 1) * hidden] = gux[part, 0, :, 0:hidden].astype(F32)
        fu_o[:, part * hidden : (part + 1) * hidden] = gux[part, 1, :, 0:hidden].astype(F32)


def local_block(
    tokens, w_query, w_key, w_value, w_out, w_gate, persist_keys, persist_values, norm_gain,
    ff_gate, ff_up, ff_down, retention, doc_starts, valid, teacher,
):
    _, block, width = tokens.shape
    length = block * lax.axis_size("seq")
    hidden = ff_gate.shape[1] // 4
    pad = -(-hidden // 256) * 256
    share = ff_down.shape[0]
    table = scratch_table(width, block, hidden, pad, length)
    names = tuple(table)
    vmem = pl.BlockSpec(memory_space=pltpu.VMEM)
    shape = jax.ShapeDtypeStruct
    outs = (
        shape((block, width), BF16),
        shape((block, width), F32),
        shape((8, 32, 512), BF16),
        shape((32, width), F32),
        shape((16, 128), F32),
        shape((32, 128), F32),
        shape((4, 2, 32, pad), BF16),
        shape((share, width), F32),
    )
    scratch = [pltpu.VMEM(*table[name]) for name in names]
    for count in FLAGS.values():
        scratch += [pltpu.SemaphoreType.DMA((count,))] * 2
    result = pl.pallas_call(
        functools.partial(block_kernel, names, width, hidden, doc_starts.shape[1]),
        out_shape=outs,
        in_specs=[vmem] * 15 + [pl.BlockSpec(memory_space=pltpu.SMEM)],
        out_specs=[vmem] * len(outs),
        scratch_shapes=scratch,
        compiler_params=pltpu.CompilerParams(
            collective_id=0, has_side_effects=True, vmem_limit_bytes=VMEM_LIMIT
        ),
        name="block",
    )(
        tokens[0], w_query, w_key, w_value, w_out, w_gate, ff_gate, ff_up, ff_down, teacher[0],
        jnp.transpose(retention, (0, 2, 1)), persist_keys, persist_values, norm_gain[None],
        valid, doc_starts,
    )
    square = shape((32, width), F32)
    wide = shape((32, 4 * hidden), F32)
    finals = (
        outs[0], shape((1, 1), F32), outs[1], square, square, square, square, square,
        shape((P_SIZE, 32), F32), shape((P_SIZE, 32), F32), shape((1, 32), F32), wide, wide,
        outs[7],
    )
    done = pl.pallas_call(
        functools.partial(finish_kernel, width, hidden),
        out_shape=finals,
        in_specs=[vmem] * len(outs),
        out_specs=[vmem] * len(finals),
        name="finish",
    )(*result)
    (out, loss, gtok, gq, gk, gv, gwo, gwg, gpk, gpv, gain, fg, fu, fd) = done
    return (
        out[None], loss[0, 0], gtok[None], gq, gk, gv, gwo, gwg, gpk, gpv, gain[0], fg, fu, fd,
    )


VMEM_LIMIT = 62 << 20


def entering(value, axis, join, neutral, backward):
    count = lax.axis_size(axis)
    place = lax.axis_index(axis)
    ahead = count - 1 - place if backward else place
    gathered = jax.tree.map(
        lambda a, kind: lax.all_gather(a.astype(kind), axis), value, (jnp.bfloat16, jnp.bfloat16)
    )
    state = jax.tree.map(lambda a, e: jnp.zeros_like(a) + jnp.asarray(e, a.dtype), value, neutral)

    def one(hop, state):
        source = count - 1 - hop if backward else hop
        return join(
            state,
            jax.tree.map(
                lambda a, own: lax.dynamic_index_in_dim(a, source, 0, False).astype(own.dtype),
                gathered,
                value,
            ),
        )

    return lax.fori_loop(0, ahead, one, state)


def passed_along(value, axis, by):
    peers = lax.axis_size(axis)
    pairs = [(i, i + by) for i in range(peers) if 0 <= i + by < peers]
    return lax.ppermute(value, axis, pairs)


def from_behind(block, axis, distance):
    devices = range(lax.axis_size(axis))
    route = [((i - distance) % len(devices), i) for i in devices]
    return lax.ppermute(block, axis, route)


def product(left, right):
    return jnp.dot(left, right, preferred_element_type=jnp.float32)


def rows_outer(left, right):
    return jnp.einsum("nd,ne->de", left, right, preferred_element_type=jnp.float32)


def back_product(grad, weight):
    return jnp.einsum("ne,de->nd", grad, weight, preferred_element_type=jnp.float32)


def doc_index(starts, positions):
    return jnp.sum((starts[:, None, :] <= positions[None, :, None]).astype(jnp.int32), axis=-1) - 1


def doc_begin(starts, positions):
    return jnp.any(starts[:, None, :] == positions[None, :, None], axis=-1)


def chain_forward(earlier, later):
    return (earlier[0] * later[0], later[0][..., None, None] * earlier[1] + later[1])


def chain_backward(earlier, later):
    return (earlier[0] * later[0], later[1] + later[0][..., None, None] * earlier[1])


def masked_scores(query_rows, key_rows, query_pos, key_pos, query_seg, key_seg, scale):
    raw = (
        jnp.einsum("sqhd,skhd->sqhk", query_rows, key_rows, preferred_element_type=jnp.float32)
        * scale
    )
    allowed = (key_pos[None, None, :] <= query_pos[None, :, None]) & (
        key_seg[:, None, :] == query_seg[:, :, None]
    )
    return jnp.where(allowed[:, :, None, :], raw, MASKED)


def softmax_grads(
    query_rows,
    key_rows,
    value_rows,
    dout_rows,
    query_pos,
    key_pos,
    query_seg,
    key_seg,
    query_lse,
    query_delta,
    scale,
):
    scores = masked_scores(query_rows, key_rows, query_pos, key_pos, query_seg, key_seg, scale)
    probs = jnp.exp(scores - query_lse[..., None])
    prob_grad = jnp.einsum(
        "sqhd,skhd->sqhk", dout_rows, value_rows, preferred_element_type=jnp.float32
    )
    score_grad = (probs * (prob_grad - query_delta[..., None])).astype(jnp.bfloat16)
    return (probs.astype(jnp.bfloat16), score_grad)


def local(
    tokens,
    w_query,
    w_key,
    w_value,
    w_out,
    w_gate,
    persist_keys,
    persist_values,
    norm_gain,
    ff_gate,
    ff_up,
    ff_down,
    retention,
    doc_starts,
    valid,
    teacher,
):
    gathered = (
        lax.all_gather(w_query, ("head", "seq"), axis=0, tiled=True),
        lax.all_gather(w_key, ("head", "seq"), axis=0, tiled=True),
        lax.all_gather(w_value, ("head", "seq"), axis=0, tiled=True),
        lax.all_gather(w_out, ("head", "seq"), axis=0, tiled=True),
        lax.all_gather(w_gate, ("head", "seq"), axis=0, tiled=True),
        lax.all_gather(jnp.transpose(persist_keys), ("head", "seq"), axis=0, tiled=True),
        lax.all_gather(jnp.transpose(persist_values), ("head", "seq"), axis=0, tiled=True),
        lax.all_gather(norm_gain, ("head", "seq"), axis=0, tiled=True),
        lax.all_gather(ff_gate, ("head", "seq"), axis=0, tiled=True),
        lax.all_gather(ff_up, ("head", "seq"), axis=0, tiled=True),
        lax.all_gather(ff_down, ("head", "seq"), axis=0, tiled=True),
    )
    (
        query_weight,
        key_weight,
        value_weight,
        out_weight,
        gate_weight,
        fixed_key_cols,
        fixed_value_cols,
        gain_weight,
        ffn_gate,
        ffn_up,
        ffn_down,
    ) = gathered
    fixed_key_all = jnp.transpose(fixed_key_cols)
    fixed_value_all = jnp.transpose(fixed_value_cols)
    local_seqs, block, width = tokens.shape
    groups = lax.axis_size("head")
    heads = HEAD_COUNT // groups
    head_place = lax.axis_index("head")
    seq_place = lax.axis_index("seq")
    seq_count = lax.axis_size("seq")
    all_seqs = local_seqs * groups
    length = block * seq_count
    token_count = local_seqs * block
    scale = HD ** (-0.5)
    mem_scale = 0.125 / HD
    token_rows = tokens.reshape(token_count, width)
    query_tok = (
        product(token_rows, query_weight)
        .astype(jnp.bfloat16)
        .reshape(local_seqs, block, HEAD_COUNT, HD)
    )
    key_tok = (
        product(token_rows, key_weight)
        .astype(jnp.bfloat16)
        .reshape(local_seqs, block, HEAD_COUNT, HD)
    )
    value_tok = (
        product(token_rows, value_weight)
        .astype(jnp.bfloat16)
        .reshape(local_seqs, block, HEAD_COUNT, HD)
    )
    gate_pre = product(token_rows, gate_weight)
    query_heads, key_heads, value_heads = (
        lax.all_to_all(query_tok, "head", split_axis=2, concat_axis=0, tiled=True),
        lax.all_to_all(key_tok, "head", split_axis=2, concat_axis=0, tiled=True),
        lax.all_to_all(value_tok, "head", split_axis=2, concat_axis=0, tiled=True),
    )
    fixed_keys = lax.dynamic_slice_in_dim(
        fixed_key_all.reshape(P_SIZE, HEAD_COUNT, HD), head_place * heads, heads, 1
    )
    fixed_values = lax.dynamic_slice_in_dim(
        fixed_value_all.reshape(P_SIZE, HEAD_COUNT, HD), head_place * heads, heads, 1
    )
    own_start = seq_place * block
    own_pos = own_start + jnp.arange(block, dtype=jnp.int32)
    own_seg = doc_index(doc_starts, own_pos)
    own_begin = doc_begin(doc_starts, own_pos)
    last_row = own_start + block - 1
    fixed_scores = (
        jnp.einsum("sqhd,phd->sqhp", query_heads, fixed_keys, preferred_element_type=jnp.float32)
        * scale
    )
    top_start = jnp.max(fixed_scores, axis=-1)
    fixed_exp = jnp.exp(fixed_scores - top_start[..., None])
    acc_start = jnp.einsum(
        "sqhp,phd->sqhd",
        fixed_exp.astype(jnp.bfloat16),
        fixed_values,
        preferred_element_type=jnp.float32,
    )
    key_rows = lax.all_gather(key_heads, "seq", axis=1, tiled=True)
    value_rows = lax.all_gather(value_heads, "seq", axis=1, tiled=True)
    piece_keys = key_rows.shape[1]

    def attend_compute(state):
        running_top, running_total, running_acc = state
        key_pos = jnp.arange(piece_keys, dtype=jnp.int32)
        scores = masked_scores(
            query_heads, key_rows, own_pos, key_pos, own_seg, doc_index(doc_starts, key_pos), scale
        )
        new_top = jnp.maximum(running_top, jnp.max(scores, axis=-1))
        shrink = jnp.exp(running_top - new_top)
        weights_exp = jnp.exp(scores - new_top[..., None])
        new_total = running_total * shrink + jnp.sum(weights_exp, axis=-1)
        new_acc = running_acc * shrink[..., None] + jnp.einsum(
            "sqhk,skhd->sqhd",
            weights_exp.astype(jnp.bfloat16),
            value_rows,
            preferred_element_type=jnp.float32,
        )
        return (new_top, new_total, new_acc)

    final_top, final_total, final_acc = lax.cond(
        jnp.int32(0) <= last_row,
        attend_compute,
        lambda state: state,
        (top_start, jnp.sum(fixed_exp, axis=-1), acc_start),
    )
    attn_rows = final_acc / final_total[..., None]
    lse = final_top + jnp.log(final_total)
    log_retention = jnp.log(retention)
    running = jnp.cumsum(log_retention, axis=1)
    lane = jnp.transpose(running, (0, 2, 1))
    index = jnp.arange(block)
    linked = (index[None, :] <= index[:, None])[None] & (own_seg[:, None, :] == own_seg[:, :, None])
    decay = jnp.where(
        linked[:, None], jnp.exp(jnp.minimum(lane[:, :, :, None] - lane[:, :, None, :], 0.0)), 0.0
    )
    intersection = jnp.einsum(
        "sthd,suhd->shtu", query_heads, key_heads, preferred_element_type=jnp.float32
    )
    mixing = (mem_scale * intersection * decay).astype(jnp.bfloat16)
    inner_mem = jnp.einsum(
        "shtu,suhd->sthd", mixing, value_heads, preferred_element_type=jnp.float32
    )
    carried = ((own_seg == own_seg[:, :1]) & jnp.logical_not(own_begin[:, :1])).astype(jnp.float32)
    lead = jnp.exp(running) * carried[..., None]
    trail = jnp.where(
        (own_seg == own_seg[:, -1:])[..., None], jnp.exp(running[:, -1:, :] - running), 0.0
    )
    query_full = query_heads.astype(jnp.float32)
    key_full = key_heads.astype(jnp.float32)
    value_full = value_heads.astype(jnp.float32)
    block_state = jnp.einsum(
        "suhd,suhe->shde", key_full * trail[..., None], value_full, precision=HIGHEST
    )
    block_keep = lead[:, -1, :]
    identity = (jnp.ones_like(block_keep), jnp.zeros_like(block_state))
    chained = entering((block_keep, block_state), "seq", chain_forward, identity, False)
    state_in = chained[1]
    outer_mem = (
        mem_scale
        * lead[..., None]
        * jnp.einsum("sthd,shde->sthe", query_full, state_in, precision=HIGHEST)
    )
    mixed_heads = (attn_rows + inner_mem + outer_mem).astype(jnp.bfloat16)
    mixed_rows = lax.all_to_all(
        mixed_heads, "head", split_axis=0, concat_axis=2, tiled=True
    ).reshape(token_count, width)
    branch = product(mixed_rows, out_weight)
    gate_sigmoid = jax.nn.sigmoid(gate_pre)
    hidden = token_rows.astype(jnp.float32) + gate_sigmoid * branch
    inv_rms = lax.rsqrt(jnp.mean(hidden * hidden, axis=-1, keepdims=True) + EPSILON)
    normed = hidden * inv_rms
    gain_full = gain_weight.astype(jnp.float32)
    scaled = (normed * gain_full).astype(jnp.bfloat16)
    gate_act = product(scaled, ffn_gate)
    up_act = product(scaled, ffn_up)
    act_sigmoid = jax.nn.sigmoid(gate_act)
    silu_act = gate_act * act_sigmoid
    inner = (silu_act * up_act).astype(jnp.bfloat16)
    final = hidden + product(inner, ffn_down)
    output = final.astype(jnp.bfloat16).reshape(local_seqs, block, width)
    valid_rows = valid.reshape(token_count).astype(jnp.float32)
    error = final - teacher.reshape(token_count, width).astype(jnp.float32)
    sums = lax.psum(
        (jnp.sum(valid_rows * jnp.sum(error * error, axis=-1)), jnp.sum(valid_rows)),
        ("head", "seq"),
    )
    loss = sums[0] / (2.0 * width * sums[1])
    total_tokens = all_seqs * length
    d_out = valid_rows[:, None] * error * (total_tokens / sums[1])
    d_ffn = d_out.astype(jnp.bfloat16)
    grad_down = rows_outer(inner, d_ffn)
    d_inner = back_product(d_ffn, ffn_down)
    d_gate_act = (d_inner * up_act * act_sigmoid * (1.0 + gate_act * (1.0 - act_sigmoid))).astype(
        jnp.bfloat16
    )
    d_up_act = (d_inner * silu_act).astype(jnp.bfloat16)
    grad_ffn_gate = rows_outer(scaled, d_gate_act)
    grad_ffn_up = rows_outer(scaled, d_up_act)
    d_scaled = back_product(d_gate_act, ffn_gate) + back_product(d_up_act, ffn_up)
    grad_gain = jnp.sum(d_scaled * normed, axis=0)
    d_normed = d_scaled * gain_full
    d_hidden = d_out + inv_rms * (
        d_normed - normed * jnp.mean(d_normed * normed, axis=-1, keepdims=True)
    )
    d_branch = (d_hidden * gate_sigmoid).astype(jnp.bfloat16)
    d_gate = (d_hidden * branch * gate_sigmoid * (1.0 - gate_sigmoid)).astype(jnp.bfloat16)
    grad_out_weight = rows_outer(mixed_rows, d_branch)
    grad_gate_weight = rows_outer(token_rows, d_gate)
    d_mixed = (
        back_product(d_branch, out_weight)
        .astype(jnp.bfloat16)
        .reshape(local_seqs, block, HEAD_COUNT, HD)
    )
    dout_heads = lax.all_to_all(d_mixed, "head", split_axis=2, concat_axis=0, tiled=True)
    dout_full = dout_heads.astype(jnp.float32)
    delta = jnp.sum(dout_full * attn_rows, axis=-1)
    fixed_probs = jnp.exp(fixed_scores - lse[..., None])
    fixed_prob_grad = jnp.einsum(
        "sqhd,phd->sqhp", dout_heads, fixed_values, preferred_element_type=jnp.float32
    )
    fixed_score_grad = (fixed_probs * (fixed_prob_grad - delta[..., None])).astype(jnp.bfloat16)
    fixed_key_grad = (
        jnp.einsum(
            "sqhp,sqhd->phd", fixed_score_grad, query_heads, preferred_element_type=jnp.float32
        )
        * scale
    )
    fixed_value_grad = jnp.einsum(
        "sqhp,sqhd->phd",
        fixed_probs.astype(jnp.bfloat16),
        dout_heads,
        preferred_element_type=jnp.float32,
    )
    query_grad_start = (
        jnp.einsum(
            "sqhp,phd->sqhd", fixed_score_grad, fixed_keys, preferred_element_type=jnp.float32
        )
        * scale
    )
    fold_start = (query_grad_start,)
    back_key_rows = lax.all_gather(key_heads, "seq", axis=1, tiled=True)
    back_value_rows = lax.all_gather(value_heads, "seq", axis=1, tiled=True)
    back_piece_keys = back_key_rows.shape[1]

    def back_compute(state):
        key_pos = jnp.arange(back_piece_keys, dtype=jnp.int32)
        probs_low, score_grad = softmax_grads(
            query_heads,
            back_key_rows,
            back_value_rows,
            dout_heads,
            own_pos,
            key_pos,
            own_seg,
            doc_index(doc_starts, key_pos),
            lse,
            delta,
            scale,
        )
        query_grad = (
            state[0]
            + jnp.einsum(
                "sqhk,skhd->sqhd", score_grad, back_key_rows, preferred_element_type=jnp.float32
            )
            * scale
        )
        return (query_grad,)

    folded = lax.cond(jnp.int32(0) <= last_row, back_compute, lambda state: state, fold_start)
    query_att = folded[0]
    empty_local = jnp.zeros((all_seqs, block, heads, HD), jnp.float32)

    def visit(turn, state):
        key_rows, value_rows, key_acc, value_acc = state
        owner = (seq_place - turn) % seq_count
        start = owner * block

        def visit_compute(accs):
            key_pos = start + jnp.arange(block, dtype=jnp.int32)
            probs_low, score_grad = softmax_grads(
                query_heads,
                key_rows,
                value_rows,
                dout_heads,
                own_pos,
                key_pos,
                own_seg,
                doc_index(doc_starts, key_pos),
                lse,
                delta,
                scale,
            )
            key_next = (
                accs[0]
                + jnp.einsum(
                    "sqhk,sqhd->skhd", score_grad, query_heads, preferred_element_type=jnp.float32
                )
                * scale
            )
            value_next = accs[1] + jnp.einsum(
                "sqhk,sqhd->skhd", probs_low, dout_heads, preferred_element_type=jnp.float32
            )
            return (key_next, value_next)

        key_acc, value_acc = lax.cond(
            start <= last_row, visit_compute, lambda accs: accs, (key_acc, value_acc)
        )
        key_rows, value_rows = passed_along((key_rows, value_rows), "seq", 1)
        key_acc, value_acc = (
            from_behind(key_acc.astype(jnp.bfloat16), "seq", 1).astype(key_acc.dtype),
            from_behind(value_acc.astype(jnp.bfloat16), "seq", 1).astype(value_acc.dtype),
        )
        return (key_rows, value_rows, key_acc, value_acc)

    travelled = lax.fori_loop(
        0, seq_count, visit, (key_heads, value_heads, empty_local, empty_local)
    )
    key_att = travelled[2]
    value_att = travelled[3]
    mix_grad_raw = jnp.einsum(
        "sthe,suhe->shtu", dout_heads, value_heads, preferred_element_type=jnp.float32
    )
    intersection_grad = (mem_scale * mix_grad_raw * decay).astype(jnp.bfloat16)
    local_grad = mem_scale * jnp.einsum(
        "sthd,sthe->shde", query_full * lead[..., None], dout_full, precision=HIGHEST
    )
    state_grads = entering((block_keep, local_grad), "seq", chain_backward, identity, True)
    carry_grad = state_grads[1]
    query_mem = jnp.einsum(
        "shtu,suhd->sthd", intersection_grad, key_heads, preferred_element_type=jnp.float32
    )
    query_mem = query_mem + mem_scale * lead[..., None] * jnp.einsum(
        "sthe,shde->sthd", dout_full, state_in, precision=HIGHEST
    )
    key_mem = jnp.einsum(
        "shtu,sthd->suhd", intersection_grad, query_heads, preferred_element_type=jnp.float32
    )
    key_mem = key_mem + trail[..., None] * jnp.einsum(
        "suhe,shde->suhd", value_full, carry_grad, precision=HIGHEST
    )
    value_mem = jnp.einsum(
        "shtu,sthe->suhe", mixing, dout_heads, preferred_element_type=jnp.float32
    )
    value_mem = value_mem + jnp.einsum(
        "suhd,shde->suhe", key_full * trail[..., None], carry_grad, precision=HIGHEST
    )
    query_grad_heads = (query_att + query_mem).astype(jnp.bfloat16)
    key_grad_heads = (key_att + key_mem).astype(jnp.bfloat16)
    value_grad_heads = (value_att + value_mem).astype(jnp.bfloat16)
    query_back, key_back, value_back = (
        lax.all_to_all(query_grad_heads, "head", split_axis=0, concat_axis=2, tiled=True),
        lax.all_to_all(key_grad_heads, "head", split_axis=0, concat_axis=2, tiled=True),
        lax.all_to_all(value_grad_heads, "head", split_axis=0, concat_axis=2, tiled=True),
    )
    query_back = query_back.reshape(token_count, width)
    key_back = key_back.reshape(token_count, width)
    value_back = value_back.reshape(token_count, width)
    grad_query_weight = rows_outer(token_rows, query_back)
    grad_key_weight = rows_outer(token_rows, key_back)
    grad_value_weight = rows_outer(token_rows, value_back)
    token_grad = (
        d_hidden + back_product(d_gate, gate_weight) + back_product(query_back, query_weight)
    )
    token_grad = (
        token_grad + back_product(key_back, key_weight) + back_product(value_back, value_weight)
    )
    fixed_key_full = lax.dynamic_update_slice_in_dim(
        jnp.zeros((P_SIZE, HEAD_COUNT, HD), jnp.float32), fixed_key_grad, head_place * heads, 1
    ).reshape(P_SIZE, width)
    fixed_value_full = lax.dynamic_update_slice_in_dim(
        jnp.zeros((P_SIZE, HEAD_COUNT, HD), jnp.float32), fixed_value_grad, head_place * heads, 1
    ).reshape(P_SIZE, width)
    shards = (
        lax.psum_scatter(grad_query_weight, ("head", "seq"), scatter_dimension=0, tiled=True),
        lax.psum_scatter(grad_key_weight, ("head", "seq"), scatter_dimension=0, tiled=True),
        lax.psum_scatter(grad_value_weight, ("head", "seq"), scatter_dimension=0, tiled=True),
        lax.psum_scatter(grad_out_weight, ("head", "seq"), scatter_dimension=0, tiled=True),
        lax.psum_scatter(grad_gate_weight, ("head", "seq"), scatter_dimension=0, tiled=True),
        lax.psum_scatter(
            jnp.transpose(fixed_key_full), ("head", "seq"), scatter_dimension=0, tiled=True
        ),
        lax.psum_scatter(
            jnp.transpose(fixed_value_full), ("head", "seq"), scatter_dimension=0, tiled=True
        ),
        lax.psum_scatter(grad_gain, ("head", "seq"), scatter_dimension=0, tiled=True),
        lax.psum_scatter(grad_ffn_gate, ("head", "seq"), scatter_dimension=0, tiled=True),
        lax.psum_scatter(grad_ffn_up, ("head", "seq"), scatter_dimension=0, tiled=True),
        lax.psum_scatter(grad_down, ("head", "seq"), scatter_dimension=0, tiled=True),
    )
    return (
        output,
        loss,
        token_grad.reshape(local_seqs, block, width),
        shards[0],
        shards[1],
        shards[2],
        shards[3],
        shards[4],
        jnp.transpose(shards[5]),
        jnp.transpose(shards[6]),
        shards[7],
        shards[8],
        shards[9],
        shards[10],
    )


def solution(mesh):
    in_specs = (
        P("head", "seq", None),
        P(("head", "seq"), None),
        P(("head", "seq"), None),
        P(("head", "seq"), None),
        P(("head", "seq"), None),
        P(("head", "seq"), None),
        P(None, ("head", "seq")),
        P(None, ("head", "seq")),
        P(("head", "seq")),
        P(("head", "seq"), None),
        P(("head", "seq"), None),
        P(("head", "seq"), None),
        P(None, "seq", "head"),
        P(),
        P("head", "seq"),
        P("head", "seq", None),
    )
    out_specs = (
        P("head", "seq", None),
        P(),
        P("head", "seq", None),
        P(("head", "seq"), None),
        P(("head", "seq"), None),
        P(("head", "seq"), None),
        P(("head", "seq"), None),
        P(("head", "seq"), None),
        P(None, ("head", "seq")),
        P(None, ("head", "seq")),
        P(("head", "seq")),
        P(("head", "seq"), None),
        P(("head", "seq"), None),
        P(("head", "seq"), None),
    )
    fits = mesh.shape["head"] == 4 and mesh.shape["seq"] == HEAD_COUNT
    body = local_block if fits else local
    return jax.shard_map(body, mesh=mesh, in_specs=in_specs, out_specs=out_specs, check_vma=False)
```

```python
import functools
import types

import jax
import jax.numpy as jnp
from jax import lax
from jax.experimental import pallas as pl
from jax.experimental.pallas import tpu as pltpu
from jax.sharding import PartitionSpec as P

HEAD_COUNT = 8
HD = 128
P_SIZE = 16


HIGHEST = lax.Precision.HIGHEST
MASKED = -1e30
EPSILON = 1e-06
F32 = jnp.float32
BF16 = jnp.bfloat16
MESH_IDS = pl.DeviceIdType.MESH


def nn(left, right):
    return lax.dot_general(left, right, (((1,), (0,)), ((), ())), preferred_element_type=F32)


def nt(left, right):
    return lax.dot_general(left, right, (((1,), (1,)), ((), ())), preferred_element_type=F32)


def tn(left, right):
    return lax.dot_general(left, right, (((0,), (0,)), ((), ())), preferred_element_type=F32)


def tn_exact(left, right):
    return lax.dot_general(
        left, right, (((0,), (0,)), ((), ())), precision=HIGHEST, preferred_element_type=F32
    )


def nt_exact(left, right):
    return lax.dot_general(
        left, right, (((1,), (1,)), ((), ())), precision=HIGHEST, preferred_element_type=F32
    )


def nn_exact(left, right):
    return lax.dot_general(
        left, right, (((1,), (0,)), ((), ())), precision=HIGHEST, preferred_element_type=F32
    )


def block_rows(index, size):
    return pl.ds(pl.multiple_of(index * size, size), size)


def each(first, last, body):
    def step(index, carry):
        body(index)
        return carry

    lax.fori_loop(first, last, step, 0)


SEQ_FLAGS = dict(
    w1=8, t2=8, p2=8, x=8, wo=8, fxg=8, fxu=8, mx=8, dm=8, gxg=8, gxu=8, rgo=8, gt=8, gwa=8,
    fin2=8, pers=8, sc=8, y=8, df=8, ds=8, fd=1, gfd=1, gos=1,
)
XY_FLAGS = dict(
    t1=4, p1=4, w2=4, wox=4, fgx=4, fux=4, fdx=4, fdy=4, rg=3, ru=3, rdx=3, rdy=3, rox=3, roy=3,
    rwx=3, rwy=3, fin1=4,
)
FLAGS = SEQ_FLAGS | XY_FLAGS


def scratch_table(width, tokens, hidden, hidden_pad, length):
    seqs, blocks, block = 4, 8, 128
    table = dict(
        x_all=((length, width), BF16),
        wcs=((blocks, 32, 512), BF16),
        wqk=((width, 512), BF16),
        tile=((4, 8, 128), F32),
        pin=((32, 128), BF16),
        vcol=((block, 1), F32),
        t1=((4, 8, 128), F32),
        p1=((4, 32, 128), BF16),
        t2s=((16, 128), F32),
        t2=((8, 16, 128), F32),
        p2=((8, 32, 128), BF16),
        fs=((4, 2, 32, hidden_pad), BF16),
        fgu=((2, 4, 256, hidden_pad), BF16),
        fdp=((8, 96, width), BF16),
        ffd=((hidden_pad, width), BF16),
        wo_all=((4, 4, 2, 32, width), BF16),
        q=((length, HD), BF16),
        k=((length, HD), BF16),
        v=((length, HD), BF16),
        fkv=((32, HD), BF16),
        gain=((1, width), F32),
        rrow=((1, length), F32),
        rcol=((block, 8), F32),
        probs=((length, length), BF16),
        decay=((length, length), BF16),
        both=((length, length), BF16),
        fprobs=((length, P_SIZE), BF16),
        mgs=((length, 2 * HD), BF16),
        mg=((8, block, 2 * HD), BF16),
        mx=((block, width), BF16),
        gp=((block, width), BF16),
        hid=((block, width), F32),
        br=((block, width), F32),
        inv=((block, 128), F32),
        own=((block, width), F32),
        dout=((block, width), F32),
        sc=((4 * block, width), BF16),
        gact=((4 * block, hidden_pad), F32),
        uact=((4 * block, hidden_pad), F32),
        inner=((4 * block, hidden_pad), BF16),
        ysend=((4, block, width), BF16),
        yrecv=((4, block, width), BF16),
        df=((4 * block, width), BF16),
        dga=((4 * block, hidden_pad), BF16),
        dua=((4 * block, hidden_pad), BF16),
        dbr=((block, width), BF16),
        dgt=((block, width), BF16),
        dms=((block, width), BF16),
        dm=((length, HD), BF16),
        dgs=((8, block, 2 * HD), BF16),
        dmg=((8, block, 2 * HD), BF16),
        dq=((length, 512), BF16),
        ggain=((1, width), F32),
        gus=((2, 4, 256, hidden_pad), BF16),
        gpre=((2, 256, hidden_pad), BF16),
        gland=((2, 2, 256, hidden_pad), BF16),
        gxs=((8, 2, 32, hidden_pad), BF16),
        gxr=((8, 2, 32, hidden_pad), BF16),
        gds=((8, 96, width), BF16),
        dpre=((2, 96, width), BF16),
        dland=((2, 2, 96, width), BF16),
        dsum=((2, 96, width), BF16),
        dfar=((96, width), BF16),
        gwos=((4, 4, 2, 32, width), BF16),
        gwor=((4, 4, 32, width), BF16),
        opre=((2, 2, 32, width), BF16),
        oland=((2, 4, 32, width), BF16),
        gos=((4, 32, width), BF16),
        goz=((4, 32, width), BF16),
        gws=((4, 256, 512), BF16),
        wpre=((2, 128, 512), BF16),
        wland=((2, 256, 512), BF16),
        gas=((8, 32, 512), BF16),
        gar=((8, 32, 512), BF16),
        gts=((4, 2, block, width), BF16),
        gtr=((4, block, width), BF16),
        pgrad=((32, HD), F32),
        fin0=((48, 128), F32),
        fin1=((4, 48, 128), F32),
        fin2s=((48, 128), F32),
        fin2=((8, 16, 128), F32),
        pers=((32, 128), F32),
    )
    return table


def block_kernel(names, width, hidden, ndoc, *refs):
    (
        tok, wq, wk, wv, wo, wg, fgi, fui, fdi, tea, ret, pk, pv, gin, val, docs,
        out_o, gtok_o, gar_o, gwo_o, fin_o, pers_o, gux_o, fd_o,
    ) = refs[:24]
    m = types.SimpleNamespace(**dict(zip(names, refs[24 : 24 + len(names)])))
    sems = refs[24 + len(names) :]
    s = types.SimpleNamespace(**dict(zip(FLAGS, zip(sems[0::2], sems[1::2]))))
    pad = m.ffd.shape[0]
    length = m.x_all.shape[0]
    scale = HD ** (-0.5)
    mem_scale = 0.125 / HD

    a = lax.axis_index("head")
    b = lax.axis_index("seq")
    z = lax.div(b, 2)
    c = lax.rem(b, 2)
    sib = 2 * z + 1 - c
    near = z + 1 - 2 * lax.rem(z, 2)
    mirror = 3 - z
    across = 3 - near
    inner_chip = (z == 1) | (z == 2)
    inside = lax.div(lax.rem(z, 3) + 1, 2)
    order = (
        near + inside * (mirror - near),
        across + inside * (near - across),
        mirror + inside * (across - mirror),
    )
    part = lax.div(b, 4)
    mine = lax.rem(b, 4)
    partner = 2 * near + c
    far = b + 4 - 8 * part
    mate, pmate, cross = lax.rem(sib, 4), lax.rem(partner, 4), lax.rem(2 * near + 1 - c, 4)
    nx = a + 1 - 2 * lax.rem(a, 2)
    ny = lax.rem(a + 2, 4)
    diagonal = 3 - a

    def copy(src, dst, ssem, rsem, device):
        return pltpu.make_async_remote_copy(
            src_ref=src, dst_ref=dst, send_sem=ssem, recv_sem=rsem,
            device_id=device, device_id_type=MESH_IDS,
        )

    def sent(flag, total):
        copy(total, total, flag, flag, (a, sib)).wait_send()

    def landed_all(flag, total):
        copy(total, total, flag, flag, (a, sib)).wait_recv()

    def seq_peers(body):
        each(1, 8, lambda step: body(lax.rem(b + step, 8)))

    def xy_peers(body):
        each(1, 4, lambda step: body(lax.rem(a + step, 4)))

    def seq_start(pair, src, dst, peer):
        copy(src, dst, pair[0].at[0], pair[1].at[b], (a, peer)).start()

    def seq_wait(pair, dst, peer):
        landed_all(pair[1].at[peer], dst)

    def all_start(pair, src, dst, peer):
        copy(src, dst, pair[0].at[0], pair[1].at[0], (a, peer)).start()

    def xy_start(pair, src, dst, peer):
        copy(src, dst, pair[0].at[0], pair[1].at[a], (peer, b)).start()

    def xy_wait(pair, dst, peer):
        landed_all(pair[1].at[peer], dst)

    def xy_all_start(pair, src, dst, peer):
        copy(src, dst, pair[0].at[0], pair[1].at[0], (peer, b)).start()

    def all_wait(pair, total):
        landed_all(pair[1].at[0], total)

    finals = []

    def drain(pair, total):
        finals.append(lambda: sent(pair[0].at[0], total))

    def line_copy(pair, src, dst, zt):
        return copy(src, dst, pair[0].at[0], pair[1].at[z], (a, 2 * zt + c))

    def pass_copy(pair, src, dst, zs):
        return copy(src, dst, pair[0].at[1], pair[1].at[4 + zs], (a, sib))

    def line_start_far(pair, src, place, four, two):
        @pl.when(inner_chip)
        def _():
            line_copy(pair, src, place(z), mirror).start()

        @pl.when(jnp.logical_not(inner_chip))
        def _():
            line_copy(pair, src, place(z), across).start()

        def line_sent():
            @pl.when(inner_chip)
            def _():
                sent(pair[0].at[0], four)

            @pl.when(jnp.logical_not(inner_chip))
            def _():
                sent(pair[0].at[0], two)

        finals.append(line_sent)

    def line_start_near(pair, src, place):
        line_copy(pair, src, place(z), near).start()

    def line_wait(pair, place, zs):
        landed_all(pair[1].at[zs], place(zs))

    def line_hand_on(pair, place, zs):
        block = place(zs)

        @pl.when(inner_chip)
        def _():
            copy(block, block, pair[0].at[0], pair[1].at[zs], (a, 2 * near + c)).start()

    def gather_line(pair, view, zs):
        block = view(2 * zs + c)
        line_wait(pair, lambda _: block, zs)
        pass_copy(pair, block, block, zs).start()

    def gather_pass(pair, view, zs):
        landed_all(pair[1].at[4 + zs], view(2 * zs + 1 - c))

    def quad_start(pair, view, first, second):
        block = view(a)
        copy(block, block, pair[0].at[0], pair[1].at[0], (first, b)).start()
        copy(block, block, pair[0].at[0], pair[1].at[1], (second, b)).start()

    def quad_pass(pair, view, first, second):
        block = view(first)
        landed_all(pair[1].at[0], block)
        copy(block, block, pair[0].at[0], pair[1].at[1], (second, b)).start()

    def fold_start(pair, view, pre, land, first):
        copy(view(diagonal), pre, pair[0].at[0], pair[1].at[0], (first, b)).start()
        copy(view(first), land.at[0], pair[0].at[0], pair[1].at[1], (first, b)).start()

    def fold_pass(pair, view, pre, land, add, second):
        landed_all(pair[1].at[0], pre)
        add(second)
        copy(view(second), land.at[1], pair[0].at[0], pair[1].at[1], (second, b)).start()

    def fold_finish(pair, land, three):
        landed_all(pair[1].at[1], land)
        drain(pair, three)

    barrier = pltpu.get_barrier_semaphore()
    seq_peers(lambda p: pl.semaphore_signal(barrier, 1, device_id=(a, p), device_id_type=MESH_IDS))
    xy_peers(lambda p: pl.semaphore_signal(barrier, 1, device_id=(p, b), device_id_type=MESH_IDS))

    for head in range(8):
        for place, weight in enumerate((wq, wk, wv, wg)):
            m.wcs[head, :, place * 128 : place * 128 + 128] = weight[
                :, head * 128 : head * 128 + 128
            ]
    own_rows = block_rows(b, 128)
    piece = pl.ds(pl.multiple_of(a * 256 + b * 32, 32), 32)
    m.x_all[own_rows, :] = tok[...]
    m.wqk[piece, :] = m.wcs[b]
    m.wo_all[a, z, c] = wo[...]
    down = fdi[...].astype(F32)
    m.fdp[2 * a + part] = jnp.concatenate(
        [down, jnp.zeros((96 - down.shape[0], width), F32)], axis=0
    ).astype(BF16)
    slot32 = block_rows(b, 32)
    row_id = lax.broadcasted_iota(jnp.int32, (128, 128), 0)
    col_id = lax.broadcasted_iota(jnp.int32, (128, 128), 1)
    place = (
        lax.broadcasted_iota(jnp.int32, (32, 128), 1)
        == lax.broadcasted_iota(jnp.int32, (32, 128), 0) + 32 * lax.rem(b, 4)
    ).astype(BF16)
    m.pin[0:16, :] = nn(pk[...], place).astype(BF16)
    m.pin[16:32, :] = nn(pv[...], place).astype(BF16)
    counted_row = val[...].astype(F32)
    m.vcol[...] = jnp.sum(jnp.where(row_id == col_id, counted_row, 0.0), axis=1, keepdims=True)
    gain_row = nn(gin[...], place)
    m.tile[...] = jnp.zeros_like(m.tile)
    for group in range(4):
        m.tile[group, 0:2, :] = jnp.log(ret[group])
        m.tile[group, 2:3, :] = counted_row
        m.tile[group, 3:4, :] = gain_row
    m.t1[a] = m.tile[a]
    m.p1[a] = m.pin[...]
    pl.semaphore_wait(barrier, 10)

    xy_peers(lambda p: xy_all_start(s.t1, m.tile.at[p], m.t1.at[a], p))
    xy_peers(lambda p: xy_all_start(s.p1, m.pin, m.p1.at[a], p))
    seq_peers(lambda p: all_start(s.w1, m.wcs.at[p], m.wqk.at[piece, :], p))
    all_wait(s.t1, m.t1.at[pl.ds(0, 3)])
    all_wait(s.p1, m.p1.at[pl.ds(0, 3)])
    for group in range(4):
        m.t2s[2 * group : 2 * group + 2, :] = m.t1[group, 0:2, :]
        m.t2s[8 + group : 9 + group, :] = m.t1[group, 3:4, :]
    m.t2s[12:13, :] = (m.t1[0, 2:3, :] + m.t1[1, 2:3, :]) + (m.t1[2, 2:3, :] + m.t1[3, 2:3, :])
    m.t2s[13:16, :] = jnp.zeros((3, 128), F32)
    m.t2[b] = m.t2s[...]
    m.p2[b] = m.p1[lax.div(b, 2)]
    seq_peers(lambda p: all_start(s.t2, m.t2s, m.t2.at[b], p))
    half = 4 * c

    def persist_send(p):
        @pl.when(lax.rem(p, 2) == lax.div(b, 4))
        def _():
            all_start(s.p2, m.p1.at[lax.div(p, 2)], m.p2.at[b], p)

    def persist_wait():
        pl.when(part == c)(lambda: all_wait(s.p2, m.p2.at[pl.ds(0, 3)]))
        pl.when(part != c)(lambda: all_wait(s.p2, m.p2.at[pl.ds(0, 4)]))

    def persist_drain():
        pl.when(part == c)(lambda: sent(s.p2[0].at[0], m.p2.at[pl.ds(0, 3)]))
        pl.when(part != c)(lambda: sent(s.p2[0].at[0], m.p2.at[pl.ds(0, 4)]))

    seq_peers(persist_send)
    finals.append(persist_drain)
    drain(s.t2, m.t2.at[pl.ds(0, 7)])

    drain(s.t1, m.t1.at[pl.ds(0, 3)])
    drain(s.p1, m.p1.at[pl.ds(0, 3)])
    drain(s.w1, m.wcs.at[pl.ds(0, 7)])
    x_view = lambda i: m.x_all.at[block_rows(i, 128), :]
    x_place = lambda zs: x_view(2 * zs + c)
    wo_place = lambda zs: m.wo_all.at[a, zs, c]
    line_start_near(s.wo, wo, wo_place)
    line_start_far(s.wo, wo, wo_place, m.wo_all.at[0, :, 0], m.wo_all.at[0, pl.ds(0, 2), 0])
    line_start_near(s.x, tok, x_place)
    line_start_far(
        s.x, tok, x_place, m.x_all.at[pl.ds(0, 512), :], m.x_all.at[pl.ds(0, 256), :]
    )
    pass_copy(s.x, tok, x_view(b), z).start()
    finals.append(lambda: sent(s.x[0].at[1], m.x_all.at[pl.ds(0, 512), :]))
    down_x = lambda i: m.fdp.at[2 * i]
    down_y = lambda i: m.fdp.at[2 * i + 1]

    run = hidden // 8
    for place, weight in enumerate((fgi, fui)):
        for group in range(4):
            m.fs[group, place, :, hidden:pad] = jnp.zeros((32, pad - hidden), BF16)
            for i in range(8):
                start = run * (4 * i + group)
                m.fs[group, place, :, run * i : run * i + run] = weight[:, start : start + run]
    m.fgu[:, a, slot32, :] = m.fs[mine]

    def column_start(pair, place, p):
        seq_start(pair, m.fs.at[lax.rem(p, 4), place], m.fgu.at[place, a, slot32, :], p)

    def columns(pair, place):
        seq_peers(lambda p: column_start(pair, place, p))

    def columns_far(pair, place):
        def one(p):
            @pl.when(lax.div(p, 2) != near)
            def _():
                column_start(pair, place, p)

        seq_peers(one)

    def columns_near(pair, place):
        column_start(pair, place, 2 * near)
        column_start(pair, place, 2 * near + 1)

    drain(s.fxg, m.gxr.at[pl.ds(0, 7), 0])
    drain(s.fxu, m.gxr.at[pl.ds(0, 7), 1])
    own_down = m.fdp.at[2 * a + part]
    far_down = m.fdp.at[2 * a + 1 - part]
    down_copy = copy(own_down, own_down, s.fd[0].at[0], s.fd[1].at[0], (a, far))
    finals.append(down_copy.wait_send)

    @pl.when(jnp.logical_not(inner_chip))
    def _():
        columns(s.fxg, 0)
        columns(s.fxu, 1)
        down_copy.start()


    all_wait(s.w1, m.wqk.at[pl.ds(0, 224), :])
    quarter = lambda i: m.wqk.at[block_rows(i, 256), :]
    xy_peers(lambda p: xy_all_start(s.w2, quarter(a), quarter(a), p))
    drain(s.w2, m.wqk.at[pl.ds(0, 768), :])

    def piece_view(place, p):
        return lambda i: m.fgu.at[place, i, block_rows(p, 32), :]

    ways = ((nx, ny), (ny, nx))

    def pieces_on(peers, pair, quad_pair, place):
        for p in peers:
            seq_wait(pair, piece_view(place, p)(a), p)
            quad_start(quad_pair, piece_view(place, p), *ways[place])

    quad_start(s.fgx, piece_view(0, b), nx, ny)
    quad_start(s.fux, piece_view(1, b), ny, nx)

    @pl.when(part == 0)
    def _():
        quad_start(s.fdx, down_x, nx, ny)

    @pl.when(part == 1)
    def _():
        quad_start(s.fdy, down_y, ny, nx)


    def project(i):
        rows = block_rows(i, 128)
        wide = nn(m.x_all[rows, :], m.wqk[...])
        m.q[rows, :] = wide[:, 0:128].astype(BF16)
        m.k[rows, :] = wide[:, 128:256].astype(BF16)
        m.v[rows, :] = wide[:, 256:384].astype(BF16)
        m.mgs[rows, 128:256] = wide[:, 384:512].astype(BF16)

    head_cols = pl.ds(pl.multiple_of(b * 128, 128), 128)

    @pl.when(inner_chip)
    def _():
        line_wait(s.wo, wo_place, mirror)
        line_hand_on(s.wo, wo_place, mirror)
        line_wait(s.wo, wo_place, across)
        line_hand_on(s.wo, wo_place, across)

    gather_line(s.x, x_view, order[0])
    line_hand_on(s.x, x_place, mirror)
    @pl.when(inner_chip)
    def _():
        columns_far(s.fxg, 0)

    all_wait(s.w2, m.wqk.at[pl.ds(0, 768), :])
    project(b)
    gather_pass(s.x, x_view, z)
    project(sib)
    project(2 * order[0] + c)
    line_wait(s.wo, wo_place, near)

    @pl.when(jnp.logical_not(inner_chip))
    def _():
        line_wait(s.wo, wo_place, across)
        line_wait(s.wo, wo_place, mirror)

    wo_half = lambda i: m.wo_all.at[i, :, c]
    xy_peers(lambda p: xy_start(s.wox, wo_half(a), wo_half(a), p))
    drain(s.wox, m.wo_all.at[pl.ds(0, 3), :, 0])
    wo_pass = lambda i, block: copy(
        block, block, s.wo[0].at[1], s.wo[1].at[4], (a, sib)
    )
    wo_pass(a, wo_half(a)).start()
    finals.append(lambda: sent(s.wo[0].at[1], m.wo_all.at[:, :, 0]))
    chips = tuple(2 * zs + core for zs in order for core in range(2))
    pieces_on((sib,) + chips[0:2], s.fxg, s.fgx, 0)

    gather_line(s.x, x_view, order[1])
    gather_line(s.x, x_view, order[2])
    line_hand_on(s.x, x_place, across)

    @pl.when(inner_chip)
    def _():
        columns_near(s.fxg, 0)
        columns(s.fxu, 1)
        down_copy.start()

    project(2 * order[1] + c)
    project(2 * order[2] + c)

    def arrived_pass(zs):
        gather_pass(s.x, x_view, zs)
        project(2 * zs + 1 - c)

    for zs in order:
        arrived_pass(zs)
    all_wait(s.t2, m.t2.at[pl.ds(0, 7)])
    persist_wait()
    small = m.t2[...]
    place16 = lax.broadcasted_iota(jnp.int32, (8, 16, 128), 1)
    rates = jnp.sum(jnp.where(place16 == b, small, 0.0), axis=1)
    valid_total = jnp.sum(jnp.where(place16 == 12, small, 0.0))
    for group in range(8):
        line = 8 + group // 2
        first = 4 * (group % 2)
        m.gain[:, group * 128 : group * 128 + 128] = (
            m.t2[first, line : line + 1, :] + m.t2[first + 1, line : line + 1, :]
        ) + (m.t2[first + 2, line : line + 1, :] + m.t2[first + 3, line : line + 1, :])
    m.fkv[...] = (
        (m.p2[half].astype(F32) + m.p2[half + 1].astype(F32))
        + (m.p2[half + 2].astype(F32) + m.p2[half + 3].astype(F32))
    ).astype(BF16)
    lower = (col_id <= row_id).astype(F32)
    within = nt_exact(rates, lower)
    earlier = (
        lax.broadcasted_iota(jnp.int32, (8, 8), 1) < lax.broadcasted_iota(jnp.int32, (8, 8), 0)
    ).astype(F32)
    base = nn_exact(earlier, jnp.broadcast_to(jnp.sum(rates, axis=1, keepdims=True), (8, 128)))
    running = within + base
    for i in range(8):
        m.rrow[:, i * 128 : i * 128 + 128] = running[i : i + 1, :]
    eye = (col_id == row_id).astype(F32)
    m.rcol[...] = nt_exact(eye, running)

    local_pos = lax.broadcasted_iota(jnp.int32, (128, 1), 0)
    lane8 = lax.broadcasted_iota(jnp.int32, (128, 8), 1)

    m.probs[...] = jnp.zeros_like(m.probs)
    m.both[...] = jnp.zeros_like(m.both)

    def by_extent(i, body):
        for j in range(4):
            pl.when(lax.div(i, 2) == j)(lambda j=j: body(i, 256 * (j + 1)))

    def attend_keys(i, extent):
        rows = block_rows(i, 128)
        keys = slice(0, extent)
        query = m.q[rows, :]
        raw = nt(query, m.k[keys, :])
        pos = i * 128 + local_pos
        begin = jnp.zeros_like(pos)
        for j in range(ndoc):
            start = docs[a, j]
            begin = jnp.where(start <= pos, jnp.maximum(begin, start), begin)
        key_pos = lax.broadcasted_iota(jnp.int32, (128, extent), 1)
        allowed = (key_pos <= pos) & (key_pos >= begin)
        scores = jnp.where(allowed, raw * scale, MASKED)
        fixed = nt(query, m.fkv[0:16, :]) * scale
        top = jnp.maximum(
            jnp.max(scores, axis=1, keepdims=True), jnp.max(fixed, axis=1, keepdims=True)
        )
        weight = jnp.exp(scores - top)
        fixed_weight = jnp.exp(fixed - top)
        share = 1.0 / (
            jnp.sum(weight, axis=1, keepdims=True) + jnp.sum(fixed_weight, axis=1, keepdims=True)
        )
        prob = weight * share
        fixed_prob = (fixed_weight * share).astype(BF16)
        reach = jnp.sum(jnp.where(lane8 == i, m.rcol[...], 0.0), axis=1, keepdims=True)
        kept = jnp.where(
            allowed, jnp.exp(jnp.minimum(reach - m.rrow[:, keys], 0.0)) * mem_scale, 0.0
        )
        joint = (prob + kept * raw).astype(BF16)
        m.probs[rows, keys] = prob.astype(BF16)
        m.decay[rows, keys] = kept.astype(BF16)
        m.both[rows, keys] = joint
        m.fprobs[rows, :] = fixed_prob
        mixed = nn(joint, m.v[keys, :]) + nn(fixed_prob, m.fkv[16:32, :])
        m.mgs[rows, 0:128] = mixed.astype(BF16)

    attend = lambda i: by_extent(i, attend_keys)

    def attend_send(step):
        i = lax.rem(b + step, 8)
        attend(i)
        all_start(s.mx, m.mgs.at[block_rows(i, 128), :], m.mg.at[b], i)

    each(1, 4, attend_send)
    pieces_on(chips[2:6], s.fxg, s.fgx, 0)
    pieces_on((sib,) + chips[0:2], s.fxu, s.fux, 1)
    each(4, 8, attend_send)
    drain(s.mx, m.mgs.at[pl.ds(0, 896), :])
    attend(b)
    m.mg[b] = m.mgs[own_rows, :]
    quad_pass(s.fgx, lambda i: m.fgu.at[0, i], nx, ny)
    pieces_on(chips[2:6], s.fxu, s.fux, 1)
    copy(far_down, far_down, s.fd[0].at[0], s.fd[1].at[0], (a, far)).wait_recv()

    @pl.when(part == 1)
    def _():
        quad_start(s.fdx, down_x, nx, ny)

    @pl.when(part == 0)
    def _():
        quad_start(s.fdy, down_y, ny, nx)


    def wo_arrived(p):
        xy_wait(s.wox, wo_half(p), p)
        wo_pass(p, wo_half(p)).start()

    xy_peers(wo_arrived)
    landed_all(s.wo[1].at[4], m.wo_all.at[:, :, 1 - c])
    quad_pass(s.fux, lambda i: m.fgu.at[1, i], ny, nx)
    all_wait(s.mx, m.mg.at[pl.ds(0, 7)])
    for head in range(8):
        m.mx[:, head * 128 : head * 128 + 128] = m.mg[head, :, 0:128]
        m.gp[:, head * 128 : head * 128 + 128] = m.mg[head, :, 128:256]

    out_w = lambda: m.wo_all[...].reshape(width, width)
    m.br[...] = nn(m.mx[...], out_w())

    half_row = lambda i: pl.ds(
        pl.multiple_of((4 * lax.div(i, 2) + mine) * 64 + lax.rem(i, 2) * 32, 32), 32
    )
    quad = lambda ref, h, i: ref.at[block_rows(4 * h + i, 64), :]

    def half_copy(pair, src, dst, h, slot, peer):
        return copy(src, dst, pair[0].at[h], pair[1].at[2 * h + slot], (a, peer))

    def half_gather(pair, ref, h):
        block = quad(ref, h, mine)
        half_copy(pair, block, block, h, 0, partner).start()
        half_copy(pair, block, block, h, 1, sib).start()

    def half_wait(pair, ref, h):
        block = quad(ref, h, pmate)
        landed_all(pair[1].at[2 * h], block)
        half_copy(pair, block, block, h, 1, sib).start()
        landed_all(pair[1].at[2 * h + 1], ref.at[pl.ds(0, 128), :])
        finals.append(lambda: sent(pair[0].at[h], ref.at[pl.ds(0, 192), :]))

    def half_scatter(pair, value, h):
        for i in range(4):
            m.ysend[i, h * 64 : h * 64 + 64, :] = value[i * 64 : i * 64 + 64, :].astype(BF16)
        rows = pl.ds(h * 64, 64)
        half_copy(pair, m.ysend.at[cross, rows, :], m.yrecv.at[1, rows, :], h, 1, sib).start()
        half_copy(pair, m.ysend.at[mate, rows, :], m.yrecv.at[0, rows, :], h, 0, sib).start()

    def half_on(pair, h):
        rows = pl.ds(h * 64, 64)
        landed_all(pair[1].at[2 * h + 1], m.yrecv.at[1, rows, :])
        m.ysend[pmate, rows, :] = (
            m.ysend[pmate, rows, :].astype(F32) + m.yrecv[1, rows, :].astype(F32)
        ).astype(BF16)
        half_copy(
            pair, m.ysend.at[pmate, rows, :], m.yrecv.at[2, rows, :], h, 0, partner
        ).start()

    def half_sent(pair, h):
        sent(pair[0].at[h], m.ysend.at[pl.ds(0, 3), pl.ds(h * 64, 64), :])

    def half_land(pair, h):
        landed_all(pair[1].at[2 * h], m.yrecv.at[pl.ds(0, 2), pl.ds(h * 64, 64), :])

    def normalise(i):
        rows = block_rows(i, 32)
        opened = jax.nn.sigmoid(m.gp[rows, :].astype(F32))
        hidden_rows = tok[rows, :].astype(F32) + opened * m.br[rows, :]
        inv = lax.rsqrt(jnp.mean(hidden_rows * hidden_rows, axis=1, keepdims=True) + EPSILON)
        m.hid[rows, :] = hidden_rows
        m.inv[rows, :] = jnp.broadcast_to(inv, (32, 128))
        m.sc[half_row(i), :] = (
            hidden_rows * inv * m.gain[...]
        ).astype(BF16)

    each(0, 2, normalise)
    half_gather(s.sc, m.sc, 0)
    each(2, 4, normalise)
    half_gather(s.sc, m.sc, 1)

    quad_pass(s.fdx, down_x, nx, ny)
    quad_pass(s.fdy, down_y, ny, nx)
    landed_all(s.fgx[1].at[1], m.fgu.at[0, pl.ds(0, 2)])
    landed_all(s.fux[1].at[1], m.fgu.at[1, pl.ds(0, 2)])
    drain(s.fgx, m.fgu.at[0, pl.ds(0, 3)])
    drain(s.fux, m.fgu.at[1, pl.ds(0, 3)])
    drain(s.fdx, m.fdp.at[pl.ds(0, 3)])
    drain(s.fdy, m.fdp.at[pl.ds(0, 3)])
    half_wait(s.sc, m.sc, 0)

    gate_w = lambda: m.fgu[0].reshape(width, pad)
    up_w = lambda: m.fgu[1].reshape(width, pad)

    def feed(i):
        rows = block_rows(i, 256)
        scaled = m.sc[rows, :]
        gate_act = nn(scaled, gate_w())
        up_act = nn(scaled, up_w())
        m.gact[rows, :] = gate_act
        m.uact[rows, :] = up_act
        m.inner[rows, :] = (gate_act * jax.nn.sigmoid(gate_act) * up_act).astype(BF16)

    feed(0)
    landed_all(s.fdx[1].at[1], m.fdp.at[pl.ds(0, 2)])
    landed_all(s.fdy[1].at[1], m.fdp.at[pl.ds(0, 2)])
    share_rows = m.fdp.shape[1] - 8
    for i in range(4):
        m.ffd[2 * i * share_rows : 2 * (i + 1) * share_rows, :] = jnp.concatenate(
            [m.fdp[2 * i + j, 0:share_rows, :].astype(F32) for j in range(2)], axis=0
        ).astype(BF16)
    m.ffd[hidden:pad, :] = jnp.zeros((pad - hidden, width), BF16)

    def feed_out(h):
        half_scatter(s.y, nn(m.inner[block_rows(h, 256), :], m.ffd[...]), h)
        m.own[block_rows(h, 64), :] = nn(m.inner[block_rows(4 * h + mine, 64), :], m.ffd[...])
        half_on(s.y, h)

    feed_out(0)
    half_wait(s.sc, m.sc, 1)
    feed(1)
    feed_out(1)
    half_land(s.y, 0)

    token_total = float(4 * length)
    m.fin0[...] = jnp.zeros_like(m.fin0)

    def finish(i):
        rows = block_rows(i, 32)
        final = m.hid[rows, :] + m.own[rows, :]
        final = final + m.yrecv[0, rows, :].astype(F32) + m.yrecv[2, rows, :].astype(F32)
        out_o[rows, :] = final.astype(BF16)
        error = final - tea[rows, :].astype(F32)
        counted = m.vcol[rows, :] * error
        grad = counted * (token_total / valid_total)
        m.dout[rows, :] = grad
        m.df[half_row(i), :] = grad.astype(BF16)
        squares = jnp.sum(counted * error, axis=0, keepdims=True)
        lanes = squares[:, 0:128]
        for j in range(1, width // 128):
            lanes = lanes + squares[:, j * 128 : j * 128 + 128]
        m.fin0[40:41, :] += lanes

    each(0, 2, finish)
    half_gather(s.df, m.df, 0)
    half_land(s.y, 1)
    each(2, 4, finish)
    half_gather(s.df, m.df, 1)
    half_wait(s.df, m.df, 0)

    def feed_back(i):
        rows = block_rows(i, 256)
        d_inner = nt(m.df[rows, :], m.ffd[...])
        gate_act = m.gact[rows, :]
        opened = jax.nn.sigmoid(gate_act)
        m.dga[rows, :] = (
            d_inner * m.uact[rows, :] * opened * (1.0 + gate_act * (1.0 - opened))
        ).astype(BF16)
        m.dua[rows, :] = (d_inner * gate_act * opened).astype(BF16)

    feed_back(0)

    def feed_in(h):
        rows = block_rows(h, 256)
        half_sent(s.y, h)
        half_scatter(s.ds, nt(m.dga[rows, :], gate_w()) + nt(m.dua[rows, :], up_w()), h)
        rows = block_rows(4 * h + mine, 64)
        m.own[block_rows(h, 64), :] = nt(m.dga[rows, :], gate_w()) + nt(m.dua[rows, :], up_w())
        half_on(s.ds, h)

    feed_in(0)
    half_wait(s.df, m.df, 1)
    feed_back(1)
    feed_in(1)
    finals.append(lambda: (half_sent(s.ds, 0), half_sent(s.ds, 1)))

    def share_copy(pair, share, landing, zt):
        return copy(share, landing.at[z], pair[0].at[0], pair[1].at[0], (a, 2 * zt + c))

    def sum_near(pair, share, landing):
        share_copy(pair, share(near), landing, near).start()

    def sum_far(pair, share, landing, zt, slot, flag):
        copy(
            share(zt), landing.at[slot], pair[0].at[0], pair[1].at[flag], (a, 2 * near + c)
        ).start()

    def sum_start(pair, share, landing):
        @pl.when(jnp.logical_not(inner_chip))
        def _():
            sum_far(pair, share, landing, across, mirror, 1)
            sum_far(pair, share, landing, mirror, near, 2)

        sum_near(pair, share, landing)

    def sum_pass(pair, share, landing, add):
        @pl.when(inner_chip)
        def _():
            for zt, slot, flag in ((mirror, across, 1), (across, z, 2)):
                landed_all(pair[1].at[flag], landing.at[slot])
                add(zt, slot)
                share_copy(pair, share(zt), landing, zt).start()

    second = across + inside * (mirror - across)

    def sum_finish(pair, landing, three):
        landed_all(pair[1].at[0], landing.at[pl.ds(0, 2)])
        drain(pair, three)

    def landed(landing, where):
        return landing[(near,) + where].astype(F32) + landing[(second,) + where].astype(F32)

    def fold_add(view, pre, chunk):
        def add(second):
            rows = view(second).shape[0]

            def one(i):
                part_rows = pl.ds(pl.multiple_of(i * chunk, chunk), chunk)
                target = view(second)
                target[part_rows] = (
                    target[part_rows].astype(F32) + pre[part_rows].astype(F32)
                ).astype(BF16)

            each(0, rows // chunk, one)

        return add

    gate_share = lambda i: m.gus.at[0, i]
    up_share = lambda i: m.gus.at[1, i]

    def one_grad(i, place, grads):
        cols = pl.ds(pl.multiple_of(i * 256, 256), 256)
        m.gus[place, i] = tn(m.sc[:, cols], grads[...]).astype(BF16)

    one_grad(diagonal, 0, m.dga)
    one_grad(ny, 0, m.dga)
    fold_start(s.rg, gate_share, m.gpre.at[0], m.gland.at[0], ny)
    one_grad(diagonal, 1, m.dua)
    one_grad(nx, 1, m.dua)
    fold_start(s.ru, up_share, m.gpre.at[1], m.gland.at[1], nx)

    half_land(s.ds, 0)
    m.ggain[...] = jnp.zeros_like(m.ggain)

    def norm_back(i):
        rows = block_rows(i, 32)
        d_scaled = m.own[rows, :] + m.yrecv[0, rows, :].astype(F32)
        d_scaled = d_scaled + m.yrecv[2, rows, :].astype(F32)
        inv = m.inv[rows, 0:1]
        normed = m.hid[rows, :] * inv
        m.ggain[...] += jnp.sum(d_scaled * normed, axis=0, keepdims=True)
        d_normed = d_scaled * m.gain[...]
        lean = jnp.mean(d_normed * normed, axis=1, keepdims=True)
        d_hidden = m.dout[rows, :] + inv * (d_normed - normed * lean)
        m.dout[rows, :] = d_hidden
        opened = jax.nn.sigmoid(m.gp[rows, :].astype(F32))
        m.dbr[rows, :] = (d_hidden * opened).astype(BF16)
        m.dgt[rows, :] = (d_hidden * m.br[rows, :] * opened * (1.0 - opened)).astype(BF16)

    each(0, 2, norm_back)
    half_land(s.ds, 1)
    each(2, 4, norm_back)
    gate_cols = pl.ds(384, 128)
    cols_of = lambda i: pl.ds(pl.multiple_of(i * 128, 128), 128)
    m.dms[...] = nt(m.dbr[...], out_w()).astype(BF16)
    for head in range(8):
        cols = slice(head * 128, head * 128 + 128)
        m.dgs[head, :, 0:128] = m.dms[:, cols]
        m.dgs[head, :, 128:256] = m.dgt[:, cols]
    seq_peers(lambda p: seq_start(s.dm, m.dgs.at[p], m.dmg.at[b], p))
    drain(s.dm, m.dgs.at[pl.ds(0, 7)])
    m.dmg[b] = m.dgs[b]

    one_grad(nx, 0, m.dga)
    fold_pass(
        s.rg, gate_share, m.gpre.at[0], m.gland.at[0], fold_add(gate_share, m.gpre.at[0], 32), nx
    )
    one_grad(ny, 1, m.dua)
    fold_pass(
        s.ru, up_share, m.gpre.at[1], m.gland.at[1], fold_add(up_share, m.gpre.at[1], 32), ny
    )
    one_grad(a, 0, m.dga)
    one_grad(a, 1, m.dua)

    def down_grad(i):
        cols = pl.ds(pl.multiple_of(i * 256, 256), 256)
        m.ffd[block_rows(i, 256), :] = tn(m.inner[:, cols], m.df[...]).astype(BF16)

    each(0, pad // 256, down_grad)
    for i in range(4):
        double = m.ffd[2 * i * share_rows : 2 * (i + 1) * share_rows, :].astype(F32)
        for j in range(2):
            m.gds[2 * i + j] = jnp.concatenate(
                [double[j * share_rows : (j + 1) * share_rows, :], jnp.zeros((8, width), F32)],
                axis=0,
            ).astype(BF16)
    down_x_share = lambda i: m.gds.at[2 * i]
    down_y_share = lambda i: m.gds.at[2 * i + 1]
    fold_start(s.rdx, down_x_share, m.dpre.at[0], m.dland.at[0], ny)
    fold_start(s.rdy, down_y_share, m.dpre.at[1], m.dland.at[1], nx)

    def out_grad(i):
        cols = pl.ds(pl.multiple_of(i * 256, 256), 256)
        m.gwos[i] = tn(m.mx[:, cols], m.dbr[...]).astype(BF16).reshape(4, 2, 32, width)

    each(0, 4, out_grad)
    gos_copy = copy(m.gwos.at[:, :, 1 - c], m.gwor, s.gos[0].at[0], s.gos[1].at[0], (a, sib))
    gos_copy.start()
    finals.append(gos_copy.wait_send)
    m.pgrad[...] = jnp.zeros_like(m.pgrad)

    def attend_back_keys(i, extent):
        rows = block_rows(i, 128)
        keys = slice(0, extent)
        d_mixed = m.dmg[i, :, 0:128]
        m.dm[rows, :] = d_mixed
        m.dq[rows, gate_cols] = m.dmg[i, :, 128:256]
        d_joint = nt(d_mixed, m.v[keys, :])
        prob = m.probs[rows, keys].astype(F32)
        turned = prob * d_joint
        fixed_prob = m.fprobs[rows, :]
        fixed_full = fixed_prob.astype(F32)
        fixed_turned = fixed_full * nt(d_mixed, m.fkv[16:32, :])
        delta = jnp.sum(turned, axis=1, keepdims=True) + jnp.sum(
            fixed_turned, axis=1, keepdims=True
        )
        d_raw = (
            scale * (turned - prob * delta) + m.decay[rows, keys].astype(F32) * d_joint
        ).astype(BF16)
        m.probs[rows, keys] = d_raw
        d_fixed = (fixed_turned - fixed_full * delta).astype(BF16)
        m.dq[rows, 0:128] = (
            nn(d_raw, m.k[keys, :]) + scale * nn(d_fixed, m.fkv[0:16, :])
        ).astype(BF16)
        m.pgrad[0:16, :] += scale * tn(d_fixed, m.q[rows, :])
        m.pgrad[16:32, :] += tn(fixed_prob, d_mixed)

    attend_back = lambda i: by_extent(i, attend_back_keys)

    attend_back(b)

    def attend_back_next(step):
        i = lax.rem(b + step, 8)
        seq_wait(s.dm, m.dmg.at[i], i)
        attend_back(i)

    each(1, 4, attend_back_next)
    each(4, 6, attend_back_next)
    def owner_all(fold, pair, share, place):
        fold_finish(fold, m.gland.at[place], m.gus.at[place, pl.ds(0, 3)])

        def owner_rows(p):
            rows = block_rows(p, 32)
            total = m.gus[place, a, rows, :].astype(F32) + m.gland[place, 0, rows, :].astype(F32)
            m.gxs[p, place] = (total + m.gland[place, 1, rows, :].astype(F32)).astype(BF16)

        def owner_send(p):
            owner_rows(p)
            all_start(pair, m.gxs.at[p, place], m.gxr.at[b, place], p)

        seq_peers(owner_send)
        drain(pair, m.gxs.at[pl.ds(0, 7), place])
        owner_rows(b)
        m.gxr[b, place] = m.gxs[b, place]

    owner_all(s.rg, s.gxg, gate_share, 0)
    each(6, 8, attend_back_next)
    fold_pass(
        s.rdx, down_x_share, m.dpre.at[0], m.dland.at[0],
        fold_add(down_x_share, m.dpre.at[0], 32), nx,
    )
    fold_pass(
        s.rdy, down_y_share, m.dpre.at[1], m.dland.at[1],
        fold_add(down_y_share, m.dpre.at[1], 32), ny,
    )
    owner_all(s.ru, s.gxu, up_share, 1)

    m.fin0[0:32, :] = m.pgrad[...]
    for j in range(8):
        m.fin0[32 + j : 33 + j, :] = m.ggain[:, j * 128 : j * 128 + 128]
    m.fin1[a] = m.fin0[...]
    xy_peers(lambda p: xy_all_start(s.fin1, m.fin0, m.fin1.at[a], p))
    drain(s.fin1, m.fin1.at[pl.ds(0, 3)])

    query_turned = jnp.transpose(m.q[...].astype(F32)).astype(BF16)
    mixed_turned = jnp.transpose(m.dm[...].astype(F32)).astype(BF16)

    def key_value_grad(i):
        cols = cols_of(i)
        rows = block_rows(i, 128)
        m.dq[rows, 128:256] = jnp.transpose(nn(query_turned, m.probs[:, cols])).astype(BF16)
        m.dq[rows, 256:384] = jnp.transpose(nn(mixed_turned, m.both[:, cols])).astype(BF16)

    each(0, 8, key_value_grad)

    def token_grad(i):
        return nt(m.dq[block_rows(i, 128), :], m.wqk[...])

    def token_sib(zt):
        m.gts[zt, 1 - c] = token_grad(2 * zt + 1 - c).astype(BF16)
        copy(
            m.gts.at[zt, 1 - c], m.gtr.at[zt], s.gt[0].at[1], s.gt[1].at[4 + zt],
            (a, sib),
        ).start()

    for zt in (near + (1 - inside) * (across - near), mirror, across + (1 - inside) * (near - across), z):
        token_sib(zt)

    fold_finish(s.rdx, m.dland.at[0], m.gds.at[pl.ds(0, 3)])
    fold_finish(s.rdy, m.dland.at[1], m.gds.at[pl.ds(0, 3)])

    def down_sum(j):
        total = m.gds[2 * a + j].astype(F32) + m.dland[j, 0].astype(F32)
        return total + m.dland[j, 1].astype(F32)

    m.dsum[0] = down_sum(1 - part).astype(BF16)
    far_copy = copy(m.dsum.at[0], m.dfar, s.gfd[0].at[0], s.gfd[1].at[0], (a, far))
    far_copy.start()
    finals.append(far_copy.wait_send)

    token_share = lambda zt: m.gts.at[zt, c]

    def token_line(zt):
        mine = token_grad(2 * zt + c)
        copy(
            m.gtr.at[zt], m.gtr.at[zt], s.gt[0].at[1], s.gt[1].at[4 + zt], (a, sib)
        ).wait_recv()
        m.gts[zt, c] = (mine + m.gtr[zt].astype(F32)).astype(BF16)

    def pass_token(zt, slot):
        m.gts[zt, c] = (m.gts[zt, c].astype(F32) + m.yrecv[slot].astype(F32)).astype(BF16)

    token_line(near + (1 - inside) * (across - near))

    @pl.when(inner_chip)
    def _():
        sum_near(s.gt, token_share, m.yrecv)

    @pl.when(jnp.logical_not(inner_chip))
    def _():
        sum_far(s.gt, token_share, m.yrecv, across, mirror, 1)

    token_line(mirror)

    @pl.when(jnp.logical_not(inner_chip))
    def _():
        sum_far(s.gt, token_share, m.yrecv, mirror, near, 2)

    token_line(across + (1 - inside) * (near - across))

    @pl.when(jnp.logical_not(inner_chip))
    def _():
        sum_near(s.gt, token_share, m.yrecv)

    m.own[...] = token_grad(b)
    finals.append(lambda: sent(s.gt[0].at[1], m.gtr))

    def head_weight_grad(i):
        cols = pl.ds(pl.multiple_of(i * 256, 256), 256)
        m.gws[i] = tn(m.x_all[:, cols], m.dq[...]).astype(BF16)

    each(0, 4, head_weight_grad)
    weight_x = lambda i: m.gws.at[i, pl.ds(0, 128), :]
    weight_y = lambda i: m.gws.at[i, pl.ds(128, 128), :]
    land_x = m.wland.at[:, pl.ds(0, 128), :]
    land_y = m.wland.at[:, pl.ds(128, 128), :]
    fold_start(s.rwx, weight_x, m.wpre.at[0], land_x, ny)
    fold_start(s.rwy, weight_y, m.wpre.at[1], land_y, nx)

    gos_copy.wait_recv()

    def out_add(k):
        i = lax.div(k, 4)
        j = lax.rem(k, 4)
        m.gwos[i, j, c] = (
            m.gwos[i, j, c].astype(F32) + m.gwor[i, j].astype(F32)
        ).astype(BF16)

    each(0, 16, out_add)
    out_x = lambda i: m.gwos.at[i, pl.ds(0, 2), c]
    out_y = lambda i: m.gwos.at[i, pl.ds(2, 2), c]
    oland_x = m.oland.at[:, pl.ds(0, 2)]
    oland_y = m.oland.at[:, pl.ds(2, 2)]
    fold_start(s.rox, out_x, m.opre.at[0], oland_x, ny)
    fold_start(s.roy, out_y, m.opre.at[1], oland_y, nx)

    fold_pass(s.rwx, weight_x, m.wpre.at[0], land_x, fold_add(weight_x, m.wpre.at[0], 32), nx)
    fold_pass(s.rwy, weight_y, m.wpre.at[1], land_y, fold_add(weight_y, m.wpre.at[1], 32), ny)
    all_wait(s.fin1, m.fin1.at[pl.ds(0, 3)])
    m.fin2s[...] = (m.fin1[0] + m.fin1[1]) + (m.fin1[2] + m.fin1[3])
    m.fin2[b] = m.fin2s[32:48, :]
    seq_peers(lambda p: all_start(s.fin2, m.fin2s.at[pl.ds(32, 16), :], m.fin2.at[b], p))
    drain(s.fin2, m.fin2.at[pl.ds(0, 7)])
    holder = 2 * a + lax.div(b, 4)
    keeps = lambda p: (lax.div(b, 2) == a) & (lax.div(p, 4) == c)

    def pers_send(p):
        @pl.when(keeps(p))
        def _():
            copy(
                m.fin2s.at[pl.ds(0, 32), :], m.pers, s.pers[0].at[p], s.pers[1].at[0], (a, p)
            ).start()

    def pers_drain(p):
        @pl.when(keeps(p))
        def _():
            copy(m.pers, m.pers, s.pers[0].at[p], s.pers[1].at[0], (a, p)).wait_send()

    seq_peers(pers_send)
    finals.append(lambda: seq_peers(pers_drain))

    @pl.when(holder == b)
    def _():
        m.pers[...] = m.fin2s[0:32, :]

    fold_pass(s.rox, out_x, m.opre.at[0], oland_x, fold_add(out_x, m.opre.at[0], 1), nx)
    fold_pass(s.roy, out_y, m.opre.at[1], oland_y, fold_add(out_y, m.opre.at[1], 1), ny)
    sum_pass(s.gt, token_share, m.yrecv, pass_token)
    fold_finish(s.rwx, land_x, m.gws.at[pl.ds(0, 3), pl.ds(0, 128), :])
    fold_finish(s.rwy, land_y, m.gws.at[pl.ds(0, 3), pl.ds(0, 128), :])

    def head_sum(p):
        rows = block_rows(p, 32)
        total = m.gws[a, rows, :].astype(F32) + m.wland[0, rows, :].astype(F32)
        m.gas[p] = (total + m.wland[1, rows, :].astype(F32)).astype(BF16)

    def head_sum_send(p):
        head_sum(p)
        all_start(s.gwa, m.gas.at[p], m.gar.at[b], p)

    seq_peers(head_sum_send)
    drain(s.gwa, m.gas.at[pl.ds(0, 7)])
    head_sum(b)
    m.gar[b] = m.gas[b]

    fold_finish(s.rox, oland_x, m.gwos.at[pl.ds(0, 3), pl.ds(0, 2), 0])
    fold_finish(s.roy, oland_y, m.gwos.at[pl.ds(0, 3), pl.ds(0, 2), 0])

    def out_sum(i):
        total = m.gwos[a, i, c].astype(F32) + m.oland[0, i].astype(F32)
        m.gos[i] = (total + m.oland[1, i].astype(F32)).astype(BF16)

    each(0, 4, out_sum)
    out_share = lambda zt: m.gos.at[zt]

    def pass_out(zt, slot):
        m.gos[zt] = (m.gos[zt].astype(F32) + m.goz[slot].astype(F32)).astype(BF16)

    sum_start(s.rgo, out_share, m.goz)
    own_half = down_sum(part)
    far_copy.wait_recv()
    fd_o[...] = own_half[0:share_rows, :] + m.dfar[0:share_rows, :].astype(F32)
    sum_pass(s.rgo, out_share, m.goz, pass_out)

    sum_finish(s.gt, m.yrecv, m.yrecv.at[pl.ds(0, 3)])
    copy(
        m.gtr.at[z], m.gtr.at[z], s.gt[0].at[1], s.gt[1].at[4 + z], (a, sib)
    ).wait_recv()

    def token_sum(i):
        rows = block_rows(i, 32)
        total = m.dout[rows, :] + m.own[rows, :]
        total = total + m.gtr[z, rows, :].astype(F32)
        gtok_o[rows, :] = total + landed(m.yrecv, (rows, slice(None)))

    each(0, 4, token_sum)

    all_wait(s.gwa, m.gar.at[pl.ds(0, 7)])
    gar_o[...] = m.gar[...]

    all_wait(s.gxg, m.gxr.at[pl.ds(0, 7), 0])
    all_wait(s.gxu, m.gxr.at[pl.ds(0, 7), 1])
    gux_o[...] = m.gxr[...]

    sum_finish(s.rgo, m.goz, m.goz.at[pl.ds(0, 3)])
    gwo_o[...] = m.gos[z].astype(F32) + landed(m.goz, ())

    all_wait(s.fin2, m.fin2.at[pl.ds(0, 7)])
    everything = jnp.sum(m.fin2[...], axis=0)
    fin_o[0:8, :] = everything[0:8, :]
    loss = jnp.sum(everything[8:9, :]) / (2.0 * width * valid_total)
    fin_o[8:16, :] = jnp.full((8, 128), loss, F32)

    @pl.when(holder != b)
    def _():
        copy(m.pers, m.pers, s.pers[0].at[0], s.pers[1].at[0], (a, holder)).wait_recv()

    pers_o[...] = m.pers[...]

    for last in finals:
        last()


def finish_kernel(
    width, hidden, out, gtok, gar, gwo, fin, pers, gux, fd,
    out_o, loss_o, gtok_o, gq_o, gk_o, gv_o, gwo_o, gwg_o, pk_o, pv_o, gain_o, fg_o, fu_o, fd_o,
):
    a = lax.axis_index("head")
    b = lax.axis_index("seq")
    quarter = lax.rem(b, 4)

    def lanes(value):
        picked = value[:, 0:32]
        for j in range(1, 4):
            picked = jnp.where(quarter == j, value[:, 32 * j : 32 * j + 32], picked)
        return picked

    out_o[...] = out[...]
    gtok_o[...] = gtok[...]
    gwo_o[...] = gwo[...]
    fd_o[...] = fd[...]
    loss_o[...] = fin[8:9, 0:1]
    pk_o[...] = lanes(pers[0:16, :])
    pv_o[...] = lanes(pers[16:32, :])
    gain_o[...] = lanes(fin[pl.ds(2 * a + lax.div(b, 4), 1), :])
    for head in range(8):
        cols = slice(head * 128, head * 128 + 128)
        gq_o[:, cols] = gar[head, :, 0:128].astype(F32)
        gk_o[:, cols] = gar[head, :, 128:256].astype(F32)
        gv_o[:, cols] = gar[head, :, 256:384].astype(F32)
        gwg_o[:, cols] = gar[head, :, 384:512].astype(F32)
    run = hidden // 8
    for place, target in enumerate((fg_o, fu_o)):
        for group in range(4):
            total = gux[group, place].astype(F32) + gux[group + 4, place].astype(F32)
            for i in range(8):
                start = run * (4 * i + group)
                target[:, start : start + run] = total[:, run * i : run * i + run]


def local_block(
    tokens, w_query, w_key, w_value, w_out, w_gate, persist_keys, persist_values, norm_gain,
    ff_gate, ff_up, ff_down, retention, doc_starts, valid, teacher,
):
    _, block, width = tokens.shape
    length = block * lax.axis_size("seq")
    hidden = ff_gate.shape[1] // 4
    pad = -(-hidden // 256) * 256
    share = ff_down.shape[0]
    table = scratch_table(width, block, hidden, pad, length)
    names = tuple(table)
    vmem = pl.BlockSpec(memory_space=pltpu.VMEM)
    shape = jax.ShapeDtypeStruct
    outs = (
        shape((block, width), BF16),
        shape((block, width), F32),
        shape((8, 32, 512), BF16),
        shape((32, width), F32),
        shape((16, 128), F32),
        shape((32, 128), F32),
        shape((8, 2, 32, pad), BF16),
        shape((share, width), F32),
    )
    scratch = [pltpu.VMEM(*table[name]) for name in names]
    for count in FLAGS.values():
        scratch += [pltpu.SemaphoreType.DMA((count,))] * 2
    result = pl.pallas_call(
        functools.partial(block_kernel, names, width, hidden, doc_starts.shape[1]),
        out_shape=outs,
        in_specs=[vmem] * 15 + [pl.BlockSpec(memory_space=pltpu.SMEM)],
        out_specs=[vmem] * len(outs),
        scratch_shapes=scratch,
        compiler_params=pltpu.CompilerParams(
            collective_id=0, has_side_effects=True, vmem_limit_bytes=VMEM_LIMIT
        ),
        name="block",
    )(
        tokens[0], w_query, w_key, w_value, w_out, w_gate, ff_gate, ff_up, ff_down, teacher[0],
        jnp.transpose(retention, (0, 2, 1)), persist_keys, persist_values, norm_gain[None],
        valid, doc_starts,
    )
    square = shape((32, width), F32)
    wide = shape((32, 4 * hidden), F32)
    finals = (
        outs[0], shape((1, 1), F32), outs[1], square, square, square, square, square,
        shape((P_SIZE, 32), F32), shape((P_SIZE, 32), F32), shape((1, 32), F32), wide, wide,
        outs[7],
    )
    done = pl.pallas_call(
        functools.partial(finish_kernel, width, hidden),
        out_shape=finals,
        in_specs=[vmem] * len(outs),
        out_specs=[vmem] * len(finals),
        name="finish",
    )(*result)
    (out, loss, gtok, gq, gk, gv, gwo, gwg, gpk, gpv, gain, fg, fu, fd) = done
    return (
        out[None], loss[0, 0], gtok[None], gq, gk, gv, gwo, gwg, gpk, gpv, gain[0], fg, fu, fd,
    )


VMEM_LIMIT = 62 << 20


def entering(value, axis, join, neutral, backward):
    count = lax.axis_size(axis)
    place = lax.axis_index(axis)
    ahead = count - 1 - place if backward else place
    gathered = jax.tree.map(
        lambda a, kind: lax.all_gather(a.astype(kind), axis), value, (jnp.bfloat16, jnp.bfloat16)
    )
    state = jax.tree.map(lambda a, e: jnp.zeros_like(a) + jnp.asarray(e, a.dtype), value, neutral)

    def one(hop, state):
        source = count - 1 - hop if backward else hop
        return join(
            state,
            jax.tree.map(
                lambda a, own: lax.dynamic_index_in_dim(a, source, 0, False).astype(own.dtype),
                gathered,
                value,
            ),
        )

    return lax.fori_loop(0, ahead, one, state)


def passed_along(value, axis, by):
    peers = lax.axis_size(axis)
    pairs = [(i, i + by) for i in range(peers) if 0 <= i + by < peers]
    return lax.ppermute(value, axis, pairs)


def from_behind(block, axis, distance):
    devices = range(lax.axis_size(axis))
    route = [((i - distance) % len(devices), i) for i in devices]
    return lax.ppermute(block, axis, route)


def product(left, right):
    return jnp.dot(left, right, preferred_element_type=jnp.float32)


def rows_outer(left, right):
    return jnp.einsum("nd,ne->de", left, right, preferred_element_type=jnp.float32)


def back_product(grad, weight):
    return jnp.einsum("ne,de->nd", grad, weight, preferred_element_type=jnp.float32)


def doc_index(starts, positions):
    return jnp.sum((starts[:, None, :] <= positions[None, :, None]).astype(jnp.int32), axis=-1) - 1


def doc_begin(starts, positions):
    return jnp.any(starts[:, None, :] == positions[None, :, None], axis=-1)


def chain_forward(earlier, later):
    return (earlier[0] * later[0], later[0][..., None, None] * earlier[1] + later[1])


def chain_backward(earlier, later):
    return (earlier[0] * later[0], later[1] + later[0][..., None, None] * earlier[1])


def masked_scores(query_rows, key_rows, query_pos, key_pos, query_seg, key_seg, scale):
    raw = (
        jnp.einsum("sqhd,skhd->sqhk", query_rows, key_rows, preferred_element_type=jnp.float32)
        * scale
    )
    allowed = (key_pos[None, None, :] <= query_pos[None, :, None]) & (
        key_seg[:, None, :] == query_seg[:, :, None]
    )
    return jnp.where(allowed[:, :, None, :], raw, MASKED)


def softmax_grads(
    query_rows,
    key_rows,
    value_rows,
    dout_rows,
    query_pos,
    key_pos,
    query_seg,
    key_seg,
    query_lse,
    query_delta,
    scale,
):
    scores = masked_scores(query_rows, key_rows, query_pos, key_pos, query_seg, key_seg, scale)
    probs = jnp.exp(scores - query_lse[..., None])
    prob_grad = jnp.einsum(
        "sqhd,skhd->sqhk", dout_rows, value_rows, preferred_element_type=jnp.float32
    )
    score_grad = (probs * (prob_grad - query_delta[..., None])).astype(jnp.bfloat16)
    return (probs.astype(jnp.bfloat16), score_grad)


def local(
    tokens,
    w_query,
    w_key,
    w_value,
    w_out,
    w_gate,
    persist_keys,
    persist_values,
    norm_gain,
    ff_gate,
    ff_up,
    ff_down,
    retention,
    doc_starts,
    valid,
    teacher,
):
    gathered = (
        lax.all_gather(w_query, ("head", "seq"), axis=0, tiled=True),
        lax.all_gather(w_key, ("head", "seq"), axis=0, tiled=True),
        lax.all_gather(w_value, ("head", "seq"), axis=0, tiled=True),
        lax.all_gather(w_out, ("head", "seq"), axis=0, tiled=True),
        lax.all_gather(w_gate, ("head", "seq"), axis=0, tiled=True),
        lax.all_gather(jnp.transpose(persist_keys), ("head", "seq"), axis=0, tiled=True),
        lax.all_gather(jnp.transpose(persist_values), ("head", "seq"), axis=0, tiled=True),
        lax.all_gather(norm_gain, ("head", "seq"), axis=0, tiled=True),
        lax.all_gather(ff_gate, ("head", "seq"), axis=0, tiled=True),
        lax.all_gather(ff_up, ("head", "seq"), axis=0, tiled=True),
        lax.all_gather(ff_down, ("head", "seq"), axis=0, tiled=True),
    )
    (
        query_weight,
        key_weight,
        value_weight,
        out_weight,
        gate_weight,
        fixed_key_cols,
        fixed_value_cols,
        gain_weight,
        ffn_gate,
        ffn_up,
        ffn_down,
    ) = gathered
    fixed_key_all = jnp.transpose(fixed_key_cols)
    fixed_value_all = jnp.transpose(fixed_value_cols)
    local_seqs, block, width = tokens.shape
    groups = lax.axis_size("head")
    heads = HEAD_COUNT // groups
    head_place = lax.axis_index("head")
    seq_place = lax.axis_index("seq")
    seq_count = lax.axis_size("seq")
    all_seqs = local_seqs * groups
    length = block * seq_count
    token_count = local_seqs * block
    scale = HD ** (-0.5)
    mem_scale = 0.125 / HD
    token_rows = tokens.reshape(token_count, width)
    query_tok = (
        product(token_rows, query_weight)
        .astype(jnp.bfloat16)
        .reshape(local_seqs, block, HEAD_COUNT, HD)
    )
    key_tok = (
        product(token_rows, key_weight)
        .astype(jnp.bfloat16)
        .reshape(local_seqs, block, HEAD_COUNT, HD)
    )
    value_tok = (
        product(token_rows, value_weight)
        .astype(jnp.bfloat16)
        .reshape(local_seqs, block, HEAD_COUNT, HD)
    )
    gate_pre = product(token_rows, gate_weight)
    query_heads, key_heads, value_heads = (
        lax.all_to_all(query_tok, "head", split_axis=2, concat_axis=0, tiled=True),
        lax.all_to_all(key_tok, "head", split_axis=2, concat_axis=0, tiled=True),
        lax.all_to_all(value_tok, "head", split_axis=2, concat_axis=0, tiled=True),
    )
    fixed_keys = lax.dynamic_slice_in_dim(
        fixed_key_all.reshape(P_SIZE, HEAD_COUNT, HD), head_place * heads, heads, 1
    )
    fixed_values = lax.dynamic_slice_in_dim(
        fixed_value_all.reshape(P_SIZE, HEAD_COUNT, HD), head_place * heads, heads, 1
    )
    own_start = seq_place * block
    own_pos = own_start + jnp.arange(block, dtype=jnp.int32)
    own_seg = doc_index(doc_starts, own_pos)
    own_begin = doc_begin(doc_starts, own_pos)
    last_row = own_start + block - 1
    fixed_scores = (
        jnp.einsum("sqhd,phd->sqhp", query_heads, fixed_keys, preferred_element_type=jnp.float32)
        * scale
    )
    top_start = jnp.max(fixed_scores, axis=-1)
    fixed_exp = jnp.exp(fixed_scores - top_start[..., None])
    acc_start = jnp.einsum(
        "sqhp,phd->sqhd",
        fixed_exp.astype(jnp.bfloat16),
        fixed_values,
        preferred_element_type=jnp.float32,
    )
    key_rows = lax.all_gather(key_heads, "seq", axis=1, tiled=True)
    value_rows = lax.all_gather(value_heads, "seq", axis=1, tiled=True)
    piece_keys = key_rows.shape[1]

    def attend_compute(state):
        running_top, running_total, running_acc = state
        key_pos = jnp.arange(piece_keys, dtype=jnp.int32)
        scores = masked_scores(
            query_heads, key_rows, own_pos, key_pos, own_seg, doc_index(doc_starts, key_pos), scale
        )
        new_top = jnp.maximum(running_top, jnp.max(scores, axis=-1))
        shrink = jnp.exp(running_top - new_top)
        weights_exp = jnp.exp(scores - new_top[..., None])
        new_total = running_total * shrink + jnp.sum(weights_exp, axis=-1)
        new_acc = running_acc * shrink[..., None] + jnp.einsum(
            "sqhk,skhd->sqhd",
            weights_exp.astype(jnp.bfloat16),
            value_rows,
            preferred_element_type=jnp.float32,
        )
        return (new_top, new_total, new_acc)

    final_top, final_total, final_acc = lax.cond(
        jnp.int32(0) <= last_row,
        attend_compute,
        lambda state: state,
        (top_start, jnp.sum(fixed_exp, axis=-1), acc_start),
    )
    attn_rows = final_acc / final_total[..., None]
    lse = final_top + jnp.log(final_total)
    log_retention = jnp.log(retention)
    running = jnp.cumsum(log_retention, axis=1)
    lane = jnp.transpose(running, (0, 2, 1))
    index = jnp.arange(block)
    linked = (index[None, :] <= index[:, None])[None] & (own_seg[:, None, :] == own_seg[:, :, None])
    decay = jnp.where(
        linked[:, None], jnp.exp(jnp.minimum(lane[:, :, :, None] - lane[:, :, None, :], 0.0)), 0.0
    )
    intersection = jnp.einsum(
        "sthd,suhd->shtu", query_heads, key_heads, preferred_element_type=jnp.float32
    )
    mixing = (mem_scale * intersection * decay).astype(jnp.bfloat16)
    inner_mem = jnp.einsum(
        "shtu,suhd->sthd", mixing, value_heads, preferred_element_type=jnp.float32
    )
    carried = ((own_seg == own_seg[:, :1]) & jnp.logical_not(own_begin[:, :1])).astype(jnp.float32)
    lead = jnp.exp(running) * carried[..., None]
    trail = jnp.where(
        (own_seg == own_seg[:, -1:])[..., None], jnp.exp(running[:, -1:, :] - running), 0.0
    )
    query_full = query_heads.astype(jnp.float32)
    key_full = key_heads.astype(jnp.float32)
    value_full = value_heads.astype(jnp.float32)
    block_state = jnp.einsum(
        "suhd,suhe->shde", key_full * trail[..., None], value_full, precision=HIGHEST
    )
    block_keep = lead[:, -1, :]
    identity = (jnp.ones_like(block_keep), jnp.zeros_like(block_state))
    chained = entering((block_keep, block_state), "seq", chain_forward, identity, False)
    state_in = chained[1]
    outer_mem = (
        mem_scale
        * lead[..., None]
        * jnp.einsum("sthd,shde->sthe", query_full, state_in, precision=HIGHEST)
    )
    mixed_heads = (attn_rows + inner_mem + outer_mem).astype(jnp.bfloat16)
    mixed_rows = lax.all_to_all(
        mixed_heads, "head", split_axis=0, concat_axis=2, tiled=True
    ).reshape(token_count, width)
    branch = product(mixed_rows, out_weight)
    gate_sigmoid = jax.nn.sigmoid(gate_pre)
    hidden = token_rows.astype(jnp.float32) + gate_sigmoid * branch
    inv_rms = lax.rsqrt(jnp.mean(hidden * hidden, axis=-1, keepdims=True) + EPSILON)
    normed = hidden * inv_rms
    gain_full = gain_weight.astype(jnp.float32)
    scaled = (normed * gain_full).astype(jnp.bfloat16)
    gate_act = product(scaled, ffn_gate)
    up_act = product(scaled, ffn_up)
    act_sigmoid = jax.nn.sigmoid(gate_act)
    silu_act = gate_act * act_sigmoid
    inner = (silu_act * up_act).astype(jnp.bfloat16)
    final = hidden + product(inner, ffn_down)
    output = final.astype(jnp.bfloat16).reshape(local_seqs, block, width)
    valid_rows = valid.reshape(token_count).astype(jnp.float32)
    error = final - teacher.reshape(token_count, width).astype(jnp.float32)
    sums = lax.psum(
        (jnp.sum(valid_rows * jnp.sum(error * error, axis=-1)), jnp.sum(valid_rows)),
        ("head", "seq"),
    )
    loss = sums[0] / (2.0 * width * sums[1])
    total_tokens = all_seqs * length
    d_out = valid_rows[:, None] * error * (total_tokens / sums[1])
    d_ffn = d_out.astype(jnp.bfloat16)
    grad_down = rows_outer(inner, d_ffn)
    d_inner = back_product(d_ffn, ffn_down)
    d_gate_act = (d_inner * up_act * act_sigmoid * (1.0 + gate_act * (1.0 - act_sigmoid))).astype(
        jnp.bfloat16
    )
    d_up_act = (d_inner * silu_act).astype(jnp.bfloat16)
    grad_ffn_gate = rows_outer(scaled, d_gate_act)
    grad_ffn_up = rows_outer(scaled, d_up_act)
    d_scaled = back_product(d_gate_act, ffn_gate) + back_product(d_up_act, ffn_up)
    grad_gain = jnp.sum(d_scaled * normed, axis=0)
    d_normed = d_scaled * gain_full
    d_hidden = d_out + inv_rms * (
        d_normed - normed * jnp.mean(d_normed * normed, axis=-1, keepdims=True)
    )
    d_branch = (d_hidden * gate_sigmoid).astype(jnp.bfloat16)
    d_gate = (d_hidden * branch * gate_sigmoid * (1.0 - gate_sigmoid)).astype(jnp.bfloat16)
    grad_out_weight = rows_outer(mixed_rows, d_branch)
    grad_gate_weight = rows_outer(token_rows, d_gate)
    d_mixed = (
        back_product(d_branch, out_weight)
        .astype(jnp.bfloat16)
        .reshape(local_seqs, block, HEAD_COUNT, HD)
    )
    dout_heads = lax.all_to_all(d_mixed, "head", split_axis=2, concat_axis=0, tiled=True)
    dout_full = dout_heads.astype(jnp.float32)
    delta = jnp.sum(dout_full * attn_rows, axis=-1)
    fixed_probs = jnp.exp(fixed_scores - lse[..., None])
    fixed_prob_grad = jnp.einsum(
        "sqhd,phd->sqhp", dout_heads, fixed_values, preferred_element_type=jnp.float32
    )
    fixed_score_grad = (fixed_probs * (fixed_prob_grad - delta[..., None])).astype(jnp.bfloat16)
    fixed_key_grad = (
        jnp.einsum(
            "sqhp,sqhd->phd", fixed_score_grad, query_heads, preferred_element_type=jnp.float32
        )
        * scale
    )
    fixed_value_grad = jnp.einsum(
        "sqhp,sqhd->phd",
        fixed_probs.astype(jnp.bfloat16),
        dout_heads,
        preferred_element_type=jnp.float32,
    )
    query_grad_start = (
        jnp.einsum(
            "sqhp,phd->sqhd", fixed_score_grad, fixed_keys, preferred_element_type=jnp.float32
        )
        * scale
    )
    fold_start = (query_grad_start,)
    back_key_rows = lax.all_gather(key_heads, "seq", axis=1, tiled=True)
    back_value_rows = lax.all_gather(value_heads, "seq", axis=1, tiled=True)
    back_piece_keys = back_key_rows.shape[1]

    def back_compute(state):
        key_pos = jnp.arange(back_piece_keys, dtype=jnp.int32)
        probs_low, score_grad = softmax_grads(
            query_heads,
            back_key_rows,
            back_value_rows,
            dout_heads,
            own_pos,
            key_pos,
            own_seg,
            doc_index(doc_starts, key_pos),
            lse,
            delta,
            scale,
        )
        query_grad = (
            state[0]
            + jnp.einsum(
                "sqhk,skhd->sqhd", score_grad, back_key_rows, preferred_element_type=jnp.float32
            )
            * scale
        )
        return (query_grad,)

    folded = lax.cond(jnp.int32(0) <= last_row, back_compute, lambda state: state, fold_start)
    query_att = folded[0]
    empty_local = jnp.zeros((all_seqs, block, heads, HD), jnp.float32)

    def visit(turn, state):
        key_rows, value_rows, key_acc, value_acc = state
        owner = (seq_place - turn) % seq_count
        start = owner * block

        def visit_compute(accs):
            key_pos = start + jnp.arange(block, dtype=jnp.int32)
            probs_low, score_grad = softmax_grads(
                query_heads,
                key_rows,
                value_rows,
                dout_heads,
                own_pos,
                key_pos,
                own_seg,
                doc_index(doc_starts, key_pos),
                lse,
                delta,
                scale,
            )
            key_next = (
                accs[0]
                + jnp.einsum(
                    "sqhk,sqhd->skhd", score_grad, query_heads, preferred_element_type=jnp.float32
                )
                * scale
            )
            value_next = accs[1] + jnp.einsum(
                "sqhk,sqhd->skhd", probs_low, dout_heads, preferred_element_type=jnp.float32
            )
            return (key_next, value_next)

        key_acc, value_acc = lax.cond(
            start <= last_row, visit_compute, lambda accs: accs, (key_acc, value_acc)
        )
        key_rows, value_rows = passed_along((key_rows, value_rows), "seq", 1)
        key_acc, value_acc = (
            from_behind(key_acc.astype(jnp.bfloat16), "seq", 1).astype(key_acc.dtype),
            from_behind(value_acc.astype(jnp.bfloat16), "seq", 1).astype(value_acc.dtype),
        )
        return (key_rows, value_rows, key_acc, value_acc)

    travelled = lax.fori_loop(
        0, seq_count, visit, (key_heads, value_heads, empty_local, empty_local)
    )
    key_att = travelled[2]
    value_att = travelled[3]
    mix_grad_raw = jnp.einsum(
        "sthe,suhe->shtu", dout_heads, value_heads, preferred_element_type=jnp.float32
    )
    intersection_grad = (mem_scale * mix_grad_raw * decay).astype(jnp.bfloat16)
    local_grad = mem_scale * jnp.einsum(
        "sthd,sthe->shde", query_full * lead[..., None], dout_full, precision=HIGHEST
    )
    state_grads = entering((block_keep, local_grad), "seq", chain_backward, identity, True)
    carry_grad = state_grads[1]
    query_mem = jnp.einsum(
        "shtu,suhd->sthd", intersection_grad, key_heads, preferred_element_type=jnp.float32
    )
    query_mem = query_mem + mem_scale * lead[..., None] * jnp.einsum(
        "sthe,shde->sthd", dout_full, state_in, precision=HIGHEST
    )
    key_mem = jnp.einsum(
        "shtu,sthd->suhd", intersection_grad, query_heads, preferred_element_type=jnp.float32
    )
    key_mem = key_mem + trail[..., None] * jnp.einsum(
        "suhe,shde->suhd", value_full, carry_grad, precision=HIGHEST
    )
    value_mem = jnp.einsum(
        "shtu,sthe->suhe", mixing, dout_heads, preferred_element_type=jnp.float32
    )
    value_mem = value_mem + jnp.einsum(
        "suhd,shde->suhe", key_full * trail[..., None], carry_grad, precision=HIGHEST
    )
    query_grad_heads = (query_att + query_mem).astype(jnp.bfloat16)
    key_grad_heads = (key_att + key_mem).astype(jnp.bfloat16)
    value_grad_heads = (value_att + value_mem).astype(jnp.bfloat16)
    query_back, key_back, value_back = (
        lax.all_to_all(query_grad_heads, "head", split_axis=0, concat_axis=2, tiled=True),
        lax.all_to_all(key_grad_heads, "head", split_axis=0, concat_axis=2, tiled=True),
        lax.all_to_all(value_grad_heads, "head", split_axis=0, concat_axis=2, tiled=True),
    )
    query_back = query_back.reshape(token_count, width)
    key_back = key_back.reshape(token_count, width)
    value_back = value_back.reshape(token_count, width)
    grad_query_weight = rows_outer(token_rows, query_back)
    grad_key_weight = rows_outer(token_rows, key_back)
    grad_value_weight = rows_outer(token_rows, value_back)
    token_grad = (
        d_hidden + back_product(d_gate, gate_weight) + back_product(query_back, query_weight)
    )
    token_grad = (
        token_grad + back_product(key_back, key_weight) + back_product(value_back, value_weight)
    )
    fixed_key_full = lax.dynamic_update_slice_in_dim(
        jnp.zeros((P_SIZE, HEAD_COUNT, HD), jnp.float32), fixed_key_grad, head_place * heads, 1
    ).reshape(P_SIZE, width)
    fixed_value_full = lax.dynamic_update_slice_in_dim(
        jnp.zeros((P_SIZE, HEAD_COUNT, HD), jnp.float32), fixed_value_grad, head_place * heads, 1
    ).reshape(P_SIZE, width)
    shards = (
        lax.psum_scatter(grad_query_weight, ("head", "seq"), scatter_dimension=0, tiled=True),
        lax.psum_scatter(grad_key_weight, ("head", "seq"), scatter_dimension=0, tiled=True),
        lax.psum_scatter(grad_value_weight, ("head", "seq"), scatter_dimension=0, tiled=True),
        lax.psum_scatter(grad_out_weight, ("head", "seq"), scatter_dimension=0, tiled=True),
        lax.psum_scatter(grad_gate_weight, ("head", "seq"), scatter_dimension=0, tiled=True),
        lax.psum_scatter(
            jnp.transpose(fixed_key_full), ("head", "seq"), scatter_dimension=0, tiled=True
        ),
        lax.psum_scatter(
            jnp.transpose(fixed_value_full), ("head", "seq"), scatter_dimension=0, tiled=True
        ),
        lax.psum_scatter(grad_gain, ("head", "seq"), scatter_dimension=0, tiled=True),
        lax.psum_scatter(grad_ffn_gate, ("head", "seq"), scatter_dimension=0, tiled=True),
        lax.psum_scatter(grad_ffn_up, ("head", "seq"), scatter_dimension=0, tiled=True),
        lax.psum_scatter(grad_down, ("head", "seq"), scatter_dimension=0, tiled=True),
    )
    return (
        output,
        loss,
        token_grad.reshape(local_seqs, block, width),
        shards[0],
        shards[1],
        shards[2],
        shards[3],
        shards[4],
        jnp.transpose(shards[5]),
        jnp.transpose(shards[6]),
        shards[7],
        shards[8],
        shards[9],
        shards[10],
    )


def solution(mesh):
    in_specs = (
        P("head", "seq", None),
        P(("head", "seq"), None),
        P(("head", "seq"), None),
        P(("head", "seq"), None),
        P(("head", "seq"), None),
        P(("head", "seq"), None),
        P(None, ("head", "seq")),
        P(None, ("head", "seq")),
        P(("head", "seq")),
        P(("head", "seq"), None),
        P(("head", "seq"), None),
        P(("head", "seq"), None),
        P(None, "seq", "head"),
        P(),
        P("head", "seq"),
        P("head", "seq", None),
    )
    out_specs = (
        P("head", "seq", None),
        P(),
        P("head", "seq", None),
        P(("head", "seq"), None),
        P(("head", "seq"), None),
        P(("head", "seq"), None),
        P(("head", "seq"), None),
        P(("head", "seq"), None),
        P(None, ("head", "seq")),
        P(None, ("head", "seq")),
        P(("head", "seq")),
        P(("head", "seq"), None),
        P(("head", "seq"), None),
        P(("head", "seq"), None),
    )
    fits = mesh.shape["head"] == 4 and mesh.shape["seq"] == HEAD_COUNT
    body = local_block if fits else local
    return jax.shard_map(body, mesh=mesh, in_specs=in_specs, out_specs=out_specs, check_vma=False)
```

```python
import functools
import types

import jax
import jax.numpy as jnp
from jax import lax
from jax.experimental import pallas as pl
from jax.experimental.pallas import tpu as pltpu
from jax.sharding import PartitionSpec as P

HEAD_COUNT = 8
HD = 128
P_SIZE = 16


HIGHEST = lax.Precision.HIGHEST
MASKED = -1e30
EPSILON = 1e-06
F32 = jnp.float32
BF16 = jnp.bfloat16
MESH_IDS = pl.DeviceIdType.MESH


def nn(left, right):
    return lax.dot_general(left, right, (((1,), (0,)), ((), ())), preferred_element_type=F32)


def nt(left, right):
    return lax.dot_general(left, right, (((1,), (1,)), ((), ())), preferred_element_type=F32)


def tn(left, right):
    return lax.dot_general(left, right, (((0,), (0,)), ((), ())), preferred_element_type=F32)


def tn_exact(left, right):
    return lax.dot_general(
        left, right, (((0,), (0,)), ((), ())), precision=HIGHEST, preferred_element_type=F32
    )


def nt_exact(left, right):
    return lax.dot_general(
        left, right, (((1,), (1,)), ((), ())), precision=HIGHEST, preferred_element_type=F32
    )


def nn_exact(left, right):
    return lax.dot_general(
        left, right, (((1,), (0,)), ((), ())), precision=HIGHEST, preferred_element_type=F32
    )


def block_rows(index, size):
    return pl.ds(pl.multiple_of(index * size, size), size)


def each(first, last, body):
    def step(index, carry):
        body(index)
        return carry

    lax.fori_loop(first, last, step, 0)


SEQ_FLAGS = dict(
    w1=8, t2=8, p2=8, x=8, wo=8, fxg=8, fxu=8, mx=8, dm=8, gxg=8, gxu=8, rgo=8, gt=8, gwa=8,
    fin2=8, pers=8, sc=8, y=8, df=8, ds=8, fd=1, gfd=1, gos=1,
)
XY_FLAGS = dict(
    t1=4, p1=4, w2=4, wox=4, fgx=4, fux=4, fdx=4, fdy=4, rg=3, ru=3, rdx=3, rdy=3, rox=3, roy=3,
    rwx=3, rwy=3, fin1=4,
)
FLAGS = SEQ_FLAGS | XY_FLAGS


def scratch_table(width, tokens, hidden, hidden_pad, length):
    seqs, blocks, block = 4, 8, 128
    table = dict(
        x_all=((length, width), BF16),
        wcs=((blocks, 32, 512), BF16),
        wqk=((width, 512), BF16),
        tile=((4, 8, 128), F32),
        pin=((32, 128), BF16),
        vcol=((block, 1), F32),
        t1=((4, 8, 128), F32),
        p1=((4, 32, 128), BF16),
        t2s=((16, 128), F32),
        t2=((8, 16, 128), F32),
        p2=((8, 32, 128), BF16),
        fs=((4, 2, 32, hidden_pad), BF16),
        fgu=((2, 4, 256, hidden_pad), BF16),
        fdp=((8, 96, width), BF16),
        ffd=((hidden_pad, width), BF16),
        wo_all=((4, 4, 2, 32, width), BF16),
        q=((length, HD), BF16),
        k=((length, HD), BF16),
        v=((length, HD), BF16),
        fkv=((32, HD), BF16),
        gain=((1, width), F32),
        rrow=((1, length), F32),
        rcol=((block, 8), F32),
        probs=((length, length), BF16),
        decay=((length, length), BF16),
        both=((length, length), BF16),
        fprobs=((length, P_SIZE), BF16),
        mgs=((length, 2 * HD), BF16),
        mg=((8, block, 2 * HD), BF16),
        mx=((block, width), BF16),
        gp=((block, width), BF16),
        hid=((block, width), F32),
        br=((block, width), F32),
        inv=((block, 128), F32),
        own=((block, width), F32),
        dout=((block, width), F32),
        sc=((4 * block, width), BF16),
        gact=((4 * block, hidden_pad), F32),
        uact=((4 * block, hidden_pad), F32),
        inner=((4 * block, hidden_pad), BF16),
        ysend=((4, block, width), BF16),
        yrecv=((4, block, width), BF16),
        df=((4 * block, width), BF16),
        dga=((4 * block, hidden_pad), BF16),
        dua=((4 * block, hidden_pad), BF16),
        dbr=((block, width), BF16),
        dgt=((block, width), BF16),
        dms=((block, width), BF16),
        dm=((length, HD), BF16),
        dgs=((8, block, 2 * HD), BF16),
        dmg=((8, block, 2 * HD), BF16),
        dq=((length, 512), BF16),
        ggain=((1, width), F32),
        gus=((2, 4, 256, hidden_pad), BF16),
        gpre=((2, 256, hidden_pad), BF16),
        gland=((2, 2, 256, hidden_pad), BF16),
        gxs=((8, 2, 32, hidden_pad), BF16),
        gxr=((8, 2, 32, hidden_pad), BF16),
        gds=((8, 96, width), BF16),
        dpre=((2, 96, width), BF16),
        dland=((2, 2, 96, width), BF16),
        dsum=((2, 96, width), BF16),
        dfar=((96, width), BF16),
        gwos=((4, 4, 2, 32, width), BF16),
        gwor=((4, 4, 32, width), BF16),
        opre=((2, 2, 32, width), BF16),
        oland=((2, 4, 32, width), BF16),
        gos=((4, 32, width), BF16),
        goz=((4, 32, width), BF16),
        gws=((4, 256, 512), BF16),
        wpre=((2, 128, 512), BF16),
        wland=((2, 256, 512), BF16),
        gas=((8, 32, 512), BF16),
        gar=((8, 32, 512), BF16),
        gts=((4, 2, block, width), BF16),
        gtr=((4, block, width), BF16),
        pgrad=((32, HD), F32),
        fin0=((48, 128), F32),
        fin1=((4, 48, 128), F32),
        fin2s=((48, 128), F32),
        fin2=((8, 16, 128), F32),
        pers=((32, 128), F32),
    )
    return table


def block_kernel(names, width, hidden, ndoc, *refs):
    (
        tok, wq, wk, wv, wo, wg, fgi, fui, fdi, tea, ret, pk, pv, gin, val, docs,
        out_o, gtok_o, gar_o, gwo_o, fin_o, pers_o, gux_o, fd_o,
    ) = refs[:24]
    m = types.SimpleNamespace(**dict(zip(names, refs[24 : 24 + len(names)])))
    sems = refs[24 + len(names) :]
    s = types.SimpleNamespace(**dict(zip(FLAGS, zip(sems[0::2], sems[1::2]))))
    pad = m.ffd.shape[0]
    length = m.x_all.shape[0]
    scale = HD ** (-0.5)
    mem_scale = 0.125 / HD

    a = lax.axis_index("head")
    b = lax.axis_index("seq")
    z = lax.div(b, 2)
    c = lax.rem(b, 2)
    sib = 2 * z + 1 - c
    near = z + 1 - 2 * lax.rem(z, 2)
    mirror = 3 - z
    across = 3 - near
    inner_chip = (z == 1) | (z == 2)
    inside = lax.div(lax.rem(z, 3) + 1, 2)
    order = (
        near + inside * (mirror - near),
        across + inside * (near - across),
        mirror + inside * (across - mirror),
    )
    part = lax.div(b, 4)
    mine = lax.rem(b, 4)
    partner = 2 * near + c
    far = b + 4 - 8 * part
    mate, pmate, cross = lax.rem(sib, 4), lax.rem(partner, 4), lax.rem(2 * near + 1 - c, 4)
    nx = a + 1 - 2 * lax.rem(a, 2)
    ny = lax.rem(a + 2, 4)
    diagonal = 3 - a

    def copy(src, dst, ssem, rsem, device):
        return pltpu.make_async_remote_copy(
            src_ref=src, dst_ref=dst, send_sem=ssem, recv_sem=rsem,
            device_id=device, device_id_type=MESH_IDS,
        )

    def sent(flag, total):
        copy(total, total, flag, flag, (a, sib)).wait_send()

    def landed_all(flag, total):
        copy(total, total, flag, flag, (a, sib)).wait_recv()

    def seq_peers(body):
        each(1, 8, lambda step: body(lax.rem(b + step, 8)))

    def xy_peers(body):
        each(1, 4, lambda step: body(lax.rem(a + step, 4)))

    def seq_start(pair, src, dst, peer):
        copy(src, dst, pair[0].at[0], pair[1].at[b], (a, peer)).start()

    def seq_wait(pair, dst, peer):
        landed_all(pair[1].at[peer], dst)

    def all_start(pair, src, dst, peer):
        copy(src, dst, pair[0].at[0], pair[1].at[0], (a, peer)).start()

    def xy_start(pair, src, dst, peer):
        copy(src, dst, pair[0].at[0], pair[1].at[a], (peer, b)).start()

    def xy_wait(pair, dst, peer):
        landed_all(pair[1].at[peer], dst)

    def xy_all_start(pair, src, dst, peer):
        copy(src, dst, pair[0].at[0], pair[1].at[0], (peer, b)).start()

    def all_wait(pair, total):
        landed_all(pair[1].at[0], total)

    finals = []

    def drain(pair, total):
        finals.append(lambda: sent(pair[0].at[0], total))

    def line_copy(pair, src, dst, zt):
        return copy(src, dst, pair[0].at[0], pair[1].at[z], (a, 2 * zt + c))

    def pass_copy(pair, src, dst, zs):
        return copy(src, dst, pair[0].at[1], pair[1].at[4 + zs], (a, sib))

    def line_start_far(pair, src, place, four, two):
        @pl.when(inner_chip)
        def _():
            line_copy(pair, src, place(z), mirror).start()

        @pl.when(jnp.logical_not(inner_chip))
        def _():
            line_copy(pair, src, place(z), across).start()

        def line_sent():
            @pl.when(inner_chip)
            def _():
                sent(pair[0].at[0], four)

            @pl.when(jnp.logical_not(inner_chip))
            def _():
                sent(pair[0].at[0], two)

        finals.append(line_sent)

    def line_start_near(pair, src, place):
        line_copy(pair, src, place(z), near).start()

    def line_wait(pair, place, zs):
        landed_all(pair[1].at[zs], place(zs))

    def line_hand_on(pair, place, zs):
        block = place(zs)

        @pl.when(inner_chip)
        def _():
            copy(block, block, pair[0].at[0], pair[1].at[zs], (a, 2 * near + c)).start()

    def gather_line(pair, view, zs):
        block = view(2 * zs + c)
        line_wait(pair, lambda _: block, zs)
        pass_copy(pair, block, block, zs).start()

    def gather_pass(pair, view, zs):
        landed_all(pair[1].at[4 + zs], view(2 * zs + 1 - c))

    def quad_start(pair, view, first, second):
        block = view(a)
        copy(block, block, pair[0].at[0], pair[1].at[0], (first, b)).start()
        copy(block, block, pair[0].at[0], pair[1].at[1], (second, b)).start()

    def quad_pass(pair, view, first, second):
        block = view(first)
        landed_all(pair[1].at[0], block)
        copy(block, block, pair[0].at[0], pair[1].at[1], (second, b)).start()

    def fold_start(pair, view, pre, land, first):
        copy(view(diagonal), pre, pair[0].at[0], pair[1].at[0], (first, b)).start()
        copy(view(first), land.at[0], pair[0].at[0], pair[1].at[1], (first, b)).start()

    def fold_pass(pair, view, pre, land, add, second):
        landed_all(pair[1].at[0], pre)
        add(second)
        copy(view(second), land.at[1], pair[0].at[0], pair[1].at[1], (second, b)).start()

    def fold_finish(pair, land, three):
        landed_all(pair[1].at[1], land)
        drain(pair, three)

    barrier = pltpu.get_barrier_semaphore()
    seq_peers(lambda p: pl.semaphore_signal(barrier, 1, device_id=(a, p), device_id_type=MESH_IDS))
    xy_peers(lambda p: pl.semaphore_signal(barrier, 1, device_id=(p, b), device_id_type=MESH_IDS))

    for head in range(8):
        for place, weight in enumerate((wq, wk, wv, wg)):
            m.wcs[head, :, place * 128 : place * 128 + 128] = weight[
                :, head * 128 : head * 128 + 128
            ]
    own_rows = block_rows(b, 128)
    piece = pl.ds(pl.multiple_of(a * 256 + b * 32, 32), 32)
    m.x_all[own_rows, :] = tok[...]
    m.wqk[piece, :] = m.wcs[b]
    m.wo_all[a, z, c] = wo[...]
    down = fdi[...].astype(F32)
    m.fdp[2 * a + part] = jnp.concatenate(
        [down, jnp.zeros((96 - down.shape[0], width), F32)], axis=0
    ).astype(BF16)
    slot32 = block_rows(b, 32)
    row_id = lax.broadcasted_iota(jnp.int32, (128, 128), 0)
    col_id = lax.broadcasted_iota(jnp.int32, (128, 128), 1)
    place = (
        lax.broadcasted_iota(jnp.int32, (32, 128), 1)
        == lax.broadcasted_iota(jnp.int32, (32, 128), 0) + 32 * lax.rem(b, 4)
    ).astype(BF16)
    m.pin[0:16, :] = nn(pk[...], place).astype(BF16)
    m.pin[16:32, :] = nn(pv[...], place).astype(BF16)
    counted_row = val[...].astype(F32)
    m.vcol[...] = jnp.sum(jnp.where(row_id == col_id, counted_row, 0.0), axis=1, keepdims=True)
    gain_row = nn(gin[...], place)
    m.tile[...] = jnp.zeros_like(m.tile)
    for group in range(4):
        m.tile[group, 0:2, :] = jnp.log(ret[group])
        m.tile[group, 2:3, :] = counted_row
        m.tile[group, 3:4, :] = gain_row
    m.t1[a] = m.tile[a]
    m.p1[a] = m.pin[...]
    pl.semaphore_wait(barrier, 10)

    xy_peers(lambda p: xy_all_start(s.t1, m.tile.at[p], m.t1.at[a], p))
    xy_peers(lambda p: xy_all_start(s.p1, m.pin, m.p1.at[a], p))
    seq_peers(lambda p: all_start(s.w1, m.wcs.at[p], m.wqk.at[piece, :], p))
    all_wait(s.t1, m.t1.at[pl.ds(0, 3)])
    all_wait(s.p1, m.p1.at[pl.ds(0, 3)])
    for group in range(4):
        m.t2s[2 * group : 2 * group + 2, :] = m.t1[group, 0:2, :]
        m.t2s[8 + group : 9 + group, :] = m.t1[group, 3:4, :]
    m.t2s[12:13, :] = (m.t1[0, 2:3, :] + m.t1[1, 2:3, :]) + (m.t1[2, 2:3, :] + m.t1[3, 2:3, :])
    m.t2s[13:16, :] = jnp.zeros((3, 128), F32)
    m.t2[b] = m.t2s[...]
    m.p2[b] = m.p1[lax.div(b, 2)]
    seq_peers(lambda p: all_start(s.t2, m.t2s, m.t2.at[b], p))
    half = 4 * c

    def persist_send(p):
        @pl.when(lax.rem(p, 2) == lax.div(b, 4))
        def _():
            all_start(s.p2, m.p1.at[lax.div(p, 2)], m.p2.at[b], p)

    def persist_wait():
        pl.when(part == c)(lambda: all_wait(s.p2, m.p2.at[pl.ds(0, 3)]))
        pl.when(part != c)(lambda: all_wait(s.p2, m.p2.at[pl.ds(0, 4)]))

    def persist_drain():
        pl.when(part == c)(lambda: sent(s.p2[0].at[0], m.p2.at[pl.ds(0, 3)]))
        pl.when(part != c)(lambda: sent(s.p2[0].at[0], m.p2.at[pl.ds(0, 4)]))

    seq_peers(persist_send)
    finals.append(persist_drain)
    drain(s.t2, m.t2.at[pl.ds(0, 7)])

    drain(s.t1, m.t1.at[pl.ds(0, 3)])
    drain(s.p1, m.p1.at[pl.ds(0, 3)])
    drain(s.w1, m.wcs.at[pl.ds(0, 7)])
    x_view = lambda i: m.x_all.at[block_rows(i, 128), :]
    x_place = lambda zs: x_view(2 * zs + c)
    wo_place = lambda zs: m.wo_all.at[a, zs, c]
    line_start_near(s.wo, wo, wo_place)
    line_start_far(s.wo, wo, wo_place, m.wo_all.at[0, :, 0], m.wo_all.at[0, pl.ds(0, 2), 0])
    line_start_far(
        s.x, tok, x_place, m.x_all.at[pl.ds(0, 512), :], m.x_all.at[pl.ds(0, 256), :]
    )
    line_start_near(s.x, tok, x_place)
    pass_copy(s.x, tok, x_view(b), z).start()
    finals.append(lambda: sent(s.x[0].at[1], m.x_all.at[pl.ds(0, 512), :]))
    down_x = lambda i: m.fdp.at[2 * i]
    down_y = lambda i: m.fdp.at[2 * i + 1]

    run = hidden // 8
    for place, weight in enumerate((fgi, fui)):
        for group in range(4):
            m.fs[group, place, :, hidden:pad] = jnp.zeros((32, pad - hidden), BF16)
            for i in range(8):
                start = run * (4 * i + group)
                m.fs[group, place, :, run * i : run * i + run] = weight[:, start : start + run]
    m.fgu[:, a, slot32, :] = m.fs[mine]

    def column_start(pair, place, p):
        seq_start(pair, m.fs.at[lax.rem(p, 4), place], m.fgu.at[place, a, slot32, :], p)

    def columns(pair, place):
        seq_peers(lambda p: column_start(pair, place, p))

    def columns_far(pair, place):
        def one(p):
            @pl.when(lax.div(p, 2) != near)
            def _():
                column_start(pair, place, p)

        seq_peers(one)

    def columns_near(pair, place):
        column_start(pair, place, 2 * near)
        column_start(pair, place, 2 * near + 1)

    drain(s.fxg, m.gxr.at[pl.ds(0, 7), 0])
    drain(s.fxu, m.gxr.at[pl.ds(0, 7), 1])
    own_down = m.fdp.at[2 * a + part]
    far_down = m.fdp.at[2 * a + 1 - part]
    down_copy = copy(own_down, own_down, s.fd[0].at[0], s.fd[1].at[0], (a, far))
    finals.append(down_copy.wait_send)

    @pl.when(jnp.logical_not(inner_chip))
    def _():
        columns(s.fxg, 0)


    all_wait(s.w1, m.wqk.at[pl.ds(0, 224), :])
    quarter = lambda i: m.wqk.at[block_rows(i, 256), :]
    xy_peers(lambda p: xy_all_start(s.w2, quarter(a), quarter(a), p))
    drain(s.w2, m.wqk.at[pl.ds(0, 768), :])

    def piece_view(place, p):
        return lambda i: m.fgu.at[place, i, block_rows(p, 32), :]

    ways = ((nx, ny), (ny, nx))

    def pieces_on(peers, pair, quad_pair, place):
        for p in peers:
            seq_wait(pair, piece_view(place, p)(a), p)
            quad_start(quad_pair, piece_view(place, p), *ways[place])

    quad_start(s.fgx, piece_view(0, b), nx, ny)
    quad_start(s.fux, piece_view(1, b), ny, nx)

    @pl.when(part == 0)
    def _():
        quad_start(s.fdx, down_x, nx, ny)

    @pl.when(part == 1)
    def _():
        quad_start(s.fdy, down_y, ny, nx)


    def project(i):
        rows = block_rows(i, 128)
        wide = nn(m.x_all[rows, :], m.wqk[...])
        m.q[rows, :] = wide[:, 0:128].astype(BF16)
        m.k[rows, :] = wide[:, 128:256].astype(BF16)
        m.v[rows, :] = wide[:, 256:384].astype(BF16)
        m.mgs[rows, 128:256] = wide[:, 384:512].astype(BF16)

    head_cols = pl.ds(pl.multiple_of(b * 128, 128), 128)

    @pl.when(inner_chip)
    def _():
        line_wait(s.wo, wo_place, mirror)
        line_hand_on(s.wo, wo_place, mirror)
        line_wait(s.wo, wo_place, across)
        line_hand_on(s.wo, wo_place, across)

    gather_line(s.x, x_view, order[0])
    line_hand_on(s.x, x_place, mirror)
    @pl.when(inner_chip)
    def _():
        columns_far(s.fxg, 0)

    all_wait(s.w2, m.wqk.at[pl.ds(0, 768), :])
    project(b)
    gather_pass(s.x, x_view, z)
    project(sib)
    project(2 * order[0] + c)
    line_wait(s.wo, wo_place, near)

    @pl.when(jnp.logical_not(inner_chip))
    def _():
        line_wait(s.wo, wo_place, across)
        line_wait(s.wo, wo_place, mirror)

    wo_half = lambda i: m.wo_all.at[i, :, c]
    xy_peers(lambda p: xy_start(s.wox, wo_half(a), wo_half(a), p))
    drain(s.wox, m.wo_all.at[pl.ds(0, 3), :, 0])
    wo_pass = lambda i, block: copy(
        block, block, s.wo[0].at[1], s.wo[1].at[4], (a, sib)
    )
    wo_pass(a, wo_half(a)).start()
    finals.append(lambda: sent(s.wo[0].at[1], m.wo_all.at[:, :, 0]))
    chips = tuple(2 * zs + core for zs in order for core in range(2))

    gather_line(s.x, x_view, order[1])
    gather_line(s.x, x_view, order[2])
    line_hand_on(s.x, x_place, across)

    @pl.when(inner_chip)
    def _():
        columns_near(s.fxg, 0)

    columns(s.fxu, 1)

    project(2 * order[1] + c)
    project(2 * order[2] + c)

    def arrived_pass(zs):
        gather_pass(s.x, x_view, zs)
        project(2 * zs + 1 - c)

    for zs in order:
        arrived_pass(zs)
    all_wait(s.t2, m.t2.at[pl.ds(0, 7)])
    persist_wait()
    small = m.t2[...]
    place16 = lax.broadcasted_iota(jnp.int32, (8, 16, 128), 1)
    rates = jnp.sum(jnp.where(place16 == b, small, 0.0), axis=1)
    valid_total = jnp.sum(jnp.where(place16 == 12, small, 0.0))
    for group in range(8):
        line = 8 + group // 2
        first = 4 * (group % 2)
        m.gain[:, group * 128 : group * 128 + 128] = (
            m.t2[first, line : line + 1, :] + m.t2[first + 1, line : line + 1, :]
        ) + (m.t2[first + 2, line : line + 1, :] + m.t2[first + 3, line : line + 1, :])
    m.fkv[...] = (
        (m.p2[half].astype(F32) + m.p2[half + 1].astype(F32))
        + (m.p2[half + 2].astype(F32) + m.p2[half + 3].astype(F32))
    ).astype(BF16)
    lower = (col_id <= row_id).astype(F32)
    within = nt_exact(rates, lower)
    earlier = (
        lax.broadcasted_iota(jnp.int32, (8, 8), 1) < lax.broadcasted_iota(jnp.int32, (8, 8), 0)
    ).astype(F32)
    base = nn_exact(earlier, jnp.broadcast_to(jnp.sum(rates, axis=1, keepdims=True), (8, 128)))
    running = within + base
    for i in range(8):
        m.rrow[:, i * 128 : i * 128 + 128] = running[i : i + 1, :]
    eye = (col_id == row_id).astype(F32)
    m.rcol[...] = nt_exact(eye, running)

    local_pos = lax.broadcasted_iota(jnp.int32, (128, 1), 0)
    lane8 = lax.broadcasted_iota(jnp.int32, (128, 8), 1)

    m.probs[...] = jnp.zeros_like(m.probs)
    m.both[...] = jnp.zeros_like(m.both)

    def by_extent(i, body):
        for j in range(4):
            pl.when(lax.div(i, 2) == j)(lambda j=j: body(i, 256 * (j + 1)))

    def attend_keys(i, extent):
        rows = block_rows(i, 128)
        keys = slice(0, extent)
        query = m.q[rows, :]
        raw = nt(query, m.k[keys, :])
        pos = i * 128 + local_pos
        begin = jnp.zeros_like(pos)
        for j in range(ndoc):
            start = docs[a, j]
            begin = jnp.where(start <= pos, jnp.maximum(begin, start), begin)
        key_pos = lax.broadcasted_iota(jnp.int32, (128, extent), 1)
        allowed = (key_pos <= pos) & (key_pos >= begin)
        scores = jnp.where(allowed, raw * scale, MASKED)
        fixed = nt(query, m.fkv[0:16, :]) * scale
        top = jnp.maximum(
            jnp.max(scores, axis=1, keepdims=True), jnp.max(fixed, axis=1, keepdims=True)
        )
        weight = jnp.exp(scores - top)
        fixed_weight = jnp.exp(fixed - top)
        share = 1.0 / (
            jnp.sum(weight, axis=1, keepdims=True) + jnp.sum(fixed_weight, axis=1, keepdims=True)
        )
        prob = weight * share
        fixed_prob = (fixed_weight * share).astype(BF16)
        reach = jnp.sum(jnp.where(lane8 == i, m.rcol[...], 0.0), axis=1, keepdims=True)
        kept = jnp.where(
            allowed, jnp.exp(jnp.minimum(reach - m.rrow[:, keys], 0.0)) * mem_scale, 0.0
        )
        joint = (prob + kept * raw).astype(BF16)
        m.probs[rows, keys] = prob.astype(BF16)
        m.decay[rows, keys] = kept.astype(BF16)
        m.both[rows, keys] = joint
        m.fprobs[rows, :] = fixed_prob
        mixed = nn(joint, m.v[keys, :]) + nn(fixed_prob, m.fkv[16:32, :])
        m.mgs[rows, 0:128] = mixed.astype(BF16)

    attend = lambda i: by_extent(i, attend_keys)

    pieces_on((sib,) + chips[0:2], s.fxg, s.fgx, 0)

    def attend_step(step):
        i = lax.rem(b + step, 8)
        attend(i)

        @pl.when(step < 8)
        def _():
            all_start(s.mx, m.mgs.at[block_rows(i, 128), :], m.mg.at[b], i)

        @pl.when(step == 3)
        def _():
            pieces_on(chips[2:6], s.fxg, s.fgx, 0)
            pieces_on((sib,) + chips[0:2], s.fxu, s.fux, 1)

    each(1, 9, attend_step)
    drain(s.mx, m.mgs.at[pl.ds(0, 896), :])
    m.mg[b] = m.mgs[own_rows, :]
    down_copy.start()
    quad_pass(s.fgx, lambda i: m.fgu.at[0, i], nx, ny)
    pieces_on(chips[2:6], s.fxu, s.fux, 1)
    copy(far_down, far_down, s.fd[0].at[0], s.fd[1].at[0], (a, far)).wait_recv()

    @pl.when(part == 1)
    def _():
        quad_start(s.fdx, down_x, nx, ny)

    @pl.when(part == 0)
    def _():
        quad_start(s.fdy, down_y, ny, nx)


    def wo_arrived(p):
        xy_wait(s.wox, wo_half(p), p)
        wo_pass(p, wo_half(p)).start()

    xy_peers(wo_arrived)
    landed_all(s.wo[1].at[4], m.wo_all.at[:, :, 1 - c])
    quad_pass(s.fux, lambda i: m.fgu.at[1, i], ny, nx)
    all_wait(s.mx, m.mg.at[pl.ds(0, 7)])
    for head in range(8):
        m.mx[:, head * 128 : head * 128 + 128] = m.mg[head, :, 0:128]
        m.gp[:, head * 128 : head * 128 + 128] = m.mg[head, :, 128:256]

    out_w = lambda: m.wo_all[...].reshape(width, width)
    m.br[...] = nn(m.mx[...], out_w())

    half_row = lambda i: pl.ds(
        pl.multiple_of((4 * lax.div(i, 2) + mine) * 64 + lax.rem(i, 2) * 32, 32), 32
    )
    quad = lambda ref, h, i: ref.at[block_rows(4 * h + i, 64), :]

    def half_copy(pair, src, dst, h, slot, peer):
        return copy(src, dst, pair[0].at[h], pair[1].at[2 * h + slot], (a, peer))

    def half_gather(pair, ref, h):
        block = quad(ref, h, mine)
        half_copy(pair, block, block, h, 0, partner).start()
        half_copy(pair, block, block, h, 1, sib).start()

    def half_wait(pair, ref, h):
        block = quad(ref, h, pmate)
        landed_all(pair[1].at[2 * h], block)
        half_copy(pair, block, block, h, 1, sib).start()
        landed_all(pair[1].at[2 * h + 1], ref.at[pl.ds(0, 128), :])
        finals.append(lambda: sent(pair[0].at[h], ref.at[pl.ds(0, 192), :]))

    def half_scatter(pair, value, h):
        for i in range(4):
            m.ysend[i, h * 64 : h * 64 + 64, :] = value[i * 64 : i * 64 + 64, :].astype(BF16)
        rows = pl.ds(h * 64, 64)
        half_copy(pair, m.ysend.at[cross, rows, :], m.yrecv.at[1, rows, :], h, 1, sib).start()
        half_copy(pair, m.ysend.at[mate, rows, :], m.yrecv.at[0, rows, :], h, 0, sib).start()

    def half_on(pair, h):
        rows = pl.ds(h * 64, 64)
        landed_all(pair[1].at[2 * h + 1], m.yrecv.at[1, rows, :])
        m.ysend[pmate, rows, :] = (
            m.ysend[pmate, rows, :].astype(F32) + m.yrecv[1, rows, :].astype(F32)
        ).astype(BF16)
        half_copy(
            pair, m.ysend.at[pmate, rows, :], m.yrecv.at[2, rows, :], h, 0, partner
        ).start()

    def half_sent(pair, h):
        sent(pair[0].at[h], m.ysend.at[pl.ds(0, 3), pl.ds(h * 64, 64), :])

    def half_land(pair, h):
        landed_all(pair[1].at[2 * h], m.yrecv.at[pl.ds(0, 2), pl.ds(h * 64, 64), :])

    def normalise(i):
        rows = block_rows(i, 32)
        opened = jax.nn.sigmoid(m.gp[rows, :].astype(F32))
        hidden_rows = tok[rows, :].astype(F32) + opened * m.br[rows, :]
        inv = lax.rsqrt(jnp.mean(hidden_rows * hidden_rows, axis=1, keepdims=True) + EPSILON)
        m.hid[rows, :] = hidden_rows
        m.inv[rows, :] = jnp.broadcast_to(inv, (32, 128))
        m.sc[half_row(i), :] = (
            hidden_rows * inv * m.gain[...]
        ).astype(BF16)

    each(0, 2, normalise)
    half_gather(s.sc, m.sc, 0)
    each(2, 4, normalise)
    half_gather(s.sc, m.sc, 1)

    quad_pass(s.fdx, down_x, nx, ny)
    quad_pass(s.fdy, down_y, ny, nx)
    landed_all(s.fgx[1].at[1], m.fgu.at[0, pl.ds(0, 2)])
    landed_all(s.fux[1].at[1], m.fgu.at[1, pl.ds(0, 2)])
    drain(s.fgx, m.fgu.at[0, pl.ds(0, 3)])
    drain(s.fux, m.fgu.at[1, pl.ds(0, 3)])
    drain(s.fdx, m.fdp.at[pl.ds(0, 3)])
    drain(s.fdy, m.fdp.at[pl.ds(0, 3)])
    half_wait(s.sc, m.sc, 0)

    gate_w = lambda: m.fgu[0].reshape(width, pad)
    up_w = lambda: m.fgu[1].reshape(width, pad)

    def feed(i):
        rows = block_rows(i, 256)
        scaled = m.sc[rows, :]
        gate_act = nn(scaled, gate_w())
        up_act = nn(scaled, up_w())
        m.gact[rows, :] = gate_act
        m.uact[rows, :] = up_act
        m.inner[rows, :] = (gate_act * jax.nn.sigmoid(gate_act) * up_act).astype(BF16)

    feed(0)
    landed_all(s.fdx[1].at[1], m.fdp.at[pl.ds(0, 2)])
    landed_all(s.fdy[1].at[1], m.fdp.at[pl.ds(0, 2)])
    share_rows = m.fdp.shape[1] - 8
    for i in range(4):
        m.ffd[2 * i * share_rows : 2 * (i + 1) * share_rows, :] = jnp.concatenate(
            [m.fdp[2 * i + j, 0:share_rows, :].astype(F32) for j in range(2)], axis=0
        ).astype(BF16)
    m.ffd[hidden:pad, :] = jnp.zeros((pad - hidden, width), BF16)

    def feed_out(h):
        half_scatter(s.y, nn(m.inner[block_rows(h, 256), :], m.ffd[...]), h)
        m.own[block_rows(h, 64), :] = nn(m.inner[block_rows(4 * h + mine, 64), :], m.ffd[...])
        half_on(s.y, h)

    feed_out(0)
    half_wait(s.sc, m.sc, 1)
    feed(1)
    feed_out(1)
    half_land(s.y, 0)

    token_total = float(4 * length)
    m.fin0[...] = jnp.zeros_like(m.fin0)

    def finish(i):
        rows = block_rows(i, 32)
        final = m.hid[rows, :] + m.own[rows, :]
        final = final + m.yrecv[0, rows, :].astype(F32) + m.yrecv[2, rows, :].astype(F32)
        out_o[rows, :] = final.astype(BF16)
        error = final - tea[rows, :].astype(F32)
        counted = m.vcol[rows, :] * error
        grad = counted * (token_total / valid_total)
        m.dout[rows, :] = grad
        m.df[half_row(i), :] = grad.astype(BF16)
        squares = jnp.sum(counted * error, axis=0, keepdims=True)
        lanes = squares[:, 0:128]
        for j in range(1, width // 128):
            lanes = lanes + squares[:, j * 128 : j * 128 + 128]
        m.fin0[40:41, :] += lanes

    each(0, 2, finish)
    half_gather(s.df, m.df, 0)
    half_land(s.y, 1)
    each(2, 4, finish)
    half_gather(s.df, m.df, 1)
    half_wait(s.df, m.df, 0)

    def feed_back(i):
        rows = block_rows(i, 256)
        d_inner = nt(m.df[rows, :], m.ffd[...])
        gate_act = m.gact[rows, :]
        opened = jax.nn.sigmoid(gate_act)
        m.dga[rows, :] = (
            d_inner * m.uact[rows, :] * opened * (1.0 + gate_act * (1.0 - opened))
        ).astype(BF16)
        m.dua[rows, :] = (d_inner * gate_act * opened).astype(BF16)

    feed_back(0)

    def feed_in(h):
        rows = block_rows(h, 256)
        half_sent(s.y, h)
        half_scatter(s.ds, nt(m.dga[rows, :], gate_w()) + nt(m.dua[rows, :], up_w()), h)
        rows = block_rows(4 * h + mine, 64)
        m.own[block_rows(h, 64), :] = nt(m.dga[rows, :], gate_w()) + nt(m.dua[rows, :], up_w())
        half_on(s.ds, h)

    feed_in(0)
    half_wait(s.df, m.df, 1)
    feed_back(1)
    feed_in(1)
    finals.append(lambda: (half_sent(s.ds, 0), half_sent(s.ds, 1)))

    def share_copy(pair, share, landing, zt):
        return copy(share, landing.at[z], pair[0].at[0], pair[1].at[0], (a, 2 * zt + c))

    def sum_near(pair, share, landing):
        share_copy(pair, share(near), landing, near).start()

    def sum_far(pair, share, landing, zt, slot, flag):
        copy(
            share(zt), landing.at[slot], pair[0].at[0], pair[1].at[flag], (a, 2 * near + c)
        ).start()

    def sum_start(pair, share, landing):
        @pl.when(jnp.logical_not(inner_chip))
        def _():
            sum_far(pair, share, landing, across, mirror, 1)
            sum_far(pair, share, landing, mirror, near, 2)

        sum_near(pair, share, landing)

    def sum_pass(pair, share, landing, add):
        @pl.when(inner_chip)
        def _():
            for zt, slot, flag in ((mirror, across, 1), (across, z, 2)):
                landed_all(pair[1].at[flag], landing.at[slot])
                add(zt, slot)
                share_copy(pair, share(zt), landing, zt).start()

    second = across + inside * (mirror - across)

    def sum_finish(pair, landing, three):
        landed_all(pair[1].at[0], landing.at[pl.ds(0, 2)])
        drain(pair, three)

    def landed(landing, where):
        return landing[(near,) + where].astype(F32) + landing[(second,) + where].astype(F32)

    def fold_add(view, pre, chunk):
        def add(second):
            rows = view(second).shape[0]

            def one(i):
                part_rows = pl.ds(pl.multiple_of(i * chunk, chunk), chunk)
                target = view(second)
                target[part_rows] = (
                    target[part_rows].astype(F32) + pre[part_rows].astype(F32)
                ).astype(BF16)

            each(0, rows // chunk, one)

        return add

    gate_share = lambda i: m.gus.at[0, i]
    up_share = lambda i: m.gus.at[1, i]

    def one_grad(i, place, grads):
        cols = pl.ds(pl.multiple_of(i * 256, 256), 256)
        m.gus[place, i] = tn(m.sc[:, cols], grads[...]).astype(BF16)

    one_grad(diagonal, 0, m.dga)
    one_grad(ny, 0, m.dga)
    fold_start(s.rg, gate_share, m.gpre.at[0], m.gland.at[0], ny)
    one_grad(diagonal, 1, m.dua)
    one_grad(nx, 1, m.dua)
    fold_start(s.ru, up_share, m.gpre.at[1], m.gland.at[1], nx)

    half_land(s.ds, 0)
    m.ggain[...] = jnp.zeros_like(m.ggain)

    def norm_back(i):
        rows = block_rows(i, 32)
        d_scaled = m.own[rows, :] + m.yrecv[0, rows, :].astype(F32)
        d_scaled = d_scaled + m.yrecv[2, rows, :].astype(F32)
        inv = m.inv[rows, 0:1]
        normed = m.hid[rows, :] * inv
        m.ggain[...] += jnp.sum(d_scaled * normed, axis=0, keepdims=True)
        d_normed = d_scaled * m.gain[...]
        lean = jnp.mean(d_normed * normed, axis=1, keepdims=True)
        d_hidden = m.dout[rows, :] + inv * (d_normed - normed * lean)
        m.dout[rows, :] = d_hidden
        opened = jax.nn.sigmoid(m.gp[rows, :].astype(F32))
        m.dbr[rows, :] = (d_hidden * opened).astype(BF16)
        m.dgt[rows, :] = (d_hidden * m.br[rows, :] * opened * (1.0 - opened)).astype(BF16)

    each(0, 2, norm_back)
    half_land(s.ds, 1)
    each(2, 4, norm_back)
    gate_cols = pl.ds(384, 128)
    cols_of = lambda i: pl.ds(pl.multiple_of(i * 128, 128), 128)
    m.dms[...] = nt(m.dbr[...], out_w()).astype(BF16)
    for head in range(8):
        cols = slice(head * 128, head * 128 + 128)
        m.dgs[head, :, 0:128] = m.dms[:, cols]
        m.dgs[head, :, 128:256] = m.dgt[:, cols]
    seq_peers(lambda p: seq_start(s.dm, m.dgs.at[p], m.dmg.at[b], p))
    drain(s.dm, m.dgs.at[pl.ds(0, 7)])
    m.dmg[b] = m.dgs[b]

    one_grad(nx, 0, m.dga)
    fold_pass(
        s.rg, gate_share, m.gpre.at[0], m.gland.at[0], fold_add(gate_share, m.gpre.at[0], 32), nx
    )
    one_grad(ny, 1, m.dua)
    fold_pass(
        s.ru, up_share, m.gpre.at[1], m.gland.at[1], fold_add(up_share, m.gpre.at[1], 32), ny
    )
    one_grad(a, 0, m.dga)
    one_grad(a, 1, m.dua)

    def down_grad(i):
        cols = pl.ds(pl.multiple_of(i * 256, 256), 256)
        m.ffd[block_rows(i, 256), :] = tn(m.inner[:, cols], m.df[...]).astype(BF16)

    each(0, pad // 256, down_grad)
    for i in range(4):
        double = m.ffd[2 * i * share_rows : 2 * (i + 1) * share_rows, :].astype(F32)
        for j in range(2):
            m.gds[2 * i + j] = jnp.concatenate(
                [double[j * share_rows : (j + 1) * share_rows, :], jnp.zeros((8, width), F32)],
                axis=0,
            ).astype(BF16)
    down_x_share = lambda i: m.gds.at[2 * i]
    down_y_share = lambda i: m.gds.at[2 * i + 1]
    fold_start(s.rdx, down_x_share, m.dpre.at[0], m.dland.at[0], ny)
    fold_start(s.rdy, down_y_share, m.dpre.at[1], m.dland.at[1], nx)

    def out_grad(i):
        cols = pl.ds(pl.multiple_of(i * 256, 256), 256)
        m.gwos[i] = tn(m.mx[:, cols], m.dbr[...]).astype(BF16).reshape(4, 2, 32, width)

    each(0, 4, out_grad)
    gos_copy = copy(m.gwos.at[:, :, 1 - c], m.gwor, s.gos[0].at[0], s.gos[1].at[0], (a, sib))
    gos_copy.start()
    finals.append(gos_copy.wait_send)
    m.pgrad[...] = jnp.zeros_like(m.pgrad)

    def attend_back_keys(i, extent):
        rows = block_rows(i, 128)
        keys = slice(0, extent)
        d_mixed = m.dmg[i, :, 0:128]
        m.dm[rows, :] = d_mixed
        m.dq[rows, gate_cols] = m.dmg[i, :, 128:256]
        d_joint = nt(d_mixed, m.v[keys, :])
        prob = m.probs[rows, keys].astype(F32)
        turned = prob * d_joint
        fixed_prob = m.fprobs[rows, :]
        fixed_full = fixed_prob.astype(F32)
        fixed_turned = fixed_full * nt(d_mixed, m.fkv[16:32, :])
        delta = jnp.sum(turned, axis=1, keepdims=True) + jnp.sum(
            fixed_turned, axis=1, keepdims=True
        )
        d_raw = (
            scale * (turned - prob * delta) + m.decay[rows, keys].astype(F32) * d_joint
        ).astype(BF16)
        m.probs[rows, keys] = d_raw
        d_fixed = (fixed_turned - fixed_full * delta).astype(BF16)
        m.dq[rows, 0:128] = (
            nn(d_raw, m.k[keys, :]) + scale * nn(d_fixed, m.fkv[0:16, :])
        ).astype(BF16)
        m.pgrad[0:16, :] += scale * tn(d_fixed, m.q[rows, :])
        m.pgrad[16:32, :] += tn(fixed_prob, d_mixed)

    attend_back = lambda i: by_extent(i, attend_back_keys)

    def owner_all(fold, pair, share, place):
        landed_all(fold[1].at[1], m.gland.at[place])

        def owner_rows(p):
            rows = block_rows(p, 32)
            total = m.gus[place, a, rows, :].astype(F32) + m.gland[place, 0, rows, :].astype(F32)
            m.gxs[p, place] = (total + m.gland[place, 1, rows, :].astype(F32)).astype(BF16)

        def owner_send(p):
            owner_rows(p)
            all_start(pair, m.gxs.at[p, place], m.gxr.at[b, place], p)

        seq_peers(owner_send)
        owner_rows(b)
        m.gxr[b, place] = m.gxs[b, place]

    def attend_back_step(step):
        i = lax.rem(b + step, 8)

        @pl.when(step > 0)
        def _():
            seq_wait(s.dm, m.dmg.at[i], i)

        @pl.when(step == 6)
        def _():
            owner_all(s.rg, s.gxg, gate_share, 0)

        attend_back(i)

    each(0, 8, attend_back_step)
    for place, (fold, pair) in enumerate(((s.rg, s.gxg), (s.ru, s.gxu))):
        drain(fold, m.gus.at[place, pl.ds(0, 3)])
        drain(pair, m.gxs.at[pl.ds(0, 7), place])
    fold_pass(
        s.rdx, down_x_share, m.dpre.at[0], m.dland.at[0],
        fold_add(down_x_share, m.dpre.at[0], 32), nx,
    )
    fold_pass(
        s.rdy, down_y_share, m.dpre.at[1], m.dland.at[1],
        fold_add(down_y_share, m.dpre.at[1], 32), ny,
    )
    owner_all(s.ru, s.gxu, up_share, 1)

    m.fin0[0:32, :] = m.pgrad[...]
    for j in range(8):
        m.fin0[32 + j : 33 + j, :] = m.ggain[:, j * 128 : j * 128 + 128]
    m.fin1[a] = m.fin0[...]
    xy_peers(lambda p: xy_all_start(s.fin1, m.fin0, m.fin1.at[a], p))
    drain(s.fin1, m.fin1.at[pl.ds(0, 3)])

    query_turned = jnp.transpose(m.q[...].astype(F32)).astype(BF16)
    mixed_turned = jnp.transpose(m.dm[...].astype(F32)).astype(BF16)

    def key_value_grad(i):
        cols = cols_of(i)
        rows = block_rows(i, 128)
        m.dq[rows, 128:256] = jnp.transpose(nn(query_turned, m.probs[:, cols])).astype(BF16)
        m.dq[rows, 256:384] = jnp.transpose(nn(mixed_turned, m.both[:, cols])).astype(BF16)

    each(0, 8, key_value_grad)

    def head_weight_grad(i):
        cols = pl.ds(pl.multiple_of(i * 256, 256), 256)
        m.gws[i] = tn(m.x_all[:, cols], m.dq[...]).astype(BF16)

    each(0, 4, head_weight_grad)
    weight_x = lambda i: m.gws.at[i, pl.ds(0, 128), :]
    weight_y = lambda i: m.gws.at[i, pl.ds(128, 128), :]
    land_x = m.wland.at[:, pl.ds(0, 128), :]
    land_y = m.wland.at[:, pl.ds(128, 128), :]
    fold_start(s.rwx, weight_x, m.wpre.at[0], land_x, ny)
    fold_start(s.rwy, weight_y, m.wpre.at[1], land_y, nx)

    def token_grad(i):
        return nt(m.dq[block_rows(i, 128), :], m.wqk[...])

    def token_sib(zt):
        m.gts[zt, 1 - c] = token_grad(2 * zt + 1 - c).astype(BF16)
        copy(
            m.gts.at[zt, 1 - c], m.gtr.at[zt], s.gt[0].at[1], s.gt[1].at[4 + zt],
            (a, sib),
        ).start()

    for zt in (near + (1 - inside) * (across - near), mirror, across + (1 - inside) * (near - across), z):
        token_sib(zt)

    fold_finish(s.rdx, m.dland.at[0], m.gds.at[pl.ds(0, 3)])
    fold_finish(s.rdy, m.dland.at[1], m.gds.at[pl.ds(0, 3)])

    def down_sum(j):
        total = m.gds[2 * a + j].astype(F32) + m.dland[j, 0].astype(F32)
        return total + m.dland[j, 1].astype(F32)

    m.dsum[0] = down_sum(1 - part).astype(BF16)
    far_copy = copy(m.dsum.at[0], m.dfar, s.gfd[0].at[0], s.gfd[1].at[0], (a, far))
    far_copy.start()
    finals.append(far_copy.wait_send)

    token_share = lambda zt: m.gts.at[zt, c]

    def token_line(zt):
        mine = token_grad(2 * zt + c)
        copy(
            m.gtr.at[zt], m.gtr.at[zt], s.gt[0].at[1], s.gt[1].at[4 + zt], (a, sib)
        ).wait_recv()
        m.gts[zt, c] = (mine + m.gtr[zt].astype(F32)).astype(BF16)

    def pass_token(zt, slot):
        m.gts[zt, c] = (m.gts[zt, c].astype(F32) + m.yrecv[slot].astype(F32)).astype(BF16)

    token_line(near + (1 - inside) * (across - near))

    @pl.when(inner_chip)
    def _():
        sum_near(s.gt, token_share, m.yrecv)

    @pl.when(jnp.logical_not(inner_chip))
    def _():
        sum_far(s.gt, token_share, m.yrecv, across, mirror, 1)

    token_line(mirror)

    @pl.when(jnp.logical_not(inner_chip))
    def _():
        sum_far(s.gt, token_share, m.yrecv, mirror, near, 2)

    token_line(across + (1 - inside) * (near - across))

    @pl.when(jnp.logical_not(inner_chip))
    def _():
        sum_near(s.gt, token_share, m.yrecv)

    m.own[...] = token_grad(b)
    finals.append(lambda: sent(s.gt[0].at[1], m.gtr))

    gos_copy.wait_recv()

    def out_add(k):
        i = lax.div(k, 4)
        j = lax.rem(k, 4)
        m.gwos[i, j, c] = (
            m.gwos[i, j, c].astype(F32) + m.gwor[i, j].astype(F32)
        ).astype(BF16)

    each(0, 16, out_add)
    out_x = lambda i: m.gwos.at[i, pl.ds(0, 2), c]
    out_y = lambda i: m.gwos.at[i, pl.ds(2, 2), c]
    oland_x = m.oland.at[:, pl.ds(0, 2)]
    oland_y = m.oland.at[:, pl.ds(2, 2)]
    fold_start(s.rox, out_x, m.opre.at[0], oland_x, ny)
    fold_start(s.roy, out_y, m.opre.at[1], oland_y, nx)

    sum_pass(s.gt, token_share, m.yrecv, pass_token)
    fold_pass(s.rwx, weight_x, m.wpre.at[0], land_x, fold_add(weight_x, m.wpre.at[0], 32), nx)
    fold_pass(s.rwy, weight_y, m.wpre.at[1], land_y, fold_add(weight_y, m.wpre.at[1], 32), ny)
    all_wait(s.fin1, m.fin1.at[pl.ds(0, 3)])
    m.fin2s[...] = (m.fin1[0] + m.fin1[1]) + (m.fin1[2] + m.fin1[3])
    m.fin2[b] = m.fin2s[32:48, :]
    seq_peers(lambda p: all_start(s.fin2, m.fin2s.at[pl.ds(32, 16), :], m.fin2.at[b], p))
    drain(s.fin2, m.fin2.at[pl.ds(0, 7)])
    holder = 2 * a + lax.div(b, 4)
    keeps = lambda p: (lax.div(b, 2) == a) & (lax.div(p, 4) == c)

    def pers_send(p):
        @pl.when(keeps(p))
        def _():
            copy(
                m.fin2s.at[pl.ds(0, 32), :], m.pers, s.pers[0].at[p], s.pers[1].at[0], (a, p)
            ).start()

    def pers_drain(p):
        @pl.when(keeps(p))
        def _():
            copy(m.pers, m.pers, s.pers[0].at[p], s.pers[1].at[0], (a, p)).wait_send()

    seq_peers(pers_send)
    finals.append(lambda: seq_peers(pers_drain))

    @pl.when(holder == b)
    def _():
        m.pers[...] = m.fin2s[0:32, :]

    fold_pass(s.rox, out_x, m.opre.at[0], oland_x, fold_add(out_x, m.opre.at[0], 1), nx)
    fold_pass(s.roy, out_y, m.opre.at[1], oland_y, fold_add(out_y, m.opre.at[1], 1), ny)
    fold_finish(s.rwx, land_x, m.gws.at[pl.ds(0, 3), pl.ds(0, 128), :])
    fold_finish(s.rwy, land_y, m.gws.at[pl.ds(0, 3), pl.ds(0, 128), :])

    def head_sum(p):
        rows = block_rows(p, 32)
        total = m.gws[a, rows, :].astype(F32) + m.wland[0, rows, :].astype(F32)
        m.gas[p] = (total + m.wland[1, rows, :].astype(F32)).astype(BF16)

    def head_sum_send(p):
        head_sum(p)
        all_start(s.gwa, m.gas.at[p], m.gar.at[b], p)

    seq_peers(head_sum_send)
    drain(s.gwa, m.gas.at[pl.ds(0, 7)])
    head_sum(b)
    m.gar[b] = m.gas[b]

    fold_finish(s.rox, oland_x, m.gwos.at[pl.ds(0, 3), pl.ds(0, 2), 0])
    fold_finish(s.roy, oland_y, m.gwos.at[pl.ds(0, 3), pl.ds(0, 2), 0])

    def out_sum(i):
        total = m.gwos[a, i, c].astype(F32) + m.oland[0, i].astype(F32)
        m.gos[i] = (total + m.oland[1, i].astype(F32)).astype(BF16)

    each(0, 4, out_sum)
    out_share = lambda zt: m.gos.at[zt]

    def pass_out(zt, slot):
        m.gos[zt] = (m.gos[zt].astype(F32) + m.goz[slot].astype(F32)).astype(BF16)

    sum_start(s.rgo, out_share, m.goz)
    own_half = down_sum(part)
    far_copy.wait_recv()
    fd_o[...] = own_half[0:share_rows, :] + m.dfar[0:share_rows, :].astype(F32)
    sum_pass(s.rgo, out_share, m.goz, pass_out)

    sum_finish(s.gt, m.yrecv, m.yrecv.at[pl.ds(0, 3)])
    copy(
        m.gtr.at[z], m.gtr.at[z], s.gt[0].at[1], s.gt[1].at[4 + z], (a, sib)
    ).wait_recv()

    def token_sum(i):
        rows = block_rows(i, 32)
        total = m.dout[rows, :] + m.own[rows, :]
        total = total + m.gtr[z, rows, :].astype(F32)
        gtok_o[rows, :] = total + landed(m.yrecv, (rows, slice(None)))

    each(0, 4, token_sum)

    all_wait(s.gwa, m.gar.at[pl.ds(0, 7)])
    gar_o[...] = m.gar[...]

    all_wait(s.gxg, m.gxr.at[pl.ds(0, 7), 0])
    all_wait(s.gxu, m.gxr.at[pl.ds(0, 7), 1])
    gux_o[...] = m.gxr[...]

    sum_finish(s.rgo, m.goz, m.goz.at[pl.ds(0, 3)])
    gwo_o[...] = m.gos[z].astype(F32) + landed(m.goz, ())

    all_wait(s.fin2, m.fin2.at[pl.ds(0, 7)])
    everything = jnp.sum(m.fin2[...], axis=0)
    fin_o[0:8, :] = everything[0:8, :]
    loss = jnp.sum(everything[8:9, :]) / (2.0 * width * valid_total)
    fin_o[8:16, :] = jnp.full((8, 128), loss, F32)

    @pl.when(holder != b)
    def _():
        copy(m.pers, m.pers, s.pers[0].at[0], s.pers[1].at[0], (a, holder)).wait_recv()

    pers_o[...] = m.pers[...]

    for last in finals:
        last()


def finish_kernel(
    width, hidden, out, gtok, gar, gwo, fin, pers, gux, fd,
    out_o, loss_o, gtok_o, gq_o, gk_o, gv_o, gwo_o, gwg_o, pk_o, pv_o, gain_o, fg_o, fu_o, fd_o,
):
    a = lax.axis_index("head")
    b = lax.axis_index("seq")
    quarter = lax.rem(b, 4)

    def lanes(value):
        picked = value[:, 0:32]
        for j in range(1, 4):
            picked = jnp.where(quarter == j, value[:, 32 * j : 32 * j + 32], picked)
        return picked

    out_o[...] = out[...]
    gtok_o[...] = gtok[...]
    gwo_o[...] = gwo[...]
    fd_o[...] = fd[...]
    loss_o[...] = fin[8:9, 0:1]
    pk_o[...] = lanes(pers[0:16, :])
    pv_o[...] = lanes(pers[16:32, :])
    gain_o[...] = lanes(fin[pl.ds(2 * a + lax.div(b, 4), 1), :])
    for head in range(8):
        cols = slice(head * 128, head * 128 + 128)
        gq_o[:, cols] = gar[head, :, 0:128].astype(F32)
        gk_o[:, cols] = gar[head, :, 128:256].astype(F32)
        gv_o[:, cols] = gar[head, :, 256:384].astype(F32)
        gwg_o[:, cols] = gar[head, :, 384:512].astype(F32)
    run = hidden // 8
    for place, target in enumerate((fg_o, fu_o)):
        for group in range(4):
            total = gux[group, place].astype(F32) + gux[group + 4, place].astype(F32)
            for i in range(8):
                start = run * (4 * i + group)
                target[:, start : start + run] = total[:, run * i : run * i + run]


def local_block(
    tokens, w_query, w_key, w_value, w_out, w_gate, persist_keys, persist_values, norm_gain,
    ff_gate, ff_up, ff_down, retention, doc_starts, valid, teacher,
):
    _, block, width = tokens.shape
    length = block * lax.axis_size("seq")
    hidden = ff_gate.shape[1] // 4
    pad = -(-hidden // 256) * 256
    share = ff_down.shape[0]
    table = scratch_table(width, block, hidden, pad, length)
    names = tuple(table)
    vmem = pl.BlockSpec(memory_space=pltpu.VMEM)
    shape = jax.ShapeDtypeStruct
    outs = (
        shape((block, width), BF16),
        shape((block, width), F32),
        shape((8, 32, 512), BF16),
        shape((32, width), F32),
        shape((16, 128), F32),
        shape((32, 128), F32),
        shape((8, 2, 32, pad), BF16),
        shape((share, width), F32),
    )
    scratch = [pltpu.VMEM(*table[name]) for name in names]
    for count in FLAGS.values():
        scratch += [pltpu.SemaphoreType.DMA((count,))] * 2
    result = pl.pallas_call(
        functools.partial(block_kernel, names, width, hidden, doc_starts.shape[1]),
        out_shape=outs,
        in_specs=[vmem] * 15 + [pl.BlockSpec(memory_space=pltpu.SMEM)],
        out_specs=[vmem] * len(outs),
        scratch_shapes=scratch,
        compiler_params=pltpu.CompilerParams(
            collective_id=0, has_side_effects=True, vmem_limit_bytes=VMEM_LIMIT
        ),
        name="block",
    )(
        tokens[0], w_query, w_key, w_value, w_out, w_gate, ff_gate, ff_up, ff_down, teacher[0],
        jnp.transpose(retention, (0, 2, 1)), persist_keys, persist_values, norm_gain[None],
        valid, doc_starts,
    )
    square = shape((32, width), F32)
    wide = shape((32, 4 * hidden), F32)
    finals = (
        outs[0], shape((1, 1), F32), outs[1], square, square, square, square, square,
        shape((P_SIZE, 32), F32), shape((P_SIZE, 32), F32), shape((1, 32), F32), wide, wide,
        outs[7],
    )
    done = pl.pallas_call(
        functools.partial(finish_kernel, width, hidden),
        out_shape=finals,
        in_specs=[vmem] * len(outs),
        out_specs=[vmem] * len(finals),
        name="finish",
    )(*result)
    (out, loss, gtok, gq, gk, gv, gwo, gwg, gpk, gpv, gain, fg, fu, fd) = done
    return (
        out[None], loss[0, 0], gtok[None], gq, gk, gv, gwo, gwg, gpk, gpv, gain[0], fg, fu, fd,
    )


VMEM_LIMIT = 62 << 20


def entering(value, axis, join, neutral, backward):
    count = lax.axis_size(axis)
    place = lax.axis_index(axis)
    ahead = count - 1 - place if backward else place
    gathered = jax.tree.map(
        lambda a, kind: lax.all_gather(a.astype(kind), axis), value, (jnp.bfloat16, jnp.bfloat16)
    )
    state = jax.tree.map(lambda a, e: jnp.zeros_like(a) + jnp.asarray(e, a.dtype), value, neutral)

    def one(hop, state):
        source = count - 1 - hop if backward else hop
        return join(
            state,
            jax.tree.map(
                lambda a, own: lax.dynamic_index_in_dim(a, source, 0, False).astype(own.dtype),
                gathered,
                value,
            ),
        )

    return lax.fori_loop(0, ahead, one, state)


def passed_along(value, axis, by):
    peers = lax.axis_size(axis)
    pairs = [(i, i + by) for i in range(peers) if 0 <= i + by < peers]
    return lax.ppermute(value, axis, pairs)


def from_behind(block, axis, distance):
    devices = range(lax.axis_size(axis))
    route = [((i - distance) % len(devices), i) for i in devices]
    return lax.ppermute(block, axis, route)


def product(left, right):
    return jnp.dot(left, right, preferred_element_type=jnp.float32)


def rows_outer(left, right):
    return jnp.einsum("nd,ne->de", left, right, preferred_element_type=jnp.float32)


def back_product(grad, weight):
    return jnp.einsum("ne,de->nd", grad, weight, preferred_element_type=jnp.float32)


def doc_index(starts, positions):
    return jnp.sum((starts[:, None, :] <= positions[None, :, None]).astype(jnp.int32), axis=-1) - 1


def doc_begin(starts, positions):
    return jnp.any(starts[:, None, :] == positions[None, :, None], axis=-1)


def chain_forward(earlier, later):
    return (earlier[0] * later[0], later[0][..., None, None] * earlier[1] + later[1])


def chain_backward(earlier, later):
    return (earlier[0] * later[0], later[1] + later[0][..., None, None] * earlier[1])


def masked_scores(query_rows, key_rows, query_pos, key_pos, query_seg, key_seg, scale):
    raw = (
        jnp.einsum("sqhd,skhd->sqhk", query_rows, key_rows, preferred_element_type=jnp.float32)
        * scale
    )
    allowed = (key_pos[None, None, :] <= query_pos[None, :, None]) & (
        key_seg[:, None, :] == query_seg[:, :, None]
    )
    return jnp.where(allowed[:, :, None, :], raw, MASKED)


def softmax_grads(
    query_rows,
    key_rows,
    value_rows,
    dout_rows,
    query_pos,
    key_pos,
    query_seg,
    key_seg,
    query_lse,
    query_delta,
    scale,
):
    scores = masked_scores(query_rows, key_rows, query_pos, key_pos, query_seg, key_seg, scale)
    probs = jnp.exp(scores - query_lse[..., None])
    prob_grad = jnp.einsum(
        "sqhd,skhd->sqhk", dout_rows, value_rows, preferred_element_type=jnp.float32
    )
    score_grad = (probs * (prob_grad - query_delta[..., None])).astype(jnp.bfloat16)
    return (probs.astype(jnp.bfloat16), score_grad)


def local(
    tokens,
    w_query,
    w_key,
    w_value,
    w_out,
    w_gate,
    persist_keys,
    persist_values,
    norm_gain,
    ff_gate,
    ff_up,
    ff_down,
    retention,
    doc_starts,
    valid,
    teacher,
):
    gathered = (
        lax.all_gather(w_query, ("head", "seq"), axis=0, tiled=True),
        lax.all_gather(w_key, ("head", "seq"), axis=0, tiled=True),
        lax.all_gather(w_value, ("head", "seq"), axis=0, tiled=True),
        lax.all_gather(w_out, ("head", "seq"), axis=0, tiled=True),
        lax.all_gather(w_gate, ("head", "seq"), axis=0, tiled=True),
        lax.all_gather(jnp.transpose(persist_keys), ("head", "seq"), axis=0, tiled=True),
        lax.all_gather(jnp.transpose(persist_values), ("head", "seq"), axis=0, tiled=True),
        lax.all_gather(norm_gain, ("head", "seq"), axis=0, tiled=True),
        lax.all_gather(ff_gate, ("head", "seq"), axis=0, tiled=True),
        lax.all_gather(ff_up, ("head", "seq"), axis=0, tiled=True),
        lax.all_gather(ff_down, ("head", "seq"), axis=0, tiled=True),
    )
    (
        query_weight,
        key_weight,
        value_weight,
        out_weight,
        gate_weight,
        fixed_key_cols,
        fixed_value_cols,
        gain_weight,
        ffn_gate,
        ffn_up,
        ffn_down,
    ) = gathered
    fixed_key_all = jnp.transpose(fixed_key_cols)
    fixed_value_all = jnp.transpose(fixed_value_cols)
    local_seqs, block, width = tokens.shape
    groups = lax.axis_size("head")
    heads = HEAD_COUNT // groups
    head_place = lax.axis_index("head")
    seq_place = lax.axis_index("seq")
    seq_count = lax.axis_size("seq")
    all_seqs = local_seqs * groups
    length = block * seq_count
    token_count = local_seqs * block
    scale = HD ** (-0.5)
    mem_scale = 0.125 / HD
    token_rows = tokens.reshape(token_count, width)
    query_tok = (
        product(token_rows, query_weight)
        .astype(jnp.bfloat16)
        .reshape(local_seqs, block, HEAD_COUNT, HD)
    )
    key_tok = (
        product(token_rows, key_weight)
        .astype(jnp.bfloat16)
        .reshape(local_seqs, block, HEAD_COUNT, HD)
    )
    value_tok = (
        product(token_rows, value_weight)
        .astype(jnp.bfloat16)
        .reshape(local_seqs, block, HEAD_COUNT, HD)
    )
    gate_pre = product(token_rows, gate_weight)
    query_heads, key_heads, value_heads = (
        lax.all_to_all(query_tok, "head", split_axis=2, concat_axis=0, tiled=True),
        lax.all_to_all(key_tok, "head", split_axis=2, concat_axis=0, tiled=True),
        lax.all_to_all(value_tok, "head", split_axis=2, concat_axis=0, tiled=True),
    )
    fixed_keys = lax.dynamic_slice_in_dim(
        fixed_key_all.reshape(P_SIZE, HEAD_COUNT, HD), head_place * heads, heads, 1
    )
    fixed_values = lax.dynamic_slice_in_dim(
        fixed_value_all.reshape(P_SIZE, HEAD_COUNT, HD), head_place * heads, heads, 1
    )
    own_start = seq_place * block
    own_pos = own_start + jnp.arange(block, dtype=jnp.int32)
    own_seg = doc_index(doc_starts, own_pos)
    own_begin = doc_begin(doc_starts, own_pos)
    last_row = own_start + block - 1
    fixed_scores = (
        jnp.einsum("sqhd,phd->sqhp", query_heads, fixed_keys, preferred_element_type=jnp.float32)
        * scale
    )
    top_start = jnp.max(fixed_scores, axis=-1)
    fixed_exp = jnp.exp(fixed_scores - top_start[..., None])
    acc_start = jnp.einsum(
        "sqhp,phd->sqhd",
        fixed_exp.astype(jnp.bfloat16),
        fixed_values,
        preferred_element_type=jnp.float32,
    )
    key_rows = lax.all_gather(key_heads, "seq", axis=1, tiled=True)
    value_rows = lax.all_gather(value_heads, "seq", axis=1, tiled=True)
    piece_keys = key_rows.shape[1]

    def attend_compute(state):
        running_top, running_total, running_acc = state
        key_pos = jnp.arange(piece_keys, dtype=jnp.int32)
        scores = masked_scores(
            query_heads, key_rows, own_pos, key_pos, own_seg, doc_index(doc_starts, key_pos), scale
        )
        new_top = jnp.maximum(running_top, jnp.max(scores, axis=-1))
        shrink = jnp.exp(running_top - new_top)
        weights_exp = jnp.exp(scores - new_top[..., None])
        new_total = running_total * shrink + jnp.sum(weights_exp, axis=-1)
        new_acc = running_acc * shrink[..., None] + jnp.einsum(
            "sqhk,skhd->sqhd",
            weights_exp.astype(jnp.bfloat16),
            value_rows,
            preferred_element_type=jnp.float32,
        )
        return (new_top, new_total, new_acc)

    final_top, final_total, final_acc = lax.cond(
        jnp.int32(0) <= last_row,
        attend_compute,
        lambda state: state,
        (top_start, jnp.sum(fixed_exp, axis=-1), acc_start),
    )
    attn_rows = final_acc / final_total[..., None]
    lse = final_top + jnp.log(final_total)
    log_retention = jnp.log(retention)
    running = jnp.cumsum(log_retention, axis=1)
    lane = jnp.transpose(running, (0, 2, 1))
    index = jnp.arange(block)
    linked = (index[None, :] <= index[:, None])[None] & (own_seg[:, None, :] == own_seg[:, :, None])
    decay = jnp.where(
        linked[:, None], jnp.exp(jnp.minimum(lane[:, :, :, None] - lane[:, :, None, :], 0.0)), 0.0
    )
    intersection = jnp.einsum(
        "sthd,suhd->shtu", query_heads, key_heads, preferred_element_type=jnp.float32
    )
    mixing = (mem_scale * intersection * decay).astype(jnp.bfloat16)
    inner_mem = jnp.einsum(
        "shtu,suhd->sthd", mixing, value_heads, preferred_element_type=jnp.float32
    )
    carried = ((own_seg == own_seg[:, :1]) & jnp.logical_not(own_begin[:, :1])).astype(jnp.float32)
    lead = jnp.exp(running) * carried[..., None]
    trail = jnp.where(
        (own_seg == own_seg[:, -1:])[..., None], jnp.exp(running[:, -1:, :] - running), 0.0
    )
    query_full = query_heads.astype(jnp.float32)
    key_full = key_heads.astype(jnp.float32)
    value_full = value_heads.astype(jnp.float32)
    block_state = jnp.einsum(
        "suhd,suhe->shde", key_full * trail[..., None], value_full, precision=HIGHEST
    )
    block_keep = lead[:, -1, :]
    identity = (jnp.ones_like(block_keep), jnp.zeros_like(block_state))
    chained = entering((block_keep, block_state), "seq", chain_forward, identity, False)
    state_in = chained[1]
    outer_mem = (
        mem_scale
        * lead[..., None]
        * jnp.einsum("sthd,shde->sthe", query_full, state_in, precision=HIGHEST)
    )
    mixed_heads = (attn_rows + inner_mem + outer_mem).astype(jnp.bfloat16)
    mixed_rows = lax.all_to_all(
        mixed_heads, "head", split_axis=0, concat_axis=2, tiled=True
    ).reshape(token_count, width)
    branch = product(mixed_rows, out_weight)
    gate_sigmoid = jax.nn.sigmoid(gate_pre)
    hidden = token_rows.astype(jnp.float32) + gate_sigmoid * branch
    inv_rms = lax.rsqrt(jnp.mean(hidden * hidden, axis=-1, keepdims=True) + EPSILON)
    normed = hidden * inv_rms
    gain_full = gain_weight.astype(jnp.float32)
    scaled = (normed * gain_full).astype(jnp.bfloat16)
    gate_act = product(scaled, ffn_gate)
    up_act = product(scaled, ffn_up)
    act_sigmoid = jax.nn.sigmoid(gate_act)
    silu_act = gate_act * act_sigmoid
    inner = (silu_act * up_act).astype(jnp.bfloat16)
    final = hidden + product(inner, ffn_down)
    output = final.astype(jnp.bfloat16).reshape(local_seqs, block, width)
    valid_rows = valid.reshape(token_count).astype(jnp.float32)
    error = final - teacher.reshape(token_count, width).astype(jnp.float32)
    sums = lax.psum(
        (jnp.sum(valid_rows * jnp.sum(error * error, axis=-1)), jnp.sum(valid_rows)),
        ("head", "seq"),
    )
    loss = sums[0] / (2.0 * width * sums[1])
    total_tokens = all_seqs * length
    d_out = valid_rows[:, None] * error * (total_tokens / sums[1])
    d_ffn = d_out.astype(jnp.bfloat16)
    grad_down = rows_outer(inner, d_ffn)
    d_inner = back_product(d_ffn, ffn_down)
    d_gate_act = (d_inner * up_act * act_sigmoid * (1.0 + gate_act * (1.0 - act_sigmoid))).astype(
        jnp.bfloat16
    )
    d_up_act = (d_inner * silu_act).astype(jnp.bfloat16)
    grad_ffn_gate = rows_outer(scaled, d_gate_act)
    grad_ffn_up = rows_outer(scaled, d_up_act)
    d_scaled = back_product(d_gate_act, ffn_gate) + back_product(d_up_act, ffn_up)
    grad_gain = jnp.sum(d_scaled * normed, axis=0)
    d_normed = d_scaled * gain_full
    d_hidden = d_out + inv_rms * (
        d_normed - normed * jnp.mean(d_normed * normed, axis=-1, keepdims=True)
    )
    d_branch = (d_hidden * gate_sigmoid).astype(jnp.bfloat16)
    d_gate = (d_hidden * branch * gate_sigmoid * (1.0 - gate_sigmoid)).astype(jnp.bfloat16)
    grad_out_weight = rows_outer(mixed_rows, d_branch)
    grad_gate_weight = rows_outer(token_rows, d_gate)
    d_mixed = (
        back_product(d_branch, out_weight)
        .astype(jnp.bfloat16)
        .reshape(local_seqs, block, HEAD_COUNT, HD)
    )
    dout_heads = lax.all_to_all(d_mixed, "head", split_axis=2, concat_axis=0, tiled=True)
    dout_full = dout_heads.astype(jnp.float32)
    delta = jnp.sum(dout_full * attn_rows, axis=-1)
    fixed_probs = jnp.exp(fixed_scores - lse[..., None])
    fixed_prob_grad = jnp.einsum(
        "sqhd,phd->sqhp", dout_heads, fixed_values, preferred_element_type=jnp.float32
    )
    fixed_score_grad = (fixed_probs * (fixed_prob_grad - delta[..., None])).astype(jnp.bfloat16)
    fixed_key_grad = (
        jnp.einsum(
            "sqhp,sqhd->phd", fixed_score_grad, query_heads, preferred_element_type=jnp.float32
        )
        * scale
    )
    fixed_value_grad = jnp.einsum(
        "sqhp,sqhd->phd",
        fixed_probs.astype(jnp.bfloat16),
        dout_heads,
        preferred_element_type=jnp.float32,
    )
    query_grad_start = (
        jnp.einsum(
            "sqhp,phd->sqhd", fixed_score_grad, fixed_keys, preferred_element_type=jnp.float32
        )
        * scale
    )
    fold_start = (query_grad_start,)
    back_key_rows = lax.all_gather(key_heads, "seq", axis=1, tiled=True)
    back_value_rows = lax.all_gather(value_heads, "seq", axis=1, tiled=True)
    back_piece_keys = back_key_rows.shape[1]

    def back_compute(state):
        key_pos = jnp.arange(back_piece_keys, dtype=jnp.int32)
        probs_low, score_grad = softmax_grads(
            query_heads,
            back_key_rows,
            back_value_rows,
            dout_heads,
            own_pos,
            key_pos,
            own_seg,
            doc_index(doc_starts, key_pos),
            lse,
            delta,
            scale,
        )
        query_grad = (
            state[0]
            + jnp.einsum(
                "sqhk,skhd->sqhd", score_grad, back_key_rows, preferred_element_type=jnp.float32
            )
            * scale
        )
        return (query_grad,)

    folded = lax.cond(jnp.int32(0) <= last_row, back_compute, lambda state: state, fold_start)
    query_att = folded[0]
    empty_local = jnp.zeros((all_seqs, block, heads, HD), jnp.float32)

    def visit(turn, state):
        key_rows, value_rows, key_acc, value_acc = state
        owner = (seq_place - turn) % seq_count
        start = owner * block

        def visit_compute(accs):
            key_pos = start + jnp.arange(block, dtype=jnp.int32)
            probs_low, score_grad = softmax_grads(
                query_heads,
                key_rows,
                value_rows,
                dout_heads,
                own_pos,
                key_pos,
                own_seg,
                doc_index(doc_starts, key_pos),
                lse,
                delta,
                scale,
            )
            key_next = (
                accs[0]
                + jnp.einsum(
                    "sqhk,sqhd->skhd", score_grad, query_heads, preferred_element_type=jnp.float32
                )
                * scale
            )
            value_next = accs[1] + jnp.einsum(
                "sqhk,sqhd->skhd", probs_low, dout_heads, preferred_element_type=jnp.float32
            )
            return (key_next, value_next)

        key_acc, value_acc = lax.cond(
            start <= last_row, visit_compute, lambda accs: accs, (key_acc, value_acc)
        )
        key_rows, value_rows = passed_along((key_rows, value_rows), "seq", 1)
        key_acc, value_acc = (
            from_behind(key_acc.astype(jnp.bfloat16), "seq", 1).astype(key_acc.dtype),
            from_behind(value_acc.astype(jnp.bfloat16), "seq", 1).astype(value_acc.dtype),
        )
        return (key_rows, value_rows, key_acc, value_acc)

    travelled = lax.fori_loop(
        0, seq_count, visit, (key_heads, value_heads, empty_local, empty_local)
    )
    key_att = travelled[2]
    value_att = travelled[3]
    mix_grad_raw = jnp.einsum(
        "sthe,suhe->shtu", dout_heads, value_heads, preferred_element_type=jnp.float32
    )
    intersection_grad = (mem_scale * mix_grad_raw * decay).astype(jnp.bfloat16)
    local_grad = mem_scale * jnp.einsum(
        "sthd,sthe->shde", query_full * lead[..., None], dout_full, precision=HIGHEST
    )
    state_grads = entering((block_keep, local_grad), "seq", chain_backward, identity, True)
    carry_grad = state_grads[1]
    query_mem = jnp.einsum(
        "shtu,suhd->sthd", intersection_grad, key_heads, preferred_element_type=jnp.float32
    )
    query_mem = query_mem + mem_scale * lead[..., None] * jnp.einsum(
        "sthe,shde->sthd", dout_full, state_in, precision=HIGHEST
    )
    key_mem = jnp.einsum(
        "shtu,sthd->suhd", intersection_grad, query_heads, preferred_element_type=jnp.float32
    )
    key_mem = key_mem + trail[..., None] * jnp.einsum(
        "suhe,shde->suhd", value_full, carry_grad, precision=HIGHEST
    )
    value_mem = jnp.einsum(
        "shtu,sthe->suhe", mixing, dout_heads, preferred_element_type=jnp.float32
    )
    value_mem = value_mem + jnp.einsum(
        "suhd,shde->suhe", key_full * trail[..., None], carry_grad, precision=HIGHEST
    )
    query_grad_heads = (query_att + query_mem).astype(jnp.bfloat16)
    key_grad_heads = (key_att + key_mem).astype(jnp.bfloat16)
    value_grad_heads = (value_att + value_mem).astype(jnp.bfloat16)
    query_back, key_back, value_back = (
        lax.all_to_all(query_grad_heads, "head", split_axis=0, concat_axis=2, tiled=True),
        lax.all_to_all(key_grad_heads, "head", split_axis=0, concat_axis=2, tiled=True),
        lax.all_to_all(value_grad_heads, "head", split_axis=0, concat_axis=2, tiled=True),
    )
    query_back = query_back.reshape(token_count, width)
    key_back = key_back.reshape(token_count, width)
    value_back = value_back.reshape(token_count, width)
    grad_query_weight = rows_outer(token_rows, query_back)
    grad_key_weight = rows_outer(token_rows, key_back)
    grad_value_weight = rows_outer(token_rows, value_back)
    token_grad = (
        d_hidden + back_product(d_gate, gate_weight) + back_product(query_back, query_weight)
    )
    token_grad = (
        token_grad + back_product(key_back, key_weight) + back_product(value_back, value_weight)
    )
    fixed_key_full = lax.dynamic_update_slice_in_dim(
        jnp.zeros((P_SIZE, HEAD_COUNT, HD), jnp.float32), fixed_key_grad, head_place * heads, 1
    ).reshape(P_SIZE, width)
    fixed_value_full = lax.dynamic_update_slice_in_dim(
        jnp.zeros((P_SIZE, HEAD_COUNT, HD), jnp.float32), fixed_value_grad, head_place * heads, 1
    ).reshape(P_SIZE, width)
    shards = (
        lax.psum_scatter(grad_query_weight, ("head", "seq"), scatter_dimension=0, tiled=True),
        lax.psum_scatter(grad_key_weight, ("head", "seq"), scatter_dimension=0, tiled=True),
        lax.psum_scatter(grad_value_weight, ("head", "seq"), scatter_dimension=0, tiled=True),
        lax.psum_scatter(grad_out_weight, ("head", "seq"), scatter_dimension=0, tiled=True),
        lax.psum_scatter(grad_gate_weight, ("head", "seq"), scatter_dimension=0, tiled=True),
        lax.psum_scatter(
            jnp.transpose(fixed_key_full), ("head", "seq"), scatter_dimension=0, tiled=True
        ),
        lax.psum_scatter(
            jnp.transpose(fixed_value_full), ("head", "seq"), scatter_dimension=0, tiled=True
        ),
        lax.psum_scatter(grad_gain, ("head", "seq"), scatter_dimension=0, tiled=True),
        lax.psum_scatter(grad_ffn_gate, ("head", "seq"), scatter_dimension=0, tiled=True),
        lax.psum_scatter(grad_ffn_up, ("head", "seq"), scatter_dimension=0, tiled=True),
        lax.psum_scatter(grad_down, ("head", "seq"), scatter_dimension=0, tiled=True),
    )
    return (
        output,
        loss,
        token_grad.reshape(local_seqs, block, width),
        shards[0],
        shards[1],
        shards[2],
        shards[3],
        shards[4],
        jnp.transpose(shards[5]),
        jnp.transpose(shards[6]),
        shards[7],
        shards[8],
        shards[9],
        shards[10],
    )


def solution(mesh):
    in_specs = (
        P("head", "seq", None),
        P(("head", "seq"), None),
        P(("head", "seq"), None),
        P(("head", "seq"), None),
        P(("head", "seq"), None),
        P(("head", "seq"), None),
        P(None, ("head", "seq")),
        P(None, ("head", "seq")),
        P(("head", "seq")),
        P(("head", "seq"), None),
        P(("head", "seq"), None),
        P(("head", "seq"), None),
        P(None, "seq", "head"),
        P(),
        P("head", "seq"),
        P("head", "seq", None),
    )
    out_specs = (
        P("head", "seq", None),
        P(),
        P("head", "seq", None),
        P(("head", "seq"), None),
        P(("head", "seq"), None),
        P(("head", "seq"), None),
        P(("head", "seq"), None),
        P(("head", "seq"), None),
        P(None, ("head", "seq")),
        P(None, ("head", "seq")),
        P(("head", "seq")),
        P(("head", "seq"), None),
        P(("head", "seq"), None),
        P(("head", "seq"), None),
    )
    fits = mesh.shape["head"] == 4 and mesh.shape["seq"] == HEAD_COUNT
    body = local_block if fits else local
    return jax.shard_map(body, mesh=mesh, in_specs=in_specs, out_specs=out_specs, check_vma=False)
```

```python
import functools
import types

import jax
import jax.numpy as jnp
from jax import lax
from jax.experimental import pallas as pl
from jax.experimental.pallas import tpu as pltpu
from jax.sharding import PartitionSpec as P

HEAD_COUNT = 8
HD = 128
P_SIZE = 16


HIGHEST = lax.Precision.HIGHEST
MASKED = -1e30
EPSILON = 1e-06
F32 = jnp.float32
BF16 = jnp.bfloat16
MESH_IDS = pl.DeviceIdType.MESH


def nn(left, right):
    return lax.dot_general(left, right, (((1,), (0,)), ((), ())), preferred_element_type=F32)


def nt(left, right):
    return lax.dot_general(left, right, (((1,), (1,)), ((), ())), preferred_element_type=F32)


def tn(left, right):
    return lax.dot_general(left, right, (((0,), (0,)), ((), ())), preferred_element_type=F32)


def tn_exact(left, right):
    return lax.dot_general(
        left, right, (((0,), (0,)), ((), ())), precision=HIGHEST, preferred_element_type=F32
    )


def nt_exact(left, right):
    return lax.dot_general(
        left, right, (((1,), (1,)), ((), ())), precision=HIGHEST, preferred_element_type=F32
    )


def nn_exact(left, right):
    return lax.dot_general(
        left, right, (((1,), (0,)), ((), ())), precision=HIGHEST, preferred_element_type=F32
    )


def block_rows(index, size):
    return pl.ds(pl.multiple_of(index * size, size), size)


def each(first, last, body):
    def step(index, carry):
        body(index)
        return carry

    lax.fori_loop(first, last, step, 0)


SEQ_FLAGS = dict(
    w1=8, t2=8, p2=8, x=8, wo=8, fxg=8, fxu=8, mx=8, dm=8, gxg=8, gxu=8, rgo=8, gt=8, gwa=8,
    fin2=8, pers=8, sc=8, y=8, df=8, ds=8, fd=1, gfd=1, gos=1,
)
XY_FLAGS = dict(
    t1=4, p1=4, w2=4, wox=4, fgx=4, fux=4, fdx=4, fdy=4, rga=3, rgb=3, rua=3, rub=3, rdx=3, rdy=3, rox=3, roy=3,
    rwx=3, rwy=3, fin1=4,
)
FLAGS = SEQ_FLAGS | XY_FLAGS


def scratch_table(width, tokens, hidden, hidden_pad, length):
    seqs, blocks, block = 4, 8, 128
    table = dict(
        x_all=((length, width), BF16),
        wcs=((blocks, 32, 512), BF16),
        wqk=((width, 512), BF16),
        tile=((4, 8, 128), F32),
        pin=((32, 128), BF16),
        vcol=((block, 1), F32),
        t1=((4, 8, 128), F32),
        p1=((4, 32, 128), BF16),
        t2s=((16, 128), F32),
        t2=((8, 16, 128), F32),
        p2=((8, 32, 128), BF16),
        fs=((4, 2, 32, hidden_pad), BF16),
        fgu=((2, 4, 256, hidden_pad), BF16),
        fdp=((8, 96, width), BF16),
        ffd=((hidden_pad, width), BF16),
        wo_all=((4, 4, 2, 32, width), BF16),
        q=((length, HD), BF16),
        k=((length, HD), BF16),
        v=((length, HD), BF16),
        fkv=((32, HD), BF16),
        gain=((1, width), F32),
        rrow=((1, length), F32),
        rcol=((block, 8), F32),
        probs=((length, length), BF16),
        decay=((length, length), BF16),
        both=((length, length), BF16),
        fprobs=((length, P_SIZE), BF16),
        mgs=((length, 2 * HD), BF16),
        mg=((8, block, 2 * HD), BF16),
        mx=((block, width), BF16),
        gp=((block, width), BF16),
        hid=((block, width), F32),
        br=((block, width), F32),
        inv=((block, 128), F32),
        own=((block, width), F32),
        dout=((block, width), F32),
        sc=((4 * block, width), BF16),
        gact=((4 * block, hidden_pad), F32),
        uact=((4 * block, hidden_pad), F32),
        inner=((4 * block, hidden_pad), BF16),
        ysend=((4, block, width), BF16),
        yrecv=((4, block, width), BF16),
        df=((4 * block, width), BF16),
        dga=((4 * block, hidden_pad), BF16),
        dua=((4 * block, hidden_pad), BF16),
        dbr=((block, width), BF16),
        dgt=((block, width), BF16),
        dms=((block, width), BF16),
        dm=((length, HD), BF16),
        dgs=((8, block, 2 * HD), BF16),
        dmg=((8, block, 2 * HD), BF16),
        dq=((length, 512), BF16),
        ggain=((1, width), F32),
        gus=((2, 4, 4, 2, 32, hidden_pad), BF16),
        gpre=((2, 2, 4, 32, hidden_pad), BF16),
        gland=((2, 2, 2, 4, 32, hidden_pad), BF16),
        gxs=((8, 2, 32, hidden_pad), BF16),
        gxr=((8, 2, 32, hidden_pad), BF16),
        gds=((8, 96, width), BF16),
        dpre=((2, 96, width), BF16),
        dland=((2, 2, 96, width), BF16),
        dsum=((2, 96, width), BF16),
        dfar=((96, width), BF16),
        gwos=((4, 4, 2, 32, width), BF16),
        gwor=((4, 4, 32, width), BF16),
        opre=((2, 2, 32, width), BF16),
        oland=((2, 4, 32, width), BF16),
        gos=((4, 32, width), BF16),
        goz=((4, 32, width), BF16),
        gws=((4, 256, 512), BF16),
        wpre=((2, 128, 512), BF16),
        wland=((2, 256, 512), BF16),
        gas=((8, 32, 512), BF16),
        gar=((8, 32, 512), BF16),
        gts=((4, 2, block, width), BF16),
        gtr=((4, block, width), BF16),
        pgrad=((32, HD), F32),
        fin0=((48, 128), F32),
        fin1=((4, 48, 128), F32),
        fin2s=((48, 128), F32),
        fin2=((8, 16, 128), F32),
        pers=((32, 128), F32),
    )
    return table


def block_kernel(names, width, hidden, ndoc, *refs):
    (
        tok, wq, wk, wv, wo, wg, fgi, fui, fdi, tea, ret, pk, pv, gin, val, docs,
        out_o, gtok_o, gar_o, gwo_o, fin_o, pers_o, gux_o, fd_o,
    ) = refs[:24]
    m = types.SimpleNamespace(**dict(zip(names, refs[24 : 24 + len(names)])))
    sems = refs[24 + len(names) :]
    s = types.SimpleNamespace(**dict(zip(FLAGS, zip(sems[0::2], sems[1::2]))))
    pad = m.ffd.shape[0]
    length = m.x_all.shape[0]
    scale = HD ** (-0.5)
    mem_scale = 0.125 / HD

    a = lax.axis_index("head")
    b = lax.axis_index("seq")
    z = lax.div(b, 2)
    c = lax.rem(b, 2)
    sib = 2 * z + 1 - c
    near = z + 1 - 2 * lax.rem(z, 2)
    mirror = 3 - z
    across = 3 - near
    inner_chip = (z == 1) | (z == 2)
    inside = lax.div(lax.rem(z, 3) + 1, 2)
    order = (
        near + inside * (mirror - near),
        across + inside * (near - across),
        mirror + inside * (across - mirror),
    )
    part = lax.div(b, 4)
    mine = lax.rem(b, 4)
    partner = 2 * near + c
    far = b + 4 - 8 * part
    mate, pmate, cross = lax.rem(sib, 4), lax.rem(partner, 4), lax.rem(2 * near + 1 - c, 4)
    nx = a + 1 - 2 * lax.rem(a, 2)
    ny = lax.rem(a + 2, 4)
    diagonal = 3 - a

    def copy(src, dst, ssem, rsem, device):
        return pltpu.make_async_remote_copy(
            src_ref=src, dst_ref=dst, send_sem=ssem, recv_sem=rsem,
            device_id=device, device_id_type=MESH_IDS,
        )

    def sent(flag, total):
        copy(total, total, flag, flag, (a, sib)).wait_send()

    def landed_all(flag, total):
        copy(total, total, flag, flag, (a, sib)).wait_recv()

    def seq_peers(body):
        each(1, 8, lambda step: body(lax.rem(b + step, 8)))

    def xy_peers(body):
        each(1, 4, lambda step: body(lax.rem(a + step, 4)))

    def seq_start(pair, src, dst, peer):
        copy(src, dst, pair[0].at[0], pair[1].at[b], (a, peer)).start()

    def seq_wait(pair, dst, peer):
        landed_all(pair[1].at[peer], dst)

    def all_start(pair, src, dst, peer):
        copy(src, dst, pair[0].at[0], pair[1].at[0], (a, peer)).start()

    def xy_start(pair, src, dst, peer):
        copy(src, dst, pair[0].at[0], pair[1].at[a], (peer, b)).start()

    def xy_wait(pair, dst, peer):
        landed_all(pair[1].at[peer], dst)

    def xy_all_start(pair, src, dst, peer):
        copy(src, dst, pair[0].at[0], pair[1].at[0], (peer, b)).start()

    def all_wait(pair, total):
        landed_all(pair[1].at[0], total)

    finals = []

    def drain(pair, total):
        finals.append(lambda: sent(pair[0].at[0], total))

    def line_copy(pair, src, dst, zt):
        return copy(src, dst, pair[0].at[0], pair[1].at[z], (a, 2 * zt + c))

    def pass_copy(pair, src, dst, zs):
        return copy(src, dst, pair[0].at[1], pair[1].at[4 + zs], (a, sib))

    def line_start_far(pair, src, place, four, two):
        @pl.when(inner_chip)
        def _():
            line_copy(pair, src, place(z), mirror).start()

        @pl.when(jnp.logical_not(inner_chip))
        def _():
            line_copy(pair, src, place(z), across).start()

        def line_sent():
            @pl.when(inner_chip)
            def _():
                sent(pair[0].at[0], four)

            @pl.when(jnp.logical_not(inner_chip))
            def _():
                sent(pair[0].at[0], two)

        finals.append(line_sent)

    def line_start_near(pair, src, place):
        line_copy(pair, src, place(z), near).start()

    def line_wait(pair, place, zs):
        landed_all(pair[1].at[zs], place(zs))

    def line_hand_on(pair, place, zs):
        block = place(zs)

        @pl.when(inner_chip)
        def _():
            copy(block, block, pair[0].at[0], pair[1].at[zs], (a, 2 * near + c)).start()

    def gather_line(pair, view, zs):
        block = view(2 * zs + c)
        line_wait(pair, lambda _: block, zs)
        pass_copy(pair, block, block, zs).start()

    def gather_pass(pair, view, zs):
        landed_all(pair[1].at[4 + zs], view(2 * zs + 1 - c))

    def quad_start(pair, view, first, second):
        block = view(a)
        copy(block, block, pair[0].at[0], pair[1].at[0], (first, b)).start()
        copy(block, block, pair[0].at[0], pair[1].at[1], (second, b)).start()

    def quad_pass(pair, view, first, second):
        block = view(first)
        landed_all(pair[1].at[0], block)
        copy(block, block, pair[0].at[0], pair[1].at[1], (second, b)).start()

    def fold_start(pair, view, pre, land, first):
        copy(view(diagonal), pre, pair[0].at[0], pair[1].at[0], (first, b)).start()
        copy(view(first), land.at[0], pair[0].at[0], pair[1].at[1], (first, b)).start()

    def fold_pass(pair, view, pre, land, add, second):
        landed_all(pair[1].at[0], pre)
        add(second)
        copy(view(second), land.at[1], pair[0].at[0], pair[1].at[1], (second, b)).start()

    def fold_finish(pair, land, three):
        landed_all(pair[1].at[1], land)
        drain(pair, three)

    barrier = pltpu.get_barrier_semaphore()
    seq_peers(lambda p: pl.semaphore_signal(barrier, 1, device_id=(a, p), device_id_type=MESH_IDS))
    xy_peers(lambda p: pl.semaphore_signal(barrier, 1, device_id=(p, b), device_id_type=MESH_IDS))

    for head in range(8):
        for place, weight in enumerate((wq, wk, wv, wg)):
            m.wcs[head, :, place * 128 : place * 128 + 128] = weight[
                :, head * 128 : head * 128 + 128
            ]
    own_rows = block_rows(b, 128)
    piece = pl.ds(pl.multiple_of(a * 256 + b * 32, 32), 32)
    m.x_all[own_rows, :] = tok[...]
    m.wqk[piece, :] = m.wcs[b]
    m.wo_all[a, z, c] = wo[...]
    down = fdi[...].astype(F32)
    m.fdp[2 * a + part] = jnp.concatenate(
        [down, jnp.zeros((96 - down.shape[0], width), F32)], axis=0
    ).astype(BF16)
    slot32 = block_rows(b, 32)
    row_id = lax.broadcasted_iota(jnp.int32, (128, 128), 0)
    col_id = lax.broadcasted_iota(jnp.int32, (128, 128), 1)
    place = (
        lax.broadcasted_iota(jnp.int32, (32, 128), 1)
        == lax.broadcasted_iota(jnp.int32, (32, 128), 0) + 32 * lax.rem(b, 4)
    ).astype(BF16)
    m.pin[0:16, :] = nn(pk[...], place).astype(BF16)
    m.pin[16:32, :] = nn(pv[...], place).astype(BF16)
    counted_row = val[...].astype(F32)
    m.vcol[...] = jnp.sum(jnp.where(row_id == col_id, counted_row, 0.0), axis=1, keepdims=True)
    gain_row = nn(gin[...], place)
    m.tile[...] = jnp.zeros_like(m.tile)
    for group in range(4):
        m.tile[group, 0:2, :] = jnp.log(ret[group])
        m.tile[group, 2:3, :] = counted_row
        m.tile[group, 3:4, :] = gain_row
    m.t1[a] = m.tile[a]
    m.p1[a] = m.pin[...]
    pl.semaphore_wait(barrier, 10)

    xy_peers(lambda p: xy_all_start(s.t1, m.tile.at[p], m.t1.at[a], p))
    xy_peers(lambda p: xy_all_start(s.p1, m.pin, m.p1.at[a], p))
    seq_peers(lambda p: all_start(s.w1, m.wcs.at[p], m.wqk.at[piece, :], p))
    wo_place = lambda zs: m.wo_all.at[a, zs, c]
    line_start_near(s.wo, wo, wo_place)
    line_start_far(s.wo, wo, wo_place, m.wo_all.at[0, :, 0], m.wo_all.at[0, pl.ds(0, 2), 0])
    all_wait(s.t1, m.t1.at[pl.ds(0, 3)])
    all_wait(s.p1, m.p1.at[pl.ds(0, 3)])
    for group in range(4):
        m.t2s[2 * group : 2 * group + 2, :] = m.t1[group, 0:2, :]
        m.t2s[8 + group : 9 + group, :] = m.t1[group, 3:4, :]
    m.t2s[12:13, :] = (m.t1[0, 2:3, :] + m.t1[1, 2:3, :]) + (m.t1[2, 2:3, :] + m.t1[3, 2:3, :])
    m.t2s[13:16, :] = jnp.zeros((3, 128), F32)
    m.t2[b] = m.t2s[...]
    m.p2[b] = m.p1[lax.div(b, 2)]
    seq_peers(lambda p: all_start(s.t2, m.t2s, m.t2.at[b], p))
    half = 4 * c

    def persist_send(p):
        @pl.when(lax.rem(p, 2) == lax.div(b, 4))
        def _():
            all_start(s.p2, m.p1.at[lax.div(p, 2)], m.p2.at[b], p)

    def persist_wait():
        pl.when(part == c)(lambda: all_wait(s.p2, m.p2.at[pl.ds(0, 3)]))
        pl.when(part != c)(lambda: all_wait(s.p2, m.p2.at[pl.ds(0, 4)]))

    def persist_drain():
        pl.when(part == c)(lambda: sent(s.p2[0].at[0], m.p2.at[pl.ds(0, 3)]))
        pl.when(part != c)(lambda: sent(s.p2[0].at[0], m.p2.at[pl.ds(0, 4)]))

    seq_peers(persist_send)
    finals.append(persist_drain)
    drain(s.t2, m.t2.at[pl.ds(0, 7)])

    drain(s.t1, m.t1.at[pl.ds(0, 3)])
    drain(s.p1, m.p1.at[pl.ds(0, 3)])
    drain(s.w1, m.wcs.at[pl.ds(0, 7)])
    x_view = lambda i: m.x_all.at[block_rows(i, 128), :]
    x_place = lambda zs: x_view(2 * zs + c)
    line_start_far(
        s.x, tok, x_place, m.x_all.at[pl.ds(0, 512), :], m.x_all.at[pl.ds(0, 256), :]
    )
    line_start_near(s.x, tok, x_place)
    pass_copy(s.x, tok, x_view(b), z).start()
    finals.append(lambda: sent(s.x[0].at[1], m.x_all.at[pl.ds(0, 512), :]))
    down_x = lambda i: m.fdp.at[2 * i]
    down_y = lambda i: m.fdp.at[2 * i + 1]

    run = hidden // 8
    for place, weight in enumerate((fgi, fui)):
        for group in range(4):
            m.fs[group, place, :, hidden:pad] = jnp.zeros((32, pad - hidden), BF16)
            for i in range(8):
                start = run * (4 * i + group)
                m.fs[group, place, :, run * i : run * i + run] = weight[:, start : start + run]
    m.fgu[:, a, slot32, :] = m.fs[mine]

    def column_start(pair, place, p):
        seq_start(pair, m.fs.at[lax.rem(p, 4), place], m.fgu.at[place, a, slot32, :], p)

    def columns(pair, place):
        seq_peers(lambda p: column_start(pair, place, p))

    def columns_far(pair, place):
        def one(p):
            @pl.when(lax.div(p, 2) != near)
            def _():
                column_start(pair, place, p)

        seq_peers(one)

    def columns_near(pair, place):
        column_start(pair, place, 2 * near)
        column_start(pair, place, 2 * near + 1)

    drain(s.fxg, m.gxr.at[pl.ds(0, 7), 0])
    drain(s.fxu, m.gxr.at[pl.ds(0, 7), 1])
    own_down = m.fdp.at[2 * a + part]
    far_down = m.fdp.at[2 * a + 1 - part]
    down_copy = copy(own_down, own_down, s.fd[0].at[0], s.fd[1].at[0], (a, far))
    finals.append(down_copy.wait_send)

    @pl.when(jnp.logical_not(inner_chip))
    def _():
        columns(s.fxg, 0)


    all_wait(s.w1, m.wqk.at[pl.ds(0, 224), :])
    quarter = lambda i: m.wqk.at[block_rows(i, 256), :]
    xy_peers(lambda p: xy_all_start(s.w2, quarter(a), quarter(a), p))
    drain(s.w2, m.wqk.at[pl.ds(0, 768), :])

    def piece_view(place, p):
        return lambda i: m.fgu.at[place, i, block_rows(p, 32), :]

    ways = ((nx, ny), (ny, nx))

    def pieces_on(peers, pair, quad_pair, place):
        for p in peers:
            seq_wait(pair, piece_view(place, p)(a), p)
            quad_start(quad_pair, piece_view(place, p), *ways[place])

    quad_start(s.fgx, piece_view(0, b), nx, ny)
    quad_start(s.fux, piece_view(1, b), ny, nx)

    @pl.when(part == 0)
    def _():
        quad_start(s.fdx, down_x, nx, ny)

    @pl.when(part == 1)
    def _():
        quad_start(s.fdy, down_y, ny, nx)


    def project(i):
        rows = block_rows(i, 128)
        wide = nn(m.x_all[rows, :], m.wqk[...])
        m.q[rows, :] = wide[:, 0:128].astype(BF16)
        m.k[rows, :] = wide[:, 128:256].astype(BF16)
        m.v[rows, :] = wide[:, 256:384].astype(BF16)
        m.mgs[rows, 128:256] = wide[:, 384:512].astype(BF16)

    head_cols = pl.ds(pl.multiple_of(b * 128, 128), 128)

    @pl.when(inner_chip)
    def _():
        line_wait(s.wo, wo_place, mirror)
        line_hand_on(s.wo, wo_place, mirror)
        line_wait(s.wo, wo_place, across)
        line_hand_on(s.wo, wo_place, across)

    gather_line(s.x, x_view, order[0])
    line_hand_on(s.x, x_place, mirror)
    @pl.when(inner_chip)
    def _():
        columns_far(s.fxg, 0)

    all_wait(s.w2, m.wqk.at[pl.ds(0, 768), :])
    project(b)
    gather_pass(s.x, x_view, z)
    project(sib)
    project(2 * order[0] + c)
    line_wait(s.wo, wo_place, near)

    @pl.when(jnp.logical_not(inner_chip))
    def _():
        line_wait(s.wo, wo_place, across)
        line_wait(s.wo, wo_place, mirror)

    wo_half = lambda i: m.wo_all.at[i, :, c]
    xy_peers(lambda p: xy_start(s.wox, wo_half(a), wo_half(a), p))
    drain(s.wox, m.wo_all.at[pl.ds(0, 3), :, 0])
    wo_pass = lambda i, block: copy(
        block, block, s.wo[0].at[1], s.wo[1].at[4], (a, sib)
    )
    wo_pass(a, wo_half(a)).start()
    finals.append(lambda: sent(s.wo[0].at[1], m.wo_all.at[:, :, 0]))
    chips = tuple(2 * zs + core for zs in order for core in range(2))

    gather_line(s.x, x_view, order[1])
    gather_line(s.x, x_view, order[2])
    line_hand_on(s.x, x_place, across)

    @pl.when(inner_chip)
    def _():
        columns_near(s.fxg, 0)

    columns(s.fxu, 1)

    project(2 * order[1] + c)
    project(2 * order[2] + c)

    def arrived_pass(zs):
        gather_pass(s.x, x_view, zs)
        project(2 * zs + 1 - c)

    for zs in order:
        arrived_pass(zs)
    all_wait(s.t2, m.t2.at[pl.ds(0, 7)])
    persist_wait()
    small = m.t2[...]
    place16 = lax.broadcasted_iota(jnp.int32, (8, 16, 128), 1)
    rates = jnp.sum(jnp.where(place16 == b, small, 0.0), axis=1)
    valid_total = jnp.sum(jnp.where(place16 == 12, small, 0.0))
    for group in range(8):
        line = 8 + group // 2
        first = 4 * (group % 2)
        m.gain[:, group * 128 : group * 128 + 128] = (
            m.t2[first, line : line + 1, :] + m.t2[first + 1, line : line + 1, :]
        ) + (m.t2[first + 2, line : line + 1, :] + m.t2[first + 3, line : line + 1, :])
    m.fkv[...] = (
        (m.p2[half].astype(F32) + m.p2[half + 1].astype(F32))
        + (m.p2[half + 2].astype(F32) + m.p2[half + 3].astype(F32))
    ).astype(BF16)
    lower = (col_id <= row_id).astype(F32)
    within = nt_exact(rates, lower)
    earlier = (
        lax.broadcasted_iota(jnp.int32, (8, 8), 1) < lax.broadcasted_iota(jnp.int32, (8, 8), 0)
    ).astype(F32)
    base = nn_exact(earlier, jnp.broadcast_to(jnp.sum(rates, axis=1, keepdims=True), (8, 128)))
    running = within + base
    for i in range(8):
        m.rrow[:, i * 128 : i * 128 + 128] = running[i : i + 1, :]
    eye = (col_id == row_id).astype(F32)
    m.rcol[...] = nt_exact(eye, running)

    local_pos = lax.broadcasted_iota(jnp.int32, (128, 1), 0)
    lane8 = lax.broadcasted_iota(jnp.int32, (128, 8), 1)

    m.probs[...] = jnp.zeros_like(m.probs)
    m.both[...] = jnp.zeros_like(m.both)

    def by_extent(i, body):
        for j in range(4):
            pl.when(lax.div(i, 2) == j)(lambda j=j: body(i, 256 * (j + 1)))

    def attend_keys(i, extent):
        rows = block_rows(i, 128)
        keys = slice(0, extent)
        query = m.q[rows, :]
        raw = nt(query, m.k[keys, :])
        pos = i * 128 + local_pos
        begin = jnp.zeros_like(pos)
        for j in range(ndoc):
            start = docs[a, j]
            begin = jnp.where(start <= pos, jnp.maximum(begin, start), begin)
        key_pos = lax.broadcasted_iota(jnp.int32, (128, extent), 1)
        allowed = (key_pos <= pos) & (key_pos >= begin)
        scores = jnp.where(allowed, raw * scale, MASKED)
        fixed = nt(query, m.fkv[0:16, :]) * scale
        top = jnp.maximum(
            jnp.max(scores, axis=1, keepdims=True), jnp.max(fixed, axis=1, keepdims=True)
        )
        weight = jnp.exp(scores - top)
        fixed_weight = jnp.exp(fixed - top)
        share = 1.0 / (
            jnp.sum(weight, axis=1, keepdims=True) + jnp.sum(fixed_weight, axis=1, keepdims=True)
        )
        prob = weight * share
        fixed_prob = (fixed_weight * share).astype(BF16)
        reach = jnp.sum(jnp.where(lane8 == i, m.rcol[...], 0.0), axis=1, keepdims=True)
        kept = jnp.where(
            allowed, jnp.exp(jnp.minimum(reach - m.rrow[:, keys], 0.0)) * mem_scale, 0.0
        )
        joint = (prob + kept * raw).astype(BF16)
        m.probs[rows, keys] = prob.astype(BF16)
        m.decay[rows, keys] = kept.astype(BF16)
        m.both[rows, keys] = joint
        m.fprobs[rows, :] = fixed_prob
        mixed = nn(joint, m.v[keys, :]) + nn(fixed_prob, m.fkv[16:32, :])
        m.mgs[rows, 0:128] = mixed.astype(BF16)

    attend = lambda i: by_extent(i, attend_keys)

    pieces_on((sib,) + chips[0:2], s.fxg, s.fgx, 0)

    def attend_step(step):
        i = lax.rem(b + step, 8)
        attend(i)

        @pl.when(step < 8)
        def _():
            all_start(s.mx, m.mgs.at[block_rows(i, 128), :], m.mg.at[b], i)

        @pl.when(step == 3)
        def _():
            pieces_on(chips[2:6], s.fxg, s.fgx, 0)
            pieces_on((sib,) + chips[0:2], s.fxu, s.fux, 1)

    each(1, 9, attend_step)
    drain(s.mx, m.mgs.at[pl.ds(0, 896), :])
    m.mg[b] = m.mgs[own_rows, :]
    down_copy.start()
    quad_pass(s.fgx, lambda i: m.fgu.at[0, i], nx, ny)
    pieces_on(chips[2:6], s.fxu, s.fux, 1)
    copy(far_down, far_down, s.fd[0].at[0], s.fd[1].at[0], (a, far)).wait_recv()

    @pl.when(part == 1)
    def _():
        quad_start(s.fdx, down_x, nx, ny)

    @pl.when(part == 0)
    def _():
        quad_start(s.fdy, down_y, ny, nx)


    def wo_arrived(p):
        xy_wait(s.wox, wo_half(p), p)
        wo_pass(p, wo_half(p)).start()

    xy_peers(wo_arrived)
    landed_all(s.wo[1].at[4], m.wo_all.at[:, :, 1 - c])
    quad_pass(s.fux, lambda i: m.fgu.at[1, i], ny, nx)
    all_wait(s.mx, m.mg.at[pl.ds(0, 7)])
    for head in range(8):
        m.mx[:, head * 128 : head * 128 + 128] = m.mg[head, :, 0:128]
        m.gp[:, head * 128 : head * 128 + 128] = m.mg[head, :, 128:256]

    out_w = lambda: m.wo_all[...].reshape(width, width)
    m.br[...] = nn(m.mx[...], out_w())

    half_row = lambda i: pl.ds(
        pl.multiple_of((4 * lax.div(i, 2) + mine) * 64 + lax.rem(i, 2) * 32, 32), 32
    )
    quad = lambda ref, h, i: ref.at[block_rows(4 * h + i, 64), :]

    def half_copy(pair, src, dst, h, slot, peer):
        return copy(src, dst, pair[0].at[h], pair[1].at[2 * h + slot], (a, peer))

    def half_gather(pair, ref, h):
        block = quad(ref, h, mine)
        half_copy(pair, block, block, h, 0, partner).start()
        half_copy(pair, block, block, h, 1, sib).start()

    def half_wait(pair, ref, h):
        block = quad(ref, h, pmate)
        landed_all(pair[1].at[2 * h], block)
        half_copy(pair, block, block, h, 1, sib).start()
        landed_all(pair[1].at[2 * h + 1], ref.at[pl.ds(0, 128), :])
        finals.append(lambda: sent(pair[0].at[h], ref.at[pl.ds(0, 192), :]))

    def half_scatter(pair, value, h):
        for i in range(4):
            m.ysend[i, h * 64 : h * 64 + 64, :] = value[i * 64 : i * 64 + 64, :].astype(BF16)
        rows = pl.ds(h * 64, 64)
        half_copy(pair, m.ysend.at[cross, rows, :], m.yrecv.at[1, rows, :], h, 1, sib).start()
        half_copy(pair, m.ysend.at[mate, rows, :], m.yrecv.at[0, rows, :], h, 0, sib).start()

    def half_on(pair, h):
        rows = pl.ds(h * 64, 64)
        landed_all(pair[1].at[2 * h + 1], m.yrecv.at[1, rows, :])
        m.ysend[pmate, rows, :] = (
            m.ysend[pmate, rows, :].astype(F32) + m.yrecv[1, rows, :].astype(F32)
        ).astype(BF16)
        half_copy(
            pair, m.ysend.at[pmate, rows, :], m.yrecv.at[2, rows, :], h, 0, partner
        ).start()

    def half_sent(pair, h):
        sent(pair[0].at[h], m.ysend.at[pl.ds(0, 3), pl.ds(h * 64, 64), :])

    def half_land(pair, h):
        landed_all(pair[1].at[2 * h], m.yrecv.at[pl.ds(0, 2), pl.ds(h * 64, 64), :])

    def normalise(i):
        rows = block_rows(i, 32)
        opened = jax.nn.sigmoid(m.gp[rows, :].astype(F32))
        hidden_rows = tok[rows, :].astype(F32) + opened * m.br[rows, :]
        inv = lax.rsqrt(jnp.mean(hidden_rows * hidden_rows, axis=1, keepdims=True) + EPSILON)
        m.hid[rows, :] = hidden_rows
        m.inv[rows, :] = jnp.broadcast_to(inv, (32, 128))
        m.sc[half_row(i), :] = (
            hidden_rows * inv * m.gain[...]
        ).astype(BF16)

    each(0, 2, normalise)
    half_gather(s.sc, m.sc, 0)
    each(2, 4, normalise)
    half_gather(s.sc, m.sc, 1)

    quad_pass(s.fdx, down_x, nx, ny)
    quad_pass(s.fdy, down_y, ny, nx)
    landed_all(s.fgx[1].at[1], m.fgu.at[0, pl.ds(0, 2)])
    landed_all(s.fux[1].at[1], m.fgu.at[1, pl.ds(0, 2)])
    drain(s.fgx, m.fgu.at[0, pl.ds(0, 3)])
    drain(s.fux, m.fgu.at[1, pl.ds(0, 3)])
    drain(s.fdx, m.fdp.at[pl.ds(0, 3)])
    drain(s.fdy, m.fdp.at[pl.ds(0, 3)])
    half_wait(s.sc, m.sc, 0)

    gate_w = lambda: m.fgu[0].reshape(width, pad)
    up_w = lambda: m.fgu[1].reshape(width, pad)

    def feed(i):
        rows = block_rows(i, 256)
        scaled = m.sc[rows, :]
        gate_act = nn(scaled, gate_w())
        up_act = nn(scaled, up_w())
        m.gact[rows, :] = gate_act
        m.uact[rows, :] = up_act
        m.inner[rows, :] = (gate_act * jax.nn.sigmoid(gate_act) * up_act).astype(BF16)

    feed(0)
    landed_all(s.fdx[1].at[1], m.fdp.at[pl.ds(0, 2)])
    landed_all(s.fdy[1].at[1], m.fdp.at[pl.ds(0, 2)])
    share_rows = m.fdp.shape[1] - 8
    for i in range(4):
        m.ffd[2 * i * share_rows : 2 * (i + 1) * share_rows, :] = jnp.concatenate(
            [m.fdp[2 * i + j, 0:share_rows, :].astype(F32) for j in range(2)], axis=0
        ).astype(BF16)
    m.ffd[hidden:pad, :] = jnp.zeros((pad - hidden, width), BF16)

    def feed_out(h):
        half_scatter(s.y, nn(m.inner[block_rows(h, 256), :], m.ffd[...]), h)
        m.own[block_rows(h, 64), :] = nn(m.inner[block_rows(4 * h + mine, 64), :], m.ffd[...])
        half_on(s.y, h)

    feed_out(0)
    half_wait(s.sc, m.sc, 1)
    feed(1)
    feed_out(1)
    half_land(s.y, 0)

    token_total = float(4 * length)
    m.fin0[...] = jnp.zeros_like(m.fin0)

    def finish(i):
        rows = block_rows(i, 32)
        final = m.hid[rows, :] + m.own[rows, :]
        final = final + m.yrecv[0, rows, :].astype(F32) + m.yrecv[2, rows, :].astype(F32)
        out_o[rows, :] = final.astype(BF16)
        error = final - tea[rows, :].astype(F32)
        counted = m.vcol[rows, :] * error
        grad = counted * (token_total / valid_total)
        m.dout[rows, :] = grad
        m.df[half_row(i), :] = grad.astype(BF16)
        squares = jnp.sum(counted * error, axis=0, keepdims=True)
        lanes = squares[:, 0:128]
        for j in range(1, width // 128):
            lanes = lanes + squares[:, j * 128 : j * 128 + 128]
        m.fin0[40:41, :] += lanes

    each(0, 2, finish)
    half_gather(s.df, m.df, 0)
    half_land(s.y, 1)
    each(2, 4, finish)
    half_gather(s.df, m.df, 1)
    half_wait(s.df, m.df, 0)

    def feed_back(i):
        rows = block_rows(i, 256)
        d_inner = nt(m.df[rows, :], m.ffd[...])
        gate_act = m.gact[rows, :]
        opened = jax.nn.sigmoid(gate_act)
        m.dga[rows, :] = (
            d_inner * m.uact[rows, :] * opened * (1.0 + gate_act * (1.0 - opened))
        ).astype(BF16)
        m.dua[rows, :] = (d_inner * gate_act * opened).astype(BF16)

    feed_back(0)

    def feed_in(h):
        rows = block_rows(h, 256)
        half_sent(s.y, h)
        half_scatter(s.ds, nt(m.dga[rows, :], gate_w()) + nt(m.dua[rows, :], up_w()), h)
        rows = block_rows(4 * h + mine, 64)
        m.own[block_rows(h, 64), :] = nt(m.dga[rows, :], gate_w()) + nt(m.dua[rows, :], up_w())
        half_on(s.ds, h)

    feed_in(0)
    half_wait(s.df, m.df, 1)
    feed_back(1)
    feed_in(1)
    finals.append(lambda: (half_sent(s.ds, 0), half_sent(s.ds, 1)))

    def share_copy(pair, share, landing, zt):
        return copy(share, landing.at[z], pair[0].at[0], pair[1].at[0], (a, 2 * zt + c))

    def sum_near(pair, share, landing):
        share_copy(pair, share(near), landing, near).start()

    def sum_far(pair, share, landing, zt, slot, flag):
        copy(
            share(zt), landing.at[slot], pair[0].at[0], pair[1].at[flag], (a, 2 * near + c)
        ).start()

    def sum_start(pair, share, landing):
        @pl.when(jnp.logical_not(inner_chip))
        def _():
            sum_far(pair, share, landing, across, mirror, 1)
            sum_far(pair, share, landing, mirror, near, 2)

        sum_near(pair, share, landing)

    def sum_pass(pair, share, landing, add):
        @pl.when(inner_chip)
        def _():
            for zt, slot, flag in ((mirror, across, 1), (across, z, 2)):
                landed_all(pair[1].at[flag], landing.at[slot])
                add(zt, slot)
                share_copy(pair, share(zt), landing, zt).start()

    second = across + inside * (mirror - across)

    def sum_finish(pair, landing, three):
        landed_all(pair[1].at[0], landing.at[pl.ds(0, 2)])
        drain(pair, three)

    def landed(landing, where):
        return landing[(near,) + where].astype(F32) + landing[(second,) + where].astype(F32)

    def fold_add(view, pre, chunk):
        def add(second):
            rows = view(second).shape[0]

            def one(i):
                part_rows = pl.ds(pl.multiple_of(i * chunk, chunk), chunk)
                target = view(second)
                target[part_rows] = (
                    target[part_rows].astype(F32) + pre[part_rows].astype(F32)
                ).astype(BF16)

            each(0, rows // chunk, one)

        return add

    folds = ((s.rga, s.rgb), (s.rua, s.rub))
    weight_share = lambda place, core: lambda i: m.gus.at[place, i, :, core]

    def one_grad(i, place, grads):
        cols = pl.ds(pl.multiple_of(i * 256, 256), 256)
        m.gus[place, i] = tn(m.sc[:, cols], grads[...]).astype(BF16).reshape(4, 2, 32, pad)

    def weight_start(place, core):
        fold_start(
            folds[place][core], weight_share(place, core), m.gpre.at[place, core],
            m.gland.at[place, core], (ny, nx)[place],
        )

    def weight_pass(place, core):
        share, pre = weight_share(place, core), m.gpre.at[place, core]
        fold_pass(
            folds[place][core], share, pre, m.gland.at[place, core], fold_add(share, pre, 1),
            (nx, ny)[place],
        )

    one_grad(diagonal, 0, m.dga)
    one_grad(ny, 0, m.dga)
    weight_start(0, 0)
    one_grad(diagonal, 1, m.dua)
    one_grad(nx, 1, m.dua)
    weight_start(1, 0)
    weight_start(0, 1)
    weight_start(1, 1)

    half_land(s.ds, 0)
    m.ggain[...] = jnp.zeros_like(m.ggain)

    def norm_back(i):
        rows = block_rows(i, 32)
        d_scaled = m.own[rows, :] + m.yrecv[0, rows, :].astype(F32)
        d_scaled = d_scaled + m.yrecv[2, rows, :].astype(F32)
        inv = m.inv[rows, 0:1]
        normed = m.hid[rows, :] * inv
        m.ggain[...] += jnp.sum(d_scaled * normed, axis=0, keepdims=True)
        d_normed = d_scaled * m.gain[...]
        lean = jnp.mean(d_normed * normed, axis=1, keepdims=True)
        d_hidden = m.dout[rows, :] + inv * (d_normed - normed * lean)
        m.dout[rows, :] = d_hidden
        opened = jax.nn.sigmoid(m.gp[rows, :].astype(F32))
        m.dbr[rows, :] = (d_hidden * opened).astype(BF16)
        m.dgt[rows, :] = (d_hidden * m.br[rows, :] * opened * (1.0 - opened)).astype(BF16)

    each(0, 2, norm_back)
    half_land(s.ds, 1)
    each(2, 4, norm_back)
    gate_cols = pl.ds(384, 128)
    cols_of = lambda i: pl.ds(pl.multiple_of(i * 128, 128), 128)
    m.dms[...] = nt(m.dbr[...], out_w()).astype(BF16)
    for head in range(8):
        cols = slice(head * 128, head * 128 + 128)
        m.dgs[head, :, 0:128] = m.dms[:, cols]
        m.dgs[head, :, 128:256] = m.dgt[:, cols]
    seq_peers(lambda p: seq_start(s.dm, m.dgs.at[p], m.dmg.at[b], p))
    drain(s.dm, m.dgs.at[pl.ds(0, 7)])
    m.dmg[b] = m.dgs[b]

    one_grad(nx, 0, m.dga)
    weight_pass(0, 0)
    one_grad(ny, 1, m.dua)
    weight_pass(1, 0)
    one_grad(a, 0, m.dga)
    one_grad(a, 1, m.dua)
    weight_pass(0, 1)
    weight_pass(1, 1)

    def down_grad(i):
        cols = pl.ds(pl.multiple_of(i * 256, 256), 256)
        m.ffd[block_rows(i, 256), :] = tn(m.inner[:, cols], m.df[...]).astype(BF16)

    each(0, pad // 256, down_grad)
    for i in range(4):
        double = m.ffd[2 * i * share_rows : 2 * (i + 1) * share_rows, :].astype(F32)
        for j in range(2):
            m.gds[2 * i + j] = jnp.concatenate(
                [double[j * share_rows : (j + 1) * share_rows, :], jnp.zeros((8, width), F32)],
                axis=0,
            ).astype(BF16)
    down_x_share = lambda i: m.gds.at[2 * i]
    down_y_share = lambda i: m.gds.at[2 * i + 1]
    fold_start(s.rdx, down_x_share, m.dpre.at[0], m.dland.at[0], ny)
    fold_start(s.rdy, down_y_share, m.dpre.at[1], m.dland.at[1], nx)

    def out_grad(i):
        cols = pl.ds(pl.multiple_of(i * 256, 256), 256)
        m.gwos[i] = tn(m.mx[:, cols], m.dbr[...]).astype(BF16).reshape(4, 2, 32, width)

    each(0, 4, out_grad)
    gos_copy = copy(m.gwos.at[:, :, 1 - c], m.gwor, s.gos[0].at[0], s.gos[1].at[0], (a, sib))
    gos_copy.start()
    finals.append(gos_copy.wait_send)
    m.pgrad[...] = jnp.zeros_like(m.pgrad)

    def attend_back_keys(i, extent):
        rows = block_rows(i, 128)
        keys = slice(0, extent)
        d_mixed = m.dmg[i, :, 0:128]
        m.dm[rows, :] = d_mixed
        m.dq[rows, gate_cols] = m.dmg[i, :, 128:256]
        d_joint = nt(d_mixed, m.v[keys, :])
        prob = m.probs[rows, keys].astype(F32)
        turned = prob * d_joint
        fixed_prob = m.fprobs[rows, :]
        fixed_full = fixed_prob.astype(F32)
        fixed_turned = fixed_full * nt(d_mixed, m.fkv[16:32, :])
        delta = jnp.sum(turned, axis=1, keepdims=True) + jnp.sum(
            fixed_turned, axis=1, keepdims=True
        )
        d_raw = (
            scale * (turned - prob * delta) + m.decay[rows, keys].astype(F32) * d_joint
        ).astype(BF16)
        m.probs[rows, keys] = d_raw
        d_fixed = (fixed_turned - fixed_full * delta).astype(BF16)
        m.dq[rows, 0:128] = (
            nn(d_raw, m.k[keys, :]) + scale * nn(d_fixed, m.fkv[0:16, :])
        ).astype(BF16)
        m.pgrad[0:16, :] += scale * tn(d_fixed, m.q[rows, :])
        m.pgrad[16:32, :] += tn(fixed_prob, d_mixed)

    attend_back = lambda i: by_extent(i, attend_back_keys)

    def owners(core):
        for place, pair in enumerate((s.gxg, s.gxu)):
            landed_all(folds[place][core][1].at[1], m.gland.at[place, core])

            def one(zt):
                p = 2 * zt + core
                total = m.gus[place, a, zt, core].astype(F32)
                total = total + m.gland[place, core, 0, zt].astype(F32)
                total = total + m.gland[place, core, 1, zt].astype(F32)
                m.gxs[p, place] = total.astype(BF16)

                @pl.when(p != b)
                def _():
                    all_start(pair, m.gxs.at[p, place], m.gxr.at[b, place], p)

                @pl.when(p == b)
                def _():
                    m.gxr[b, place] = m.gxs[b, place]

            each(1, 5, lambda step: one(lax.rem(z + step, 4)))

    def attend_back_step(step):
        i = lax.rem(b + step, 8)

        @pl.when(step > 0)
        def _():
            seq_wait(s.dm, m.dmg.at[i], i)

        pl.when(step == 2)(lambda: owners(0))
        attend_back(i)

    each(0, 8, attend_back_step)
    for place, pair in enumerate((s.gxg, s.gxu)):
        for core in range(2):
            drain(folds[place][core], m.gus.at[place, pl.ds(0, 3), :, core])
        drain(pair, m.gxs.at[pl.ds(0, 7), place])
    fold_pass(
        s.rdx, down_x_share, m.dpre.at[0], m.dland.at[0],
        fold_add(down_x_share, m.dpre.at[0], 32), nx,
    )
    fold_pass(
        s.rdy, down_y_share, m.dpre.at[1], m.dland.at[1],
        fold_add(down_y_share, m.dpre.at[1], 32), ny,
    )
    owners(1)

    m.fin0[0:32, :] = m.pgrad[...]
    for j in range(8):
        m.fin0[32 + j : 33 + j, :] = m.ggain[:, j * 128 : j * 128 + 128]
    m.fin1[a] = m.fin0[...]
    xy_peers(lambda p: xy_all_start(s.fin1, m.fin0, m.fin1.at[a], p))
    drain(s.fin1, m.fin1.at[pl.ds(0, 3)])

    query_turned = jnp.transpose(m.q[...].astype(F32)).astype(BF16)
    mixed_turned = jnp.transpose(m.dm[...].astype(F32)).astype(BF16)

    def key_value_grad(i):
        cols = cols_of(i)
        rows = block_rows(i, 128)
        m.dq[rows, 128:256] = jnp.transpose(nn(query_turned, m.probs[:, cols])).astype(BF16)
        m.dq[rows, 256:384] = jnp.transpose(nn(mixed_turned, m.both[:, cols])).astype(BF16)

    each(0, 8, key_value_grad)

    def head_weight_grad(i):
        cols = pl.ds(pl.multiple_of(i * 256, 256), 256)
        m.gws[i] = tn(m.x_all[:, cols], m.dq[...]).astype(BF16)

    each(0, 4, head_weight_grad)
    weight_x = lambda i: m.gws.at[i, pl.ds(0, 128), :]
    weight_y = lambda i: m.gws.at[i, pl.ds(128, 128), :]
    land_x = m.wland.at[:, pl.ds(0, 128), :]
    land_y = m.wland.at[:, pl.ds(128, 128), :]
    fold_start(s.rwx, weight_x, m.wpre.at[0], land_x, ny)
    fold_start(s.rwy, weight_y, m.wpre.at[1], land_y, nx)

    def token_grad(i):
        return nt(m.dq[block_rows(i, 128), :], m.wqk[...])

    def token_sib(zt):
        m.gts[zt, 1 - c] = token_grad(2 * zt + 1 - c).astype(BF16)
        copy(
            m.gts.at[zt, 1 - c], m.gtr.at[zt], s.gt[0].at[1], s.gt[1].at[4 + zt],
            (a, sib),
        ).start()

    for zt in (near + (1 - inside) * (across - near), mirror, across + (1 - inside) * (near - across), z):
        token_sib(zt)

    fold_finish(s.rdx, m.dland.at[0], m.gds.at[pl.ds(0, 3)])
    fold_finish(s.rdy, m.dland.at[1], m.gds.at[pl.ds(0, 3)])

    def down_sum(j):
        total = m.gds[2 * a + j].astype(F32) + m.dland[j, 0].astype(F32)
        return total + m.dland[j, 1].astype(F32)

    m.dsum[0] = down_sum(1 - part).astype(BF16)
    far_copy = copy(m.dsum.at[0], m.dfar, s.gfd[0].at[0], s.gfd[1].at[0], (a, far))
    far_copy.start()
    finals.append(far_copy.wait_send)

    token_share = lambda zt: m.gts.at[zt, c]

    def token_line(zt):
        mine = token_grad(2 * zt + c)
        copy(
            m.gtr.at[zt], m.gtr.at[zt], s.gt[0].at[1], s.gt[1].at[4 + zt], (a, sib)
        ).wait_recv()
        m.gts[zt, c] = (mine + m.gtr[zt].astype(F32)).astype(BF16)

    def pass_token(zt, slot):
        m.gts[zt, c] = (m.gts[zt, c].astype(F32) + m.yrecv[slot].astype(F32)).astype(BF16)

    token_line(near + (1 - inside) * (across - near))

    @pl.when(inner_chip)
    def _():
        sum_near(s.gt, token_share, m.yrecv)

    @pl.when(jnp.logical_not(inner_chip))
    def _():
        sum_far(s.gt, token_share, m.yrecv, across, mirror, 1)

    token_line(mirror)

    @pl.when(jnp.logical_not(inner_chip))
    def _():
        sum_far(s.gt, token_share, m.yrecv, mirror, near, 2)

    token_line(across + (1 - inside) * (near - across))

    @pl.when(jnp.logical_not(inner_chip))
    def _():
        sum_near(s.gt, token_share, m.yrecv)

    m.own[...] = token_grad(b)
    finals.append(lambda: sent(s.gt[0].at[1], m.gtr))

    gos_copy.wait_recv()

    def out_add(k):
        i = lax.div(k, 4)
        j = lax.rem(k, 4)
        m.gwos[i, j, c] = (
            m.gwos[i, j, c].astype(F32) + m.gwor[i, j].astype(F32)
        ).astype(BF16)

    each(0, 16, out_add)
    out_x = lambda i: m.gwos.at[i, pl.ds(0, 2), c]
    out_y = lambda i: m.gwos.at[i, pl.ds(2, 2), c]
    oland_x = m.oland.at[:, pl.ds(0, 2)]
    oland_y = m.oland.at[:, pl.ds(2, 2)]
    fold_start(s.rox, out_x, m.opre.at[0], oland_x, ny)
    fold_start(s.roy, out_y, m.opre.at[1], oland_y, nx)

    sum_pass(s.gt, token_share, m.yrecv, pass_token)
    fold_pass(s.rwx, weight_x, m.wpre.at[0], land_x, fold_add(weight_x, m.wpre.at[0], 32), nx)
    fold_pass(s.rwy, weight_y, m.wpre.at[1], land_y, fold_add(weight_y, m.wpre.at[1], 32), ny)
    all_wait(s.fin1, m.fin1.at[pl.ds(0, 3)])
    m.fin2s[...] = (m.fin1[0] + m.fin1[1]) + (m.fin1[2] + m.fin1[3])
    m.fin2[b] = m.fin2s[32:48, :]
    seq_peers(lambda p: all_start(s.fin2, m.fin2s.at[pl.ds(32, 16), :], m.fin2.at[b], p))
    drain(s.fin2, m.fin2.at[pl.ds(0, 7)])
    holder = 2 * a + lax.div(b, 4)
    keeps = lambda p: (lax.div(b, 2) == a) & (lax.div(p, 4) == c)

    def pers_send(p):
        @pl.when(keeps(p))
        def _():
            copy(
                m.fin2s.at[pl.ds(0, 32), :], m.pers, s.pers[0].at[p], s.pers[1].at[0], (a, p)
            ).start()

    def pers_drain(p):
        @pl.when(keeps(p))
        def _():
            copy(m.pers, m.pers, s.pers[0].at[p], s.pers[1].at[0], (a, p)).wait_send()

    seq_peers(pers_send)
    finals.append(lambda: seq_peers(pers_drain))

    @pl.when(holder == b)
    def _():
        m.pers[...] = m.fin2s[0:32, :]

    fold_pass(s.rox, out_x, m.opre.at[0], oland_x, fold_add(out_x, m.opre.at[0], 1), nx)
    fold_pass(s.roy, out_y, m.opre.at[1], oland_y, fold_add(out_y, m.opre.at[1], 1), ny)
    fold_finish(s.rwx, land_x, m.gws.at[pl.ds(0, 3), pl.ds(0, 128), :])
    fold_finish(s.rwy, land_y, m.gws.at[pl.ds(0, 3), pl.ds(0, 128), :])

    def head_sum(p):
        rows = block_rows(p, 32)
        total = m.gws[a, rows, :].astype(F32) + m.wland[0, rows, :].astype(F32)
        m.gas[p] = (total + m.wland[1, rows, :].astype(F32)).astype(BF16)

    def head_sum_send(p):
        head_sum(p)
        all_start(s.gwa, m.gas.at[p], m.gar.at[b], p)

    seq_peers(head_sum_send)
    drain(s.gwa, m.gas.at[pl.ds(0, 7)])
    head_sum(b)
    m.gar[b] = m.gas[b]

    fold_finish(s.rox, oland_x, m.gwos.at[pl.ds(0, 3), pl.ds(0, 2), 0])
    fold_finish(s.roy, oland_y, m.gwos.at[pl.ds(0, 3), pl.ds(0, 2), 0])

    def out_sum(i):
        total = m.gwos[a, i, c].astype(F32) + m.oland[0, i].astype(F32)
        m.gos[i] = (total + m.oland[1, i].astype(F32)).astype(BF16)

    each(0, 4, out_sum)
    out_share = lambda zt: m.gos.at[zt]

    def pass_out(zt, slot):
        m.gos[zt] = (m.gos[zt].astype(F32) + m.goz[slot].astype(F32)).astype(BF16)

    sum_start(s.rgo, out_share, m.goz)
    own_half = down_sum(part)
    far_copy.wait_recv()
    fd_o[...] = own_half[0:share_rows, :] + m.dfar[0:share_rows, :].astype(F32)
    sum_pass(s.rgo, out_share, m.goz, pass_out)

    sum_finish(s.gt, m.yrecv, m.yrecv.at[pl.ds(0, 3)])
    copy(
        m.gtr.at[z], m.gtr.at[z], s.gt[0].at[1], s.gt[1].at[4 + z], (a, sib)
    ).wait_recv()

    def token_sum(i):
        rows = block_rows(i, 32)
        total = m.dout[rows, :] + m.own[rows, :]
        total = total + m.gtr[z, rows, :].astype(F32)
        gtok_o[rows, :] = total + landed(m.yrecv, (rows, slice(None)))

    each(0, 4, token_sum)

    all_wait(s.gwa, m.gar.at[pl.ds(0, 7)])
    gar_o[...] = m.gar[...]

    all_wait(s.gxg, m.gxr.at[pl.ds(0, 7), 0])
    all_wait(s.gxu, m.gxr.at[pl.ds(0, 7), 1])
    gux_o[...] = m.gxr[...]

    sum_finish(s.rgo, m.goz, m.goz.at[pl.ds(0, 3)])
    gwo_o[...] = m.gos[z].astype(F32) + landed(m.goz, ())

    all_wait(s.fin2, m.fin2.at[pl.ds(0, 7)])
    everything = jnp.sum(m.fin2[...], axis=0)
    fin_o[0:8, :] = everything[0:8, :]
    loss = jnp.sum(everything[8:9, :]) / (2.0 * width * valid_total)
    fin_o[8:16, :] = jnp.full((8, 128), loss, F32)

    @pl.when(holder != b)
    def _():
        copy(m.pers, m.pers, s.pers[0].at[0], s.pers[1].at[0], (a, holder)).wait_recv()

    pers_o[...] = m.pers[...]

    for last in finals:
        last()


def finish_kernel(
    width, hidden, out, gtok, gar, gwo, fin, pers, gux, fd,
    out_o, loss_o, gtok_o, gq_o, gk_o, gv_o, gwo_o, gwg_o, pk_o, pv_o, gain_o, fg_o, fu_o, fd_o,
):
    a = lax.axis_index("head")
    b = lax.axis_index("seq")
    quarter = lax.rem(b, 4)

    def lanes(value):
        picked = value[:, 0:32]
        for j in range(1, 4):
            picked = jnp.where(quarter == j, value[:, 32 * j : 32 * j + 32], picked)
        return picked

    out_o[...] = out[...]
    gtok_o[...] = gtok[...]
    gwo_o[...] = gwo[...]
    fd_o[...] = fd[...]
    loss_o[...] = fin[8:9, 0:1]
    pk_o[...] = lanes(pers[0:16, :])
    pv_o[...] = lanes(pers[16:32, :])
    gain_o[...] = lanes(fin[pl.ds(2 * a + lax.div(b, 4), 1), :])
    for head in range(8):
        cols = slice(head * 128, head * 128 + 128)
        gq_o[:, cols] = gar[head, :, 0:128].astype(F32)
        gk_o[:, cols] = gar[head, :, 128:256].astype(F32)
        gv_o[:, cols] = gar[head, :, 256:384].astype(F32)
        gwg_o[:, cols] = gar[head, :, 384:512].astype(F32)
    run = hidden // 8
    for place, target in enumerate((fg_o, fu_o)):
        for group in range(4):
            total = gux[group, place].astype(F32) + gux[group + 4, place].astype(F32)
            for i in range(8):
                start = run * (4 * i + group)
                target[:, start : start + run] = total[:, run * i : run * i + run]


def local_block(
    tokens, w_query, w_key, w_value, w_out, w_gate, persist_keys, persist_values, norm_gain,
    ff_gate, ff_up, ff_down, retention, doc_starts, valid, teacher,
):
    _, block, width = tokens.shape
    length = block * lax.axis_size("seq")
    hidden = ff_gate.shape[1] // 4
    pad = -(-hidden // 256) * 256
    share = ff_down.shape[0]
    table = scratch_table(width, block, hidden, pad, length)
    names = tuple(table)
    vmem = pl.BlockSpec(memory_space=pltpu.VMEM)
    shape = jax.ShapeDtypeStruct
    outs = (
        shape((block, width), BF16),
        shape((block, width), F32),
        shape((8, 32, 512), BF16),
        shape((32, width), F32),
        shape((16, 128), F32),
        shape((32, 128), F32),
        shape((8, 2, 32, pad), BF16),
        shape((share, width), F32),
    )
    scratch = [pltpu.VMEM(*table[name]) for name in names]
    for count in FLAGS.values():
        scratch += [pltpu.SemaphoreType.DMA((count,))] * 2
    result = pl.pallas_call(
        functools.partial(block_kernel, names, width, hidden, doc_starts.shape[1]),
        out_shape=outs,
        in_specs=[vmem] * 15 + [pl.BlockSpec(memory_space=pltpu.SMEM)],
        out_specs=[vmem] * len(outs),
        scratch_shapes=scratch,
        compiler_params=pltpu.CompilerParams(
            collective_id=0, has_side_effects=True, vmem_limit_bytes=VMEM_LIMIT
        ),
        name="block",
    )(
        tokens[0], w_query, w_key, w_value, w_out, w_gate, ff_gate, ff_up, ff_down, teacher[0],
        jnp.transpose(retention, (0, 2, 1)), persist_keys, persist_values, norm_gain[None],
        valid, doc_starts,
    )
    square = shape((32, width), F32)
    wide = shape((32, 4 * hidden), F32)
    finals = (
        outs[0], shape((1, 1), F32), outs[1], square, square, square, square, square,
        shape((P_SIZE, 32), F32), shape((P_SIZE, 32), F32), shape((1, 32), F32), wide, wide,
        outs[7],
    )
    done = pl.pallas_call(
        functools.partial(finish_kernel, width, hidden),
        out_shape=finals,
        in_specs=[vmem] * len(outs),
        out_specs=[vmem] * len(finals),
        name="finish",
    )(*result)
    (out, loss, gtok, gq, gk, gv, gwo, gwg, gpk, gpv, gain, fg, fu, fd) = done
    return (
        out[None], loss[0, 0], gtok[None], gq, gk, gv, gwo, gwg, gpk, gpv, gain[0], fg, fu, fd,
    )


VMEM_LIMIT = 62 << 20


def entering(value, axis, join, neutral, backward):
    count = lax.axis_size(axis)
    place = lax.axis_index(axis)
    ahead = count - 1 - place if backward else place
    gathered = jax.tree.map(
        lambda a, kind: lax.all_gather(a.astype(kind), axis), value, (jnp.bfloat16, jnp.bfloat16)
    )
    state = jax.tree.map(lambda a, e: jnp.zeros_like(a) + jnp.asarray(e, a.dtype), value, neutral)

    def one(hop, state):
        source = count - 1 - hop if backward else hop
        return join(
            state,
            jax.tree.map(
                lambda a, own: lax.dynamic_index_in_dim(a, source, 0, False).astype(own.dtype),
                gathered,
                value,
            ),
        )

    return lax.fori_loop(0, ahead, one, state)


def passed_along(value, axis, by):
    peers = lax.axis_size(axis)
    pairs = [(i, i + by) for i in range(peers) if 0 <= i + by < peers]
    return lax.ppermute(value, axis, pairs)


def from_behind(block, axis, distance):
    devices = range(lax.axis_size(axis))
    route = [((i - distance) % len(devices), i) for i in devices]
    return lax.ppermute(block, axis, route)


def product(left, right):
    return jnp.dot(left, right, preferred_element_type=jnp.float32)


def rows_outer(left, right):
    return jnp.einsum("nd,ne->de", left, right, preferred_element_type=jnp.float32)


def back_product(grad, weight):
    return jnp.einsum("ne,de->nd", grad, weight, preferred_element_type=jnp.float32)


def doc_index(starts, positions):
    return jnp.sum((starts[:, None, :] <= positions[None, :, None]).astype(jnp.int32), axis=-1) - 1


def doc_begin(starts, positions):
    return jnp.any(starts[:, None, :] == positions[None, :, None], axis=-1)


def chain_forward(earlier, later):
    return (earlier[0] * later[0], later[0][..., None, None] * earlier[1] + later[1])


def chain_backward(earlier, later):
    return (earlier[0] * later[0], later[1] + later[0][..., None, None] * earlier[1])


def masked_scores(query_rows, key_rows, query_pos, key_pos, query_seg, key_seg, scale):
    raw = (
        jnp.einsum("sqhd,skhd->sqhk", query_rows, key_rows, preferred_element_type=jnp.float32)
        * scale
    )
    allowed = (key_pos[None, None, :] <= query_pos[None, :, None]) & (
        key_seg[:, None, :] == query_seg[:, :, None]
    )
    return jnp.where(allowed[:, :, None, :], raw, MASKED)


def softmax_grads(
    query_rows,
    key_rows,
    value_rows,
    dout_rows,
    query_pos,
    key_pos,
    query_seg,
    key_seg,
    query_lse,
    query_delta,
    scale,
):
    scores = masked_scores(query_rows, key_rows, query_pos, key_pos, query_seg, key_seg, scale)
    probs = jnp.exp(scores - query_lse[..., None])
    prob_grad = jnp.einsum(
        "sqhd,skhd->sqhk", dout_rows, value_rows, preferred_element_type=jnp.float32
    )
    score_grad = (probs * (prob_grad - query_delta[..., None])).astype(jnp.bfloat16)
    return (probs.astype(jnp.bfloat16), score_grad)


def local(
    tokens,
    w_query,
    w_key,
    w_value,
    w_out,
    w_gate,
    persist_keys,
    persist_values,
    norm_gain,
    ff_gate,
    ff_up,
    ff_down,
    retention,
    doc_starts,
    valid,
    teacher,
):
    gathered = (
        lax.all_gather(w_query, ("head", "seq"), axis=0, tiled=True),
        lax.all_gather(w_key, ("head", "seq"), axis=0, tiled=True),
        lax.all_gather(w_value, ("head", "seq"), axis=0, tiled=True),
        lax.all_gather(w_out, ("head", "seq"), axis=0, tiled=True),
        lax.all_gather(w_gate, ("head", "seq"), axis=0, tiled=True),
        lax.all_gather(jnp.transpose(persist_keys), ("head", "seq"), axis=0, tiled=True),
        lax.all_gather(jnp.transpose(persist_values), ("head", "seq"), axis=0, tiled=True),
        lax.all_gather(norm_gain, ("head", "seq"), axis=0, tiled=True),
        lax.all_gather(ff_gate, ("head", "seq"), axis=0, tiled=True),
        lax.all_gather(ff_up, ("head", "seq"), axis=0, tiled=True),
        lax.all_gather(ff_down, ("head", "seq"), axis=0, tiled=True),
    )
    (
        query_weight,
        key_weight,
        value_weight,
        out_weight,
        gate_weight,
        fixed_key_cols,
        fixed_value_cols,
        gain_weight,
        ffn_gate,
        ffn_up,
        ffn_down,
    ) = gathered
    fixed_key_all = jnp.transpose(fixed_key_cols)
    fixed_value_all = jnp.transpose(fixed_value_cols)
    local_seqs, block, width = tokens.shape
    groups = lax.axis_size("head")
    heads = HEAD_COUNT // groups
    head_place = lax.axis_index("head")
    seq_place = lax.axis_index("seq")
    seq_count = lax.axis_size("seq")
    all_seqs = local_seqs * groups
    length = block * seq_count
    token_count = local_seqs * block
    scale = HD ** (-0.5)
    mem_scale = 0.125 / HD
    token_rows = tokens.reshape(token_count, width)
    query_tok = (
        product(token_rows, query_weight)
        .astype(jnp.bfloat16)
        .reshape(local_seqs, block, HEAD_COUNT, HD)
    )
    key_tok = (
        product(token_rows, key_weight)
        .astype(jnp.bfloat16)
        .reshape(local_seqs, block, HEAD_COUNT, HD)
    )
    value_tok = (
        product(token_rows, value_weight)
        .astype(jnp.bfloat16)
        .reshape(local_seqs, block, HEAD_COUNT, HD)
    )
    gate_pre = product(token_rows, gate_weight)
    query_heads, key_heads, value_heads = (
        lax.all_to_all(query_tok, "head", split_axis=2, concat_axis=0, tiled=True),
        lax.all_to_all(key_tok, "head", split_axis=2, concat_axis=0, tiled=True),
        lax.all_to_all(value_tok, "head", split_axis=2, concat_axis=0, tiled=True),
    )
    fixed_keys = lax.dynamic_slice_in_dim(
        fixed_key_all.reshape(P_SIZE, HEAD_COUNT, HD), head_place * heads, heads, 1
    )
    fixed_values = lax.dynamic_slice_in_dim(
        fixed_value_all.reshape(P_SIZE, HEAD_COUNT, HD), head_place * heads, heads, 1
    )
    own_start = seq_place * block
    own_pos = own_start + jnp.arange(block, dtype=jnp.int32)
    own_seg = doc_index(doc_starts, own_pos)
    own_begin = doc_begin(doc_starts, own_pos)
    last_row = own_start + block - 1
    fixed_scores = (
        jnp.einsum("sqhd,phd->sqhp", query_heads, fixed_keys, preferred_element_type=jnp.float32)
        * scale
    )
    top_start = jnp.max(fixed_scores, axis=-1)
    fixed_exp = jnp.exp(fixed_scores - top_start[..., None])
    acc_start = jnp.einsum(
        "sqhp,phd->sqhd",
        fixed_exp.astype(jnp.bfloat16),
        fixed_values,
        preferred_element_type=jnp.float32,
    )
    key_rows = lax.all_gather(key_heads, "seq", axis=1, tiled=True)
    value_rows = lax.all_gather(value_heads, "seq", axis=1, tiled=True)
    piece_keys = key_rows.shape[1]

    def attend_compute(state):
        running_top, running_total, running_acc = state
        key_pos = jnp.arange(piece_keys, dtype=jnp.int32)
        scores = masked_scores(
            query_heads, key_rows, own_pos, key_pos, own_seg, doc_index(doc_starts, key_pos), scale
        )
        new_top = jnp.maximum(running_top, jnp.max(scores, axis=-1))
        shrink = jnp.exp(running_top - new_top)
        weights_exp = jnp.exp(scores - new_top[..., None])
        new_total = running_total * shrink + jnp.sum(weights_exp, axis=-1)
        new_acc = running_acc * shrink[..., None] + jnp.einsum(
            "sqhk,skhd->sqhd",
            weights_exp.astype(jnp.bfloat16),
            value_rows,
            preferred_element_type=jnp.float32,
        )
        return (new_top, new_total, new_acc)

    final_top, final_total, final_acc = lax.cond(
        jnp.int32(0) <= last_row,
        attend_compute,
        lambda state: state,
        (top_start, jnp.sum(fixed_exp, axis=-1), acc_start),
    )
    attn_rows = final_acc / final_total[..., None]
    lse = final_top + jnp.log(final_total)
    log_retention = jnp.log(retention)
    running = jnp.cumsum(log_retention, axis=1)
    lane = jnp.transpose(running, (0, 2, 1))
    index = jnp.arange(block)
    linked = (index[None, :] <= index[:, None])[None] & (own_seg[:, None, :] == own_seg[:, :, None])
    decay = jnp.where(
        linked[:, None], jnp.exp(jnp.minimum(lane[:, :, :, None] - lane[:, :, None, :], 0.0)), 0.0
    )
    intersection = jnp.einsum(
        "sthd,suhd->shtu", query_heads, key_heads, preferred_element_type=jnp.float32
    )
    mixing = (mem_scale * intersection * decay).astype(jnp.bfloat16)
    inner_mem = jnp.einsum(
        "shtu,suhd->sthd", mixing, value_heads, preferred_element_type=jnp.float32
    )
    carried = ((own_seg == own_seg[:, :1]) & jnp.logical_not(own_begin[:, :1])).astype(jnp.float32)
    lead = jnp.exp(running) * carried[..., None]
    trail = jnp.where(
        (own_seg == own_seg[:, -1:])[..., None], jnp.exp(running[:, -1:, :] - running), 0.0
    )
    query_full = query_heads.astype(jnp.float32)
    key_full = key_heads.astype(jnp.float32)
    value_full = value_heads.astype(jnp.float32)
    block_state = jnp.einsum(
        "suhd,suhe->shde", key_full * trail[..., None], value_full, precision=HIGHEST
    )
    block_keep = lead[:, -1, :]
    identity = (jnp.ones_like(block_keep), jnp.zeros_like(block_state))
    chained = entering((block_keep, block_state), "seq", chain_forward, identity, False)
    state_in = chained[1]
    outer_mem = (
        mem_scale
        * lead[..., None]
        * jnp.einsum("sthd,shde->sthe", query_full, state_in, precision=HIGHEST)
    )
    mixed_heads = (attn_rows + inner_mem + outer_mem).astype(jnp.bfloat16)
    mixed_rows = lax.all_to_all(
        mixed_heads, "head", split_axis=0, concat_axis=2, tiled=True
    ).reshape(token_count, width)
    branch = product(mixed_rows, out_weight)
    gate_sigmoid = jax.nn.sigmoid(gate_pre)
    hidden = token_rows.astype(jnp.float32) + gate_sigmoid * branch
    inv_rms = lax.rsqrt(jnp.mean(hidden * hidden, axis=-1, keepdims=True) + EPSILON)
    normed = hidden * inv_rms
    gain_full = gain_weight.astype(jnp.float32)
    scaled = (normed * gain_full).astype(jnp.bfloat16)
    gate_act = product(scaled, ffn_gate)
    up_act = product(scaled, ffn_up)
    act_sigmoid = jax.nn.sigmoid(gate_act)
    silu_act = gate_act * act_sigmoid
    inner = (silu_act * up_act).astype(jnp.bfloat16)
    final = hidden + product(inner, ffn_down)
    output = final.astype(jnp.bfloat16).reshape(local_seqs, block, width)
    valid_rows = valid.reshape(token_count).astype(jnp.float32)
    error = final - teacher.reshape(token_count, width).astype(jnp.float32)
    sums = lax.psum(
        (jnp.sum(valid_rows * jnp.sum(error * error, axis=-1)), jnp.sum(valid_rows)),
        ("head", "seq"),
    )
    loss = sums[0] / (2.0 * width * sums[1])
    total_tokens = all_seqs * length
    d_out = valid_rows[:, None] * error * (total_tokens / sums[1])
    d_ffn = d_out.astype(jnp.bfloat16)
    grad_down = rows_outer(inner, d_ffn)
    d_inner = back_product(d_ffn, ffn_down)
    d_gate_act = (d_inner * up_act * act_sigmoid * (1.0 + gate_act * (1.0 - act_sigmoid))).astype(
        jnp.bfloat16
    )
    d_up_act = (d_inner * silu_act).astype(jnp.bfloat16)
    grad_ffn_gate = rows_outer(scaled, d_gate_act)
    grad_ffn_up = rows_outer(scaled, d_up_act)
    d_scaled = back_product(d_gate_act, ffn_gate) + back_product(d_up_act, ffn_up)
    grad_gain = jnp.sum(d_scaled * normed, axis=0)
    d_normed = d_scaled * gain_full
    d_hidden = d_out + inv_rms * (
        d_normed - normed * jnp.mean(d_normed * normed, axis=-1, keepdims=True)
    )
    d_branch = (d_hidden * gate_sigmoid).astype(jnp.bfloat16)
    d_gate = (d_hidden * branch * gate_sigmoid * (1.0 - gate_sigmoid)).astype(jnp.bfloat16)
    grad_out_weight = rows_outer(mixed_rows, d_branch)
    grad_gate_weight = rows_outer(token_rows, d_gate)
    d_mixed = (
        back_product(d_branch, out_weight)
        .astype(jnp.bfloat16)
        .reshape(local_seqs, block, HEAD_COUNT, HD)
    )
    dout_heads = lax.all_to_all(d_mixed, "head", split_axis=2, concat_axis=0, tiled=True)
    dout_full = dout_heads.astype(jnp.float32)
    delta = jnp.sum(dout_full * attn_rows, axis=-1)
    fixed_probs = jnp.exp(fixed_scores - lse[..., None])
    fixed_prob_grad = jnp.einsum(
        "sqhd,phd->sqhp", dout_heads, fixed_values, preferred_element_type=jnp.float32
    )
    fixed_score_grad = (fixed_probs * (fixed_prob_grad - delta[..., None])).astype(jnp.bfloat16)
    fixed_key_grad = (
        jnp.einsum(
            "sqhp,sqhd->phd", fixed_score_grad, query_heads, preferred_element_type=jnp.float32
        )
        * scale
    )
    fixed_value_grad = jnp.einsum(
        "sqhp,sqhd->phd",
        fixed_probs.astype(jnp.bfloat16),
        dout_heads,
        preferred_element_type=jnp.float32,
    )
    query_grad_start = (
        jnp.einsum(
            "sqhp,phd->sqhd", fixed_score_grad, fixed_keys, preferred_element_type=jnp.float32
        )
        * scale
    )
    fold_start = (query_grad_start,)
    back_key_rows = lax.all_gather(key_heads, "seq", axis=1, tiled=True)
    back_value_rows = lax.all_gather(value_heads, "seq", axis=1, tiled=True)
    back_piece_keys = back_key_rows.shape[1]

    def back_compute(state):
        key_pos = jnp.arange(back_piece_keys, dtype=jnp.int32)
        probs_low, score_grad = softmax_grads(
            query_heads,
            back_key_rows,
            back_value_rows,
            dout_heads,
            own_pos,
            key_pos,
            own_seg,
            doc_index(doc_starts, key_pos),
            lse,
            delta,
            scale,
        )
        query_grad = (
            state[0]
            + jnp.einsum(
                "sqhk,skhd->sqhd", score_grad, back_key_rows, preferred_element_type=jnp.float32
            )
            * scale
        )
        return (query_grad,)

    folded = lax.cond(jnp.int32(0) <= last_row, back_compute, lambda state: state, fold_start)
    query_att = folded[0]
    empty_local = jnp.zeros((all_seqs, block, heads, HD), jnp.float32)

    def visit(turn, state):
        key_rows, value_rows, key_acc, value_acc = state
        owner = (seq_place - turn) % seq_count
        start = owner * block

        def visit_compute(accs):
            key_pos = start + jnp.arange(block, dtype=jnp.int32)
            probs_low, score_grad = softmax_grads(
                query_heads,
                key_rows,
                value_rows,
                dout_heads,
                own_pos,
                key_pos,
                own_seg,
                doc_index(doc_starts, key_pos),
                lse,
                delta,
                scale,
            )
            key_next = (
                accs[0]
                + jnp.einsum(
                    "sqhk,sqhd->skhd", score_grad, query_heads, preferred_element_type=jnp.float32
                )
                * scale
            )
            value_next = accs[1] + jnp.einsum(
                "sqhk,sqhd->skhd", probs_low, dout_heads, preferred_element_type=jnp.float32
            )
            return (key_next, value_next)

        key_acc, value_acc = lax.cond(
            start <= last_row, visit_compute, lambda accs: accs, (key_acc, value_acc)
        )
        key_rows, value_rows = passed_along((key_rows, value_rows), "seq", 1)
        key_acc, value_acc = (
            from_behind(key_acc.astype(jnp.bfloat16), "seq", 1).astype(key_acc.dtype),
            from_behind(value_acc.astype(jnp.bfloat16), "seq", 1).astype(value_acc.dtype),
        )
        return (key_rows, value_rows, key_acc, value_acc)

    travelled = lax.fori_loop(
        0, seq_count, visit, (key_heads, value_heads, empty_local, empty_local)
    )
    key_att = travelled[2]
    value_att = travelled[3]
    mix_grad_raw = jnp.einsum(
        "sthe,suhe->shtu", dout_heads, value_heads, preferred_element_type=jnp.float32
    )
    intersection_grad = (mem_scale * mix_grad_raw * decay).astype(jnp.bfloat16)
    local_grad = mem_scale * jnp.einsum(
        "sthd,sthe->shde", query_full * lead[..., None], dout_full, precision=HIGHEST
    )
    state_grads = entering((block_keep, local_grad), "seq", chain_backward, identity, True)
    carry_grad = state_grads[1]
    query_mem = jnp.einsum(
        "shtu,suhd->sthd", intersection_grad, key_heads, preferred_element_type=jnp.float32
    )
    query_mem = query_mem + mem_scale * lead[..., None] * jnp.einsum(
        "sthe,shde->sthd", dout_full, state_in, precision=HIGHEST
    )
    key_mem = jnp.einsum(
        "shtu,sthd->suhd", intersection_grad, query_heads, preferred_element_type=jnp.float32
    )
    key_mem = key_mem + trail[..., None] * jnp.einsum(
        "suhe,shde->suhd", value_full, carry_grad, precision=HIGHEST
    )
    value_mem = jnp.einsum(
        "shtu,sthe->suhe", mixing, dout_heads, preferred_element_type=jnp.float32
    )
    value_mem = value_mem + jnp.einsum(
        "suhd,shde->suhe", key_full * trail[..., None], carry_grad, precision=HIGHEST
    )
    query_grad_heads = (query_att + query_mem).astype(jnp.bfloat16)
    key_grad_heads = (key_att + key_mem).astype(jnp.bfloat16)
    value_grad_heads = (value_att + value_mem).astype(jnp.bfloat16)
    query_back, key_back, value_back = (
        lax.all_to_all(query_grad_heads, "head", split_axis=0, concat_axis=2, tiled=True),
        lax.all_to_all(key_grad_heads, "head", split_axis=0, concat_axis=2, tiled=True),
        lax.all_to_all(value_grad_heads, "head", split_axis=0, concat_axis=2, tiled=True),
    )
    query_back = query_back.reshape(token_count, width)
    key_back = key_back.reshape(token_count, width)
    value_back = value_back.reshape(token_count, width)
    grad_query_weight = rows_outer(token_rows, query_back)
    grad_key_weight = rows_outer(token_rows, key_back)
    grad_value_weight = rows_outer(token_rows, value_back)
    token_grad = (
        d_hidden + back_product(d_gate, gate_weight) + back_product(query_back, query_weight)
    )
    token_grad = (
        token_grad + back_product(key_back, key_weight) + back_product(value_back, value_weight)
    )
    fixed_key_full = lax.dynamic_update_slice_in_dim(
        jnp.zeros((P_SIZE, HEAD_COUNT, HD), jnp.float32), fixed_key_grad, head_place * heads, 1
    ).reshape(P_SIZE, width)
    fixed_value_full = lax.dynamic_update_slice_in_dim(
        jnp.zeros((P_SIZE, HEAD_COUNT, HD), jnp.float32), fixed_value_grad, head_place * heads, 1
    ).reshape(P_SIZE, width)
    shards = (
        lax.psum_scatter(grad_query_weight, ("head", "seq"), scatter_dimension=0, tiled=True),
        lax.psum_scatter(grad_key_weight, ("head", "seq"), scatter_dimension=0, tiled=True),
        lax.psum_scatter(grad_value_weight, ("head", "seq"), scatter_dimension=0, tiled=True),
        lax.psum_scatter(grad_out_weight, ("head", "seq"), scatter_dimension=0, tiled=True),
        lax.psum_scatter(grad_gate_weight, ("head", "seq"), scatter_dimension=0, tiled=True),
        lax.psum_scatter(
            jnp.transpose(fixed_key_full), ("head", "seq"), scatter_dimension=0, tiled=True
        ),
        lax.psum_scatter(
            jnp.transpose(fixed_value_full), ("head", "seq"), scatter_dimension=0, tiled=True
        ),
        lax.psum_scatter(grad_gain, ("head", "seq"), scatter_dimension=0, tiled=True),
        lax.psum_scatter(grad_ffn_gate, ("head", "seq"), scatter_dimension=0, tiled=True),
        lax.psum_scatter(grad_ffn_up, ("head", "seq"), scatter_dimension=0, tiled=True),
        lax.psum_scatter(grad_down, ("head", "seq"), scatter_dimension=0, tiled=True),
    )
    return (
        output,
        loss,
        token_grad.reshape(local_seqs, block, width),
        shards[0],
        shards[1],
        shards[2],
        shards[3],
        shards[4],
        jnp.transpose(shards[5]),
        jnp.transpose(shards[6]),
        shards[7],
        shards[8],
        shards[9],
        shards[10],
    )


def solution(mesh):
    in_specs = (
        P("head", "seq", None),
        P(("head", "seq"), None),
        P(("head", "seq"), None),
        P(("head", "seq"), None),
        P(("head", "seq"), None),
        P(("head", "seq"), None),
        P(None, ("head", "seq")),
        P(None, ("head", "seq")),
        P(("head", "seq")),
        P(("head", "seq"), None),
        P(("head", "seq"), None),
        P(("head", "seq"), None),
        P(None, "seq", "head"),
        P(),
        P("head", "seq"),
        P("head", "seq", None),
    )
    out_specs = (
        P("head", "seq", None),
        P(),
        P("head", "seq", None),
        P(("head", "seq"), None),
        P(("head", "seq"), None),
        P(("head", "seq"), None),
        P(("head", "seq"), None),
        P(("head", "seq"), None),
        P(None, ("head", "seq")),
        P(None, ("head", "seq")),
        P(("head", "seq")),
        P(("head", "seq"), None),
        P(("head", "seq"), None),
        P(("head", "seq"), None),
    )
    fits = mesh.shape["head"] == 4 and mesh.shape["seq"] == HEAD_COUNT
    body = local_block if fits else local
    return jax.shard_map(body, mesh=mesh, in_specs=in_specs, out_specs=out_specs, check_vma=False)
```
